32 devices in a mesh: seq: 4 (over y, x), mp: 8 (over z, core).
Axes of the slice: x: 2, y: 2, z: 4, core: 2. Of those that a mesh axis runs over, the one named last changes fastest.
Arguments:
- hidden: bfloat16 [2, 4096, 2048], P(None, ('seq', 'mp')), may hold values from -6 to 6
- cotangent: bfloat16 [2, 4096, 2048], P(None, ('seq', 'mp')), may hold values from -6 to 6
- lengths: int32 [2], replicated, may hold values from 1024 to 4096, as said below
- gain_mix: float32 [2048], replicated, may hold values from 0.5 to 1.5
- gain_mlp: float32 [2048], replicated, may hold values from 0.5 to 1.5
- conv_weight: float32 [3, 2048], replicated, may hold values from -3 to 3
- mixer_in: bfloat16 [3, 2048, 2048], P(None, 'seq', 'mp'), may hold values from -0.125 to 0.125
- mixer_out: bfloat16 [2048, 2048], P('mp', 'seq'), may hold values from -0.125 to 0.125
- gate_up: bfloat16 [2, 2048, 8192], P(None, 'seq', 'mp'), may hold values from -0.125 to 0.125
- mlp_down: bfloat16 [8192, 2048], P('mp', 'seq'), may hold values from -0.0625 to 0.0625
Outputs:
- output: bfloat16 [2, 4096, 2048], P(None, ('seq', 'mp'))
- grad_hidden: float32 [2, 4096, 2048], P(None, ('seq', 'mp'))
- grad_gain_mix: float32 [2048], replicated
- grad_gain_mlp: float32 [2048], replicated
- grad_conv: float32 [3, 2048], replicated
- grad_mixer_in: float32 [3, 2048, 2048], P(None, 'seq', 'mp')
- grad_mixer_out: float32 [2048, 2048], P('mp', 'seq')
- grad_gate_up: float32 [2, 2048, 8192], P(None, 'seq', 'mp')
- grad_mlp_down: float32 [8192, 2048], P('mp', 'seq')
The draws below stay inside these ranges and needn't reach their ends.
Inputs may be any that keep to these rules, and one draw needn't show every extreme that they name: `lengths`: each slot's valid tokens are its first positions; in every draw one slot, which one drawn from the seed, is valid over all 4096 positions.
All inputs are finite; a program needn't handle non-finite values.
Results may differ from the reference program's by a relative error of at most 0.012.
Values may be sent and summed in bfloat16 or wider, within the bound.
A program may use at most 192 MiB of HBM per device.

```python
import jax
import jax.numpy as jnp
from jax import lax

D = 2048
FF = 8192
KSIZE = 3
SLOTS = 2
MIN_LEN = 1024
SLOT_LEN = 4096


def draw_lengths(key, part):
    key = jax.random.fold_in(key, 11)
    full_key, other_key = jax.random.split(key)
    longest = jax.random.randint(full_key, (), 0, SLOTS)
    drawn = jax.random.randint(other_key, (SLOTS,), MIN_LEN, SLOT_LEN + 1)
    return jnp.where(jnp.arange(SLOTS) == longest, SLOT_LEN, drawn).astype(jnp.int32)


def level_of(own_key, dims, cuts, least, top_value):
    loudness, own = 1.0, jax.random.fold_in(own_key, 6)
    for dim, blocks in cuts:
        steps = jnp.exp(jax.random.uniform(jax.random.fold_in(own, dim), (blocks,), jnp.float32, least / len(cuts), top_value / len(cuts)))
        loudness = loudness * jnp.repeat(steps, dims[dim] // blocks).reshape([-1 if axis == dim else 1 for axis in range(len(dims))])
    return loudness


def gaussian(rng, shape, spread, bound, cuts=(), kind=jnp.bfloat16):
    loudness = level_of(rng, shape, cuts, -0.22, 0.18) if cuts else 1.0
    values = jax.random.normal(rng, shape, jnp.float32) * spread * loudness
    return jnp.minimum(jnp.maximum(values, -bound), bound).astype(kind)


def setup_inputs(seed: int = 0) -> dict:
    splits = jax.random.split(jax.random.key(seed), 11)
    hidden = gaussian(splits[0], (SLOTS, SLOT_LEN, D), 1.0, 6.0, ((1, 32),))
    cotangent = gaussian(splits[1], (SLOTS, SLOT_LEN, D), 1.0, 6.0, ((1, 32),))
    lengths = draw_lengths(jax.random.fold_in(splits[10], 71), 0)
    gain_mix = jnp.clip(1.0 + 0.1 * jax.random.normal(splits[3], (D,), jnp.float32), 0.5, 1.5)
    gain_mlp = jnp.clip(1.0 + 0.1 * jax.random.normal(splits[4], (D,), jnp.float32), 0.5, 1.5)
    conv_weight = gaussian(splits[5], (KSIZE, D), 0.5, 3.0, (), jnp.float32)
    mixer_in = gaussian(splits[6], (3, D, D), D ** -0.5, 0.125, ((1, 4), (2, 8)))
    mixer_out = gaussian(splits[7], (D, D), D ** -0.5, 0.125, ((0, 8), (1, 4)))
    gate_up = gaussian(splits[8], (2, D, FF), D ** -0.5, 0.125, ((1, 4), (2, 8)))
    mlp_down = gaussian(splits[9], (FF, D), FF ** -0.5, 0.0625, ((0, 8), (1, 4)))
    return {"hidden": hidden, "cotangent": cotangent, "lengths": lengths, "gain_mix": gain_mix, "gain_mlp": gain_mlp, "conv_weight": conv_weight, "mixer_in": mixer_in, "mixer_out": mixer_out, "gate_up": gate_up, "mlp_down": mlp_down}


EPS = 1e-05
HIGH = lax.Precision.HIGHEST

@jax.custom_vjp
def low(v):
    return lax.optimization_barrier(v.astype(jnp.bfloat16)).astype(jnp.float32)

@jax.custom_vjp
def low_back(v):
    return v

def low_keep(v):
    return (low(v), None)

def low_pass(kept, grad):
    return (grad,)

def back_keep(v):
    return (v, None)

def back_low(kept, grad):
    return (low(grad),)
low.defvjp(low_keep, low_pass)
low_back.defvjp(back_keep, back_low)

def normalize(values, gain):
    return values * lax.rsqrt(lax.optimization_barrier(jnp.mean(values * values, axis=-1, keepdims=True)) + EPS) * gain

def block(source, gain_mix, gain_mlp, conv_weight, mixer_in, mixer_out, gate_up, mlp_down, mask):
    normed_mix = low(normalize(source, gain_mix))
    projected = low_back(jnp.einsum('td,kdc->ktc', normed_mix, mixer_in, precision=HIGH))
    product = projected[0] * projected[2]
    padded = jnp.pad(product, ((KSIZE - 1, 0), (0, 0)))
    conv_out = jnp.zeros_like(product)
    for offset in range(KSIZE):
        conv_out = conv_out + conv_weight[offset] * padded[KSIZE - 1 - offset:KSIZE - 1 - offset + SLOT_LEN]
    mixed = low(projected[1] * conv_out)
    mix_out = low_back(jnp.dot(mixed, mixer_out, precision=HIGH))
    middle = source + mix_out
    normed_mlp = low(normalize(middle, gain_mlp))
    gated = low_back(jnp.einsum('td,kdf->ktf', normed_mlp, gate_up, precision=HIGH))
    activation = low(jax.nn.silu(gated[0]) * gated[1])
    mlp_out = low_back(jnp.dot(activation, mlp_down, precision=HIGH))
    return mask[:, None] * (middle + mlp_out)

def reference(hidden, cotangent, lengths, gain_mix, gain_mlp, conv_weight, mixer_in, mixer_out, gate_up, mlp_down):
    params = (gain_mix.astype(jnp.float32), gain_mlp.astype(jnp.float32), conv_weight.astype(jnp.float32), mixer_in.astype(jnp.float32), mixer_out.astype(jnp.float32), gate_up.astype(jnp.float32), mlp_down.astype(jnp.float32))

    def one_slot(totals, items):
        source, arriving, length = items
        mask = (jnp.arange(SLOT_LEN) < length).astype(jnp.float32)

        def forward(src, *weights):
            return block(src, *weights, mask)
        result, pull = jax.vjp(forward, source.astype(jnp.float32), *params)
        grads = pull(arriving.astype(jnp.float32))
        totals = tuple((total + grad for total, grad in zip(totals, grads[1:])))
        return (totals, (result.astype(jnp.bfloat16), grads[0]))
    start = tuple((jnp.zeros(param.shape, jnp.float32) for param in params))
    totals, (output, grad_hidden) = lax.scan(one_slot, start, (hidden, cotangent, lengths))
    return (output, grad_hidden, totals[0], totals[1], totals[2], totals[3], totals[4], totals[5], totals[6])
```

```python
import jax
import jax.numpy as jnp
from jax import lax
from jax.sharding import PartitionSpec as P

EPS = 1e-05


def shifted(value, axis, steps):
    count = lax.axis_size(axis)
    leading, last = (max(0, -steps), min(count, count - steps))
    return lax.ppermute(value, axis, [(source, source + steps) for source in range(leading, last)])


def scatter_sum(value, axis, dim):
    low = value.astype(jnp.bfloat16)
    return lax.psum_scatter(low, axis, scatter_dimension=dim, tiled=True).astype(jnp.float32)


def normalize(values, gain):
    scale = lax.rsqrt(jnp.mean(values * values, axis=-1, keepdims=True) + EPS)
    return (values * scale * gain, scale)


def norm_back(grad, values, scale, gain):
    unit = values * scale
    scaled = grad * gain
    gain_grad = jnp.sum(grad * unit, axis=0)
    input_grad = scale * (scaled - unit * jnp.mean(scaled * unit, axis=-1, keepdims=True))
    return (input_grad, gain_grad)


def local(
    hidden,
    cotangent,
    lengths,
    gain_mix,
    gain_mlp,
    conv_weight,
    mixer_in,
    mixer_out,
    gate_up,
    mlp_down,
):
    model_count = lax.axis_size("mp")
    seq_pos = lax.axis_index("seq")
    model_pos = lax.axis_index("mp")
    share_rows = hidden.shape[1]
    block_rows = share_rows * model_count
    channels = mixer_in.shape[2]
    width = hidden.shape[2]
    units = gate_up.shape[2]
    taps = conv_weight.shape[0]
    local_taps = lax.dynamic_slice_in_dim(conv_weight, model_pos * channels, channels, 1)
    share_start = (seq_pos * model_count + model_pos) * share_rows
    share_pos = share_start + jnp.arange(share_rows, dtype=jnp.int32)
    in_total = jnp.zeros((3, width, channels), jnp.float32)
    out_total = jnp.zeros((channels, width), jnp.float32)
    pair_total = jnp.zeros((2, width, units), jnp.float32)
    down_total = jnp.zeros((units, width), jnp.float32)
    gain_mix_total = jnp.zeros((width,), jnp.float32)
    gain_mlp_total = jnp.zeros((width,), jnp.float32)
    taps_total = jnp.zeros((taps, channels), jnp.float32)
    outputs = []
    input_grads = []
    for slot_index in range(hidden.shape[0]):
        in_full, out_full, pair_full, down_full = (
            lax.all_gather(mixer_in, "seq", axis=1, tiled=True),
            lax.all_gather(mixer_out, "seq", axis=1, tiled=True),
            lax.all_gather(gate_up, "seq", axis=1, tiled=True),
            lax.all_gather(mlp_down, "seq", axis=1, tiled=True),
        )
        mask_rows = (share_pos < lengths[slot_index]).astype(jnp.float32)[:, None]
        source = hidden[slot_index].astype(jnp.float32)
        normed, scale_mix = normalize(source, gain_mix)
        normed_rows = lax.all_gather(normed.astype(jnp.bfloat16), "mp", axis=0, tiled=True)
        projected = jnp.einsum(
            "td,kdc->ktc", normed_rows, in_full, preferred_element_type=jnp.float32
        )
        b_gate = projected[0]
        c_gate = projected[1]
        x_value = projected[2]
        product = b_gate * x_value
        earlier = shifted(product[block_rows - (taps - 1) :], "seq", 1)
        extended = jnp.concatenate([earlier, product], axis=0)
        conv_out = jnp.zeros_like(product)
        for offset in range(taps):
            conv_out = (
                conv_out
                + local_taps[offset] * extended[taps - 1 - offset : taps - 1 - offset + block_rows]
            )
        mixed = (c_gate * conv_out).astype(jnp.bfloat16)
        mix_share = scatter_sum(
            jnp.dot(mixed, out_full, preferred_element_type=jnp.float32),
            "mp",
             0,
        )
        middle = source + mix_share
        normed_two, scale_mlp = normalize(middle, gain_mlp)
        mlp_rows = lax.all_gather(normed_two.astype(jnp.bfloat16), "mp", axis=0, tiled=True)
        gated = jnp.einsum("td,kdf->ktf", mlp_rows, pair_full, preferred_element_type=jnp.float32)
        gate_part = gated[0]
        up_part = gated[1]
        activated = jax.nn.silu(gate_part)
        hidden_act = (activated * up_part).astype(jnp.bfloat16)
        mlp_share = scatter_sum(
            jnp.dot(hidden_act, down_full, preferred_element_type=jnp.float32),
            "mp",
             0,
        )
        outputs.append((mask_rows * (middle + mlp_share)).astype(jnp.bfloat16))
        in_back, out_back, pair_back, down_back = (
            lax.all_gather(mixer_in, "seq", axis=1, tiled=True),
            lax.all_gather(mixer_out, "seq", axis=1, tiled=True),
            lax.all_gather(gate_up, "seq", axis=1, tiled=True),
            lax.all_gather(mlp_down, "seq", axis=1, tiled=True),
        )
        top_grad = cotangent[slot_index].astype(jnp.float32) * mask_rows
        top_rows = lax.all_gather(top_grad.astype(jnp.bfloat16), "mp", axis=0, tiled=True)
        down_total = down_total + jnp.einsum(
            "tf,td->fd", hidden_act, top_rows, preferred_element_type=jnp.float32
        )
        act_grad = jnp.einsum("td,fd->tf", top_rows, down_back, preferred_element_type=jnp.float32)
        sigma = jax.nn.sigmoid(gate_part)
        gate_grad = (act_grad * up_part * sigma * (1.0 + gate_part * (1.0 - sigma))).astype(
            jnp.bfloat16
        )
        up_grad = (act_grad * activated).astype(jnp.bfloat16)
        pair_grad = jnp.stack([gate_grad, up_grad])
        pair_total = pair_total + jnp.einsum(
            "td,ktf->kdf", mlp_rows, pair_grad, preferred_element_type=jnp.float32
        )
        normed_two_grad = scatter_sum(
            jnp.einsum("ktf,kdf->td", pair_grad, pair_back, preferred_element_type=jnp.float32),
            "mp",
             0,
        )
        middle_grad, gain_part = norm_back(normed_two_grad, middle, scale_mlp, gain_mlp)
        gain_mlp_total = gain_mlp_total + gain_part
        middle_grad = middle_grad + top_grad
        mix_rows = lax.all_gather(middle_grad.astype(jnp.bfloat16), "mp", axis=0, tiled=True)
        out_total = out_total + jnp.einsum(
            "tc,td->cd", mixed, mix_rows, preferred_element_type=jnp.float32
        )
        mixed_grad = jnp.einsum("td,cd->tc", mix_rows, out_back, preferred_element_type=jnp.float32)
        c_grad = mixed_grad * conv_out
        conv_grad = mixed_grad * c_gate
        later = shifted(conv_grad[: taps - 1], "seq", -1)
        tail = jnp.concatenate([conv_grad, later], axis=0)
        product_grad = jnp.zeros_like(conv_grad)
        tap_rows = []
        for offset in range(taps):
            product_grad = product_grad + local_taps[offset] * tail[offset : offset + block_rows]
            tap_rows.append(
                jnp.sum(
                    conv_grad * extended[taps - 1 - offset : taps - 1 - offset + block_rows], axis=0
                )
            )
        taps_total = taps_total + jnp.stack(tap_rows)
        stacked = jnp.stack([product_grad * x_value, c_grad, product_grad * b_gate]).astype(
            jnp.bfloat16
        )
        in_total = in_total + jnp.einsum(
            "td,ktc->kdc", normed_rows, stacked, preferred_element_type=jnp.float32
        )
        normed_grad = scatter_sum(
            jnp.einsum("ktc,kdc->td", stacked, in_back, preferred_element_type=jnp.float32),
            "mp",
             0,
        )
        source_grad, gain_part = norm_back(normed_grad, source, scale_mix, gain_mix)
        gain_mix_total = gain_mix_total + gain_part
        input_grads.append(source_grad + middle_grad)
    in_grad, out_grad, pair_out, down_out = (
        scatter_sum(in_total, "seq", 1),
        scatter_sum(out_total, "seq", 1),
        scatter_sum(pair_total, "seq", 1),
        scatter_sum(down_total, "seq", 1),
    )
    taps_full = lax.dynamic_update_slice_in_dim(
        jnp.zeros((taps, width), jnp.float32), taps_total, model_pos * channels, 1
    )
    gain_mix_grad, gain_mlp_grad, taps_grad = lax.psum(
        (gain_mix_total, gain_mlp_total, taps_full), ("seq", "mp")
    )
    return (
        jnp.stack(outputs),
        jnp.stack(input_grads),
        gain_mix_grad,
        gain_mlp_grad,
        taps_grad,
        in_grad,
        out_grad,
        pair_out,
        down_out,
    )


def solution(mesh):
    placed = (
        P(None, ("seq", "mp"), None),
        P(None, ("seq", "mp"), None),
        P(),
        P(),
        P(),
        P(),
        P(None, "seq", "mp"),
        P("mp", "seq"),
        P(None, "seq", "mp"),
        P("mp", "seq"),
    )
    return jax.shard_map(
        local,
        mesh=mesh,
        in_specs=placed,
        out_specs=(
            P(None, ("seq", "mp"), None),
            P(None, ("seq", "mp"), None),
            P(),
            P(),
            P(),
            P(None, "seq", "mp"),
            P("mp", "seq"),
            P(None, "seq", "mp"),
            P("mp", "seq"),
        ),
        check_vma=False,
    )
```

```python
import functools

import jax
import jax.numpy as jnp
from jax import lax
from jax.experimental import pallas as pl
from jax.experimental.pallas import tpu as pltpu
from jax.sharding import PartitionSpec as P

EPS = 1e-05
MESH = pl.DeviceIdType.MESH
BF = jnp.bfloat16
F32 = jnp.float32
HALVES = 2
VMEM_LIMIT = 60 * 2**20


def nn(a, b):
    return lax.dot_general(a, b, (((1,), (0,)), ((), ())), preferred_element_type=F32)


def nt(a, b):
    return lax.dot_general(a, b, (((1,), (1,)), ((), ())), preferred_element_type=F32)


def tn(a, b):
    return lax.dot_general(a, b, (((0,), (0,)), ((), ())), preferred_element_type=F32)


class Place:
    def __init__(self, seqs, models):
        self.seqs, self.chips = seqs, models // 2
        self.s = lax.axis_index("seq")
        self.m = lax.axis_index("mp")
        self.z = self.m // 2
        self.c = self.m % 2
        self.sibling = {"mp": self.m + 1 - 2 * self.c}
        self.above = {"mp": self.m + 2}
        self.below = {"mp": self.m - 2}
        self.has_above = self.z < self.chips - 1
        self.has_below = self.z > 0

    def peer(self, step):
        return {"seq": lax.rem(self.s + step, self.seqs)}

    def enter(self):
        barrier = pltpu.get_barrier_semaphore()

        def greet(where):
            pl.semaphore_signal(barrier, inc=1, device_id=where, device_id_type=MESH)

        greet(self.sibling)
        for step in range(1, self.seqs):
            greet(self.peer(step))
        pl.when(self.has_above)(lambda: greet(self.above))
        pl.when(self.has_below)(lambda: greet(self.below))
        chips = self.chips
        lines = (self.z + chips - 1) // chips + (2 * chips - 2 - self.z) // chips
        pl.semaphore_wait(barrier, self.seqs + lines)


def remote(src, dst, send, recv, where):
    return pltpu.make_async_remote_copy(
        src_ref=src, dst_ref=dst, send_sem=send, recv_sem=recv, device_id=where, device_id_type=MESH
    )


class Gather:
    def __init__(self, place, rows, own, sems):
        self.p, self.rows, self.own = place, rows, own
        self.share = rows.shape[0] // (2 * place.chips)
        self.piece = self.share // HALVES
        self.send, self.recv = sems

    def at(self, chip, core, half):
        return self.rows.at[pl.ds((chip * 2 + core) * self.share + half * self.piece, self.piece)]

    def copy(self, kind, chip, half, own=False):
        p = self.p
        where = (p.above, p.below, p.sibling)[kind]
        dst = self.at(chip, p.c, half)
        src = self.own.at[pl.ds(half * self.piece, self.piece)] if own and self.own is not None else dst
        return remote(src, dst, self.send.at[kind, chip, half], self.recv.at[kind // 2, chip, half], where)

    def start(self):
        p = self.p
        for half in range(HALVES):
            pl.when(p.has_above)(lambda h=half: self.copy(0, p.z, h, True).start())
            pl.when(p.has_below)(lambda h=half: self.copy(1, p.z, h, True).start())
        for half in range(HALVES):
            self.copy(2, p.z, half, True).start()

    def round(self, k):
        p = self.p
        for half in range(HALVES):

            @pl.when(p.z >= k)
            def _(half=half):
                chip = p.z - k
                self.copy(0, chip, half).wait_recv()
                pl.when(p.has_above)(lambda: self.copy(0, chip, half).start())
                self.copy(2, chip, half).start()

            @pl.when(p.z + k <= p.chips - 1)
            def _(half=half):
                chip = p.z + k
                self.copy(1, chip, half).wait_recv()
                pl.when(p.has_below)(lambda: self.copy(1, chip, half).start())
                self.copy(2, chip, half).start()

    def rounds(self):
        return [functools.partial(self.round, k) for k in range(1, self.p.chips)]

    def arrived(self):
        p = self.p
        for chip in range(p.chips):
            for half in range(HALVES):
                dst = self.at(chip, 1 - p.c, half)
                remote(dst, dst, self.send.at[2, chip, half], self.recv.at[1, chip, half], p.sibling).wait_recv()

    def drain(self):
        p = self.p
        for chip in range(p.chips):
            for half in range(HALVES):
                pl.when(p.has_above & (chip <= p.z))(lambda ch=chip, h=half: self.copy(0, ch, h).wait_send())
                pl.when(p.has_below & (chip >= p.z))(lambda ch=chip, h=half: self.copy(1, ch, h).wait_send())
                self.copy(2, chip, half).wait_send()


class Scatter:
    def __init__(self, place, part, from_core, from_line, sems):
        self.p, self.part, self.from_core, self.from_line = place, part, from_core, from_line
        self.share = from_core.shape[1]
        self.piece = self.share // HALVES
        self.core_send, self.core_recv, self.line_send, self.line_recv = sems

    def rows(self, chip, core):
        return self.part.at[pl.ds((chip * 2 + core) * self.share, self.share)]

    def core_copy(self, chip):
        p = self.p
        return remote(
            self.rows(chip, 1 - p.c), self.from_core.at[chip], self.core_send.at[chip], self.core_recv.at[chip], p.sibling
        )

    def give(self, chip):
        self.core_copy(chip).start()

    def mine(self, chip, half):
        return self.part.at[pl.ds((chip * 2 + self.p.c) * self.share + half * self.piece, self.piece)]

    def line_copy(self, down, chip, slot, half):
        p = self.p
        dst = self.from_line.at[slot, pl.ds(half * self.piece, self.piece)]
        return remote(
            self.mine(chip, half),
            dst,
            self.line_send.at[down, chip, half],
            self.line_recv.at[slot, half],
            p.below if down else p.above,
        )

    def total(self, chip, half, slots):
        span = pl.ds(half * self.piece, self.piece)
        value = self.mine(chip, half)[...].astype(F32) + self.from_core[chip, span].astype(F32)
        for slot in slots:
            value = value + self.from_line[slot, span].astype(F32)
        return value

    def hop(self, down, chip, slot, has_source):
        self.core_copy(chip).wait_recv()
        for half in range(HALVES):

            @pl.when(has_source)
            def _(half=half):
                self.line_copy(down, chip, chip, half).wait_recv()
                self.mine(chip, half)[...] = self.total(chip, half, [chip]).astype(BF)

            @pl.when(jnp.logical_not(has_source))
            def _(half=half):
                self.mine(chip, half)[...] = self.total(chip, half, []).astype(BF)

            self.line_copy(down, chip, slot, half).start()

    def round(self, r):
        p = self.p
        last = p.chips - 1

        @pl.when((p.z <= r) & p.has_above)
        def _():
            chip = last - r + p.z
            self.hop(0, chip, chip, p.has_below)

        @pl.when((last - p.z <= r) & p.has_below)
        def _():
            chip = r - last + p.z
            self.hop(1, chip, p.chips if r == last - 1 else chip, p.has_above)

    def rounds(self):
        return [functools.partial(self.round, r) for r in range(self.p.chips - 1)]

    def finish(self, store):
        p = self.p
        self.core_copy(p.z).wait_recv()
        for half in range(HALVES):
            pl.when(p.has_below)(lambda h=half: self.line_copy(0, p.z, p.z, h).wait_recv())
            pl.when(p.has_above)(lambda h=half: self.line_copy(1, p.z, p.chips, h).wait_recv())
            for up in (False, True):
                for low in (False, True):

                    @pl.when((p.has_above == up) & (p.has_below == low))
                    def _(half=half, up=up, low=low):
                        slots = ([p.z] if low else []) + ([p.chips] if up else [])
                        store(half * self.piece, self.piece, self.total(p.z, half, slots))

    def drain(self):
        p = self.p
        for chip in range(p.chips):
            self.core_copy(chip).wait_send()
            for half in range(HALVES):
                pl.when(p.has_above & (chip > p.z))(lambda ch=chip, h=half: self.line_copy(0, ch, ch, h).wait_send())
                pl.when(p.has_below & (chip < p.z))(lambda ch=chip, h=half: self.line_copy(1, ch, ch, h).wait_send())


def gather_sems(count, chips):
    return [pltpu.SemaphoreType.DMA((count, 3, chips, HALVES)), pltpu.SemaphoreType.DMA((count, 2, chips, HALVES))]


def scatter_sems(count, chips):
    return [
        pltpu.SemaphoreType.DMA((count, chips)),
        pltpu.SemaphoreType.DMA((count, chips)),
        pltpu.SemaphoreType.DMA((count, 2, chips, HALVES)),
        pltpu.SemaphoreType.DMA((count, chips + 1, HALVES)),
    ]


def picks(sems, index):
    return [sem.at[index] for sem in sems]


def far_first(place):
    low, high = 0, place.chips - 1
    order = []
    for _ in range(place.chips):
        left = place.z - low >= high - place.z
        order.append(jnp.where(left, low, high))
        low, high = jnp.where(left, low + 1, low), jnp.where(left, high, high - 1)
    return order


def weave(*lists):
    for step in range(max(len(steps) for steps in lists)):
        for steps in lists:
            if step < len(steps):
                steps[step]()


class Shards:
    def __init__(self, place, shard, full, dim, sems):
        self.p, self.shard, self.full, self.dim = place, shard, full, dim
        self.send, self.recv, self.local = sems

    def at(self, owner):
        size = self.shard.shape[self.dim]
        span = pl.ds(pl.multiple_of(owner * size, size), size)
        return self.full.at[(slice(None),) * self.dim + (span,)]

    def copy(self, step):
        p = self.p
        return remote(self.shard, self.at(p.s), self.send.at[step - 1], self.recv.at[step - 1], p.peer(step))

    def local_copy(self):
        return pltpu.make_async_copy(self.shard, self.at(self.p.s), self.local)

    def start(self):
        for step in range(1, self.p.seqs):
            self.copy(step).start()
        self.local_copy().start()

    def arrived(self):
        self.local_copy().wait()
        for step in range(1, self.p.seqs):
            self.copy(step).wait_recv()

    def drain(self):
        for step in range(1, self.p.seqs):
            self.copy(step).wait_send()


def mixer_forward_kernel(
    seqs,
    models,
    normed_ref,
    top_ref,
    taps_ref,
    in_ref,
    out_ref,
    pair_ref,
    down_ref,
    normed_rows,
    top_rows,
    in_rows,
    out_rows,
    pair_rows,
    down_rows,
    gates_out,
    product_out,
    mixed_out,
    mix_out,
    in_full,
    out_full,
    rows,
    gates,
    product,
    mixed,
    part,
    from_core,
    from_line,
    total,
    w_send,
    w_recv,
    w_local,
    halo_send,
    halo_recv,
    keep,
    *sems,
):
    p = Place(seqs, models)
    chips = p.chips
    g_sems, s_sems = sems[:2], sems[2:]
    slots, block = rows.shape[0], rows.shape[1]
    tile = block // chips
    share = tile // 2
    channels = in_full.shape[2]
    p.enter()

    firsts = [Gather(p, rows.at[slot], normed_ref.at[slot], picks(g_sems, slot)) for slot in range(slots)]
    tops = [Gather(p, top_rows.at[slot], top_ref.at[slot], picks(g_sems, slots + slot)) for slot in range(slots)]
    sums = [
        Scatter(p, part.at[slot], from_core.at[slot], from_line.at[slot], picks(s_sems, slot)) for slot in range(slots)
    ]
    weights = [
        Shards(p, shard, full, dim, (w_send.at[i], w_recv.at[i], w_local.at[i]))
        for i, (shard, full, dim) in enumerate(
            ((in_ref, in_full, 1), (out_ref, out_full, 1), (pair_ref, pair_rows, 1), (down_ref, down_rows, 1))
        )
    ]

    def own(slot, which, source):
        span = pl.ds(p.m * share, share)
        return pltpu.make_async_copy(source.at[slot], which.at[slot, span], keep.at[slot + (slots if which is top_rows else 0)])

    for slot in range(slots):
        own(slot, rows, normed_ref).start()
        own(slot, top_rows, top_ref).start()

    def halo(slot):
        return remote(
            product.at[slot, pl.ds(block, 8)],
            product.at[slot, pl.ds(0, 8)],
            halo_send.at[slot],
            halo_recv.at[slot],
            p.peer(1),
        )

    has_later, has_earlier = p.s < seqs - 1, p.s > 0
    for slot in range(slots):

        @pl.when(jnp.logical_not(has_earlier))
        def _(slot=slot):
            product[slot, pl.ds(0, 8)] = jnp.zeros((8, channels), F32)

    def project(slot):
        @pl.loop(0, chips)
        def _(i):
            span = pl.ds(i * tile, tile)
            source = rows[slot, span]
            b_gate = nn(source, in_full[0])
            x_value = nn(source, in_full[2])
            gates[slot, 0, span] = b_gate
            gates[slot, 1, span] = nn(source, in_full[1])
            gates[slot, 2, span] = x_value
            product[slot, pl.ds(8 + i * tile, tile)] = b_gate * x_value

        pl.when(has_later)(lambda: halo(slot).start())

    def convolve(slot):
        pl.when(has_earlier)(lambda: halo(slot).wait_recv())
        for i in range(chips):
            conv = 0.0
            for offset in range(taps_ref.shape[0]):
                conv = conv + taps_ref[offset : offset + 1] * product[slot, pl.ds(8 + i * tile - offset, tile)]
            mixed[slot, pl.ds(i * tile, tile)] = (gates[slot, 1, pl.ds(i * tile, tile)] * conv).astype(BF)

    def project_out(slot):
        for chip in far_first(p):
            span = pl.ds(chip * tile, tile)
            part[slot, span] = nn(mixed[slot, span], out_full[...]).astype(BF)
            sums[slot].give(chip)

    def finish(slot):
        def store(first, size, value):
            total[slot, pl.ds(first, size)] = value

        sums[slot].finish(store)

    firsts[0].start()
    weights[0].start()
    weights[1].start()
    steps = firsts[0].rounds()
    for step in steps[:-1]:
        step()
    firsts[1].start()
    steps[-1]()
    own(0, rows, normed_ref).wait()
    firsts[0].arrived()
    weights[0].arrived()
    weights[1].arrived()
    weights[2].start()
    weights[3].start()
    project(0)
    steps = firsts[1].rounds()
    steps[0]()
    convolve(0)
    project_out(0)
    weave(sums[0].rounds(), steps[1:])
    tops[0].start()
    own(1, rows, normed_ref).wait()
    firsts[1].arrived()
    project(1)
    steps = tops[0].rounds()
    steps[0]()
    convolve(1)
    project_out(1)
    finish(0)
    weave(sums[1].rounds(), steps[1:])
    tops[1].start()
    finish(1)
    stores = [
        pltpu.make_async_copy(src, dst, keep.at[2 * slots + i])
        for i, (src, dst) in enumerate(
            (
                (rows, normed_rows),
                (in_full, in_rows),
                (out_full, out_rows),
                (gates, gates_out),
                (product, product_out),
                (mixed, mixed_out),
                (total, mix_out),
            )
        )
    ]
    for store in stores:
        store.start()
    weave(tops[1].rounds())
    for slot in range(slots):
        own(slot, top_rows, top_ref).wait()
        tops[slot].arrived()
    weights[2].arrived()
    weights[3].arrived()
    for store in stores:
        store.wait()
    for thing in firsts + tops + sums + weights:
        thing.drain()
    for slot in range(slots):
        pl.when(has_later)(lambda slot=slot: halo(slot).wait_send())


def mixer_forward(seqs, models, normed, top, taps, mixer_in, mixer_out, gate_up, mlp_down):
    slots, share, width = normed.shape
    chips = models // 2
    block = share * models
    channels = mixer_in.shape[2]
    units = gate_up.shape[2]
    hbm = pl.BlockSpec(memory_space=pltpu.HBM)
    shape = jax.ShapeDtypeStruct
    return pl.pallas_call(
        functools.partial(mixer_forward_kernel, seqs, models),
        out_shape=[
            shape((slots, block, width), BF),
            shape((slots, block, width), BF),
            shape((3, width, channels), BF),
            shape((channels, width), BF),
            shape((2, width, units), BF),
            shape((units, width), BF),
            shape((slots, 3, block, channels), F32),
            shape((slots, block + 8, channels), F32),
            shape((slots, block, channels), BF),
            shape((slots, share, width), F32),
        ],
        in_specs=[hbm, hbm, pl.BlockSpec(memory_space=pltpu.VMEM)] + [hbm] * 4,
        out_specs=[hbm] * 10,
        scratch_shapes=[
            pltpu.VMEM((3, width, channels), BF),
            pltpu.VMEM((channels, width), BF),
            pltpu.VMEM((slots, block, width), BF),
            pltpu.VMEM((slots, 3, block, channels), F32),
            pltpu.VMEM((slots, block + 8, channels), F32),
            pltpu.VMEM((slots, block, channels), BF),
            pltpu.VMEM((slots, block, width), BF),
            pltpu.VMEM((slots, chips, share, width), BF),
            pltpu.VMEM((slots, chips + 1, share, width), BF),
            pltpu.VMEM((slots, share, width), F32),
            pltpu.SemaphoreType.DMA((4, seqs - 1)),
            pltpu.SemaphoreType.DMA((4, seqs - 1)),
            pltpu.SemaphoreType.DMA((4,)),
            pltpu.SemaphoreType.DMA((slots,)),
            pltpu.SemaphoreType.DMA((slots,)),
            pltpu.SemaphoreType.DMA((2 * slots + 7,)),
            *gather_sems(2 * slots, chips),
            *scatter_sems(slots, chips),
        ],
        compiler_params=pltpu.CompilerParams(collective_id=1, has_side_effects=True, vmem_limit_bytes=VMEM_LIMIT),
    )(normed, top, taps, mixer_in, mixer_out, gate_up, mlp_down)


def shifted(value, axis, steps):
    count = lax.axis_size(axis)
    leading, last = (max(0, -steps), min(count, count - steps))
    return lax.ppermute(value, axis, [(source, source + steps) for source in range(leading, last)])


def scatter_sum(value, axis, dim):
    low = value.astype(BF)
    return lax.psum_scatter(low, axis, scatter_dimension=dim, tiled=True).astype(F32)


def normalize(values, gain):
    scale = lax.rsqrt(jnp.mean(values * values, axis=-1, keepdims=True) + EPS)
    return (values * scale * gain, scale)


def norm_back(grad, values, scale, gain):
    unit = values * scale
    scaled = grad * gain
    gain_grad = jnp.sum(grad * unit, axis=(0, 1))
    input_grad = scale * (scaled - unit * jnp.mean(scaled * unit, axis=-1, keepdims=True))
    return (input_grad, gain_grad)


def local(
    hidden,
    cotangent,
    lengths,
    gain_mix,
    gain_mlp,
    conv_weight,
    mixer_in,
    mixer_out,
    gate_up,
    mlp_down,
):
    seqs, models = lax.axis_size("seq"), lax.axis_size("mp")
    seq_pos = lax.axis_index("seq")
    model_pos = lax.axis_index("mp")
    slots, share, width = hidden.shape
    block_rows = share * models
    channels = mixer_in.shape[2]
    taps = conv_weight.shape[0]
    local_taps = lax.dynamic_slice_in_dim(conv_weight, model_pos * channels, channels, 1)
    share_start = (seq_pos * models + model_pos) * share
    share_pos = share_start + jnp.arange(share, dtype=jnp.int32)
    mask = (share_pos[None, :] < lengths[:, None]).astype(F32)[:, :, None]
    source = hidden.astype(F32)
    top_grad = cotangent.astype(F32) * mask
    normed, scale_mix = normalize(source, gain_mix)
    (
        normed_rows,
        top_rows,
        in_full,
        out_full,
        pair_full,
        down_full,
        gates,
        extended,
        mixed,
        mix_share,
    ) = mixer_forward(
        seqs,
        models,
        normed.astype(BF),
        top_grad.astype(BF),
        local_taps,
        mixer_in,
        mixer_out,
        gate_up,
        mlp_down,
    )
    middle = source + mix_share
    normed_two, scale_mlp = normalize(middle, gain_mlp)
    normed_two = normed_two.astype(BF)
    acts, pair_grads, mlp_rows, outputs, middle_grads, mixed_rows = [], [], [], [], [], []
    stackeds, input_parts, tap_totals = [], [], []
    for slot in range(slots):
        rows = lax.all_gather(normed_two[slot], "mp", axis=0, tiled=True)
        mlp_rows.append(rows)
        gated = jnp.einsum("td,kdf->ktf", rows, pair_full, preferred_element_type=F32)
        gate_part, up_part = gated[0], gated[1]
        activated = jax.nn.silu(gate_part)
        act = (activated * up_part).astype(BF)
        acts.append(act)
        outputs.append(scatter_sum(jnp.dot(act, down_full, preferred_element_type=F32), "mp", 0))
        act_grad = jnp.einsum("td,fd->tf", top_rows[slot], down_full, preferred_element_type=F32)
        sigma = jax.nn.sigmoid(gate_part)
        gate_grad = (act_grad * up_part * sigma * (1.0 + gate_part * (1.0 - sigma))).astype(BF)
        pair_grad = jnp.stack([gate_grad, (act_grad * activated).astype(BF)])
        pair_grads.append(pair_grad)
        middle_grads.append(
            scatter_sum(jnp.einsum("ktf,kdf->td", pair_grad, pair_full, preferred_element_type=F32), "mp", 0)
        )
    output = (mask * (middle + jnp.stack(outputs))).astype(BF)
    middle_grad, gain_mlp_grad = norm_back(jnp.stack(middle_grads), middle, scale_mlp, gain_mlp)
    middle_grad = middle_grad + top_grad
    act, pair_grad, rows = jnp.stack(acts), jnp.stack(pair_grads), jnp.stack(mlp_rows)
    down_total = jnp.einsum("stf,std->fd", act, top_rows, preferred_element_type=F32)
    pair_total = jnp.einsum("std,sktf->kdf", rows, pair_grad, preferred_element_type=F32)
    low_grad = middle_grad.astype(BF)
    for slot in range(slots):
        mix_rows = lax.all_gather(low_grad[slot], "mp", axis=0, tiled=True)
        mixed_rows.append(mix_rows)
        mixed_grad = jnp.einsum("td,cd->tc", mix_rows, out_full, preferred_element_type=F32)
        ext = extended[slot]
        conv_out = 0.0
        for offset in range(taps):
            conv_out = conv_out + local_taps[offset] * ext[8 - offset : 8 - offset + block_rows]
        b_gate, c_gate, x_value = gates[slot, 0], gates[slot, 1], gates[slot, 2]
        c_grad = mixed_grad * conv_out
        conv_grad = mixed_grad * c_gate
        later = shifted(conv_grad[: taps - 1], "seq", -1)
        tail = jnp.concatenate([conv_grad, later], axis=0)
        product_grad = jnp.zeros_like(conv_grad)
        tap_rows = []
        for offset in range(taps):
            product_grad = product_grad + local_taps[offset] * tail[offset : offset + block_rows]
            tap_rows.append(jnp.sum(conv_grad * ext[8 - offset : 8 - offset + block_rows], axis=0))
        tap_totals.append(jnp.stack(tap_rows))
        stacked = jnp.stack([product_grad * x_value, c_grad, product_grad * b_gate]).astype(BF)
        stackeds.append(stacked)
        input_parts.append(
            scatter_sum(jnp.einsum("ktc,kdc->td", stacked, in_full, preferred_element_type=F32), "mp", 0)
        )
    out_total = jnp.einsum("stc,std->cd", mixed, jnp.stack(mixed_rows), preferred_element_type=F32)
    in_total = jnp.einsum("std,sktc->kdc", normed_rows, jnp.stack(stackeds), preferred_element_type=F32)
    source_grad, gain_mix_grad = norm_back(jnp.stack(input_parts), source, scale_mix, gain_mix)
    taps_full = lax.dynamic_update_slice_in_dim(
        jnp.zeros((taps, width), F32), tap_totals[0] + tap_totals[1], model_pos * channels, 1
    )
    gain_mix_grad, gain_mlp_grad, taps_grad = lax.psum((gain_mix_grad, gain_mlp_grad, taps_full), ("seq", "mp"))
    return (
        output,
        source_grad + middle_grad,
        gain_mix_grad,
        gain_mlp_grad,
        taps_grad,
        scatter_sum(in_total, "seq", 1),
        scatter_sum(out_total, "seq", 1),
        scatter_sum(pair_total, "seq", 1),
        scatter_sum(down_total, "seq", 1),
    )


def solution(mesh):
    placed = (
        P(None, ("seq", "mp"), None),
        P(None, ("seq", "mp"), None),
        P(),
        P(),
        P(),
        P(),
        P(None, "seq", "mp"),
        P("mp", "seq"),
        P(None, "seq", "mp"),
        P("mp", "seq"),
    )
    return jax.shard_map(
        local,
        mesh=mesh,
        in_specs=placed,
        out_specs=(
            P(None, ("seq", "mp"), None),
            P(None, ("seq", "mp"), None),
            P(),
            P(),
            P(),
            P(None, "seq", "mp"),
            P("mp", "seq"),
            P(None, "seq", "mp"),
            P("mp", "seq"),
        ),
        check_vma=False,
    )
```

```python
import functools

import jax
import jax.numpy as jnp
from jax import lax
from jax.experimental import pallas as pl
from jax.experimental.pallas import tpu as pltpu
from jax.sharding import PartitionSpec as P

EPS = 1e-05
MESH = pl.DeviceIdType.MESH
BF = jnp.bfloat16
F32 = jnp.float32
HALVES = 2
VMEM_LIMIT = 63 * 2**20


def nn(a, b):
    return lax.dot_general(a, b, (((1,), (0,)), ((), ())), preferred_element_type=F32)


def nt(a, b):
    return lax.dot_general(a, b, (((1,), (1,)), ((), ())), preferred_element_type=F32)


def tn(a, b):
    return lax.dot_general(a, b, (((0,), (0,)), ((), ())), preferred_element_type=F32)


class Place:
    def __init__(self, seqs, models):
        self.seqs, self.chips = seqs, models // 2
        self.s = lax.axis_index("seq")
        self.m = lax.axis_index("mp")
        self.z = self.m // 2
        self.c = self.m % 2
        self.sibling = {"mp": self.m + 1 - 2 * self.c}
        self.above = {"mp": self.m + 2}
        self.below = {"mp": self.m - 2}
        self.has_above = self.z < self.chips - 1
        self.has_below = self.z > 0

    def peer(self, step):
        return {"seq": lax.rem(self.s + step, self.seqs)}

    def enter(self):
        barrier = pltpu.get_barrier_semaphore()

        def greet(where):
            pl.semaphore_signal(barrier, inc=1, device_id=where, device_id_type=MESH)

        greet(self.sibling)
        for step in range(1, self.seqs):
            greet(self.peer(step))
        pl.when(self.has_above)(lambda: greet(self.above))
        pl.when(self.has_below)(lambda: greet(self.below))
        chips = self.chips
        lines = (self.z + chips - 1) // chips + (2 * chips - 2 - self.z) // chips
        pl.semaphore_wait(barrier, self.seqs + lines)


def remote(src, dst, send, recv, where):
    return pltpu.make_async_remote_copy(
        src_ref=src, dst_ref=dst, send_sem=send, recv_sem=recv, device_id=where, device_id_type=MESH
    )


class Gather:
    def __init__(self, place, rows, own, sems):
        self.p, self.rows, self.own = place, rows, own
        self.share = rows.shape[0] // (2 * place.chips)
        self.piece = self.share // HALVES
        self.send, self.recv = sems

    def at(self, chip, core, half):
        return self.rows.at[pl.ds((chip * 2 + core) * self.share + half * self.piece, self.piece)]

    def copy(self, kind, chip, half, own=False):
        p = self.p
        where = (p.above, p.below, p.sibling)[kind]
        dst = self.at(chip, p.c, half)
        src = self.own.at[pl.ds(half * self.piece, self.piece)] if own and self.own is not None else dst
        return remote(src, dst, self.send.at[kind, chip, half], self.recv.at[kind // 2, chip, half], where)

    def start(self):
        p = self.p
        for half in range(HALVES):
            pl.when(p.has_above)(lambda h=half: self.copy(0, p.z, h, True).start())
            pl.when(p.has_below)(lambda h=half: self.copy(1, p.z, h, True).start())
        for half in range(HALVES):
            self.copy(2, p.z, half, True).start()

    def round(self, k):
        p = self.p
        for half in range(HALVES):

            @pl.when(p.z >= k)
            def _(half=half):
                chip = p.z - k
                self.copy(0, chip, half).wait_recv()
                pl.when(p.has_above)(lambda: self.copy(0, chip, half).start())
                self.copy(2, chip, half).start()

            @pl.when(p.z + k <= p.chips - 1)
            def _(half=half):
                chip = p.z + k
                self.copy(1, chip, half).wait_recv()
                pl.when(p.has_below)(lambda: self.copy(1, chip, half).start())
                self.copy(2, chip, half).start()

    def rounds(self):
        return [functools.partial(self.round, k) for k in range(1, self.p.chips)]

    def arrived(self):
        p = self.p
        for chip in range(p.chips):
            for half in range(HALVES):
                dst = self.at(chip, 1 - p.c, half)
                remote(dst, dst, self.send.at[2, chip, half], self.recv.at[1, chip, half], p.sibling).wait_recv()

    def drain(self):
        p = self.p
        for chip in range(p.chips):
            for half in range(HALVES):
                pl.when(p.has_above & (chip <= p.z))(lambda ch=chip, h=half: self.copy(0, ch, h).wait_send())
                pl.when(p.has_below & (chip >= p.z))(lambda ch=chip, h=half: self.copy(1, ch, h).wait_send())
                self.copy(2, chip, half).wait_send()


class Scatter:
    def __init__(self, place, part, from_core, from_line, sems):
        self.p, self.part, self.from_core, self.from_line = place, part, from_core, from_line
        self.share = from_core.shape[1]
        self.piece = self.share // HALVES
        self.core_send, self.core_recv, self.line_send, self.line_recv = sems

    def rows(self, chip, core):
        return self.part.at[pl.ds((chip * 2 + core) * self.share, self.share)]

    def core_copy(self, chip):
        p = self.p
        return remote(
            self.rows(chip, 1 - p.c), self.from_core.at[chip], self.core_send.at[chip], self.core_recv.at[chip], p.sibling
        )

    def give(self, chip):
        self.core_copy(chip).start()

    def mine(self, chip, half):
        return self.part.at[pl.ds((chip * 2 + self.p.c) * self.share + half * self.piece, self.piece)]

    def line_copy(self, down, chip, slot, half):
        p = self.p
        dst = self.from_line.at[slot, pl.ds(half * self.piece, self.piece)]
        return remote(
            self.mine(chip, half),
            dst,
            self.line_send.at[down, chip, half],
            self.line_recv.at[slot, half],
            p.below if down else p.above,
        )

    def total(self, chip, half, slots):
        span = pl.ds(half * self.piece, self.piece)
        value = self.mine(chip, half)[...].astype(F32) + self.from_core[chip, span].astype(F32)
        for slot in slots:
            value = value + self.from_line[slot, span].astype(F32)
        return value

    def hop(self, down, chip, slot, has_source):
        self.core_copy(chip).wait_recv()
        for half in range(HALVES):

            @pl.when(has_source)
            def _(half=half):
                self.line_copy(down, chip, chip, half).wait_recv()
                self.mine(chip, half)[...] = self.total(chip, half, [chip]).astype(BF)

            @pl.when(jnp.logical_not(has_source))
            def _(half=half):
                self.mine(chip, half)[...] = self.total(chip, half, []).astype(BF)

            self.line_copy(down, chip, slot, half).start()

    def round(self, r):
        p = self.p
        last = p.chips - 1

        @pl.when((p.z <= r) & p.has_above)
        def _():
            chip = last - r + p.z
            self.hop(0, chip, chip, p.has_below)

        @pl.when((last - p.z <= r) & p.has_below)
        def _():
            chip = r - last + p.z
            self.hop(1, chip, p.chips if r == last - 1 else chip, p.has_above)

    def rounds(self):
        return [functools.partial(self.round, r) for r in range(self.p.chips - 1)]

    def finish(self, store):
        p = self.p
        self.core_copy(p.z).wait_recv()
        for half in range(HALVES):
            pl.when(p.has_below)(lambda h=half: self.line_copy(0, p.z, p.z, h).wait_recv())
            pl.when(p.has_above)(lambda h=half: self.line_copy(1, p.z, p.chips, h).wait_recv())
            for up in (False, True):
                for low in (False, True):

                    @pl.when((p.has_above == up) & (p.has_below == low))
                    def _(half=half, up=up, low=low):
                        slots = ([p.z] if low else []) + ([p.chips] if up else [])
                        store(half * self.piece, self.piece, self.total(p.z, half, slots))

    def drain(self):
        p = self.p
        for chip in range(p.chips):
            self.core_copy(chip).wait_send()
            for half in range(HALVES):
                pl.when(p.has_above & (chip > p.z))(lambda ch=chip, h=half: self.line_copy(0, ch, ch, h).wait_send())
                pl.when(p.has_below & (chip < p.z))(lambda ch=chip, h=half: self.line_copy(1, ch, ch, h).wait_send())


def gather_sems(count, chips):
    return [pltpu.SemaphoreType.DMA((count, 3, chips, HALVES)), pltpu.SemaphoreType.DMA((count, 2, chips, HALVES))]


def scatter_sems(count, chips):
    return [
        pltpu.SemaphoreType.DMA((count, chips)),
        pltpu.SemaphoreType.DMA((count, chips)),
        pltpu.SemaphoreType.DMA((count, 2, chips, HALVES)),
        pltpu.SemaphoreType.DMA((count, chips + 1, HALVES)),
    ]


def picks(sems, index):
    return [sem.at[index] for sem in sems]


def far_first(place):
    low, high = 0, place.chips - 1
    order = []
    for _ in range(place.chips):
        left = place.z - low >= high - place.z
        order.append(jnp.where(left, low, high))
        low, high = jnp.where(left, low + 1, low), jnp.where(left, high, high - 1)
    return order


def weave(*lists):
    for step in range(max(len(steps) for steps in lists)):
        for steps in lists:
            if step < len(steps):
                steps[step]()


class Shards:
    def __init__(self, place, shard, full, dim, sems):
        self.p, self.shard, self.full, self.dim = place, shard, full, dim
        self.send, self.recv, self.local = sems

    def at(self, owner):
        size = self.shard.shape[self.dim]
        span = pl.ds(pl.multiple_of(owner * size, size), size)
        return self.full.at[(slice(None),) * self.dim + (span,)]

    def copy(self, step):
        p = self.p
        return remote(self.shard, self.at(p.s), self.send.at[step - 1], self.recv.at[step - 1], p.peer(step))

    def local_copy(self):
        return pltpu.make_async_copy(self.shard, self.at(self.p.s), self.local)

    def start(self):
        for step in range(1, self.p.seqs):
            self.copy(step).start()
        self.local_copy().start()

    def arrived(self):
        self.local_copy().wait()
        for step in range(1, self.p.seqs):
            self.copy(step).wait_recv()

    def drain(self):
        for step in range(1, self.p.seqs):
            self.copy(step).wait_send()


def mixer_forward_kernel(
    seqs,
    models,
    normed_ref,
    top_ref,
    taps_ref,
    in_ref,
    out_ref,
    pair_ref,
    down_ref,
    normed_rows,
    top_rows,
    in_rows,
    out_rows,
    pair_rows,
    down_rows,
    gates_out,
    product_out,
    mixed_out,
    mix_out,
    in_full,
    out_full,
    rows,
    gates,
    product,
    mixed,
    part,
    from_core,
    from_line,
    total,
    w_send,
    w_recv,
    w_local,
    halo_send,
    halo_recv,
    keep,
    *sems,
):
    p = Place(seqs, models)
    chips = p.chips
    g_sems, s_sems = sems[:2], sems[2:]
    slots, block = rows.shape[0], rows.shape[1]
    tile = block // chips
    share = tile // 2
    channels = in_full.shape[2]
    p.enter()

    firsts = [Gather(p, rows.at[slot], normed_ref.at[slot], picks(g_sems, slot)) for slot in range(slots)]
    tops = [Gather(p, top_rows.at[slot], top_ref.at[slot], picks(g_sems, slots + slot)) for slot in range(slots)]
    sums = [
        Scatter(p, part.at[slot], from_core.at[slot], from_line.at[slot], picks(s_sems, slot)) for slot in range(slots)
    ]
    weights = [
        Shards(p, shard, full, dim, (w_send.at[i], w_recv.at[i], w_local.at[i]))
        for i, (shard, full, dim) in enumerate(
            ((in_ref, in_full, 1), (out_ref, out_full, 1), (pair_ref, pair_rows, 1), (down_ref, down_rows, 1))
        )
    ]

    def own(slot, which, source):
        span = pl.ds(p.m * share, share)
        return pltpu.make_async_copy(source.at[slot], which.at[slot, span], keep.at[slot + (slots if which is top_rows else 0)])

    for slot in range(slots):
        own(slot, rows, normed_ref).start()
        own(slot, top_rows, top_ref).start()

    def halo(slot):
        return remote(
            product.at[slot, pl.ds(block, 8)],
            product.at[slot, pl.ds(0, 8)],
            halo_send.at[slot],
            halo_recv.at[slot],
            p.peer(1),
        )

    has_later, has_earlier = p.s < seqs - 1, p.s > 0
    for slot in range(slots):

        @pl.when(jnp.logical_not(has_earlier))
        def _(slot=slot):
            product[slot, pl.ds(0, 8)] = jnp.zeros((8, channels), F32)

    def project(slot):
        @pl.loop(0, chips)
        def _(i):
            span = pl.ds(i * tile, tile)
            source = rows[slot, span]
            b_gate = nn(source, in_full[0])
            x_value = nn(source, in_full[2])
            gates[slot, 0, span] = b_gate
            gates[slot, 1, span] = nn(source, in_full[1])
            gates[slot, 2, span] = x_value
            product[slot, pl.ds(8 + i * tile, tile)] = b_gate * x_value

        pl.when(has_later)(lambda: halo(slot).start())

    def convolve(slot):
        pl.when(has_earlier)(lambda: halo(slot).wait_recv())
        for i in range(chips):
            conv = 0.0
            for offset in range(taps_ref.shape[0]):
                conv = conv + taps_ref[offset : offset + 1] * product[slot, pl.ds(8 + i * tile - offset, tile)]
            mixed[slot, pl.ds(i * tile, tile)] = (gates[slot, 1, pl.ds(i * tile, tile)] * conv).astype(BF)

    def project_out(slot):
        for chip in far_first(p):
            span = pl.ds(chip * tile, tile)
            part[slot, span] = nn(mixed[slot, span], out_full[...]).astype(BF)
            sums[slot].give(chip)

    def finish(slot):
        def store(first, size, value):
            total[slot, pl.ds(first, size)] = value

        sums[slot].finish(store)

    firsts[0].start()
    weights[0].start()
    weights[1].start()
    steps = firsts[0].rounds()
    for step in steps[:-1]:
        step()
    firsts[1].start()
    steps[-1]()
    own(0, rows, normed_ref).wait()
    firsts[0].arrived()
    weights[0].arrived()
    weights[1].arrived()
    weights[2].start()
    weights[3].start()
    project(0)
    steps = firsts[1].rounds()
    steps[0]()
    convolve(0)
    project_out(0)
    weave(sums[0].rounds(), steps[1:])
    tops[0].start()
    own(1, rows, normed_ref).wait()
    firsts[1].arrived()
    project(1)
    steps = tops[0].rounds()
    steps[0]()
    convolve(1)
    project_out(1)
    finish(0)
    weave(sums[1].rounds(), steps[1:])
    tops[1].start()
    finish(1)
    stores = [
        pltpu.make_async_copy(src, dst, keep.at[2 * slots + i])
        for i, (src, dst) in enumerate(
            (
                (rows, normed_rows),
                (in_full, in_rows),
                (out_full, out_rows),
                (gates, gates_out),
                (product, product_out),
                (mixed, mixed_out),
                (total, mix_out),
            )
        )
    ]
    for store in stores:
        store.start()
    weave(tops[1].rounds())
    for slot in range(slots):
        own(slot, top_rows, top_ref).wait()
        tops[slot].arrived()
    weights[2].arrived()
    weights[3].arrived()
    for store in stores:
        store.wait()
    for thing in firsts + tops + sums + weights:
        thing.drain()
    for slot in range(slots):
        pl.when(has_later)(lambda slot=slot: halo(slot).wait_send())


def mixer_forward(seqs, models, normed, top, taps, mixer_in, mixer_out, gate_up, mlp_down):
    slots, share, width = normed.shape
    chips = models // 2
    block = share * models
    channels = mixer_in.shape[2]
    units = gate_up.shape[2]
    hbm = pl.BlockSpec(memory_space=pltpu.HBM)
    shape = jax.ShapeDtypeStruct
    return pl.pallas_call(
        functools.partial(mixer_forward_kernel, seqs, models),
        out_shape=[
            shape((slots, block, width), BF),
            shape((slots, block, width), BF),
            shape((3, width, channels), BF),
            shape((channels, width), BF),
            shape((2, width, units), BF),
            shape((units, width), BF),
            shape((slots, 3, block, channels), F32),
            shape((slots, block + 8, channels), F32),
            shape((slots, block, channels), BF),
            shape((slots, share, width), F32),
        ],
        in_specs=[hbm, hbm, pl.BlockSpec(memory_space=pltpu.VMEM)] + [hbm] * 4,
        out_specs=[hbm] * 10,
        scratch_shapes=[
            pltpu.VMEM((3, width, channels), BF),
            pltpu.VMEM((channels, width), BF),
            pltpu.VMEM((slots, block, width), BF),
            pltpu.VMEM((slots, 3, block, channels), F32),
            pltpu.VMEM((slots, block + 8, channels), F32),
            pltpu.VMEM((slots, block, channels), BF),
            pltpu.VMEM((slots, block, width), BF),
            pltpu.VMEM((slots, chips, share, width), BF),
            pltpu.VMEM((slots, chips + 1, share, width), BF),
            pltpu.VMEM((slots, share, width), F32),
            pltpu.SemaphoreType.DMA((4, seqs - 1)),
            pltpu.SemaphoreType.DMA((4, seqs - 1)),
            pltpu.SemaphoreType.DMA((4,)),
            pltpu.SemaphoreType.DMA((slots,)),
            pltpu.SemaphoreType.DMA((slots,)),
            pltpu.SemaphoreType.DMA((2 * slots + 7,)),
            *gather_sems(2 * slots, chips),
            *scatter_sems(slots, chips),
        ],
        compiler_params=pltpu.CompilerParams(collective_id=1, has_side_effects=True, vmem_limit_bytes=VMEM_LIMIT),
    )(normed, top, taps, mixer_in, mixer_out, gate_up, mlp_down)


def mlp_kernel(
    seqs,
    models,
    normed_ref,
    top_rows,
    pair_ref,
    down_ref,
    grad_out,
    mlp_part,
    pair_grad,
    down_grad,
    pair,
    down,
    rows,
    top_tile,
    top_cols,
    acts,
    stage,
    part,
    from_core,
    from_line,
    total,
    load,
    tile_sem,
    cols_sem,
    stage_sem,
    keep,
    *sems,
):
    p = Place(seqs, models)
    chips = p.chips
    g_sems, s_sems = sems[:2], sems[2:]
    slots, block, width = rows.shape
    units = down.shape[0]
    tile = block // chips
    share = tile // 2
    unit_block = min(512, units)
    wide_block = 512
    columns = top_cols.shape[-1]
    loads = [pltpu.make_async_copy(pair_ref, pair, load.at[0]), pltpu.make_async_copy(down_ref, down, load.at[1])]
    for thing in loads:
        thing.start()
    p.enter()
    gathers = [Gather(p, rows.at[slot], normed_ref.at[slot], picks(g_sems, slot)) for slot in range(slots)]
    sums = [
        Scatter(p, part.at[slot], from_core.at[slot], from_line.at[slot], picks(s_sems, slot)) for slot in range(slots)
    ]

    def own(slot):
        return pltpu.make_async_copy(
            normed_ref.at[slot], rows.at[slot, pl.ds(p.m * share, share)], load.at[2 + slot]
        )

    order = far_first(p)
    tiles = [(slot, chip) for slot in range(slots) for chip in order]

    def fetch(index):
        slot, chip = tiles[index]
        return pltpu.make_async_copy(
            top_rows.at[slot, pl.ds(chip * tile, tile)], top_tile.at[index % 2], tile_sem.at[index % 2]
        )

    def put(index):
        slot, chip = tiles[index]
        return pltpu.make_async_copy(
            stage.at[index % 2], mlp_part.at[slot, pl.ds(chip * tile, tile)], stage_sem.at[index % 2]
        )

    def work(index):
        slot, chip = tiles[index]
        buf = index % 2
        span = pl.ds(chip * tile, tile)
        fetch(index).wait()
        if index + 1 < len(tiles):
            fetch(index + 1).start()
        if index >= 2:
            put(index - 2).wait()

        @pl.loop(0, units // unit_block)
        def _(i):
            cut = pl.ds(pl.multiple_of(i * unit_block, unit_block), unit_block)
            source = rows[slot, span]
            gate = nn(source, pair[0, :, cut])
            up = nn(source, pair[1, :, cut])
            act_grad = nt(top_tile[buf], down[cut])
            sigma = jax.nn.sigmoid(gate)
            silu = gate * sigma
            acts[0, slot, span, cut] = (silu * up).astype(BF)
            acts[1, slot, span, cut] = (act_grad * up * sigma * (1.0 + gate * (1.0 - sigma))).astype(BF)
            acts[2, slot, span, cut] = (act_grad * silu).astype(BF)

        @pl.loop(0, width // wide_block)
        def _(i):
            cut = pl.ds(pl.multiple_of(i * wide_block, wide_block), wide_block)
            value = nt(acts[1, slot, span], pair[0, cut]) + nt(acts[2, slot, span], pair[1, cut])
            part[slot, span, cut] = value.astype(BF)
            stage[buf, :, cut] = nn(acts[0, slot, span], down[:, cut]).astype(BF)

        sums[slot].give(chip)
        put(index).start()

    def finish(slot):
        def store(first, size, value):
            total[slot, pl.ds(first, size)] = value

        sums[slot].finish(store)

    def pair_step(index):
        k, first = divmod(index, width // wide_block)
        cut = pl.ds(first * wide_block, wide_block)
        value = 0.0
        for slot in range(slots):
            value = value + tn(rows[slot, :, cut], acts[1 + k, slot])
        pair[k, cut] = value.astype(BF)
        pltpu.make_async_copy(pair.at[k, cut], pair_grad.at[k, cut], keep.at[index]).start()

    pair_steps = 2 * (width // wide_block)

    def fetch_columns(index):
        return pltpu.make_async_copy(
            top_rows.at[:, :, pl.ds(index * columns, columns)], top_cols.at[index % 2], cols_sem.at[index % 2]
        )

    def down_step(index):
        fetch_columns(index).wait()
        for first in range(0, units, unit_block):
            cut = pl.ds(first, unit_block)
            value = 0.0
            for slot in range(slots):
                value = value + tn(acts[0, slot, :, cut], top_cols[index % 2, slot])
            down[cut, pl.ds(index * columns, columns)] = value.astype(BF)
        if index + 2 < width // columns:
            fetch_columns(index + 2).start()

    for slot in range(slots):
        own(slot).start()
    fetch(0).start()
    gathers[0].start()
    steps = gathers[0].rounds()
    for step in steps[:-1]:
        step()
    gathers[1].start()
    steps[-1]()
    own(0).wait()
    gathers[0].arrived()
    for thing in loads:
        thing.wait()
    next_rows = gathers[1].rounds()
    hops = sums[0].rounds()
    for index in range(chips):
        work(index)
        if index < len(hops):
            hops[index]()
            next_rows[index]()
    own(1).wait()
    gathers[1].arrived()
    hops = sums[1].rounds()
    for index in range(chips):
        work(chips + index)
        if index == 0:
            finish(0)
        if index < len(hops):
            hops[index]()
    fetch_columns(0).start()
    fetch_columns(1).start()
    for index in range(pair_steps):
        pair_step(index)
    for index in range(width // columns):
        down_step(index)
    finish(1)
    last = [
        pltpu.make_async_copy(down, down_grad, keep.at[pair_steps]),
        pltpu.make_async_copy(total, grad_out, keep.at[pair_steps + 1]),
    ]
    for thing in last:
        thing.start()
    for index in range(pair_steps):
        k, first = divmod(index, width // wide_block)
        cut = pl.ds(first * wide_block, wide_block)
        pltpu.make_async_copy(pair.at[k, cut], pair_grad.at[k, cut], keep.at[index]).wait()
    for index in range(len(tiles) - 2, len(tiles)):
        put(index).wait()
    for thing in last:
        thing.wait()
    for thing in gathers + sums:
        thing.drain()


def mlp(seqs, models, normed, top_rows, pair_full, down_full):
    slots, share, width = normed.shape
    chips = models // 2
    block = share * models
    units = down_full.shape[0]
    hbm = pl.BlockSpec(memory_space=pltpu.HBM)
    shape = jax.ShapeDtypeStruct
    return pl.pallas_call(
        functools.partial(mlp_kernel, seqs, models),
        out_shape=[
            shape((slots, share, width), F32),
            shape((slots, block, width), BF),
            shape((2, width, units), BF),
            shape((units, width), BF),
        ],
        in_specs=[hbm] * 4,
        out_specs=[hbm] * 4,
        scratch_shapes=[
            pltpu.VMEM((2, width, units), BF),
            pltpu.VMEM((units, width), BF),
            pltpu.VMEM((slots, block, width), BF),
            pltpu.VMEM((2, block // chips, width), BF),
            pltpu.VMEM((2, slots, block, 256), BF),
            pltpu.VMEM((3, slots, block, units), BF),
            pltpu.VMEM((2, block // chips, width), BF),
            pltpu.VMEM((slots, block, width), BF),
            pltpu.VMEM((slots, chips, share, width), BF),
            pltpu.VMEM((slots, chips + 1, share, width), BF),
            pltpu.VMEM((slots, share, width), F32),
            pltpu.SemaphoreType.DMA((2 + slots,)),
            pltpu.SemaphoreType.DMA((2,)),
            pltpu.SemaphoreType.DMA((2,)),
            pltpu.SemaphoreType.DMA((2,)),
            pltpu.SemaphoreType.DMA((2 * (width // 512) + 2,)),
            *gather_sems(slots, chips),
            *scatter_sems(slots, chips),
        ],
        compiler_params=pltpu.CompilerParams(collective_id=2, has_side_effects=True, vmem_limit_bytes=VMEM_LIMIT),
    )(normed, top_rows, pair_full, down_full)


class Spread:
    def __init__(self, place, partial, got, sems):
        self.p, self.partial, self.got = place, partial, got
        self.send, self.recv, self.local = sems

    def block(self, owner):
        size = self.partial.shape[1] // self.p.seqs
        return self.partial.at[:, pl.ds(pl.multiple_of(owner * size, size), size)]

    def copy(self, step):
        p = self.p
        return remote(
            self.block(lax.rem(p.s + step, p.seqs)),
            self.got.at[step],
            self.send.at[step - 1],
            self.recv.at[step - 1],
            p.peer(step),
        )

    def local_copy(self):
        return pltpu.make_async_copy(self.block(self.p.s), self.got.at[0], self.local)

    def start(self):
        for step in range(1, self.p.seqs):
            self.copy(step).start()
        self.local_copy().start()

    def finish(self):
        self.local_copy().wait()
        for step in range(1, self.p.seqs):
            self.copy(step).wait()


def mixer_backward_kernel(
    seqs,
    models,
    low_ref,
    mlp_part,
    taps_ref,
    in_ref,
    out_ref,
    normed_rows,
    gates_ref,
    product_ref,
    mixed_ref,
    pair_grad,
    down_grad,
    mlp_out,
    grad_out,
    taps_out,
    in_got,
    out_got,
    pair_got,
    down_got,
    in_full,
    out_full,
    rows,
    columns,
    gates,
    product,
    mixed,
    conv_grad,
    stacked,
    part,
    from_core,
    from_line,
    mlp_total,
    grad_total,
    load,
    cols_sem,
    w_send,
    w_recv,
    w_local,
    halo_send,
    halo_recv,
    free,
    *sems,
):
    p = Place(seqs, models)
    chips = p.chips
    g_sems, s_sems = sems[:2], sems[2:]
    slots, block, width = rows.shape
    channels = out_full.shape[0]
    taps = taps_ref.shape[0]
    tile = block // chips
    share = tile // 2
    wide_block = 512
    cols = columns.shape[-1]
    loads = [
        pltpu.make_async_copy(src, dst, load.at[i])
        for i, (src, dst) in enumerate(
            [(mlp_part.at[slot], part.at[slot]) for slot in range(slots)]
            + [
                (low_ref.at[slot], rows.at[slot, pl.ds(p.m * share, share)])
                for slot in range(slots)
            ]
            + [
                (in_ref, in_full),
                (out_ref, out_full),
                (gates_ref, gates),
                (product_ref, product),
                (mixed_ref, mixed),
            ]
        )
    ]
    for thing in loads:
        thing.start()
    p.enter()
    gathers = [Gather(p, rows.at[slot], low_ref.at[slot], picks(g_sems, slot)) for slot in range(slots)]

    def scatter(slot, index):
        return Scatter(p, part.at[slot], from_core.at[slot], from_line.at[slot], picks(s_sems, index))

    mlp_sums = [scatter(slot, slot) for slot in range(slots)]
    sums = [scatter(slot, slots + slot) for slot in range(slots)]
    spreads = [
        Spread(p, partial, got, (w_send.at[i], w_recv.at[i], w_local.at[i]))
        for i, (partial, got) in enumerate(
            ((pair_grad, pair_got), (down_grad, down_got), (in_full, in_got), (out_full, out_got))
        )
    ]
    has_later, has_earlier = p.s < seqs - 1, p.s > 0
    order = far_first(p)

    def halo(slot):
        return remote(
            conv_grad.at[slot, pl.ds(0, 8)],
            conv_grad.at[slot, pl.ds(block, 8)],
            halo_send.at[slot],
            halo_recv.at[slot],
            p.peer(seqs - 1),
        )

    for slot in range(slots):

        @pl.when(jnp.logical_not(has_later))
        def _(slot=slot):
            conv_grad[slot, pl.ds(block, 8)] = jnp.zeros((8, channels), F32)

    taps_out[...] = jnp.zeros_like(taps_out)

    def first_pass(slot):
        for i in range(chips):
            span = pl.ds(i * tile, tile)
            mixed_grad = nt(rows[slot, span], out_full[...])
            grad = mixed_grad * gates[slot, 1, span]
            conv_grad[slot, span] = grad
            conv = 0.0
            for offset in range(taps):
                earlier = product[slot, pl.ds(8 + i * tile - offset, tile)]
                conv = conv + taps_ref[offset : offset + 1] * earlier
                taps_out[offset : offset + 1] += jnp.sum(grad * earlier, axis=0, keepdims=True)
            stacked[slot, span, pl.ds(channels, channels)] = (mixed_grad * conv).astype(BF)
            if i == 0:
                pl.when(has_earlier)(lambda: halo(slot).start())

    def second_pass(slot):
        pl.when(has_later)(lambda: halo(slot).wait_recv())
        for i in range(chips):
            span = pl.ds(i * tile, tile)
            grad = 0.0
            for offset in range(taps):
                grad = grad + taps_ref[offset : offset + 1] * conv_grad[slot, pl.ds(i * tile + offset, tile)]
            stacked[slot, span, pl.ds(0, channels)] = (grad * gates[slot, 2, span]).astype(BF)
            stacked[slot, span, pl.ds(2 * channels, channels)] = (grad * gates[slot, 0, span]).astype(BF)

    def third_pass(slot):
        for chip in order:
            span = pl.ds(chip * tile, tile)

            @pl.loop(0, width // wide_block)
            def _(i):
                cut = pl.ds(pl.multiple_of(i * wide_block, wide_block), wide_block)
                value = 0.0
                for k in range(3):
                    value = value + nt(stacked[slot, span, pl.ds(k * channels, channels)], in_full[k, cut])
                part[slot, span, cut] = value.astype(BF)

            sums[slot].give(chip)

    def finish(what, total, slot):
        def store(first, size, value):
            total[slot, pl.ds(first, size)] = value

        what[slot].finish(store)

    def neighbours(act):
        act(p.sibling)
        pl.when(p.has_above)(lambda: act(p.above))
        pl.when(p.has_below)(lambda: act(p.below))

    def give_free(slot):
        mlp_sums[slot].drain()
        neighbours(
            lambda where: pl.semaphore_signal(free.at[slot], inc=1, device_id=where, device_id_type=MESH)
        )

    def take_free(slot):
        lines = (p.z + chips - 1) // chips + (2 * chips - 2 - p.z) // chips
        pl.semaphore_wait(free.at[slot], 1 + lines)

    def fetch_columns(index):
        return pltpu.make_async_copy(
            normed_rows.at[:, :, pl.ds(index * cols, cols)], columns.at[index % 2], cols_sem.at[index % 2]
        )

    steps_in = width // cols

    def in_step(index):
        fetch_columns(index).wait()
        value = 0.0
        for slot in range(slots):
            value = value + tn(columns[index % 2, slot], stacked[slot])
        for k in range(3):
            in_full[k, pl.ds(index * cols, cols)] = value[:, k * channels : (k + 1) * channels].astype(BF)
        if index + 2 < steps_in:
            fetch_columns(index + 2).start()

    def out_step():
        for first in range(0, width, wide_block):
            cut = pl.ds(first, wide_block)
            value = 0.0
            for slot in range(slots):
                value = value + tn(mixed[slot], rows[slot, :, cut])
            out_full[:, cut] = value.astype(BF)

    spreads[0].start()
    spreads[1].start()
    gathers[0].start()
    loads[0].wait()
    for chip in order:
        mlp_sums[0].give(chip)
    hops, next_rows = mlp_sums[0].rounds(), gathers[0].rounds()
    weave(hops[:-1], next_rows[:-1])
    gathers[1].start()
    weave(hops[-1:], next_rows[-1:])
    loads[1].wait()
    for chip in order:
        mlp_sums[1].give(chip)
    loads[2].wait()
    for thing in loads[2 + slots :]:
        thing.wait()
    gathers[0].arrived()
    fetch_columns(0).start()
    fetch_columns(1).start()
    mlp_hops, next_rows, hops = mlp_sums[1].rounds(), gathers[1].rounds(), sums[0].rounds()
    first_pass(0)
    finish(mlp_sums, mlp_total, 0)
    give_free(0)
    weave(mlp_hops[:1], next_rows[:1])
    second_pass(0)
    take_free(0)
    third_pass(0)
    weave(mlp_hops[1:], next_rows[1:], hops[:1])
    loads[3].wait()
    gathers[1].arrived()
    first_pass(1)
    finish(mlp_sums, mlp_total, 1)
    give_free(1)
    hops[1]()
    second_pass(1)
    take_free(1)
    weave(hops[2:])
    third_pass(1)
    hops = sums[1].rounds()
    hops[0]()
    out_step()
    spreads[3].start()
    for index in range(steps_in):
        in_step(index)
    spreads[2].start()
    weave(hops[1:])
    finish(sums, grad_total, 0)
    finish(sums, grad_total, 1)
    last = [
        pltpu.make_async_copy(mlp_total, mlp_out, load.at[0]),
        pltpu.make_async_copy(grad_total, grad_out, load.at[1]),
    ]
    for thing in last:
        thing.start()
    for thing in spreads:
        thing.finish()
    for thing in last:
        thing.wait()
    for thing in gathers + sums:
        thing.drain()
    for slot in range(slots):
        pl.when(has_earlier)(lambda slot=slot: halo(slot).wait_send())


def mixer_backward(
    seqs, models, low, mlp_part, taps, in_full, out_full, normed_rows, gates, product, mixed, pair_grad, down_grad
):
    slots, share, width = low.shape
    chips = models // 2
    block = share * models
    channels = out_full.shape[0]
    units = down_grad.shape[0]
    hbm = pl.BlockSpec(memory_space=pltpu.HBM)
    vmem = pl.BlockSpec(memory_space=pltpu.VMEM)
    shape = jax.ShapeDtypeStruct
    return pl.pallas_call(
        functools.partial(mixer_backward_kernel, seqs, models),
        out_shape=[
            shape((slots, share, width), F32),
            shape((slots, share, width), F32),
            shape((8, channels), F32),
            shape((seqs, 3, width // seqs, channels), BF),
            shape((seqs, channels, width // seqs), BF),
            shape((seqs, 2, width // seqs, units), BF),
            shape((seqs, units, width // seqs), BF),
        ],
        in_specs=[hbm, hbm, vmem] + [hbm] * 8,
        out_specs=[hbm, hbm, vmem] + [hbm] * 4,
        scratch_shapes=[
            pltpu.VMEM((3, width, channels), BF),
            pltpu.VMEM((channels, width), BF),
            pltpu.VMEM((slots, block, width), BF),
            pltpu.VMEM((2, slots, block, 256), BF),
            pltpu.VMEM((slots, 3, block, channels), F32),
            pltpu.VMEM((slots, block + 8, channels), F32),
            pltpu.VMEM((slots, block, channels), BF),
            pltpu.VMEM((slots, block + 8, channels), F32),
            pltpu.VMEM((slots, block, 3 * channels), BF),
            pltpu.VMEM((slots, block, width), BF),
            pltpu.VMEM((slots, chips, share, width), BF),
            pltpu.VMEM((slots, chips + 1, share, width), BF),
            pltpu.VMEM((slots, share, width), F32),
            pltpu.VMEM((slots, share, width), F32),
            pltpu.SemaphoreType.DMA((2 * slots + 5,)),
            pltpu.SemaphoreType.DMA((2,)),
            pltpu.SemaphoreType.DMA((4, seqs - 1)),
            pltpu.SemaphoreType.DMA((4, seqs - 1)),
            pltpu.SemaphoreType.DMA((4,)),
            pltpu.SemaphoreType.DMA((slots,)),
            pltpu.SemaphoreType.DMA((slots,)),
            pltpu.SemaphoreType.REGULAR((slots,)),
            *gather_sems(slots, chips),
            *scatter_sems(2 * slots, chips),
        ],
        compiler_params=pltpu.CompilerParams(collective_id=3, has_side_effects=True, vmem_limit_bytes=VMEM_LIMIT),
    )(low, mlp_part, taps, in_full, out_full, normed_rows, gates, product, mixed, pair_grad, down_grad)


def small_sum_kernel(seqs, models, value_ref, out_ref, by_model, by_seq, send, recv, seq_send, seq_recv):
    s, m = lax.axis_index("seq"), lax.axis_index("mp")
    along = [{"mp": lax.rem(m + step, models)} for step in range(1, models)]
    across = [{"seq": lax.rem(s + step, seqs)} for step in range(1, seqs)]
    barrier = pltpu.get_barrier_semaphore()
    for where in along + across:
        pl.semaphore_signal(barrier, inc=1, device_id=where, device_id_type=MESH)
    pl.semaphore_wait(barrier, models + seqs - 2)
    by_model[m] = value_ref[...]
    copies = [
        remote(value_ref, by_model.at[m], send.at[i], recv.at[i], where) for i, where in enumerate(along)
    ]
    for thing in copies:
        thing.start()
    for thing in copies:
        thing.wait()
    by_seq[s] = functools.reduce(lambda a, b: a + b, [by_model[i] for i in range(models)])
    copies = [
        remote(by_seq.at[s], by_seq.at[s], seq_send.at[i], seq_recv.at[i], where) for i, where in enumerate(across)
    ]
    for thing in copies:
        thing.start()
    for thing in copies:
        thing.wait()
    out_ref[...] = functools.reduce(lambda a, b: a + b, [by_seq[i] for i in range(seqs)])


def small_sum(seqs, models, value):
    vmem = pl.BlockSpec(memory_space=pltpu.VMEM)
    return pl.pallas_call(
        functools.partial(small_sum_kernel, seqs, models),
        out_shape=jax.ShapeDtypeStruct(value.shape, F32),
        in_specs=[vmem],
        out_specs=vmem,
        scratch_shapes=[
            pltpu.VMEM((models, *value.shape), F32),
            pltpu.VMEM((seqs, *value.shape), F32),
            pltpu.SemaphoreType.DMA((models - 1,)),
            pltpu.SemaphoreType.DMA((models - 1,)),
            pltpu.SemaphoreType.DMA((seqs - 1,)),
            pltpu.SemaphoreType.DMA((seqs - 1,)),
        ],
        compiler_params=pltpu.CompilerParams(collective_id=4, has_side_effects=True),
    )(value)


def normalize(values, gain):
    scale = lax.rsqrt(jnp.mean(values * values, axis=-1, keepdims=True) + EPS)
    return (values * scale * gain, scale)


def norm_back(grad, values, scale, gain):
    unit = values * scale
    scaled = grad * gain
    gain_grad = jnp.sum(grad * unit, axis=(0, 1))
    input_grad = scale * (scaled - unit * jnp.mean(scaled * unit, axis=-1, keepdims=True))
    return (input_grad, gain_grad)


def local(
    hidden,
    cotangent,
    lengths,
    gain_mix,
    gain_mlp,
    conv_weight,
    mixer_in,
    mixer_out,
    gate_up,
    mlp_down,
):
    seqs, models = lax.axis_size("seq"), lax.axis_size("mp")
    seq_pos = lax.axis_index("seq")
    model_pos = lax.axis_index("mp")
    slots, share, width = hidden.shape
    channels = mixer_in.shape[2]
    taps = conv_weight.shape[0]
    local_taps = lax.dynamic_slice_in_dim(conv_weight, model_pos * channels, channels, 1)
    share_start = (seq_pos * models + model_pos) * share
    share_pos = share_start + jnp.arange(share, dtype=jnp.int32)
    mask = (share_pos[None, :] < lengths[:, None]).astype(F32)[:, :, None]
    source = hidden.astype(F32)
    top_grad = cotangent.astype(F32) * mask
    normed, scale_mix = normalize(source, gain_mix)
    (
        normed_rows,
        top_rows,
        in_full,
        out_full,
        pair_full,
        down_full,
        gates,
        product,
        mixed,
        mix_share,
    ) = mixer_forward(
        seqs,
        models,
        normed.astype(BF),
        top_grad.astype(BF),
        local_taps,
        mixer_in,
        mixer_out,
        gate_up,
        mlp_down,
    )
    middle = source + mix_share
    normed_two, scale_mlp = normalize(middle, gain_mlp)
    middle_grad, mlp_part, pair_total, down_total = mlp(
        seqs, models, normed_two.astype(BF), top_rows, pair_full, down_full
    )
    middle_grad, gain_mlp_grad = norm_back(middle_grad, middle, scale_mlp, gain_mlp)
    middle_grad = middle_grad + top_grad
    mlp_share, source_grad, taps_part, in_got, out_got, pair_got, down_got = mixer_backward(
        seqs,
        models,
        middle_grad.astype(BF),
        mlp_part,
        local_taps,
        in_full,
        out_full,
        normed_rows,
        gates,
        product,
        mixed,
        pair_total,
        down_total,
    )
    output = (mask * (middle + mlp_share)).astype(BF)
    source_grad, gain_mix_grad = norm_back(source_grad, source, scale_mix, gain_mix)
    small = jnp.zeros((8, width), F32)
    small = lax.dynamic_update_slice(small, taps_part[:taps], (2, model_pos * channels))
    small = small.at[0].set(gain_mix_grad).at[1].set(gain_mlp_grad)
    small = small_sum(seqs, models, small)

    def total(got):
        return jnp.sum(got.astype(F32), axis=0)

    return (
        output,
        source_grad + middle_grad,
        small[0],
        small[1],
        small[2 : 2 + taps],
        total(in_got),
        total(out_got),
        total(pair_got),
        total(down_got),
    )


def solution(mesh):
    placed = (
        P(None, ("seq", "mp"), None),
        P(None, ("seq", "mp"), None),
        P(),
        P(),
        P(),
        P(),
        P(None, "seq", "mp"),
        P("mp", "seq"),
        P(None, "seq", "mp"),
        P("mp", "seq"),
    )
    return jax.shard_map(
        local,
        mesh=mesh,
        in_specs=placed,
        out_specs=(
            P(None, ("seq", "mp"), None),
            P(None, ("seq", "mp"), None),
            P(),
            P(),
            P(),
            P(None, "seq", "mp"),
            P("mp", "seq"),
            P(None, "seq", "mp"),
            P("mp", "seq"),
        ),
        check_vma=False,
    )
```

```python
import functools

import jax
import jax.numpy as jnp
from jax import lax
from jax.experimental import pallas as pl
from jax.experimental.pallas import tpu as pltpu
from jax.sharding import PartitionSpec as P

EPS = 1e-05
MESH = pl.DeviceIdType.MESH
BF = jnp.bfloat16
F32 = jnp.float32
HALVES = 2
VMEM_LIMIT = 63 * 2**20


def nn(a, b):
    return lax.dot_general(a, b, (((1,), (0,)), ((), ())), preferred_element_type=F32)


def nt(a, b):
    return lax.dot_general(a, b, (((1,), (1,)), ((), ())), preferred_element_type=F32)


def tn(a, b):
    return lax.dot_general(a, b, (((0,), (0,)), ((), ())), preferred_element_type=F32)


class Place:
    def __init__(self, seqs, models):
        self.seqs, self.chips = seqs, models // 2
        self.s = lax.axis_index("seq")
        self.m = lax.axis_index("mp")
        self.z = self.m // 2
        self.c = self.m % 2
        self.sibling = {"mp": self.m + 1 - 2 * self.c}
        self.above = {"mp": self.m + 2}
        self.below = {"mp": self.m - 2}
        self.has_above = self.z < self.chips - 1
        self.has_below = self.z > 0

    def peer(self, step):
        return {"seq": lax.rem(self.s + step, self.seqs)}

    def enter(self):
        barrier = pltpu.get_barrier_semaphore()

        def greet(where):
            pl.semaphore_signal(barrier, inc=1, device_id=where, device_id_type=MESH)

        greet(self.sibling)
        for step in range(1, self.seqs):
            greet(self.peer(step))
        pl.when(self.has_above)(lambda: greet(self.above))
        pl.when(self.has_below)(lambda: greet(self.below))
        chips = self.chips
        lines = (self.z + chips - 1) // chips + (2 * chips - 2 - self.z) // chips
        pl.semaphore_wait(barrier, self.seqs + lines)


def remote(src, dst, send, recv, where):
    return pltpu.make_async_remote_copy(
        src_ref=src, dst_ref=dst, send_sem=send, recv_sem=recv, device_id=where, device_id_type=MESH
    )


class Gather:
    def __init__(self, place, rows, own, sems):
        self.p, self.rows, self.own = place, rows, own
        self.share = rows.shape[0] // (2 * place.chips)
        self.piece = self.share // HALVES
        self.send, self.recv = sems

    def at(self, chip, core, half):
        return self.rows.at[pl.ds((chip * 2 + core) * self.share + half * self.piece, self.piece)]

    def copy(self, kind, chip, half, own=False):
        p = self.p
        where = (p.above, p.below, p.sibling)[kind]
        dst = self.at(chip, p.c, half)
        src = self.own.at[pl.ds(half * self.piece, self.piece)] if own and self.own is not None else dst
        return remote(src, dst, self.send.at[kind, chip, half], self.recv.at[kind // 2, chip, half], where)

    def start(self):
        p = self.p
        for half in range(HALVES):
            pl.when(p.has_above)(lambda h=half: self.copy(0, p.z, h, True).start())
            pl.when(p.has_below)(lambda h=half: self.copy(1, p.z, h, True).start())
        for half in range(HALVES):
            self.copy(2, p.z, half, True).start()

    def round(self, k):
        p = self.p
        for half in range(HALVES):

            @pl.when(p.z >= k)
            def _(half=half):
                chip = p.z - k
                self.copy(0, chip, half).wait_recv()
                pl.when(p.has_above)(lambda: self.copy(0, chip, half).start())
                self.copy(2, chip, half).start()

            @pl.when(p.z + k <= p.chips - 1)
            def _(half=half):
                chip = p.z + k
                self.copy(1, chip, half).wait_recv()
                pl.when(p.has_below)(lambda: self.copy(1, chip, half).start())
                self.copy(2, chip, half).start()

    def rounds(self):
        return [functools.partial(self.round, k) for k in range(1, self.p.chips)]

    def other_core(self, chip):
        p = self.p
        for half in range(HALVES):
            dst = self.at(chip, 1 - p.c, half)
            remote(dst, dst, self.send.at[2, chip, half], self.recv.at[1, chip, half], p.sibling).wait_recv()

    def arrived(self):
        for chip in range(self.p.chips):
            self.other_core(chip)

    def drain(self):
        p = self.p
        for chip in range(p.chips):
            for half in range(HALVES):
                pl.when(p.has_above & (chip <= p.z))(lambda ch=chip, h=half: self.copy(0, ch, h).wait_send())
                pl.when(p.has_below & (chip >= p.z))(lambda ch=chip, h=half: self.copy(1, ch, h).wait_send())
                self.copy(2, chip, half).wait_send()


class Scatter:
    def __init__(self, place, part, from_core, from_line, sems):
        self.p, self.part, self.from_core, self.from_line = place, part, from_core, from_line
        self.share = from_core.shape[1]
        self.piece = self.share // HALVES
        self.core_send, self.core_recv, self.line_send, self.line_recv = sems

    def rows(self, chip, core):
        return self.part.at[pl.ds((chip * 2 + core) * self.share, self.share)]

    def core_copy(self, chip):
        p = self.p
        return remote(
            self.rows(chip, 1 - p.c), self.from_core.at[chip], self.core_send.at[chip], self.core_recv.at[chip], p.sibling
        )

    def give(self, chip):
        self.core_copy(chip).start()

    def mine(self, chip, half):
        return self.part.at[pl.ds((chip * 2 + self.p.c) * self.share + half * self.piece, self.piece)]

    def line_copy(self, down, chip, slot, half):
        p = self.p
        dst = self.from_line.at[slot, pl.ds(half * self.piece, self.piece)]
        return remote(
            self.mine(chip, half),
            dst,
            self.line_send.at[down, chip, half],
            self.line_recv.at[slot, half],
            p.below if down else p.above,
        )

    def total(self, chip, half, slots):
        span = pl.ds(half * self.piece, self.piece)
        value = self.mine(chip, half)[...].astype(F32) + self.from_core[chip, span].astype(F32)
        for slot in slots:
            value = value + self.from_line[slot, span].astype(F32)
        return value

    def hop(self, down, chip, slot, has_source):
        self.core_copy(chip).wait_recv()
        for half in range(HALVES):

            @pl.when(has_source)
            def _(half=half):
                self.line_copy(down, chip, chip, half).wait_recv()
                self.mine(chip, half)[...] = self.total(chip, half, [chip]).astype(BF)

            @pl.when(jnp.logical_not(has_source))
            def _(half=half):
                self.mine(chip, half)[...] = self.total(chip, half, []).astype(BF)

            self.line_copy(down, chip, slot, half).start()

    def round(self, r):
        p = self.p
        last = p.chips - 1

        @pl.when((p.z <= r) & p.has_above)
        def _():
            chip = last - r + p.z
            self.hop(0, chip, chip, p.has_below)

        @pl.when((last - p.z <= r) & p.has_below)
        def _():
            chip = r - last + p.z
            self.hop(1, chip, p.chips if r == last - 1 else chip, p.has_above)

    def rounds(self):
        return [functools.partial(self.round, r) for r in range(self.p.chips - 1)]

    def finish(self, store):
        p = self.p
        self.core_copy(p.z).wait_recv()
        for half in range(HALVES):
            pl.when(p.has_below)(lambda h=half: self.line_copy(0, p.z, p.z, h).wait_recv())
            pl.when(p.has_above)(lambda h=half: self.line_copy(1, p.z, p.chips, h).wait_recv())
            for up in (False, True):
                for low in (False, True):

                    @pl.when((p.has_above == up) & (p.has_below == low))
                    def _(half=half, up=up, low=low):
                        slots = ([p.z] if low else []) + ([p.chips] if up else [])
                        store(half * self.piece, self.piece, self.total(p.z, half, slots))

    def drain(self):
        p = self.p
        for chip in range(p.chips):
            self.core_copy(chip).wait_send()
            for half in range(HALVES):
                pl.when(p.has_above & (chip > p.z))(lambda ch=chip, h=half: self.line_copy(0, ch, ch, h).wait_send())
                pl.when(p.has_below & (chip < p.z))(lambda ch=chip, h=half: self.line_copy(1, ch, ch, h).wait_send())


def gather_sems(count, chips):
    return [pltpu.SemaphoreType.DMA((count, 3, chips, HALVES)), pltpu.SemaphoreType.DMA((count, 2, chips, HALVES))]


def scatter_sems(count, chips):
    return [
        pltpu.SemaphoreType.DMA((count, chips)),
        pltpu.SemaphoreType.DMA((count, chips)),
        pltpu.SemaphoreType.DMA((count, 2, chips, HALVES)),
        pltpu.SemaphoreType.DMA((count, chips + 1, HALVES)),
    ]


def picks(sems, index):
    return [sem.at[index] for sem in sems]


def far_first(place):
    low, high = 0, place.chips - 1
    order = []
    for _ in range(place.chips):
        left = place.z - low >= high - place.z
        order.append(jnp.where(left, low, high))
        low, high = jnp.where(left, low + 1, low), jnp.where(left, high, high - 1)
    return order


def weave(*lists):
    for step in range(max(len(steps) for steps in lists)):
        for steps in lists:
            if step < len(steps):
                steps[step]()


class Shards:
    def __init__(self, place, shard, full, dim, sems):
        self.p, self.shard, self.full, self.dim = place, shard, full, dim
        self.send, self.recv, self.local = sems

    def at(self, owner):
        size = self.shard.shape[self.dim]
        span = pl.ds(pl.multiple_of(owner * size, size), size)
        return self.full.at[(slice(None),) * self.dim + (span,)]

    def copy(self, step):
        p = self.p
        return remote(self.shard, self.at(p.s), self.send.at[step - 1], self.recv.at[step - 1], p.peer(step))

    def local_copy(self):
        return pltpu.make_async_copy(self.shard, self.at(self.p.s), self.local)

    def start(self):
        for step in range(1, self.p.seqs):
            self.copy(step).start()
        self.local_copy().start()

    def arrived(self):
        self.local_copy().wait()
        for step in range(1, self.p.seqs):
            self.copy(step).wait_recv()

    def drain(self):
        for step in range(1, self.p.seqs):
            self.copy(step).wait_send()


def mixer_forward_kernel(
    seqs,
    models,
    normed_ref,
    top_ref,
    taps_ref,
    in_ref,
    out_ref,
    pair_ref,
    down_ref,
    normed_rows,
    top_rows,
    in_rows,
    out_rows,
    pair_rows,
    down_rows,
    gates_out,
    product_out,
    mixed_out,
    mix_out,
    in_full,
    out_full,
    rows,
    gates,
    product,
    mixed,
    part,
    from_core,
    from_line,
    total,
    w_send,
    w_recv,
    w_local,
    halo_send,
    halo_recv,
    keep,
    *sems,
):
    p = Place(seqs, models)
    chips = p.chips
    g_sems, s_sems = sems[:2], sems[2:]
    slots, block = rows.shape[0], rows.shape[1]
    tile = block // chips
    share = tile // 2
    channels = in_full.shape[2]
    p.enter()

    firsts = [Gather(p, rows.at[slot], normed_ref.at[slot], picks(g_sems, slot)) for slot in range(slots)]
    tops = [Gather(p, top_rows.at[slot], top_ref.at[slot], picks(g_sems, slots + slot)) for slot in range(slots)]
    sums = [
        Scatter(p, part.at[slot], from_core.at[slot], from_line.at[slot], picks(s_sems, slot)) for slot in range(slots)
    ]
    weights = [
        Shards(p, shard, full, dim, (w_send.at[i], w_recv.at[i], w_local.at[i]))
        for i, (shard, full, dim) in enumerate(
            ((in_ref, in_full, 1), (out_ref, out_full, 1), (pair_ref, pair_rows, 1), (down_ref, down_rows, 1))
        )
    ]

    def own(slot, which, source):
        span = pl.ds(p.m * share, share)
        return pltpu.make_async_copy(source.at[slot], which.at[slot, span], keep.at[slot + (slots if which is top_rows else 0)])

    for slot in range(slots):
        own(slot, rows, normed_ref).start()
        own(slot, top_rows, top_ref).start()

    def halo(slot):
        return remote(
            product.at[slot, pl.ds(block, 8)],
            product.at[slot, pl.ds(0, 8)],
            halo_send.at[slot],
            halo_recv.at[slot],
            p.peer(1),
        )

    has_later, has_earlier = p.s < seqs - 1, p.s > 0
    for slot in range(slots):

        @pl.when(jnp.logical_not(has_earlier))
        def _(slot=slot):
            product[slot, pl.ds(0, 8)] = jnp.zeros((8, channels), F32)

    def project(slot):
        @pl.loop(0, chips)
        def _(i):
            span = pl.ds(i * tile, tile)
            source = rows[slot, span]
            b_gate = nn(source, in_full[0])
            x_value = nn(source, in_full[2])
            gates[slot, 0, span] = b_gate
            gates[slot, 1, span] = nn(source, in_full[1])
            gates[slot, 2, span] = x_value
            product[slot, pl.ds(8 + i * tile, tile)] = b_gate * x_value

        pl.when(has_later)(lambda: halo(slot).start())

    def convolve(slot):
        pl.when(has_earlier)(lambda: halo(slot).wait_recv())
        for i in range(chips):
            conv = 0.0
            for offset in range(taps_ref.shape[0]):
                conv = conv + taps_ref[offset : offset + 1] * product[slot, pl.ds(8 + i * tile - offset, tile)]
            mixed[slot, pl.ds(i * tile, tile)] = (gates[slot, 1, pl.ds(i * tile, tile)] * conv).astype(BF)

    def project_out(slot):
        for chip in far_first(p):
            span = pl.ds(chip * tile, tile)
            part[slot, span] = nn(mixed[slot, span], out_full[...]).astype(BF)
            sums[slot].give(chip)

    def finish(slot):
        def store(first, size, value):
            total[slot, pl.ds(first, size)] = value

        sums[slot].finish(store)

    firsts[0].start()
    weights[0].start()
    weights[1].start()
    steps = firsts[0].rounds()
    for step in steps[:-1]:
        step()
    firsts[1].start()
    steps[-1]()
    own(0, rows, normed_ref).wait()
    firsts[0].arrived()
    weights[0].arrived()
    weights[1].arrived()
    project(0)
    weights[3].start()
    steps = firsts[1].rounds()
    steps[0]()
    convolve(0)
    project_out(0)
    weave(sums[0].rounds(), steps[1:])
    tops[0].start()
    own(1, rows, normed_ref).wait()
    firsts[1].arrived()
    project(1)
    weights[2].start()
    steps = tops[0].rounds()
    steps[0]()
    convolve(1)
    project_out(1)
    finish(0)
    weave(sums[1].rounds(), steps[1:])
    tops[1].start()
    finish(1)
    stores = [
        pltpu.make_async_copy(src, dst, keep.at[2 * slots + i])
        for i, (src, dst) in enumerate(
            (
                (rows, normed_rows),
                (in_full, in_rows),
                (out_full, out_rows),
                (gates, gates_out),
                (product, product_out),
                (mixed, mixed_out),
                (total, mix_out),
            )
        )
    ]
    for store in stores:
        store.start()
    weave(tops[1].rounds())
    for slot in range(slots):
        own(slot, top_rows, top_ref).wait()
        tops[slot].arrived()
    weights[2].arrived()
    weights[3].arrived()
    for store in stores:
        store.wait()
    for thing in firsts + tops + sums + weights:
        thing.drain()
    for slot in range(slots):
        pl.when(has_later)(lambda slot=slot: halo(slot).wait_send())


def mixer_forward(seqs, models, normed, top, taps, mixer_in, mixer_out, gate_up, mlp_down):
    slots, share, width = normed.shape
    chips = models // 2
    block = share * models
    channels = mixer_in.shape[2]
    units = gate_up.shape[2]
    hbm = pl.BlockSpec(memory_space=pltpu.HBM)
    shape = jax.ShapeDtypeStruct
    return pl.pallas_call(
        functools.partial(mixer_forward_kernel, seqs, models),
        out_shape=[
            shape((slots, block, width), BF),
            shape((slots, block, width), BF),
            shape((3, width, channels), BF),
            shape((channels, width), BF),
            shape((2, width, units), BF),
            shape((units, width), BF),
            shape((slots, 3, block, channels), F32),
            shape((slots, block + 8, channels), F32),
            shape((slots, block, channels), BF),
            shape((slots, share, width), F32),
        ],
        in_specs=[hbm, hbm, pl.BlockSpec(memory_space=pltpu.VMEM)] + [hbm] * 4,
        out_specs=[hbm] * 10,
        scratch_shapes=[
            pltpu.VMEM((3, width, channels), BF),
            pltpu.VMEM((channels, width), BF),
            pltpu.VMEM((slots, block, width), BF),
            pltpu.VMEM((slots, 3, block, channels), F32),
            pltpu.VMEM((slots, block + 8, channels), F32),
            pltpu.VMEM((slots, block, channels), BF),
            pltpu.VMEM((slots, block, width), BF),
            pltpu.VMEM((slots, chips, share, width), BF),
            pltpu.VMEM((slots, chips + 1, share, width), BF),
            pltpu.VMEM((slots, share, width), F32),
            pltpu.SemaphoreType.DMA((4, seqs - 1)),
            pltpu.SemaphoreType.DMA((4, seqs - 1)),
            pltpu.SemaphoreType.DMA((4,)),
            pltpu.SemaphoreType.DMA((slots,)),
            pltpu.SemaphoreType.DMA((slots,)),
            pltpu.SemaphoreType.DMA((2 * slots + 7,)),
            *gather_sems(2 * slots, chips),
            *scatter_sems(slots, chips),
        ],
        compiler_params=pltpu.CompilerParams(collective_id=1, has_side_effects=True, vmem_limit_bytes=VMEM_LIMIT),
    )(normed, top, taps, mixer_in, mixer_out, gate_up, mlp_down)


def mlp_kernel(
    seqs,
    models,
    normed_ref,
    top_rows,
    pair_ref,
    down_ref,
    grad_out,
    mlp_part,
    pair_grad,
    down_grad,
    pair,
    down,
    rows,
    top_tile,
    top_cols,
    acts,
    stage,
    part,
    from_core,
    from_line,
    total,
    load,
    tile_sem,
    cols_sem,
    stage_sem,
    keep,
    *sems,
):
    p = Place(seqs, models)
    chips = p.chips
    g_sems, s_sems = sems[:2], sems[2:]
    slots, block, width = rows.shape
    units = down.shape[0]
    tile = block // chips
    share = tile // 2
    unit_block = min(512, units)
    wide_block = 512
    columns = top_cols.shape[-1]
    loads = [pltpu.make_async_copy(pair_ref, pair, load.at[0]), pltpu.make_async_copy(down_ref, down, load.at[1])]
    for thing in loads:
        thing.start()
    p.enter()
    gathers = [Gather(p, rows.at[slot], normed_ref.at[slot], picks(g_sems, slot)) for slot in range(slots)]
    sums = [
        Scatter(p, part.at[slot], from_core.at[slot], from_line.at[slot], picks(s_sems, slot)) for slot in range(slots)
    ]

    def own(slot):
        return pltpu.make_async_copy(
            normed_ref.at[slot], rows.at[slot, pl.ds(p.m * share, share)], load.at[2 + slot]
        )

    order = far_first(p)[::-1]
    tiles = [(slot, chip) for slot in range(slots) for chip in order]

    def fetch(index):
        slot, chip = tiles[index]
        return pltpu.make_async_copy(
            top_rows.at[slot, pl.ds(chip * tile, tile)], top_tile.at[index % 2], tile_sem.at[index % 2]
        )

    def put(index):
        slot, chip = tiles[index]
        return pltpu.make_async_copy(
            stage.at[index % 2], mlp_part.at[slot, pl.ds(chip * tile, tile)], stage_sem.at[index % 2]
        )

    def work(index):
        slot, chip = tiles[index]
        buf = index % 2
        span = pl.ds(chip * tile, tile)
        fetch(index).wait()
        if index + 1 < len(tiles):
            fetch(index + 1).start()
        if index >= 2:
            put(index - 2).wait()

        @pl.loop(0, units // unit_block)
        def _(i):
            cut = pl.ds(pl.multiple_of(i * unit_block, unit_block), unit_block)
            source = rows[slot, span]
            gate = nn(source, pair[0, :, cut])
            up = nn(source, pair[1, :, cut])
            act_grad = nt(top_tile[buf], down[cut])
            sigma = jax.nn.sigmoid(gate)
            silu = gate * sigma
            acts[0, slot, span, cut] = (silu * up).astype(BF)
            acts[1, slot, span, cut] = (act_grad * up * sigma * (1.0 + gate * (1.0 - sigma))).astype(BF)
            acts[2, slot, span, cut] = (act_grad * silu).astype(BF)

        @pl.loop(0, width // wide_block)
        def _(i):
            cut = pl.ds(pl.multiple_of(i * wide_block, wide_block), wide_block)
            value = nt(acts[1, slot, span], pair[0, cut]) + nt(acts[2, slot, span], pair[1, cut])
            part[slot, span, cut] = value.astype(BF)
            stage[buf, :, cut] = nn(acts[0, slot, span], down[:, cut]).astype(BF)

        sums[slot].give(chip)
        put(index).start()

    def finish(slot):
        def store(first, size, value):
            total[slot, pl.ds(first, size)] = value

        sums[slot].finish(store)

    def pair_step(index):
        k, first = divmod(index, width // wide_block)
        cut = pl.ds(first * wide_block, wide_block)
        value = 0.0
        for slot in range(slots):
            value = value + tn(rows[slot, :, cut], acts[1 + k, slot])
        pair[k, cut] = value.astype(BF)
        pltpu.make_async_copy(pair.at[k, cut], pair_grad.at[k, cut], keep.at[index]).start()

    pair_steps = 2 * (width // wide_block)

    def fetch_columns(index):
        return pltpu.make_async_copy(
            top_rows.at[:, :, pl.ds(index * columns, columns)], top_cols.at[index % 2], cols_sem.at[index % 2]
        )

    def down_step(index):
        fetch_columns(index).wait()
        for first in range(0, units, unit_block):
            cut = pl.ds(first, unit_block)
            value = 0.0
            for slot in range(slots):
                value = value + tn(acts[0, slot, :, cut], top_cols[index % 2, slot])
            down[cut, pl.ds(index * columns, columns)] = value.astype(BF)
        if index + 2 < width // columns:
            fetch_columns(index + 2).start()

    for slot in range(slots):
        own(slot).start()
    fetch(0).start()
    gathers[0].start()
    own(0).wait()
    own(1).wait()
    for thing in loads:
        thing.wait()
    for index in range(chips):
        if index:
            gathers[0].round(index)
        if index == chips - 2:
            gathers[1].start()
        gathers[0].other_core(order[index])
        work(index)
    hops = sums[0].rounds()
    for index in range(chips):
        if index < len(hops):
            hops[index]()
        if index:
            gathers[1].round(index)
        gathers[1].other_core(order[index])
        work(chips + index)
    hops = sums[1].rounds()
    hops[0]()
    finish(0)
    fetch_columns(0).start()
    fetch_columns(1).start()
    work_steps = [functools.partial(pair_step, index) for index in range(pair_steps)]
    work_steps += [functools.partial(down_step, index) for index in range(width // columns)]
    spaced = len(work_steps) // len(hops)
    for index, step in enumerate(work_steps):
        step()
        if (index + 1) % spaced == 0 and (index + 1) // spaced < len(hops):
            hops[(index + 1) // spaced]()
    finish(1)
    last = [
        pltpu.make_async_copy(down, down_grad, keep.at[pair_steps]),
        pltpu.make_async_copy(total, grad_out, keep.at[pair_steps + 1]),
    ]
    for thing in last:
        thing.start()
    for index in range(pair_steps):
        k, first = divmod(index, width // wide_block)
        cut = pl.ds(first * wide_block, wide_block)
        pltpu.make_async_copy(pair.at[k, cut], pair_grad.at[k, cut], keep.at[index]).wait()
    for index in range(len(tiles) - 2, len(tiles)):
        put(index).wait()
    for thing in last:
        thing.wait()
    for thing in gathers + sums:
        thing.drain()


def mlp(seqs, models, normed, top_rows, pair_full, down_full):
    slots, share, width = normed.shape
    chips = models // 2
    block = share * models
    units = down_full.shape[0]
    hbm = pl.BlockSpec(memory_space=pltpu.HBM)
    shape = jax.ShapeDtypeStruct
    return pl.pallas_call(
        functools.partial(mlp_kernel, seqs, models),
        out_shape=[
            shape((slots, share, width), F32),
            shape((slots, block, width), BF),
            shape((2, width, units), BF),
            shape((units, width), BF),
        ],
        in_specs=[hbm] * 4,
        out_specs=[hbm] * 4,
        scratch_shapes=[
            pltpu.VMEM((2, width, units), BF),
            pltpu.VMEM((units, width), BF),
            pltpu.VMEM((slots, block, width), BF),
            pltpu.VMEM((2, block // chips, width), BF),
            pltpu.VMEM((2, slots, block, 256), BF),
            pltpu.VMEM((3, slots, block, units), BF),
            pltpu.VMEM((2, block // chips, width), BF),
            pltpu.VMEM((slots, block, width), BF),
            pltpu.VMEM((slots, chips, share, width), BF),
            pltpu.VMEM((slots, chips + 1, share, width), BF),
            pltpu.VMEM((slots, share, width), F32),
            pltpu.SemaphoreType.DMA((2 + slots,)),
            pltpu.SemaphoreType.DMA((2,)),
            pltpu.SemaphoreType.DMA((2,)),
            pltpu.SemaphoreType.DMA((2,)),
            pltpu.SemaphoreType.DMA((2 * (width // 512) + 2,)),
            *gather_sems(slots, chips),
            *scatter_sems(slots, chips),
        ],
        compiler_params=pltpu.CompilerParams(collective_id=2, has_side_effects=True, vmem_limit_bytes=VMEM_LIMIT),
    )(normed, top_rows, pair_full, down_full)


class Spread:
    def __init__(self, place, partial, got, sems):
        self.p, self.partial, self.got = place, partial, got
        self.send, self.recv, self.local = sems

    def block(self, owner):
        size = self.partial.shape[1] // self.p.seqs
        return self.partial.at[:, pl.ds(pl.multiple_of(owner * size, size), size)]

    def copy(self, step):
        p = self.p
        return remote(
            self.block(lax.rem(p.s + step, p.seqs)),
            self.got(step),
            self.send.at[step - 1],
            self.recv.at[step - 1],
            p.peer(step),
        )

    def local_copy(self):
        return pltpu.make_async_copy(self.block(self.p.s), self.got(0), self.local)

    def start(self):
        for step in range(1, self.p.seqs):
            self.copy(step).start()
        self.local_copy().start()

    def finish(self):
        self.local_copy().wait()
        for step in range(1, self.p.seqs):
            self.copy(step).wait()


def mixer_backward_kernel(
    seqs,
    models,
    low_ref,
    mlp_part,
    taps_ref,
    in_ref,
    out_ref,
    normed_rows,
    gates_ref,
    product_ref,
    mixed_ref,
    pair_grad,
    down_grad,
    mlp_out,
    grad_out,
    taps_out,
    in_got,
    out_got,
    pair_got,
    down_got,
    in_full,
    out_full,
    rows,
    columns,
    gates,
    product,
    mixed,
    conv_grad,
    stacked,
    part,
    from_core,
    from_line,
    mlp_total,
    grad_total,
    load,
    cols_sem,
    w_send,
    w_recv,
    w_local,
    halo_send,
    halo_recv,
    free,
    *sems,
):
    p = Place(seqs, models)
    chips = p.chips
    g_sems, s_sems = sems[:2], sems[2:]
    slots, block, width = rows.shape
    channels = out_full.shape[0]
    taps = taps_ref.shape[0]
    tile = block // chips
    share = tile // 2
    wide_block = 512
    cols = columns.shape[-1]
    loads = [
        pltpu.make_async_copy(src, dst, load.at[i])
        for i, (src, dst) in enumerate(
            [(mlp_part.at[slot], part.at[slot]) for slot in range(slots)]
            + [
                (low_ref.at[slot], rows.at[slot, pl.ds(p.m * share, share)])
                for slot in range(slots)
            ]
            + [
                (in_ref, in_full),
                (out_ref, out_full),
                (gates_ref, gates),
                (product_ref, product),
                (mixed_ref, mixed),
            ]
        )
    ]
    for thing in loads:
        thing.start()
    p.enter()
    gathers = [Gather(p, rows.at[slot], low_ref.at[slot], picks(g_sems, slot)) for slot in range(slots)]

    def scatter(slot, index):
        return Scatter(p, part.at[slot], from_core.at[slot], from_line.at[slot], picks(s_sems, index))

    mlp_sums = [scatter(slot, slot) for slot in range(slots)]
    sums = [scatter(slot, slots + slot) for slot in range(slots)]
    spreads = [
        Spread(p, partial, got, (w_send.at[i], w_recv.at[i], w_local.at[i]))
        for i, (partial, got) in enumerate(
            (
                (pair_grad.at[pl.ds(0, 1)], lambda step: pair_got.at[step, pl.ds(0, 1)]),
                (down_grad, lambda step: down_got.at[step]),
                (in_full, lambda step: in_got.at[step]),
                (out_full, lambda step: out_got.at[step]),
                (pair_grad.at[pl.ds(1, 1)], lambda step: pair_got.at[step, pl.ds(1, 1)]),
            )
        )
    ]
    has_later, has_earlier = p.s < seqs - 1, p.s > 0
    order = far_first(p)

    def halo(slot):
        return remote(
            conv_grad.at[slot, pl.ds(0, 8)],
            conv_grad.at[slot, pl.ds(block, 8)],
            halo_send.at[slot],
            halo_recv.at[slot],
            p.peer(seqs - 1),
        )

    for slot in range(slots):

        @pl.when(jnp.logical_not(has_later))
        def _(slot=slot):
            conv_grad[slot, pl.ds(block, 8)] = jnp.zeros((8, channels), F32)

    taps_out[...] = jnp.zeros_like(taps_out)

    def first_pass(slot):
        for i in range(chips):
            span = pl.ds(i * tile, tile)
            mixed_grad = nt(rows[slot, span], out_full[...])
            grad = mixed_grad * gates[slot, 1, span]
            conv_grad[slot, span] = grad
            conv = 0.0
            for offset in range(taps):
                earlier = product[slot, pl.ds(8 + i * tile - offset, tile)]
                conv = conv + taps_ref[offset : offset + 1] * earlier
                taps_out[offset : offset + 1] += jnp.sum(grad * earlier, axis=0, keepdims=True)
            stacked[slot, span, pl.ds(channels, channels)] = (mixed_grad * conv).astype(BF)
            if i == 0:
                pl.when(has_earlier)(lambda: halo(slot).start())

    def second_pass(slot):
        pl.when(has_later)(lambda: halo(slot).wait_recv())
        for i in range(chips):
            span = pl.ds(i * tile, tile)
            grad = 0.0
            for offset in range(taps):
                grad = grad + taps_ref[offset : offset + 1] * conv_grad[slot, pl.ds(i * tile + offset, tile)]
            stacked[slot, span, pl.ds(0, channels)] = (grad * gates[slot, 2, span]).astype(BF)
            stacked[slot, span, pl.ds(2 * channels, channels)] = (grad * gates[slot, 0, span]).astype(BF)

    def third_pass(slot):
        for chip in order:
            span = pl.ds(chip * tile, tile)

            @pl.loop(0, width // wide_block)
            def _(i):
                cut = pl.ds(pl.multiple_of(i * wide_block, wide_block), wide_block)
                value = 0.0
                for k in range(3):
                    value = value + nt(stacked[slot, span, pl.ds(k * channels, channels)], in_full[k, cut])
                part[slot, span, cut] = value.astype(BF)

            sums[slot].give(chip)

    def finish(what, total, slot):
        def store(first, size, value):
            total[slot, pl.ds(first, size)] = value

        what[slot].finish(store)

    def neighbours(act):
        act(p.sibling)
        pl.when(p.has_above)(lambda: act(p.above))
        pl.when(p.has_below)(lambda: act(p.below))

    def give_free(slot):
        mlp_sums[slot].drain()
        neighbours(
            lambda where: pl.semaphore_signal(free.at[slot], inc=1, device_id=where, device_id_type=MESH)
        )

    def take_free(slot):
        lines = (p.z + chips - 1) // chips + (2 * chips - 2 - p.z) // chips
        pl.semaphore_wait(free.at[slot], 1 + lines)

    def fetch_columns(index):
        return pltpu.make_async_copy(
            normed_rows.at[:, :, pl.ds(index * cols, cols)], columns.at[index % 2], cols_sem.at[index % 2]
        )

    steps_in = width // cols

    def in_step(index):
        fetch_columns(index).wait()
        value = 0.0
        for slot in range(slots):
            value = value + tn(columns[index % 2, slot], stacked[slot])
        for k in range(3):
            in_full[k, pl.ds(index * cols, cols)] = value[:, k * channels : (k + 1) * channels].astype(BF)
        if index + 2 < steps_in:
            fetch_columns(index + 2).start()

    def out_step():
        for first in range(0, width, wide_block):
            cut = pl.ds(first, wide_block)
            value = 0.0
            for slot in range(slots):
                value = value + tn(mixed[slot], rows[slot, :, cut])
            out_full[:, cut] = value.astype(BF)

    spreads[1].start()
    gathers[0].start()
    loads[0].wait()
    for chip in order:
        mlp_sums[0].give(chip)
    hops, next_rows = mlp_sums[0].rounds(), gathers[0].rounds()
    weave(hops[:-1], next_rows[:-1])
    gathers[1].start()
    weave(hops[-1:], next_rows[-1:])
    loads[1].wait()
    for chip in order:
        mlp_sums[1].give(chip)
    loads[2].wait()
    for thing in loads[2 + slots :]:
        thing.wait()
    gathers[0].arrived()
    fetch_columns(0).start()
    fetch_columns(1).start()
    mlp_hops, next_rows, hops = mlp_sums[1].rounds(), gathers[1].rounds(), sums[0].rounds()
    first_pass(0)
    spreads[0].start()
    finish(mlp_sums, mlp_total, 0)
    give_free(0)
    weave(mlp_hops[:1], next_rows[:1])
    second_pass(0)
    take_free(0)
    third_pass(0)
    weave(mlp_hops[1:], next_rows[1:], hops[:1])
    loads[3].wait()
    gathers[1].arrived()
    first_pass(1)
    spreads[4].start()
    finish(mlp_sums, mlp_total, 1)
    give_free(1)
    hops[1]()
    second_pass(1)
    take_free(1)
    weave(hops[2:])
    third_pass(1)
    hops = sums[1].rounds()
    hops[0]()
    out_step()
    spreads[3].start()
    for index in range(steps_in):
        in_step(index)
    spreads[2].start()
    weave(hops[1:])
    finish(sums, grad_total, 0)
    finish(sums, grad_total, 1)
    last = [
        pltpu.make_async_copy(mlp_total, mlp_out, load.at[0]),
        pltpu.make_async_copy(grad_total, grad_out, load.at[1]),
    ]
    for thing in last:
        thing.start()
    for thing in spreads:
        thing.finish()
    for thing in last:
        thing.wait()
    for thing in gathers + sums:
        thing.drain()
    for slot in range(slots):
        pl.when(has_earlier)(lambda slot=slot: halo(slot).wait_send())


def mixer_backward(
    seqs, models, low, mlp_part, taps, in_full, out_full, normed_rows, gates, product, mixed, pair_grad, down_grad
):
    slots, share, width = low.shape
    chips = models // 2
    block = share * models
    channels = out_full.shape[0]
    units = down_grad.shape[0]
    hbm = pl.BlockSpec(memory_space=pltpu.HBM)
    vmem = pl.BlockSpec(memory_space=pltpu.VMEM)
    shape = jax.ShapeDtypeStruct
    return pl.pallas_call(
        functools.partial(mixer_backward_kernel, seqs, models),
        out_shape=[
            shape((slots, share, width), F32),
            shape((slots, share, width), F32),
            shape((8, channels), F32),
            shape((seqs, 3, width // seqs, channels), BF),
            shape((seqs, channels, width // seqs), BF),
            shape((seqs, 2, width // seqs, units), BF),
            shape((seqs, units, width // seqs), BF),
        ],
        in_specs=[hbm, hbm, vmem] + [hbm] * 8,
        out_specs=[hbm, hbm, vmem] + [hbm] * 4,
        scratch_shapes=[
            pltpu.VMEM((3, width, channels), BF),
            pltpu.VMEM((channels, width), BF),
            pltpu.VMEM((slots, block, width), BF),
            pltpu.VMEM((2, slots, block, 256), BF),
            pltpu.VMEM((slots, 3, block, channels), F32),
            pltpu.VMEM((slots, block + 8, channels), F32),
            pltpu.VMEM((slots, block, channels), BF),
            pltpu.VMEM((slots, block + 8, channels), F32),
            pltpu.VMEM((slots, block, 3 * channels), BF),
            pltpu.VMEM((slots, block, width), BF),
            pltpu.VMEM((slots, chips, share, width), BF),
            pltpu.VMEM((slots, chips + 1, share, width), BF),
            pltpu.VMEM((slots, share, width), F32),
            pltpu.VMEM((slots, share, width), F32),
            pltpu.SemaphoreType.DMA((2 * slots + 5,)),
            pltpu.SemaphoreType.DMA((2,)),
            pltpu.SemaphoreType.DMA((5, seqs - 1)),
            pltpu.SemaphoreType.DMA((5, seqs - 1)),
            pltpu.SemaphoreType.DMA((5,)),
            pltpu.SemaphoreType.DMA((slots,)),
            pltpu.SemaphoreType.DMA((slots,)),
            pltpu.SemaphoreType.REGULAR((slots,)),
            *gather_sems(slots, chips),
            *scatter_sems(2 * slots, chips),
        ],
        compiler_params=pltpu.CompilerParams(collective_id=3, has_side_effects=True, vmem_limit_bytes=VMEM_LIMIT),
    )(low, mlp_part, taps, in_full, out_full, normed_rows, gates, product, mixed, pair_grad, down_grad)


def small_sum_kernel(seqs, models, value_ref, out_ref, by_model, by_seq, send, recv, seq_send, seq_recv):
    s, m = lax.axis_index("seq"), lax.axis_index("mp")
    cols = by_seq.shape[-1]
    along = [lax.rem(m + step, models) for step in range(1, models)]
    across = [lax.rem(s + step, seqs) for step in range(1, seqs)]

    def span(owner):
        return pl.ds(pl.multiple_of(owner * cols, cols), cols)

    barrier = pltpu.get_barrier_semaphore()
    for where in [{"mp": peer} for peer in along] + [{"seq": peer} for peer in across]:
        pl.semaphore_signal(barrier, inc=1, device_id=where, device_id_type=MESH)
    pl.semaphore_wait(barrier, models + seqs - 2)
    by_model[m] = value_ref[:, span(m)]
    copies = [
        remote(value_ref.at[:, span(peer)], by_model.at[m], send.at[0, i], recv.at[0, i], {"mp": peer})
        for i, peer in enumerate(along)
    ]
    for thing in copies:
        thing.start()
    for thing in copies:
        thing.wait()
    by_seq[s] = functools.reduce(lambda a, b: a + b, [by_model[i] for i in range(models)])
    copies = [
        remote(by_seq.at[s], by_seq.at[s], seq_send.at[i], seq_recv.at[i], {"seq": peer})
        for i, peer in enumerate(across)
    ]
    for thing in copies:
        thing.start()
    for thing in copies:
        thing.wait()
    out_ref[:, span(m)] = functools.reduce(lambda a, b: a + b, [by_seq[i] for i in range(seqs)])
    copies = [
        remote(out_ref.at[:, span(m)], out_ref.at[:, span(m)], send.at[1, i], recv.at[1, i], {"mp": peer})
        for i, peer in enumerate(along)
    ]
    for thing in copies:
        thing.start()
    for thing in copies:
        thing.wait()


def small_sum(seqs, models, value):
    vmem = pl.BlockSpec(memory_space=pltpu.VMEM)
    height, width = value.shape
    cols = width // models
    return pl.pallas_call(
        functools.partial(small_sum_kernel, seqs, models),
        out_shape=jax.ShapeDtypeStruct(value.shape, F32),
        in_specs=[vmem],
        out_specs=vmem,
        scratch_shapes=[
            pltpu.VMEM((models, height, cols), F32),
            pltpu.VMEM((seqs, height, cols), F32),
            pltpu.SemaphoreType.DMA((2, models - 1)),
            pltpu.SemaphoreType.DMA((2, models - 1)),
            pltpu.SemaphoreType.DMA((seqs - 1,)),
            pltpu.SemaphoreType.DMA((seqs - 1,)),
        ],
        compiler_params=pltpu.CompilerParams(collective_id=4, has_side_effects=True),
    )(value)


def normalize(values, gain):
    scale = lax.rsqrt(jnp.mean(values * values, axis=-1, keepdims=True) + EPS)
    return (values * scale * gain, scale)


def norm_back(grad, values, scale, gain):
    unit = values * scale
    scaled = grad * gain
    gain_grad = jnp.sum(grad * unit, axis=(0, 1))
    input_grad = scale * (scaled - unit * jnp.mean(scaled * unit, axis=-1, keepdims=True))
    return (input_grad, gain_grad)


def local(
    hidden,
    cotangent,
    lengths,
    gain_mix,
    gain_mlp,
    conv_weight,
    mixer_in,
    mixer_out,
    gate_up,
    mlp_down,
):
    seqs, models = lax.axis_size("seq"), lax.axis_size("mp")
    seq_pos = lax.axis_index("seq")
    model_pos = lax.axis_index("mp")
    slots, share, width = hidden.shape
    channels = mixer_in.shape[2]
    taps = conv_weight.shape[0]
    local_taps = lax.dynamic_slice_in_dim(conv_weight, model_pos * channels, channels, 1)
    share_start = (seq_pos * models + model_pos) * share
    share_pos = share_start + jnp.arange(share, dtype=jnp.int32)
    mask = (share_pos[None, :] < lengths[:, None]).astype(F32)[:, :, None]
    source = hidden.astype(F32)
    top_grad = cotangent.astype(F32) * mask
    normed, scale_mix = normalize(source, gain_mix)
    (
        normed_rows,
        top_rows,
        in_full,
        out_full,
        pair_full,
        down_full,
        gates,
        product,
        mixed,
        mix_share,
    ) = mixer_forward(
        seqs,
        models,
        normed.astype(BF),
        top_grad.astype(BF),
        local_taps,
        mixer_in,
        mixer_out,
        gate_up,
        mlp_down,
    )
    middle = source + mix_share
    normed_two, scale_mlp = normalize(middle, gain_mlp)
    middle_grad, mlp_part, pair_total, down_total = mlp(
        seqs, models, normed_two.astype(BF), top_rows, pair_full, down_full
    )
    middle_grad, gain_mlp_grad = norm_back(middle_grad, middle, scale_mlp, gain_mlp)
    middle_grad = middle_grad + top_grad
    mlp_share, source_grad, taps_part, in_got, out_got, pair_got, down_got = mixer_backward(
        seqs,
        models,
        middle_grad.astype(BF),
        mlp_part,
        local_taps,
        in_full,
        out_full,
        normed_rows,
        gates,
        product,
        mixed,
        pair_total,
        down_total,
    )
    output = (mask * (middle + mlp_share)).astype(BF)
    source_grad, gain_mix_grad = norm_back(source_grad, source, scale_mix, gain_mix)
    small = jnp.zeros((8, width), F32)
    small = lax.dynamic_update_slice(small, taps_part[:taps], (2, model_pos * channels))
    small = small.at[0].set(gain_mix_grad).at[1].set(gain_mlp_grad)
    small = small_sum(seqs, models, small)

    def total(got):
        return jnp.sum(got.astype(F32), axis=0)

    return (
        output,
        source_grad + middle_grad,
        small[0],
        small[1],
        small[2 : 2 + taps],
        total(in_got),
        total(out_got),
        total(pair_got),
        total(down_got),
    )


def solution(mesh):
    placed = (
        P(None, ("seq", "mp"), None),
        P(None, ("seq", "mp"), None),
        P(),
        P(),
        P(),
        P(),
        P(None, "seq", "mp"),
        P("mp", "seq"),
        P(None, "seq", "mp"),
        P("mp", "seq"),
    )
    return jax.shard_map(
        local,
        mesh=mesh,
        in_specs=placed,
        out_specs=(
            P(None, ("seq", "mp"), None),
            P(None, ("seq", "mp"), None),
            P(),
            P(),
            P(),
            P(None, "seq", "mp"),
            P("mp", "seq"),
            P(None, "seq", "mp"),
            P("mp", "seq"),
        ),
        check_vma=False,
    )
```

```python
import functools

import jax
import jax.numpy as jnp
from jax import lax
from jax.experimental import pallas as pl
from jax.experimental.pallas import tpu as pltpu
from jax.sharding import PartitionSpec as P

EPS = 1e-05
MESH = pl.DeviceIdType.MESH
BF = jnp.bfloat16
F32 = jnp.float32
HALVES = 2
VMEM_LIMIT = 63 * 2**20


def nn(a, b):
    return lax.dot_general(a, b, (((1,), (0,)), ((), ())), preferred_element_type=F32)


def nt(a, b):
    return lax.dot_general(a, b, (((1,), (1,)), ((), ())), preferred_element_type=F32)


def tn(a, b):
    return lax.dot_general(a, b, (((0,), (0,)), ((), ())), preferred_element_type=F32)


class Place:
    def __init__(self, seqs, models):
        self.seqs, self.chips = seqs, models // 2
        self.s = lax.axis_index("seq")
        self.m = lax.axis_index("mp")
        self.z = self.m // 2
        self.c = self.m % 2
        self.sibling = {"mp": self.m + 1 - 2 * self.c}
        self.above = {"mp": self.m + 2}
        self.below = {"mp": self.m - 2}
        self.has_above = self.z < self.chips - 1
        self.has_below = self.z > 0

    def peer(self, step):
        return {"seq": lax.rem(self.s + step, self.seqs)}

    def enter(self):
        barrier = pltpu.get_barrier_semaphore()

        def greet(where):
            pl.semaphore_signal(barrier, inc=1, device_id=where, device_id_type=MESH)

        greet(self.sibling)
        for step in range(1, self.seqs):
            greet(self.peer(step))
        pl.when(self.has_above)(lambda: greet(self.above))
        pl.when(self.has_below)(lambda: greet(self.below))
        chips = self.chips
        lines = (self.z + chips - 1) // chips + (2 * chips - 2 - self.z) // chips
        pl.semaphore_wait(barrier, self.seqs + lines)


def remote(src, dst, send, recv, where):
    return pltpu.make_async_remote_copy(
        src_ref=src, dst_ref=dst, send_sem=send, recv_sem=recv, device_id=where, device_id_type=MESH
    )


class Gather:
    def __init__(self, place, rows, own, sems):
        self.p, self.rows, self.own = place, rows, own
        self.share = rows.shape[0] // (2 * place.chips)
        self.piece = self.share // HALVES
        self.send, self.recv = sems

    def at(self, chip, core, half):
        return self.rows.at[pl.ds((chip * 2 + core) * self.share + half * self.piece, self.piece)]

    def copy(self, kind, chip, half, own=False):
        p = self.p
        where = (p.above, p.below, p.sibling)[kind]
        dst = self.at(chip, p.c, half)
        src = self.own.at[pl.ds(half * self.piece, self.piece)] if own and self.own is not None else dst
        return remote(src, dst, self.send.at[kind, chip, half], self.recv.at[kind // 2, chip, half], where)

    def start(self):
        p = self.p
        for half in range(HALVES):
            pl.when(p.has_above)(lambda h=half: self.copy(0, p.z, h, True).start())
            pl.when(p.has_below)(lambda h=half: self.copy(1, p.z, h, True).start())
        for half in range(HALVES):
            self.copy(2, p.z, half, True).start()

    def round(self, k):
        p = self.p
        for half in range(HALVES):

            @pl.when(p.z >= k)
            def _(half=half):
                chip = p.z - k
                self.copy(0, chip, half).wait_recv()
                pl.when(p.has_above)(lambda: self.copy(0, chip, half).start())
                self.copy(2, chip, half).start()

            @pl.when(p.z + k <= p.chips - 1)
            def _(half=half):
                chip = p.z + k
                self.copy(1, chip, half).wait_recv()
                pl.when(p.has_below)(lambda: self.copy(1, chip, half).start())
                self.copy(2, chip, half).start()

    def rounds(self):
        return [functools.partial(self.round, k) for k in range(1, self.p.chips)]

    def other_core(self, chip):
        p = self.p
        for half in range(HALVES):
            dst = self.at(chip, 1 - p.c, half)
            remote(dst, dst, self.send.at[2, chip, half], self.recv.at[1, chip, half], p.sibling).wait_recv()

    def arrived(self):
        for chip in range(self.p.chips):
            self.other_core(chip)

    def drain(self):
        p = self.p
        for chip in range(p.chips):
            for half in range(HALVES):
                pl.when(p.has_above & (chip <= p.z))(lambda ch=chip, h=half: self.copy(0, ch, h).wait_send())
                pl.when(p.has_below & (chip >= p.z))(lambda ch=chip, h=half: self.copy(1, ch, h).wait_send())
                self.copy(2, chip, half).wait_send()


class Scatter:
    def __init__(self, place, part, from_core, from_line, sems):
        self.p, self.part, self.from_core, self.from_line = place, part, from_core, from_line
        self.share = from_core.shape[1]
        self.piece = self.share // HALVES
        self.core_send, self.core_recv, self.line_send, self.line_recv = sems

    def rows(self, chip, core):
        return self.part.at[pl.ds((chip * 2 + core) * self.share, self.share)]

    def core_copy(self, chip):
        p = self.p
        return remote(
            self.rows(chip, 1 - p.c), self.from_core.at[chip], self.core_send.at[chip], self.core_recv.at[chip], p.sibling
        )

    def give(self, chip):
        self.core_copy(chip).start()

    def mine(self, chip, half):
        return self.part.at[pl.ds((chip * 2 + self.p.c) * self.share + half * self.piece, self.piece)]

    def line_copy(self, down, chip, slot, half):
        p = self.p
        dst = self.from_line.at[slot, pl.ds(half * self.piece, self.piece)]
        return remote(
            self.mine(chip, half),
            dst,
            self.line_send.at[down, chip, half],
            self.line_recv.at[slot, half],
            p.below if down else p.above,
        )

    def total(self, chip, half, slots):
        span = pl.ds(half * self.piece, self.piece)
        value = self.mine(chip, half)[...].astype(F32) + self.from_core[chip, span].astype(F32)
        for slot in slots:
            value = value + self.from_line[slot, span].astype(F32)
        return value

    def hop(self, down, chip, slot, has_source):
        self.core_copy(chip).wait_recv()
        for half in range(HALVES):

            @pl.when(has_source)
            def _(half=half):
                self.line_copy(down, chip, chip, half).wait_recv()
                self.mine(chip, half)[...] = self.total(chip, half, [chip]).astype(BF)

            @pl.when(jnp.logical_not(has_source))
            def _(half=half):
                self.mine(chip, half)[...] = self.total(chip, half, []).astype(BF)

            self.line_copy(down, chip, slot, half).start()

    def round(self, r):
        p = self.p
        last = p.chips - 1

        @pl.when((p.z <= r) & p.has_above)
        def _():
            chip = last - r + p.z
            self.hop(0, chip, chip, p.has_below)

        @pl.when((last - p.z <= r) & p.has_below)
        def _():
            chip = r - last + p.z
            self.hop(1, chip, p.chips if r == last - 1 else chip, p.has_above)

    def rounds(self):
        return [functools.partial(self.round, r) for r in range(self.p.chips - 1)]

    def finish(self, store):
        p = self.p
        self.core_copy(p.z).wait_recv()
        for half in range(HALVES):
            pl.when(p.has_below)(lambda h=half: self.line_copy(0, p.z, p.z, h).wait_recv())
            pl.when(p.has_above)(lambda h=half: self.line_copy(1, p.z, p.chips, h).wait_recv())
            for up in (False, True):
                for low in (False, True):

                    @pl.when((p.has_above == up) & (p.has_below == low))
                    def _(half=half, up=up, low=low):
                        slots = ([p.z] if low else []) + ([p.chips] if up else [])
                        store(half * self.piece, self.piece, self.total(p.z, half, slots))

    def drain(self):
        p = self.p
        for chip in range(p.chips):
            self.core_copy(chip).wait_send()
            for half in range(HALVES):
                pl.when(p.has_above & (chip > p.z))(lambda ch=chip, h=half: self.line_copy(0, ch, ch, h).wait_send())
                pl.when(p.has_below & (chip < p.z))(lambda ch=chip, h=half: self.line_copy(1, ch, ch, h).wait_send())


def gather_sems(count, chips):
    return [pltpu.SemaphoreType.DMA((count, 3, chips, HALVES)), pltpu.SemaphoreType.DMA((count, 2, chips, HALVES))]


def scatter_sems(count, chips):
    return [
        pltpu.SemaphoreType.DMA((count, chips)),
        pltpu.SemaphoreType.DMA((count, chips)),
        pltpu.SemaphoreType.DMA((count, 2, chips, HALVES)),
        pltpu.SemaphoreType.DMA((count, chips + 1, HALVES)),
    ]


def picks(sems, index):
    return [sem.at[index] for sem in sems]


def far_first(place):
    low, high = 0, place.chips - 1
    order = []
    for _ in range(place.chips):
        left = place.z - low >= high - place.z
        order.append(jnp.where(left, low, high))
        low, high = jnp.where(left, low + 1, low), jnp.where(left, high, high - 1)
    return order


def weave(*lists):
    for step in range(max(len(steps) for steps in lists)):
        for steps in lists:
            if step < len(steps):
                steps[step]()


class Relay:
    def __init__(self, place, shard, full, first, size, sems):
        self.p, self.shard, self.full, self.first, self.size = place, shard, full, first, size
        self.send, self.recv, self.local = sems
        s = place.s
        self.square = place.seqs == 4
        if self.square:
            self.near = (s + 1 - 2 * lax.rem(s, 2), lax.rem(s + 2, 4))

    def half(self, index):
        return self.first + index * (self.size // 2), self.size // 2

    def direct(self, index, where):
        return remote(
            self.shard(self.first, self.size),
            self.full(self.p.s, self.first, self.size),
            self.send.at[index],
            self.recv.at[index],
            where,
        )

    def handed(self, index):
        view = self.full(self.near[index], *self.half(index))
        return remote(view, view, self.send.at[2 + index], self.recv.at[2 + index], {"seq": self.near[1 - index]})

    def local_copy(self):
        return pltpu.make_async_copy(
            self.shard(self.first, self.size), self.full(self.p.s, self.first, self.size), self.local
        )

    def copies(self):
        if self.square:
            return [self.direct(index, {"seq": self.near[index]}) for index in range(2)]
        return [self.direct(step - 1, self.p.peer(step)) for step in range(1, self.p.seqs)]

    def start(self):
        for thing in self.copies():
            thing.start()
        self.local_copy().start()

    def forward(self):
        if self.square:
            for thing in self.copies():
                thing.wait_recv()
            for index in range(2):
                self.handed(index).start()

    def arrived(self):
        self.local_copy().wait()
        for thing in [self.handed(index) for index in range(2)] if self.square else self.copies():
            thing.wait_recv()

    def drain(self):
        for thing in self.copies() + ([self.handed(index) for index in range(2)] if self.square else []):
            thing.wait_send()


def forward_kernel(
    seqs,
    models,
    normed_ref,
    source_ref,
    gain_ref,
    top_ref,
    taps_ref,
    in_ref,
    out_ref,
    pair_ref,
    down_ref,
    normed_rows,
    top_rows,
    in_rows,
    out_rows,
    gates_out,
    product_out,
    mixed_out,
    middle_out,
    grad_out,
    mlp_part,
    act_rows,
    pair_grad,
    down_grad,
    in_full,
    out_full,
    rows,
    gates,
    ends,
    product,
    mixed,
    pair,
    down,
    top_tile,
    acts,
    act_stage,
    stage,
    part,
    from_core,
    from_line,
    total,
    w_send,
    w_recv,
    w_local,
    halo_send,
    halo_recv,
    keep,
    tile_sem,
    out_sem,
    cols_sem,
    pair_sem,
    ends_sem,
    *sems,
):
    p = Place(seqs, models)
    chips = p.chips
    g_sems, s_sems = sems[:2], sems[2:]
    slots, block, width = rows.shape
    units = down.shape[0]
    tile = block // chips
    share = tile // 2
    channels = in_full.shape[2]
    shard = width // seqs
    unit_block = min(512, units)
    wide_block = 512
    p.enter()

    firsts = [Gather(p, rows.at[slot], normed_ref.at[slot], picks(g_sems, slot)) for slot in range(slots)]
    tops = [Gather(p, top_rows.at[slot], top_ref.at[slot], picks(g_sems, slots + slot)) for slot in range(slots)]
    seconds = [Gather(p, rows.at[slot], None, picks(g_sems, 2 * slots + slot)) for slot in range(slots)]

    def scatter(slot, index):
        return Scatter(p, part.at[slot], from_core.at[slot], from_line.at[slot], picks(s_sems, index))

    mix_sums = [scatter(slot, slot) for slot in range(slots)]
    grad_sums = [scatter(slot, slots + slot) for slot in range(slots)]

    def columns_of(owner):
        return pl.ds(pl.multiple_of(owner * shard, shard), shard)

    def pair_views(k):
        return (
            lambda first, size: pair_ref.at[k, pl.ds(first, size)],
            lambda owner, first, size: pair.at[k, pl.ds(owner * shard + first, size)],
        )

    views = [
        (
            lambda first, size: in_ref.at[:, pl.ds(first, size)],
            lambda owner, first, size: in_full.at[:, pl.ds(owner * shard + first, size)],
            0,
            shard,
        ),
        (
            lambda first, size: out_ref.at[pl.ds(first, size)],
            lambda owner, first, size: out_full.at[pl.ds(first, size), columns_of(owner)],
            0,
            channels,
        ),
    ]
    for i in range(2):
        views.append(
            (
                lambda first, size: down_ref.at[pl.ds(first, size)],
                lambda owner, first, size: down.at[pl.ds(first, size), columns_of(owner)],
                i * (units // 2),
                units // 2,
            )
        )
    for i in range(4):
        views.append((*pair_views(i // 2), (i % 2) * (shard // 2), shard // 2))
    pieces = [Relay(p, *view, (w_send.at[i], w_recv.at[i], w_local.at[i])) for i, view in enumerate(views)]
    early, late = pieces[:2], pieces[2:]
    pending = [late[0].start]
    for i in range(len(late)):

        def step(i=i):
            late[i].forward()
            if i + 1 < len(late):
                late[i + 1].start()

        pending.append(step)

    def push():
        if pending:
            pending.pop(0)()

    def own(slot, which, source):
        span = pl.ds(p.m * share, share)
        return pltpu.make_async_copy(source.at[slot], which.at[slot, span], keep.at[slot + (slots if which is top_rows else 0)])

    for slot in range(slots):
        own(slot, rows, normed_ref).start()
        own(slot, top_rows, top_ref).start()

    def saved(index, src, dst):
        return pltpu.make_async_copy(src, dst, keep.at[2 * slots + index])

    rows_saved = [saved(slot, rows.at[slot], normed_rows.at[slot]) for slot in range(slots)]
    gates_saved = [saved(slots + slot, gates, gates_out.at[slot, 1]) for slot in range(slots)]
    middle_saved = [saved(2 * slots + slot, total.at[slot], middle_out.at[slot]) for slot in range(slots)]
    grad_saved = [saved(3 * slots + slot, total.at[slot], grad_out.at[slot]) for slot in range(slots)]
    in_saved = saved(4 * slots, in_full, in_rows)
    out_saved = saved(4 * slots + 1, out_full, out_rows)
    product_saved = saved(4 * slots + 2, product, product_out)
    mixed_saved = saved(4 * slots + 3, mixed, mixed_out)
    down_saved = saved(4 * slots + 4, down, down_grad)
    act_load = saved(4 * slots + 5, act_rows, acts.at[0])

    def halo(slot):
        return remote(
            product.at[slot, pl.ds(block, 8)],
            product.at[slot, pl.ds(0, 8)],
            halo_send.at[slot],
            halo_recv.at[slot],
            p.peer(1),
        )

    has_later, has_earlier = p.s < seqs - 1, p.s > 0
    for slot in range(slots):

        @pl.when(jnp.logical_not(has_earlier))
        def _(slot=slot):
            product[slot, pl.ds(0, 8)] = jnp.zeros((8, channels), F32)

    def ends_saved(slot, i):
        span = pl.ds(i * tile, tile)
        return [
            pltpu.make_async_copy(ends.at[j], gates_out.at[slot, 2 * j, span], ends_sem.at[j]) for j in range(2)
        ]

    def project(slot):
        @pl.loop(0, chips)
        def _(i):
            span = pl.ds(i * tile, tile)
            source = rows[slot, span]
            b_gate = nn(source, in_full[0])
            x_value = nn(source, in_full[2])
            gates[span] = nn(source, in_full[1])

            @pl.when(i > 0)
            def _():
                for thing in ends_saved(slot, i - 1):
                    thing.wait()

            ends[0] = b_gate
            ends[1] = x_value
            for thing in ends_saved(slot, i):
                thing.start()
            product[slot, pl.ds(8 + i * tile, tile)] = b_gate * x_value

        for thing in ends_saved(slot, chips - 1):
            thing.wait()
        pl.when(has_later)(lambda: halo(slot).start())

    def convolve(slot):
        pl.when(has_earlier)(lambda: halo(slot).wait_recv())
        for i in range(chips):
            conv = 0.0
            for offset in range(taps_ref.shape[0]):
                conv = conv + taps_ref[offset : offset + 1] * product[slot, pl.ds(8 + i * tile - offset, tile)]
            mixed[slot, pl.ds(i * tile, tile)] = (gates[pl.ds(i * tile, tile)] * conv).astype(BF)

    def project_out(slot):
        for chip in far_first(p):
            span = pl.ds(chip * tile, tile)
            part[slot, span] = nn(mixed[slot, span], out_full[...]).astype(BF)
            mix_sums[slot].give(chip)

    def middle(slot):
        def store(first, size, value):
            span = pl.ds(first, size)
            value = value + source_ref[slot, span].astype(F32)
            total[slot, span] = value
            scale = lax.rsqrt(jnp.mean(value * value, axis=-1, keepdims=True) + EPS)
            rows[slot, pl.ds(p.m * share + first, size)] = (value * scale * gain_ref[...]).astype(BF)

        mix_sums[slot].finish(store)
        middle_saved[slot].start()
        mix_sums[slot].drain()

    def finish_grad(slot):
        middle_saved[slot].wait()

        def store(first, size, value):
            total[slot, pl.ds(first, size)] = value

        grad_sums[slot].finish(store)
        grad_saved[slot].start()

    order = far_first(p)
    tiles = [(0, chip) for chip in order] + [(slot, chip) for slot in range(1, slots) for chip in order[::-1]]

    def fetch(index):
        slot, chip = tiles[index]
        return pltpu.make_async_copy(top_rows.at[slot, pl.ds(chip * tile, tile)], top_tile, tile_sem)

    def puts(index):
        slot, chip = tiles[index]
        span = pl.ds(chip * tile, tile)
        return [
            pltpu.make_async_copy(stage, mlp_part.at[slot, span], out_sem.at[0]),
            pltpu.make_async_copy(act_stage, act_rows.at[slot, span], out_sem.at[1]),
        ]

    def work(index):
        slot, chip = tiles[index]
        span = pl.ds(chip * tile, tile)
        if index == 0 or slot > 0:
            fetch(index).start()
        fetch(index).wait()
        if index:
            for thing in puts(index - 1):
                thing.wait()

        @pl.loop(0, units // unit_block)
        def _(i):
            cut = pl.ds(pl.multiple_of(i * unit_block, unit_block), unit_block)
            source = rows[slot, span]
            gate = nn(source, pair[0, :, cut])
            up = nn(source, pair[1, :, cut])
            act_grad = nt(top_tile[...], down[cut])
            sigma = jax.nn.sigmoid(gate)
            silu = gate * sigma
            act_stage[:, cut] = (silu * up).astype(BF)
            acts[0, slot, span, cut] = (act_grad * up * sigma * (1.0 + gate * (1.0 - sigma))).astype(BF)
            acts[1, slot, span, cut] = (act_grad * silu).astype(BF)

        if index + 1 < len(tiles) and tiles[index + 1][0] == 0:
            fetch(index + 1).start()

        @pl.loop(0, width // wide_block)
        def _(i):
            cut = pl.ds(pl.multiple_of(i * wide_block, wide_block), wide_block)
            value = nt(acts[0, slot, span], pair[0, cut]) + nt(acts[1, slot, span], pair[1, cut])
            part[slot, span, cut] = value.astype(BF)
            stage[:, cut] = nn(act_stage[...], down[:, cut]).astype(BF)

        grad_sums[slot].give(chip)
        for thing in puts(index):
            thing.start()

    pair_steps = 2 * (width // wide_block)

    def pair_saved(index):
        k, first = divmod(index, width // wide_block)
        cut = pl.ds(first * wide_block, wide_block)
        return pltpu.make_async_copy(pair.at[k, cut], pair_grad.at[k, cut], pair_sem.at[index])

    def pair_step(index):
        k, first = divmod(index, width // wide_block)
        cut = pl.ds(first * wide_block, wide_block)
        value = 0.0
        for slot in range(slots):
            value = value + tn(rows[slot, :, cut], acts[k, slot])
        pair[k, cut] = value.astype(BF)
        pair_saved(index).start()
        if first == width // wide_block - 1 and k == 0:
            act_load.start()

    def fetch_columns(index):
        cut = pl.ds(index * channels, channels)
        return [
            pltpu.make_async_copy(
                top_rows.at[slot, :, cut], in_full.at[index % 2, pl.ds(slot * block, block)], cols_sem.at[index % 2, slot]
            )
            for slot in range(slots)
        ]

    def down_step(index):
        if index == 0:
            act_load.wait()
        for thing in fetch_columns(index):
            thing.wait()
        for first in range(0, units, unit_block):
            cut = pl.ds(first, unit_block)
            value = 0.0
            for slot in range(slots):
                value = value + tn(acts[0, slot, :, cut], in_full[index % 2, pl.ds(slot * block, block)])
            down[cut, pl.ds(index * channels, channels)] = value.astype(BF)
        if index + 2 < width // channels:
            for thing in fetch_columns(index + 2):
                thing.start()

    firsts[0].start()
    for piece in early:
        piece.start()
    steps = firsts[0].rounds()
    for step in steps[:-1]:
        step()
    for piece in early:
        piece.forward()
    firsts[1].start()
    steps[-1]()
    own(0, rows, normed_ref).wait()
    firsts[0].arrived()
    rows_saved[0].start()
    for piece in early:
        piece.arrived()
    in_saved.start()
    out_saved.start()
    project(0)
    gates_saved[0].start()
    push()
    steps = firsts[1].rounds()
    steps[0]()
    push()
    rows_saved[0].wait()
    firsts[0].drain()
    convolve(0)
    project_out(0)
    weave(mix_sums[0].rounds(), steps[1:], [push] * chips)
    own(1, rows, normed_ref).wait()
    firsts[1].arrived()
    rows_saved[1].start()
    gates_saved[0].wait()
    project(1)
    gates_saved[1].start()
    push()
    middle(0)
    seconds[0].start()
    rows_saved[1].wait()
    firsts[1].drain()
    convolve(1)
    project_out(1)
    steps = seconds[0].rounds()
    weave(mix_sums[1].rounds(), steps[:-1] + [tops[0].start, steps[-1]], [push] * chips)
    steps = tops[0].rounds()
    steps[0]()
    push()
    middle(1)
    product_saved.start()
    mixed_saved.start()
    for step in steps[1:-1]:
        step()
        push()
    seconds[1].start()
    steps[-1]()
    while pending:
        push()
    own(0, top_rows, top_ref).wait()
    tops[0].arrived()
    seconds[0].arrived()
    for piece in late:
        piece.arrived()
    hops, steps, more = grad_sums[0].rounds(), seconds[1].rounds(), tops[1].rounds()
    for index in range(chips):
        work(index)
        if index < len(steps):
            steps[index]()
        if index == len(steps) - 2:
            tops[1].start()
        if index < len(hops):
            hops[index]()
    own(1, top_rows, top_ref).wait()
    for index in range(chips):
        if index:
            more[index - 1]()
        seconds[1].other_core(tiles[chips + index][1])
        tops[1].other_core(tiles[chips + index][1])
        work(chips + index)
    in_saved.wait()
    for piece in pieces:
        piece.drain()
    for index in range(2):
        for thing in fetch_columns(index):
            thing.start()
    hops = grad_sums[1].rounds()
    hops[0]()
    finish_grad(0)
    for index in range(len(tiles) - 1, len(tiles)):
        for thing in puts(index):
            thing.wait()
    work_steps = [functools.partial(pair_step, index) for index in range(pair_steps)]
    work_steps += [functools.partial(down_step, index) for index in range(width // channels)]
    spaced = len(work_steps) // len(hops)
    for index, step in enumerate(work_steps):
        step()
        if (index + 1) % spaced == 0 and (index + 1) // spaced < len(hops):
            hops[(index + 1) // spaced]()
    down_saved.start()
    finish_grad(1)
    for index in range(pair_steps):
        pair_saved(index).wait()
    for thing in [gates_saved[1], out_saved, product_saved, mixed_saved, down_saved, *grad_saved]:
        thing.wait()
    for thing in tops + seconds + grad_sums:
        thing.drain()
    for slot in range(slots):
        pl.when(has_later)(lambda slot=slot: halo(slot).wait_send())


def forward(seqs, models, normed, source, gain, top, taps, mixer_in, mixer_out, gate_up, mlp_down):
    slots, share, width = normed.shape
    chips = models // 2
    block = share * models
    channels = mixer_in.shape[2]
    units = gate_up.shape[2]
    tile = block // chips
    hbm = pl.BlockSpec(memory_space=pltpu.HBM)
    vmem = pl.BlockSpec(memory_space=pltpu.VMEM)
    shape = jax.ShapeDtypeStruct
    return pl.pallas_call(
        functools.partial(forward_kernel, seqs, models),
        out_shape=[
            shape((slots, block, width), BF),
            shape((slots, block, width), BF),
            shape((3, width, channels), BF),
            shape((channels, width), BF),
            shape((slots, 3, block, channels), F32),
            shape((slots, block + 8, channels), F32),
            shape((slots, block, channels), BF),
            shape((slots, share, width), F32),
            shape((slots, share, width), F32),
            shape((slots, block, width), BF),
            shape((slots, block, units), BF),
            shape((2, width, units), BF),
            shape((units, width), BF),
        ],
        in_specs=[hbm, vmem, vmem, hbm, vmem] + [hbm] * 4,
        out_specs=[hbm] * 13,
        scratch_shapes=[
            pltpu.VMEM((3, width, channels), BF),
            pltpu.VMEM((channels, width), BF),
            pltpu.VMEM((slots, block, width), BF),
            pltpu.VMEM((block, channels), F32),
            pltpu.VMEM((2, tile, channels), F32),
            pltpu.VMEM((slots, block + 8, channels), F32),
            pltpu.VMEM((slots, block, channels), BF),
            pltpu.VMEM((2, width, units), BF),
            pltpu.VMEM((units, width), BF),
            pltpu.VMEM((tile, width), BF),
            pltpu.VMEM((2, slots, block, units), BF),
            pltpu.VMEM((tile, units), BF),
            pltpu.VMEM((tile, width), BF),
            pltpu.VMEM((slots, block, width), BF),
            pltpu.VMEM((slots, chips, share, width), BF),
            pltpu.VMEM((slots, chips + 1, share, width), BF),
            pltpu.VMEM((slots, share, width), F32),
            pltpu.SemaphoreType.DMA((8, max(4, seqs - 1))),
            pltpu.SemaphoreType.DMA((8, max(4, seqs - 1))),
            pltpu.SemaphoreType.DMA((8,)),
            pltpu.SemaphoreType.DMA((slots,)),
            pltpu.SemaphoreType.DMA((slots,)),
            pltpu.SemaphoreType.DMA((6 * slots + 6,)),
            pltpu.SemaphoreType.DMA,
            pltpu.SemaphoreType.DMA((2,)),
            pltpu.SemaphoreType.DMA((2, slots)),
            pltpu.SemaphoreType.DMA((2 * (width // 512),)),
            pltpu.SemaphoreType.DMA((2,)),
            *gather_sems(3 * slots, chips),
            *scatter_sems(2 * slots, chips),
        ],
        compiler_params=pltpu.CompilerParams(collective_id=1, has_side_effects=True, vmem_limit_bytes=VMEM_LIMIT),
    )(normed, source, gain, top, taps, mixer_in, mixer_out, gate_up, mlp_down)


class Spread:
    def __init__(self, place, partial, got, sems):
        self.p, self.partial, self.got = place, partial, got
        self.send, self.recv, self.local = sems

    def block(self, owner):
        size = self.partial.shape[1] // self.p.seqs
        return self.partial.at[:, pl.ds(pl.multiple_of(owner * size, size), size)]

    def copy(self, step):
        p = self.p
        return remote(
            self.block(lax.rem(p.s + step, p.seqs)),
            self.got(step),
            self.send.at[step - 1],
            self.recv.at[step - 1],
            p.peer(step),
        )

    def local_copy(self):
        return pltpu.make_async_copy(self.block(self.p.s), self.got(0), self.local)

    def start(self):
        for step in range(1, self.p.seqs):
            self.copy(step).start()
        self.local_copy().start()

    def finish(self):
        self.local_copy().wait()
        for step in range(1, self.p.seqs):
            self.copy(step).wait()


def mixer_backward_kernel(
    seqs,
    models,
    low_ref,
    mlp_part,
    taps_ref,
    in_ref,
    out_ref,
    normed_rows,
    gates_ref,
    product_ref,
    mixed_ref,
    pair_grad,
    down_grad,
    mlp_out,
    grad_out,
    taps_out,
    in_got,
    out_got,
    pair_got,
    down_got,
    in_full,
    out_full,
    rows,
    columns,
    gates,
    product,
    mixed,
    conv_grad,
    stacked,
    part,
    from_core,
    from_line,
    mlp_total,
    grad_total,
    load,
    cols_sem,
    w_send,
    w_recv,
    w_local,
    halo_send,
    halo_recv,
    free,
    *sems,
):
    p = Place(seqs, models)
    chips = p.chips
    g_sems, s_sems = sems[:2], sems[2:]
    slots, block, width = rows.shape
    channels = out_full.shape[0]
    taps = taps_ref.shape[0]
    tile = block // chips
    share = tile // 2
    wide_block = 512
    cols = columns.shape[-1]
    loads = [
        pltpu.make_async_copy(src, dst, load.at[i])
        for i, (src, dst) in enumerate(
            [(mlp_part.at[slot], part.at[slot]) for slot in range(slots)]
            + [
                (low_ref.at[slot], rows.at[slot, pl.ds(p.m * share, share)])
                for slot in range(slots)
            ]
            + [
                (in_ref, in_full),
                (out_ref, out_full),
                (gates_ref, gates),
                (product_ref, product),
                (mixed_ref, mixed),
            ]
        )
    ]
    for thing in loads:
        thing.start()
    p.enter()
    gathers = [Gather(p, rows.at[slot], low_ref.at[slot], picks(g_sems, slot)) for slot in range(slots)]

    def scatter(slot, index):
        return Scatter(p, part.at[slot], from_core.at[slot], from_line.at[slot], picks(s_sems, index))

    mlp_sums = [scatter(slot, slot) for slot in range(slots)]
    sums = [scatter(slot, slots + slot) for slot in range(slots)]
    spreads = [
        Spread(p, partial, got, (w_send.at[i], w_recv.at[i], w_local.at[i]))
        for i, (partial, got) in enumerate(
            (
                (pair_grad.at[pl.ds(0, 1)], lambda step: pair_got.at[step, pl.ds(0, 1)]),
                (down_grad, lambda step: down_got.at[step]),
                (in_full, lambda step: in_got.at[step]),
                (out_full, lambda step: out_got.at[step]),
                (pair_grad.at[pl.ds(1, 1)], lambda step: pair_got.at[step, pl.ds(1, 1)]),
            )
        )
    ]
    has_later, has_earlier = p.s < seqs - 1, p.s > 0
    order = far_first(p)

    def halo(slot):
        return remote(
            conv_grad.at[slot, pl.ds(0, 8)],
            conv_grad.at[slot, pl.ds(block, 8)],
            halo_send.at[slot],
            halo_recv.at[slot],
            p.peer(seqs - 1),
        )

    for slot in range(slots):

        @pl.when(jnp.logical_not(has_later))
        def _(slot=slot):
            conv_grad[slot, pl.ds(block, 8)] = jnp.zeros((8, channels), F32)

    taps_out[...] = jnp.zeros_like(taps_out)

    def first_pass(slot):
        for i in range(chips):
            span = pl.ds(i * tile, tile)
            mixed_grad = nt(rows[slot, span], out_full[...])
            grad = mixed_grad * gates[slot, 1, span]
            conv_grad[slot, span] = grad
            conv = 0.0
            for offset in range(taps):
                earlier = product[slot, pl.ds(8 + i * tile - offset, tile)]
                conv = conv + taps_ref[offset : offset + 1] * earlier
                taps_out[offset : offset + 1] += jnp.sum(grad * earlier, axis=0, keepdims=True)
            stacked[slot, span, pl.ds(channels, channels)] = (mixed_grad * conv).astype(BF)
            if i == 0:
                pl.when(has_earlier)(lambda: halo(slot).start())

    def second_pass(slot):
        pl.when(has_later)(lambda: halo(slot).wait_recv())
        for i in range(chips):
            span = pl.ds(i * tile, tile)
            grad = 0.0
            for offset in range(taps):
                grad = grad + taps_ref[offset : offset + 1] * conv_grad[slot, pl.ds(i * tile + offset, tile)]
            stacked[slot, span, pl.ds(0, channels)] = (grad * gates[slot, 2, span]).astype(BF)
            stacked[slot, span, pl.ds(2 * channels, channels)] = (grad * gates[slot, 0, span]).astype(BF)

    def third_pass(slot):
        for chip in order:
            span = pl.ds(chip * tile, tile)

            @pl.loop(0, width // wide_block)
            def _(i):
                cut = pl.ds(pl.multiple_of(i * wide_block, wide_block), wide_block)
                value = 0.0
                for k in range(3):
                    value = value + nt(stacked[slot, span, pl.ds(k * channels, channels)], in_full[k, cut])
                part[slot, span, cut] = value.astype(BF)

            sums[slot].give(chip)

    def finish(what, total, slot):
        def store(first, size, value):
            total[slot, pl.ds(first, size)] = value

        what[slot].finish(store)

    def neighbours(act):
        act(p.sibling)
        pl.when(p.has_above)(lambda: act(p.above))
        pl.when(p.has_below)(lambda: act(p.below))

    def give_free(slot):
        mlp_sums[slot].drain()
        neighbours(
            lambda where: pl.semaphore_signal(free.at[slot], inc=1, device_id=where, device_id_type=MESH)
        )

    def take_free(slot):
        lines = (p.z + chips - 1) // chips + (2 * chips - 2 - p.z) // chips
        pl.semaphore_wait(free.at[slot], 1 + lines)

    def fetch_columns(index):
        return pltpu.make_async_copy(
            normed_rows.at[:, :, pl.ds(index * cols, cols)], columns.at[index % 2], cols_sem.at[index % 2]
        )

    steps_in = width // cols

    def in_step(index):
        fetch_columns(index).wait()
        value = 0.0
        for slot in range(slots):
            value = value + tn(columns[index % 2, slot], stacked[slot])
        for k in range(3):
            in_full[k, pl.ds(index * cols, cols)] = value[:, k * channels : (k + 1) * channels].astype(BF)
        if index + 2 < steps_in:
            fetch_columns(index + 2).start()

    def out_step():
        for first in range(0, width, wide_block):
            cut = pl.ds(first, wide_block)
            value = 0.0
            for slot in range(slots):
                value = value + tn(mixed[slot], rows[slot, :, cut])
            out_full[:, cut] = value.astype(BF)

    spreads[1].start()
    gathers[0].start()
    loads[0].wait()
    for chip in order:
        mlp_sums[0].give(chip)
    hops, next_rows = mlp_sums[0].rounds(), gathers[0].rounds()
    weave(hops[:-1], next_rows[:-1])
    gathers[1].start()
    weave(hops[-1:], next_rows[-1:])
    loads[1].wait()
    for chip in order:
        mlp_sums[1].give(chip)
    loads[2].wait()
    for thing in loads[2 + slots :]:
        thing.wait()
    gathers[0].arrived()
    fetch_columns(0).start()
    fetch_columns(1).start()
    mlp_hops, next_rows, hops = mlp_sums[1].rounds(), gathers[1].rounds(), sums[0].rounds()
    first_pass(0)
    spreads[0].start()
    finish(mlp_sums, mlp_total, 0)
    give_free(0)
    weave(mlp_hops[:1], next_rows[:1])
    second_pass(0)
    take_free(0)
    third_pass(0)
    weave(mlp_hops[1:], next_rows[1:], hops[:1])
    loads[3].wait()
    gathers[1].arrived()
    first_pass(1)
    spreads[4].start()
    finish(mlp_sums, mlp_total, 1)
    give_free(1)
    hops[1]()
    second_pass(1)
    take_free(1)
    weave(hops[2:])
    third_pass(1)
    hops = sums[1].rounds()
    hops[0]()
    out_step()
    spreads[3].start()
    for index in range(steps_in):
        in_step(index)
    spreads[2].start()
    weave(hops[1:])
    finish(sums, grad_total, 0)
    finish(sums, grad_total, 1)
    last = [
        pltpu.make_async_copy(mlp_total, mlp_out, load.at[0]),
        pltpu.make_async_copy(grad_total, grad_out, load.at[1]),
    ]
    for thing in last:
        thing.start()
    for thing in spreads:
        thing.finish()
    for thing in last:
        thing.wait()
    for thing in gathers + sums:
        thing.drain()
    for slot in range(slots):
        pl.when(has_earlier)(lambda slot=slot: halo(slot).wait_send())


def mixer_backward(
    seqs, models, low, mlp_part, taps, in_full, out_full, normed_rows, gates, product, mixed, pair_grad, down_grad
):
    slots, share, width = low.shape
    chips = models // 2
    block = share * models
    channels = out_full.shape[0]
    units = down_grad.shape[0]
    hbm = pl.BlockSpec(memory_space=pltpu.HBM)
    vmem = pl.BlockSpec(memory_space=pltpu.VMEM)
    shape = jax.ShapeDtypeStruct
    return pl.pallas_call(
        functools.partial(mixer_backward_kernel, seqs, models),
        out_shape=[
            shape((slots, share, width), F32),
            shape((slots, share, width), F32),
            shape((8, channels), F32),
            shape((seqs, 3, width // seqs, channels), BF),
            shape((seqs, channels, width // seqs), BF),
            shape((seqs, 2, width // seqs, units), BF),
            shape((seqs, units, width // seqs), BF),
        ],
        in_specs=[hbm, hbm, vmem] + [hbm] * 8,
        out_specs=[hbm, hbm, vmem] + [hbm] * 4,
        scratch_shapes=[
            pltpu.VMEM((3, width, channels), BF),
            pltpu.VMEM((channels, width), BF),
            pltpu.VMEM((slots, block, width), BF),
            pltpu.VMEM((2, slots, block, 256), BF),
            pltpu.VMEM((slots, 3, block, channels), F32),
            pltpu.VMEM((slots, block + 8, channels), F32),
            pltpu.VMEM((slots, block, channels), BF),
            pltpu.VMEM((slots, block + 8, channels), F32),
            pltpu.VMEM((slots, block, 3 * channels), BF),
            pltpu.VMEM((slots, block, width), BF),
            pltpu.VMEM((slots, chips, share, width), BF),
            pltpu.VMEM((slots, chips + 1, share, width), BF),
            pltpu.VMEM((slots, share, width), F32),
            pltpu.VMEM((slots, share, width), F32),
            pltpu.SemaphoreType.DMA((2 * slots + 5,)),
            pltpu.SemaphoreType.DMA((2,)),
            pltpu.SemaphoreType.DMA((5, seqs - 1)),
            pltpu.SemaphoreType.DMA((5, seqs - 1)),
            pltpu.SemaphoreType.DMA((5,)),
            pltpu.SemaphoreType.DMA((slots,)),
            pltpu.SemaphoreType.DMA((slots,)),
            pltpu.SemaphoreType.REGULAR((slots,)),
            *gather_sems(slots, chips),
            *scatter_sems(2 * slots, chips),
        ],
        compiler_params=pltpu.CompilerParams(collective_id=3, has_side_effects=True, vmem_limit_bytes=VMEM_LIMIT),
    )(low, mlp_part, taps, in_full, out_full, normed_rows, gates, product, mixed, pair_grad, down_grad)


def small_sum_kernel(seqs, models, value_ref, out_ref, by_model, by_seq, send, recv, seq_send, seq_recv):
    s, m = lax.axis_index("seq"), lax.axis_index("mp")
    cols = by_seq.shape[-1]
    along = [lax.rem(m + step, models) for step in range(1, models)]
    across = [lax.rem(s + step, seqs) for step in range(1, seqs)]

    def span(owner):
        return pl.ds(pl.multiple_of(owner * cols, cols), cols)

    barrier = pltpu.get_barrier_semaphore()
    for where in [{"mp": peer} for peer in along] + [{"seq": peer} for peer in across]:
        pl.semaphore_signal(barrier, inc=1, device_id=where, device_id_type=MESH)
    pl.semaphore_wait(barrier, models + seqs - 2)
    by_model[m] = value_ref[:, span(m)]
    copies = [
        remote(value_ref.at[:, span(peer)], by_model.at[m], send.at[0, i], recv.at[0, i], {"mp": peer})
        for i, peer in enumerate(along)
    ]
    for thing in copies:
        thing.start()
    for thing in copies:
        thing.wait()
    by_seq[s] = functools.reduce(lambda a, b: a + b, [by_model[i] for i in range(models)])
    copies = [
        remote(by_seq.at[s], by_seq.at[s], seq_send.at[i], seq_recv.at[i], {"seq": peer})
        for i, peer in enumerate(across)
    ]
    for thing in copies:
        thing.start()
    for thing in copies:
        thing.wait()
    out_ref[:, span(m)] = functools.reduce(lambda a, b: a + b, [by_seq[i] for i in range(seqs)])
    copies = [
        remote(out_ref.at[:, span(m)], out_ref.at[:, span(m)], send.at[1, i], recv.at[1, i], {"mp": peer})
        for i, peer in enumerate(along)
    ]
    for thing in copies:
        thing.start()
    for thing in copies:
        thing.wait()


def small_sum(seqs, models, value):
    vmem = pl.BlockSpec(memory_space=pltpu.VMEM)
    height, width = value.shape
    cols = width // models
    return pl.pallas_call(
        functools.partial(small_sum_kernel, seqs, models),
        out_shape=jax.ShapeDtypeStruct(value.shape, F32),
        in_specs=[vmem],
        out_specs=vmem,
        scratch_shapes=[
            pltpu.VMEM((models, height, cols), F32),
            pltpu.VMEM((seqs, height, cols), F32),
            pltpu.SemaphoreType.DMA((2, models - 1)),
            pltpu.SemaphoreType.DMA((2, models - 1)),
            pltpu.SemaphoreType.DMA((seqs - 1,)),
            pltpu.SemaphoreType.DMA((seqs - 1,)),
        ],
        compiler_params=pltpu.CompilerParams(collective_id=4, has_side_effects=True),
    )(value)


def normalize(values, gain):
    scale = lax.rsqrt(jnp.mean(values * values, axis=-1, keepdims=True) + EPS)
    return (values * scale * gain, scale)


def norm_back(grad, values, scale, gain):
    unit = values * scale
    scaled = grad * gain
    gain_grad = jnp.sum(grad * unit, axis=(0, 1))
    input_grad = scale * (scaled - unit * jnp.mean(scaled * unit, axis=-1, keepdims=True))
    return (input_grad, gain_grad)


def local(
    hidden,
    cotangent,
    lengths,
    gain_mix,
    gain_mlp,
    conv_weight,
    mixer_in,
    mixer_out,
    gate_up,
    mlp_down,
):
    seqs, models = lax.axis_size("seq"), lax.axis_size("mp")
    seq_pos = lax.axis_index("seq")
    model_pos = lax.axis_index("mp")
    slots, share, width = hidden.shape
    channels = mixer_in.shape[2]
    taps = conv_weight.shape[0]
    local_taps = lax.dynamic_slice_in_dim(conv_weight, model_pos * channels, channels, 1)
    share_start = (seq_pos * models + model_pos) * share
    share_pos = share_start + jnp.arange(share, dtype=jnp.int32)
    mask = (share_pos[None, :] < lengths[:, None]).astype(F32)[:, :, None]
    source = hidden.astype(F32)
    top_grad = cotangent.astype(F32) * mask
    normed, scale_mix = normalize(source, gain_mix)
    (
        normed_rows,
        _,
        in_full,
        out_full,
        gates,
        product,
        mixed,
        middle,
        middle_grad,
        mlp_part,
        _,
        pair_total,
        down_total,
    ) = forward(
        seqs,
        models,
        normed.astype(BF),
        hidden,
        gain_mlp[None],
        top_grad.astype(BF),
        local_taps,
        mixer_in,
        mixer_out,
        gate_up,
        mlp_down,
    )
    scale_mlp = lax.rsqrt(jnp.mean(middle * middle, axis=-1, keepdims=True) + EPS)
    middle_grad, gain_mlp_grad = norm_back(middle_grad, middle, scale_mlp, gain_mlp)
    middle_grad = middle_grad + top_grad
    mlp_share, source_grad, taps_part, in_got, out_got, pair_got, down_got = mixer_backward(
        seqs,
        models,
        middle_grad.astype(BF),
        mlp_part,
        local_taps,
        in_full,
        out_full,
        normed_rows,
        gates,
        product,
        mixed,
        pair_total,
        down_total,
    )
    output = (mask * (middle + mlp_share)).astype(BF)
    source_grad, gain_mix_grad = norm_back(source_grad, source, scale_mix, gain_mix)
    small = jnp.zeros((8, width), F32)
    small = lax.dynamic_update_slice(small, taps_part[:taps], (2, model_pos * channels))
    small = small.at[0].set(gain_mix_grad).at[1].set(gain_mlp_grad)
    small = small_sum(seqs, models, small)

    def total(got):
        return jnp.sum(got.astype(F32), axis=0)

    return (
        output,
        source_grad + middle_grad,
        small[0],
        small[1],
        small[2 : 2 + taps],
        total(in_got),
        total(out_got),
        total(pair_got),
        total(down_got),
    )


def solution(mesh):
    placed = (
        P(None, ("seq", "mp"), None),
        P(None, ("seq", "mp"), None),
        P(),
        P(),
        P(),
        P(),
        P(None, "seq", "mp"),
        P("mp", "seq"),
        P(None, "seq", "mp"),
        P("mp", "seq"),
    )
    return jax.shard_map(
        local,
        mesh=mesh,
        in_specs=placed,
        out_specs=(
            P(None, ("seq", "mp"), None),
            P(None, ("seq", "mp"), None),
            P(),
            P(),
            P(),
            P(None, "seq", "mp"),
            P("mp", "seq"),
            P(None, "seq", "mp"),
            P("mp", "seq"),
        ),
        check_vma=False,
    )
```

```python
import functools

import jax
import jax.numpy as jnp
from jax import lax
from jax.experimental import pallas as pl
from jax.experimental.pallas import tpu as pltpu
from jax.sharding import PartitionSpec as P

EPS = 1e-05
MESH = pl.DeviceIdType.MESH
BF = jnp.bfloat16
F32 = jnp.float32
HALVES = 2
VMEM_LIMIT = 63 * 2**20


def nn(a, b):
    return lax.dot_general(a, b, (((1,), (0,)), ((), ())), preferred_element_type=F32)


def nt(a, b):
    return lax.dot_general(a, b, (((1,), (1,)), ((), ())), preferred_element_type=F32)


def tn(a, b):
    return lax.dot_general(a, b, (((0,), (0,)), ((), ())), preferred_element_type=F32)


class Place:
    def __init__(self, seqs, models):
        self.seqs, self.chips = seqs, models // 2
        self.s = lax.axis_index("seq")
        self.m = lax.axis_index("mp")
        self.z = self.m // 2
        self.c = self.m % 2
        self.sibling = {"mp": self.m + 1 - 2 * self.c}
        self.above = {"mp": self.m + 2}
        self.below = {"mp": self.m - 2}
        self.has_above = self.z < self.chips - 1
        self.has_below = self.z > 0

    def peer(self, step):
        return {"seq": lax.rem(self.s + step, self.seqs)}

    def enter(self):
        barrier = pltpu.get_barrier_semaphore()

        def greet(where):
            pl.semaphore_signal(barrier, inc=1, device_id=where, device_id_type=MESH)

        greet(self.sibling)
        for step in range(1, self.seqs):
            greet(self.peer(step))
        pl.when(self.has_above)(lambda: greet(self.above))
        pl.when(self.has_below)(lambda: greet(self.below))
        chips = self.chips
        lines = (self.z + chips - 1) // chips + (2 * chips - 2 - self.z) // chips
        pl.semaphore_wait(barrier, self.seqs + lines)


def remote(src, dst, send, recv, where):
    return pltpu.make_async_remote_copy(
        src_ref=src, dst_ref=dst, send_sem=send, recv_sem=recv, device_id=where, device_id_type=MESH
    )


class Gather:
    def __init__(self, place, rows, own, sems):
        self.p, self.rows, self.own = place, rows, own
        self.share = rows.shape[0] // (2 * place.chips)
        self.piece = self.share // HALVES
        self.send, self.recv = sems

    def at(self, chip, core, half):
        return self.rows.at[pl.ds((chip * 2 + core) * self.share + half * self.piece, self.piece)]

    def copy(self, kind, chip, half, own=False):
        p = self.p
        where = (p.above, p.below, p.sibling)[kind]
        dst = self.at(chip, p.c, half)
        src = self.own.at[pl.ds(half * self.piece, self.piece)] if own and self.own is not None else dst
        return remote(src, dst, self.send.at[kind, chip, half], self.recv.at[kind // 2, chip, half], where)

    def start(self):
        p = self.p
        for half in range(HALVES):
            pl.when(p.has_above)(lambda h=half: self.copy(0, p.z, h, True).start())
            pl.when(p.has_below)(lambda h=half: self.copy(1, p.z, h, True).start())
        for half in range(HALVES):
            self.copy(2, p.z, half, True).start()

    def round(self, k):
        p = self.p
        for half in range(HALVES):

            @pl.when(p.z >= k)
            def _(half=half):
                chip = p.z - k
                self.copy(0, chip, half).wait_recv()
                pl.when(p.has_above)(lambda: self.copy(0, chip, half).start())
                self.copy(2, chip, half).start()

            @pl.when(p.z + k <= p.chips - 1)
            def _(half=half):
                chip = p.z + k
                self.copy(1, chip, half).wait_recv()
                pl.when(p.has_below)(lambda: self.copy(1, chip, half).start())
                self.copy(2, chip, half).start()

    def rounds(self):
        return [functools.partial(self.round, k) for k in range(1, self.p.chips)]

    def other_core(self, chip):
        p = self.p
        for half in range(HALVES):
            dst = self.at(chip, 1 - p.c, half)
            remote(dst, dst, self.send.at[2, chip, half], self.recv.at[1, chip, half], p.sibling).wait_recv()

    def arrived(self):
        for chip in range(self.p.chips):
            self.other_core(chip)

    def drain(self):
        p = self.p
        for chip in range(p.chips):
            for half in range(HALVES):
                pl.when(p.has_above & (chip <= p.z))(lambda ch=chip, h=half: self.copy(0, ch, h).wait_send())
                pl.when(p.has_below & (chip >= p.z))(lambda ch=chip, h=half: self.copy(1, ch, h).wait_send())
                self.copy(2, chip, half).wait_send()


class Scatter:
    def __init__(self, place, part, from_core, from_line, sems):
        self.p, self.part, self.from_core, self.from_line = place, part, from_core, from_line
        self.share = from_core.shape[1]
        self.piece = self.share // HALVES
        self.core_send, self.core_recv, self.line_send, self.line_recv = sems

    def rows(self, chip, core):
        return self.part.at[pl.ds((chip * 2 + core) * self.share, self.share)]

    def core_copy(self, chip):
        p = self.p
        return remote(
            self.rows(chip, 1 - p.c), self.from_core.at[chip], self.core_send.at[chip], self.core_recv.at[chip], p.sibling
        )

    def give(self, chip):
        self.core_copy(chip).start()

    def mine(self, chip, half):
        return self.part.at[pl.ds((chip * 2 + self.p.c) * self.share + half * self.piece, self.piece)]

    def line_copy(self, down, chip, slot, half):
        p = self.p
        dst = self.from_line.at[slot, pl.ds(half * self.piece, self.piece)]
        return remote(
            self.mine(chip, half),
            dst,
            self.line_send.at[down, chip, half],
            self.line_recv.at[slot, half],
            p.below if down else p.above,
        )

    def total(self, chip, half, slots):
        span = pl.ds(half * self.piece, self.piece)
        value = self.mine(chip, half)[...].astype(F32) + self.from_core[chip, span].astype(F32)
        for slot in slots:
            value = value + self.from_line[slot, span].astype(F32)
        return value

    def hop(self, down, chip, slot, has_source):
        self.core_copy(chip).wait_recv()
        for half in range(HALVES):

            @pl.when(has_source)
            def _(half=half):
                self.line_copy(down, chip, chip, half).wait_recv()
                self.mine(chip, half)[...] = self.total(chip, half, [chip]).astype(BF)

            @pl.when(jnp.logical_not(has_source))
            def _(half=half):
                self.mine(chip, half)[...] = self.total(chip, half, []).astype(BF)

            self.line_copy(down, chip, slot, half).start()

    def round(self, r):
        p = self.p
        last = p.chips - 1

        @pl.when((p.z <= r) & p.has_above)
        def _():
            chip = last - r + p.z
            self.hop(0, chip, chip, p.has_below)

        @pl.when((last - p.z <= r) & p.has_below)
        def _():
            chip = r - last + p.z
            self.hop(1, chip, p.chips if r == last - 1 else chip, p.has_above)

    def rounds(self):
        return [functools.partial(self.round, r) for r in range(self.p.chips - 1)]

    def finish(self, store):
        p = self.p
        self.core_copy(p.z).wait_recv()
        for half in range(HALVES):
            pl.when(p.has_below)(lambda h=half: self.line_copy(0, p.z, p.z, h).wait_recv())
            pl.when(p.has_above)(lambda h=half: self.line_copy(1, p.z, p.chips, h).wait_recv())
            for up in (False, True):
                for low in (False, True):

                    @pl.when((p.has_above == up) & (p.has_below == low))
                    def _(half=half, up=up, low=low):
                        slots = ([p.z] if low else []) + ([p.chips] if up else [])
                        store(half * self.piece, self.piece, self.total(p.z, half, slots))

    def drain(self):
        p = self.p
        for chip in range(p.chips):
            self.core_copy(chip).wait_send()
            for half in range(HALVES):
                pl.when(p.has_above & (chip > p.z))(lambda ch=chip, h=half: self.line_copy(0, ch, ch, h).wait_send())
                pl.when(p.has_below & (chip < p.z))(lambda ch=chip, h=half: self.line_copy(1, ch, ch, h).wait_send())


def gather_sems(count, chips):
    return [pltpu.SemaphoreType.DMA((count, 3, chips, HALVES)), pltpu.SemaphoreType.DMA((count, 2, chips, HALVES))]


def scatter_sems(count, chips):
    return [
        pltpu.SemaphoreType.DMA((count, chips)),
        pltpu.SemaphoreType.DMA((count, chips)),
        pltpu.SemaphoreType.DMA((count, 2, chips, HALVES)),
        pltpu.SemaphoreType.DMA((count, chips + 1, HALVES)),
    ]


def picks(sems, index):
    return [sem.at[index] for sem in sems]


def far_first(place):
    low, high = 0, place.chips - 1
    order = []
    for _ in range(place.chips):
        left = place.z - low >= high - place.z
        order.append(jnp.where(left, low, high))
        low, high = jnp.where(left, low + 1, low), jnp.where(left, high, high - 1)
    return order


def weave(*lists):
    for step in range(max(len(steps) for steps in lists)):
        for steps in lists:
            if step < len(steps):
                steps[step]()


class Relay:
    def __init__(self, place, shard, full, first, size, sems):
        self.p, self.shard, self.full, self.first, self.size = place, shard, full, first, size
        self.send, self.recv, self.local = sems
        s = place.s
        self.square = place.seqs == 4
        if self.square:
            self.near = (s + 1 - 2 * lax.rem(s, 2), lax.rem(s + 2, 4))

    def half(self, index):
        return self.first + index * (self.size // 2), self.size // 2

    def direct(self, index, where):
        return remote(
            self.shard(self.first, self.size),
            self.full(self.p.s, self.first, self.size),
            self.send.at[index],
            self.recv.at[index],
            where,
        )

    def handed(self, index):
        view = self.full(self.near[index], *self.half(index))
        return remote(view, view, self.send.at[2 + index], self.recv.at[2 + index], {"seq": self.near[1 - index]})

    def local_copy(self):
        return pltpu.make_async_copy(
            self.shard(self.first, self.size), self.full(self.p.s, self.first, self.size), self.local
        )

    def copies(self):
        if self.square:
            return [self.direct(index, {"seq": self.near[index]}) for index in range(2)]
        return [self.direct(step - 1, self.p.peer(step)) for step in range(1, self.p.seqs)]

    def start(self):
        for thing in self.copies():
            thing.start()
        self.local_copy().start()

    def forward(self):
        if self.square:
            for thing in self.copies():
                thing.wait_recv()
            for index in range(2):
                self.handed(index).start()

    def arrived(self):
        self.local_copy().wait()
        for thing in [self.handed(index) for index in range(2)] if self.square else self.copies():
            thing.wait_recv()

    def drain(self):
        for thing in self.copies() + ([self.handed(index) for index in range(2)] if self.square else []):
            thing.wait_send()


def forward_kernel(
    seqs,
    models,
    normed_ref,
    source_ref,
    gain_ref,
    top_ref,
    taps_ref,
    in_ref,
    out_ref,
    pair_ref,
    down_ref,
    normed_rows,
    top_rows,
    in_rows,
    out_rows,
    gates_out,
    product_out,
    mixed_out,
    middle_out,
    grad_out,
    mlp_part,
    act_rows,
    pair_grad,
    down_grad,
    in_full,
    out_full,
    rows,
    gates,
    ends,
    product,
    mixed,
    pair,
    down,
    top_tile,
    acts,
    act_stage,
    stage,
    part,
    from_core,
    from_line,
    total,
    w_send,
    w_recv,
    w_local,
    halo_send,
    halo_recv,
    keep,
    tile_sem,
    out_sem,
    cols_sem,
    pair_sem,
    ends_sem,
    *sems,
):
    p = Place(seqs, models)
    chips = p.chips
    g_sems, s_sems = sems[:2], sems[2:]
    slots, block, width = rows.shape
    units = down.shape[0]
    tile = block // chips
    share = tile // 2
    channels = in_full.shape[2]
    shard = width // seqs
    unit_block = min(512, units)
    wide_block = 512
    p.enter()

    firsts = [Gather(p, rows.at[slot], normed_ref.at[slot], picks(g_sems, slot)) for slot in range(slots)]
    tops = [Gather(p, top_rows.at[slot], top_ref.at[slot], picks(g_sems, slots + slot)) for slot in range(slots)]
    seconds = [Gather(p, rows.at[slot], None, picks(g_sems, 2 * slots + slot)) for slot in range(slots)]

    def scatter(slot, index):
        return Scatter(p, part.at[slot], from_core.at[slot], from_line.at[slot], picks(s_sems, index))

    mix_sums = [scatter(slot, slot) for slot in range(slots)]
    grad_sums = [scatter(slot, slots + slot) for slot in range(slots)]

    def columns_of(owner):
        return pl.ds(pl.multiple_of(owner * shard, shard), shard)

    def pair_views(k):
        return (
            lambda first, size: pair_ref.at[k, pl.ds(first, size)],
            lambda owner, first, size: pair.at[k, pl.ds(owner * shard + first, size)],
        )

    views = [
        (
            lambda first, size: in_ref.at[:, pl.ds(first, size)],
            lambda owner, first, size: in_full.at[:, pl.ds(owner * shard + first, size)],
            0,
            shard,
        ),
        (
            lambda first, size: out_ref.at[pl.ds(first, size)],
            lambda owner, first, size: out_full.at[pl.ds(first, size), columns_of(owner)],
            0,
            channels,
        ),
    ]
    for i in range(2):
        views.append(
            (
                lambda first, size: down_ref.at[pl.ds(first, size)],
                lambda owner, first, size: down.at[pl.ds(first, size), columns_of(owner)],
                i * (units // 2),
                units // 2,
            )
        )
    for i in range(4):
        views.append((*pair_views(i // 2), (i % 2) * (shard // 2), shard // 2))
    pieces = [Relay(p, *view, (w_send.at[i], w_recv.at[i], w_local.at[i])) for i, view in enumerate(views)]
    early, late = pieces[:2], pieces[2:]
    moves = [[("start", 0), ("start", 1)], [("forward", 0), ("start", 2)], [("forward", 1), ("start", 3)]]
    moves += [[("forward", 2)], [("forward", 3)], [("start", 4), ("start", 5)], [("forward", 4)], [("forward", 5)]]

    def push():
        for name, index in moves.pop(0):
            getattr(late[index], name)()

    def own(slot, which, source):
        span = pl.ds(p.m * share, share)
        return pltpu.make_async_copy(source.at[slot], which.at[slot, span], keep.at[slot + (slots if which is top_rows else 0)])

    for slot in range(slots):
        own(slot, rows, normed_ref).start()
        own(slot, top_rows, top_ref).start()

    def saved(index, src, dst):
        return pltpu.make_async_copy(src, dst, keep.at[2 * slots + index])

    rows_saved = [saved(slot, rows.at[slot], normed_rows.at[slot]) for slot in range(slots)]
    gates_saved = [saved(slots + slot, gates, gates_out.at[slot, 1]) for slot in range(slots)]
    middle_saved = [saved(2 * slots + slot, total.at[slot], middle_out.at[slot]) for slot in range(slots)]
    grad_saved = [saved(3 * slots + slot, total.at[slot], grad_out.at[slot]) for slot in range(slots)]
    in_saved = saved(4 * slots, in_full, in_rows)
    out_saved = saved(4 * slots + 1, out_full, out_rows)
    product_saved = saved(4 * slots + 2, product, product_out)
    mixed_saved = saved(4 * slots + 3, mixed, mixed_out)
    down_saved = saved(4 * slots + 4, down, down_grad)
    act_load = saved(4 * slots + 5, act_rows, acts.at[0])

    def halo(slot):
        return remote(
            product.at[slot, pl.ds(block, 8)],
            product.at[slot, pl.ds(0, 8)],
            halo_send.at[slot],
            halo_recv.at[slot],
            p.peer(1),
        )

    has_later, has_earlier = p.s < seqs - 1, p.s > 0
    for slot in range(slots):

        @pl.when(jnp.logical_not(has_earlier))
        def _(slot=slot):
            product[slot, pl.ds(0, 8)] = jnp.zeros((8, channels), F32)

    def ends_saved(slot, i):
        span = pl.ds(i * tile, tile)
        return [
            pltpu.make_async_copy(ends.at[j], gates_out.at[slot, 2 * j, span], ends_sem.at[j]) for j in range(2)
        ]

    def project(slot):
        @pl.loop(0, chips)
        def _(i):
            span = pl.ds(i * tile, tile)
            source = rows[slot, span]
            b_gate = nn(source, in_full[0])
            x_value = nn(source, in_full[2])
            gates[span] = nn(source, in_full[1])

            @pl.when(i > 0)
            def _():
                for thing in ends_saved(slot, i - 1):
                    thing.wait()

            ends[0] = b_gate
            ends[1] = x_value
            for thing in ends_saved(slot, i):
                thing.start()
            product[slot, pl.ds(8 + i * tile, tile)] = b_gate * x_value

        for thing in ends_saved(slot, chips - 1):
            thing.wait()
        pl.when(has_later)(lambda: halo(slot).start())

    def convolve(slot):
        pl.when(has_earlier)(lambda: halo(slot).wait_recv())
        for i in range(chips):
            conv = 0.0
            for offset in range(taps_ref.shape[0]):
                conv = conv + taps_ref[offset : offset + 1] * product[slot, pl.ds(8 + i * tile - offset, tile)]
            mixed[slot, pl.ds(i * tile, tile)] = (gates[pl.ds(i * tile, tile)] * conv).astype(BF)

    def project_out(slot):
        for chip in far_first(p):
            span = pl.ds(chip * tile, tile)
            part[slot, span] = nn(mixed[slot, span], out_full[...]).astype(BF)
            mix_sums[slot].give(chip)

    def middle(slot):
        def store(first, size, value):
            span = pl.ds(first, size)
            value = value + source_ref[slot, span].astype(F32)
            total[slot, span] = value
            scale = lax.rsqrt(jnp.mean(value * value, axis=-1, keepdims=True) + EPS)
            rows[slot, pl.ds(p.m * share + first, size)] = (value * scale * gain_ref[...]).astype(BF)

        mix_sums[slot].finish(store)
        middle_saved[slot].start()
        mix_sums[slot].drain()

    def finish_grad(slot):
        middle_saved[slot].wait()

        def store(first, size, value):
            total[slot, pl.ds(first, size)] = value

        grad_sums[slot].finish(store)
        grad_saved[slot].start()

    order = far_first(p)
    tiles = [(0, chip) for chip in order] + [(slot, chip) for slot in range(1, slots) for chip in order[::-1]]

    def fetch(index):
        slot, chip = tiles[index]
        return pltpu.make_async_copy(top_rows.at[slot, pl.ds(chip * tile, tile)], top_tile, tile_sem)

    def puts(index):
        slot, chip = tiles[index]
        span = pl.ds(chip * tile, tile)
        return [
            pltpu.make_async_copy(stage, mlp_part.at[slot, span], out_sem.at[0]),
            pltpu.make_async_copy(act_stage, act_rows.at[slot, span], out_sem.at[1]),
        ]

    def work(index):
        slot, chip = tiles[index]
        span = pl.ds(chip * tile, tile)
        if index == 0 or slot > 0:
            fetch(index).start()
        fetch(index).wait()
        if index:
            for thing in puts(index - 1):
                thing.wait()

        @pl.loop(0, units // unit_block)
        def _(i):
            cut = pl.ds(pl.multiple_of(i * unit_block, unit_block), unit_block)
            source = rows[slot, span]
            gate = nn(source, pair[0, :, cut])
            up = nn(source, pair[1, :, cut])
            act_grad = nt(top_tile[...], down[cut])
            sigma = jax.nn.sigmoid(gate)
            silu = gate * sigma
            act_stage[:, cut] = (silu * up).astype(BF)
            acts[0, slot, span, cut] = (act_grad * up * sigma * (1.0 + gate * (1.0 - sigma))).astype(BF)
            acts[1, slot, span, cut] = (act_grad * silu).astype(BF)

        if index + 1 < len(tiles) and tiles[index + 1][0] == 0:
            fetch(index + 1).start()

        @pl.loop(0, width // wide_block)
        def _(i):
            cut = pl.ds(pl.multiple_of(i * wide_block, wide_block), wide_block)
            value = nt(acts[0, slot, span], pair[0, cut]) + nt(acts[1, slot, span], pair[1, cut])
            part[slot, span, cut] = value.astype(BF)
            stage[:, cut] = nn(act_stage[...], down[:, cut]).astype(BF)

        grad_sums[slot].give(chip)
        for thing in puts(index):
            thing.start()

    pair_steps = 2 * (width // wide_block)

    def pair_saved(index):
        k, first = divmod(index, width // wide_block)
        cut = pl.ds(first * wide_block, wide_block)
        return pltpu.make_async_copy(pair.at[k, cut], pair_grad.at[k, cut], pair_sem.at[index])

    def pair_step(index):
        k, first = divmod(index, width // wide_block)
        cut = pl.ds(first * wide_block, wide_block)
        value = 0.0
        for slot in range(slots):
            value = value + tn(rows[slot, :, cut], acts[k, slot])
        pair[k, cut] = value.astype(BF)
        pair_saved(index).start()
        if first == width // wide_block - 1 and k == 0:
            act_load.start()

    def fetch_columns(index):
        cut = pl.ds(index * channels, channels)
        return [
            pltpu.make_async_copy(
                top_rows.at[slot, :, cut], in_full.at[index % 2, pl.ds(slot * block, block)], cols_sem.at[index % 2, slot]
            )
            for slot in range(slots)
        ]

    def down_step(index):
        if index == 0:
            act_load.wait()
        for thing in fetch_columns(index):
            thing.wait()
        for first in range(0, units, unit_block):
            cut = pl.ds(first, unit_block)
            value = 0.0
            for slot in range(slots):
                value = value + tn(acts[0, slot, :, cut], in_full[index % 2, pl.ds(slot * block, block)])
            down[cut, pl.ds(index * channels, channels)] = value.astype(BF)
        if index + 2 < width // channels:
            for thing in fetch_columns(index + 2):
                thing.start()

    firsts[0].start()
    for piece in early:
        piece.start()
    steps = firsts[0].rounds()
    for step in steps[:-1]:
        step()
    for piece in early:
        piece.forward()
    firsts[1].start()
    steps[-1]()
    own(0, rows, normed_ref).wait()
    firsts[0].arrived()
    rows_saved[0].start()
    for piece in early:
        piece.arrived()
    in_saved.start()
    out_saved.start()
    project(0)
    gates_saved[0].start()
    push()
    steps = firsts[1].rounds()
    steps[0]()
    push()
    rows_saved[0].wait()
    firsts[0].drain()
    convolve(0)
    project_out(0)
    weave(mix_sums[0].rounds(), steps[1:-1] + [tops[0].start, steps[-1]], [push] * 3)
    own(1, rows, normed_ref).wait()
    firsts[1].arrived()
    rows_saved[1].start()
    gates_saved[0].wait()
    project(1)
    gates_saved[1].start()
    push()
    middle(0)
    seconds[0].start()
    rows_saved[1].wait()
    firsts[1].drain()
    convolve(1)
    project_out(1)
    hops, steps, more = mix_sums[1].rounds(), tops[0].rounds(), seconds[0].rounds()
    weave(steps, hops, [push] * 2)
    weave(more[:-1])
    tops[1].start()
    more[-1]()
    middle(1)
    seconds[1].start()
    product_saved.start()
    mixed_saved.start()
    own(0, top_rows, top_ref).wait()
    tops[0].arrived()
    seconds[0].arrived()
    for piece in late:
        piece.arrived()
    own(1, top_rows, top_ref).wait()
    hops, steps, more = grad_sums[0].rounds(), tops[1].rounds(), seconds[1].rounds()
    for index in range(chips):
        work(index)
        if index < len(steps):
            steps[index]()
        if 0 < index:
            hops[index - 1]()
    for index in range(chips):
        if index:
            more[index - 1]()
        else:
            tops[1].arrived()
        seconds[1].other_core(tiles[chips + index][1])
        work(chips + index)
    in_saved.wait()
    for piece in pieces:
        piece.drain()
    for index in range(2):
        for thing in fetch_columns(index):
            thing.start()
    hops = grad_sums[1].rounds()
    hops[0]()
    finish_grad(0)
    for index in range(len(tiles) - 1, len(tiles)):
        for thing in puts(index):
            thing.wait()
    work_steps = [functools.partial(pair_step, index) for index in range(pair_steps)]
    work_steps += [functools.partial(down_step, index) for index in range(width // channels)]
    spaced = len(work_steps) // len(hops)
    for index, step in enumerate(work_steps):
        step()
        if (index + 1) % spaced == 0 and (index + 1) // spaced < len(hops):
            hops[(index + 1) // spaced]()
    down_saved.start()
    finish_grad(1)
    for index in range(pair_steps):
        pair_saved(index).wait()
    for thing in [gates_saved[1], out_saved, product_saved, mixed_saved, down_saved, *grad_saved]:
        thing.wait()
    for thing in tops + seconds + grad_sums:
        thing.drain()
    for slot in range(slots):
        pl.when(has_later)(lambda slot=slot: halo(slot).wait_send())


def forward(seqs, models, normed, source, gain, top, taps, mixer_in, mixer_out, gate_up, mlp_down):
    slots, share, width = normed.shape
    chips = models // 2
    block = share * models
    channels = mixer_in.shape[2]
    units = gate_up.shape[2]
    tile = block // chips
    hbm = pl.BlockSpec(memory_space=pltpu.HBM)
    vmem = pl.BlockSpec(memory_space=pltpu.VMEM)
    shape = jax.ShapeDtypeStruct
    return pl.pallas_call(
        functools.partial(forward_kernel, seqs, models),
        out_shape=[
            shape((slots, block, width), BF),
            shape((slots, block, width), BF),
            shape((3, width, channels), BF),
            shape((channels, width), BF),
            shape((slots, 3, block, channels), F32),
            shape((slots, block + 8, channels), F32),
            shape((slots, block, channels), BF),
            shape((slots, share, width), F32),
            shape((slots, share, width), F32),
            shape((slots, block, width), BF),
            shape((slots, block, units), BF),
            shape((2, width, units), BF),
            shape((units, width), BF),
        ],
        in_specs=[hbm, vmem, vmem, hbm, vmem] + [hbm] * 4,
        out_specs=[hbm] * 13,
        scratch_shapes=[
            pltpu.VMEM((3, width, channels), BF),
            pltpu.VMEM((channels, width), BF),
            pltpu.VMEM((slots, block, width), BF),
            pltpu.VMEM((block, channels), F32),
            pltpu.VMEM((2, tile, channels), F32),
            pltpu.VMEM((slots, block + 8, channels), F32),
            pltpu.VMEM((slots, block, channels), BF),
            pltpu.VMEM((2, width, units), BF),
            pltpu.VMEM((units, width), BF),
            pltpu.VMEM((tile, width), BF),
            pltpu.VMEM((2, slots, block, units), BF),
            pltpu.VMEM((tile, units), BF),
            pltpu.VMEM((tile, width), BF),
            pltpu.VMEM((slots, block, width), BF),
            pltpu.VMEM((slots, chips, share, width), BF),
            pltpu.VMEM((slots, chips + 1, share, width), BF),
            pltpu.VMEM((slots, share, width), F32),
            pltpu.SemaphoreType.DMA((8, max(4, seqs - 1))),
            pltpu.SemaphoreType.DMA((8, max(4, seqs - 1))),
            pltpu.SemaphoreType.DMA((8,)),
            pltpu.SemaphoreType.DMA((slots,)),
            pltpu.SemaphoreType.DMA((slots,)),
            pltpu.SemaphoreType.DMA((6 * slots + 6,)),
            pltpu.SemaphoreType.DMA,
            pltpu.SemaphoreType.DMA((2,)),
            pltpu.SemaphoreType.DMA((2, slots)),
            pltpu.SemaphoreType.DMA((2 * (width // 512),)),
            pltpu.SemaphoreType.DMA((2,)),
            *gather_sems(3 * slots, chips),
            *scatter_sems(2 * slots, chips),
        ],
        compiler_params=pltpu.CompilerParams(collective_id=1, has_side_effects=True, vmem_limit_bytes=VMEM_LIMIT),
    )(normed, source, gain, top, taps, mixer_in, mixer_out, gate_up, mlp_down)


class Exchange:
    def __init__(self, place, partial, got, first, size, sems, held, came):
        self.p, self.partial, self.got, self.first, self.size = place, partial, got, first, size
        self.send, self.recv, self.local = sems
        self.held, self.came = held, came
        s = place.s
        self.square = place.seqs == 4
        if self.square:
            self.near = (s + 1 - 2 * lax.rem(s, 2), lax.rem(s + 2, 4))
            self.across = 3 - s

    def half(self, index):
        return self.first + index * (self.size // 2), self.size // 2

    def to(self, index):
        return {"seq": self.near[index]}

    def relayed(self, index):
        return remote(
            self.partial(self.across, *self.half(index)),
            self.came.at[index],
            self.send.at[index],
            self.recv.at[index],
            self.to(index),
        )

    def plain(self, index):
        span = self.half(index)
        return remote(
            self.partial(self.near[index], *span),
            self.got(1 + index, *span),
            self.send.at[2 + index],
            self.recv.at[2 + index],
            self.to(index),
        )

    def added(self, index):
        return remote(
            self.held.at[1 - index],
            self.got(1 + index, *self.half(1 - index)),
            self.send.at[4 + index],
            self.recv.at[4 + index],
            self.to(index),
        )

    def load(self, index):
        return pltpu.make_async_copy(
            self.partial(self.near[index], *self.half(1 - index)), self.held.at[1 - index], self.local.at[1 + index]
        )

    def straight(self, step):
        p = self.p
        return remote(
            self.partial(lax.rem(p.s + step, p.seqs), self.first, self.size),
            self.got(step, self.first, self.size),
            self.send.at[step - 1],
            self.recv.at[step - 1],
            p.peer(step),
        )

    def own(self):
        return pltpu.make_async_copy(
            self.partial(self.p.s, self.first, self.size), self.got(0, self.first, self.size), self.local.at[0]
        )

    def copies(self):
        if self.square:
            return [self.relayed(0), self.relayed(1), self.plain(0), self.plain(1)]
        return [self.straight(step) for step in range(1, self.p.seqs)]

    def start(self):
        for thing in self.copies():
            thing.start()
        if self.square:
            for index in range(2):
                self.load(index).start()
        self.own().start()

    def forward(self):
        if self.square:
            for index in range(2):
                self.load(index).wait()
                self.relayed(1 - index).wait_recv()
                total = self.held[1 - index].astype(F32) + self.came[1 - index].astype(F32)
                self.held[1 - index] = total.astype(BF)
                self.added(index).start()

    def finish(self):
        self.own().wait()
        if self.square:
            for thing in self.copies():
                thing.wait_send()
            for index in range(2):
                self.plain(index).wait_recv()
                self.added(index).wait()
        else:
            for thing in self.copies():
                thing.wait()


def mixer_backward_kernel(
    seqs,
    models,
    low_ref,
    mlp_part,
    taps_ref,
    in_ref,
    out_ref,
    normed_rows,
    gates_ref,
    product_ref,
    mixed_ref,
    pair_grad,
    down_grad,
    mlp_out,
    grad_out,
    taps_out,
    in_got,
    out_got,
    pair_got,
    down_got,
    in_full,
    out_full,
    rows,
    columns,
    gates,
    product,
    mixed,
    conv_grad,
    stacked,
    part,
    from_core,
    from_line,
    mlp_total,
    grad_total,
    down_room,
    pair_room,
    in_room,
    out_room,
    load,
    cols_sem,
    w_send,
    w_recv,
    w_local,
    halo_send,
    halo_recv,
    free,
    *sems,
):
    p = Place(seqs, models)
    chips = p.chips
    g_sems, s_sems = sems[:2], sems[2:]
    slots, block, width = rows.shape
    channels = out_full.shape[0]
    taps = taps_ref.shape[0]
    tile = block // chips
    share = tile // 2
    wide_block = 512
    cols = columns.shape[-1]
    loads = [
        pltpu.make_async_copy(src, dst, load.at[i])
        for i, (src, dst) in enumerate(
            [(mlp_part.at[slot], part.at[slot]) for slot in range(slots)]
            + [
                (low_ref.at[slot], rows.at[slot, pl.ds(p.m * share, share)])
                for slot in range(slots)
            ]
            + [
                (in_ref, in_full),
                (out_ref, out_full),
                (gates_ref, gates),
                (product_ref, product),
                (mixed_ref, mixed),
            ]
        )
    ]
    for thing in loads:
        thing.start()
    p.enter()
    gathers = [Gather(p, rows.at[slot], low_ref.at[slot], picks(g_sems, slot)) for slot in range(slots)]

    def scatter(slot, index):
        return Scatter(p, part.at[slot], from_core.at[slot], from_line.at[slot], picks(s_sems, index))

    mlp_sums = [scatter(slot, slot) for slot in range(slots)]
    sums = [scatter(slot, slots + slot) for slot in range(slots)]
    shard = width // seqs
    units = down_grad.shape[0]

    def columns_of(owner):
        return pl.ds(pl.multiple_of(owner * shard, shard), shard)

    views = []
    for i in range(2):
        views.append(
            (
                lambda owner, first, size: down_grad.at[pl.ds(first, size), columns_of(owner)],
                lambda index, first, size: down_got.at[index, pl.ds(first, size)],
                i * (units // 2),
                units // 2,
                down_room.at[i],
            )
        )
    for i in range(4):
        views.append(
            (
                lambda owner, first, size, k=i // 2: pair_grad.at[k, pl.ds(owner * shard + first, size)],
                lambda index, first, size, k=i // 2: pair_got.at[index, k, pl.ds(first, size)],
                (i % 2) * (shard // 2),
                shard // 2,
                pair_room.at[i],
            )
        )
    views.append(
        (
            lambda owner, first, size: in_full.at[:, pl.ds(owner * shard + first, size)],
            lambda index, first, size: in_got.at[index, :, pl.ds(first, size)],
            0,
            shard,
            in_room,
        )
    )
    views.append(
        (
            lambda owner, first, size: out_full.at[pl.ds(first, size), columns_of(owner)],
            lambda index, first, size: out_got.at[index, pl.ds(first, size)],
            0,
            channels,
            out_room,
        )
    )
    pieces = [
        Exchange(p, *view[:4], (w_send.at[i], w_recv.at[i], w_local.at[i]), view[4].at[0], view[4].at[1])
        for i, view in enumerate(views)
    ]
    moves = [[("start", 0), ("start", 1)], [("forward", 0), ("start", 2)], [("forward", 1), ("start", 3)]]
    moves += [[("forward", 2)], [("forward", 3)], [("start", 4), ("start", 5)], [("forward", 4)], [("forward", 5)]]

    def push():
        for name, index in moves.pop(0):
            getattr(pieces[index], name)()

    has_later, has_earlier = p.s < seqs - 1, p.s > 0
    order = far_first(p)

    def halo(slot):
        return remote(
            conv_grad.at[slot, pl.ds(0, 8)],
            conv_grad.at[slot, pl.ds(block, 8)],
            halo_send.at[slot],
            halo_recv.at[slot],
            p.peer(seqs - 1),
        )

    for slot in range(slots):

        @pl.when(jnp.logical_not(has_later))
        def _(slot=slot):
            conv_grad[slot, pl.ds(block, 8)] = jnp.zeros((8, channels), F32)

    taps_out[...] = jnp.zeros_like(taps_out)

    def first_pass(slot):
        for i in range(chips):
            span = pl.ds(i * tile, tile)
            mixed_grad = nt(rows[slot, span], out_full[...])
            grad = mixed_grad * gates[slot, 1, span]
            conv_grad[slot, span] = grad
            conv = 0.0
            for offset in range(taps):
                earlier = product[slot, pl.ds(8 + i * tile - offset, tile)]
                conv = conv + taps_ref[offset : offset + 1] * earlier
                taps_out[offset : offset + 1] += jnp.sum(grad * earlier, axis=0, keepdims=True)
            stacked[slot, span, pl.ds(channels, channels)] = (mixed_grad * conv).astype(BF)
            if i == 0:
                pl.when(has_earlier)(lambda: halo(slot).start())

    def second_pass(slot):
        pl.when(has_later)(lambda: halo(slot).wait_recv())
        for i in range(chips):
            span = pl.ds(i * tile, tile)
            grad = 0.0
            for offset in range(taps):
                grad = grad + taps_ref[offset : offset + 1] * conv_grad[slot, pl.ds(i * tile + offset, tile)]
            stacked[slot, span, pl.ds(0, channels)] = (grad * gates[slot, 2, span]).astype(BF)
            stacked[slot, span, pl.ds(2 * channels, channels)] = (grad * gates[slot, 0, span]).astype(BF)

    def third_pass(slot):
        for chip in order:
            span = pl.ds(chip * tile, tile)

            @pl.loop(0, width // wide_block)
            def _(i):
                cut = pl.ds(pl.multiple_of(i * wide_block, wide_block), wide_block)
                value = 0.0
                for k in range(3):
                    value = value + nt(stacked[slot, span, pl.ds(k * channels, channels)], in_full[k, cut])
                part[slot, span, cut] = value.astype(BF)

            sums[slot].give(chip)

    def finish(what, total, slot):
        def store(first, size, value):
            total[slot, pl.ds(first, size)] = value

        what[slot].finish(store)

    def neighbours(act):
        act(p.sibling)
        pl.when(p.has_above)(lambda: act(p.above))
        pl.when(p.has_below)(lambda: act(p.below))

    def give_free(slot):
        mlp_sums[slot].drain()
        neighbours(
            lambda where: pl.semaphore_signal(free.at[slot], inc=1, device_id=where, device_id_type=MESH)
        )

    def take_free(slot):
        lines = (p.z + chips - 1) // chips + (2 * chips - 2 - p.z) // chips
        pl.semaphore_wait(free.at[slot], 1 + lines)

    def fetch_columns(index):
        return pltpu.make_async_copy(
            normed_rows.at[:, :, pl.ds(index * cols, cols)], columns.at[index % 2], cols_sem.at[index % 2]
        )

    steps_in = width // cols

    def in_step(index):
        fetch_columns(index).wait()
        value = 0.0
        for slot in range(slots):
            value = value + tn(columns[index % 2, slot], stacked[slot])
        for k in range(3):
            in_full[k, pl.ds(index * cols, cols)] = value[:, k * channels : (k + 1) * channels].astype(BF)
        if index + 2 < steps_in:
            fetch_columns(index + 2).start()

    def out_step():
        for first in range(0, width, wide_block):
            cut = pl.ds(first, wide_block)
            value = 0.0
            for slot in range(slots):
                value = value + tn(mixed[slot], rows[slot, :, cut])
            out_full[:, cut] = value.astype(BF)

    gathers[0].start()
    push()
    loads[0].wait()
    for chip in order:
        mlp_sums[0].give(chip)
    hops, next_rows = mlp_sums[0].rounds(), gathers[0].rounds()
    weave(hops[:-1], next_rows[:-1], [push] * 2)
    gathers[1].start()
    weave(hops[-1:], next_rows[-1:], [push])
    loads[1].wait()
    for chip in order:
        mlp_sums[1].give(chip)
    loads[2].wait()
    for thing in loads[2 + slots :]:
        thing.wait()
    gathers[0].arrived()
    push()
    fetch_columns(0).start()
    fetch_columns(1).start()
    mlp_hops, next_rows, hops = mlp_sums[1].rounds(), gathers[1].rounds(), sums[0].rounds()
    first_pass(0)
    push()
    finish(mlp_sums, mlp_total, 0)
    give_free(0)
    weave(mlp_hops[:1], next_rows[:1])
    second_pass(0)
    take_free(0)
    third_pass(0)
    weave(mlp_hops[1:], next_rows[1:], hops[:1], [push] * 2)
    loads[3].wait()
    gathers[1].arrived()
    first_pass(1)
    finish(mlp_sums, mlp_total, 1)
    give_free(1)
    hops[1]()
    second_pass(1)
    take_free(1)
    weave(hops[2:])
    third_pass(1)
    hops = sums[1].rounds()
    hops[0]()
    out_step()
    pieces[7].start()
    for index in range(steps_in):
        in_step(index)
    pieces[6].start()
    hops[1]()
    pieces[7].forward()
    pieces[6].forward()
    weave(hops[2:])
    finish(sums, grad_total, 0)
    finish(sums, grad_total, 1)
    last = [
        pltpu.make_async_copy(mlp_total, mlp_out, load.at[0]),
        pltpu.make_async_copy(grad_total, grad_out, load.at[1]),
    ]
    for thing in last:
        thing.start()
    for thing in pieces:
        thing.finish()
    for thing in last:
        thing.wait()
    for thing in gathers + sums:
        thing.drain()
    for slot in range(slots):
        pl.when(has_earlier)(lambda slot=slot: halo(slot).wait_send())


def mixer_backward(
    seqs, models, low, mlp_part, taps, in_full, out_full, normed_rows, gates, product, mixed, pair_grad, down_grad
):
    slots, share, width = low.shape
    chips = models // 2
    block = share * models
    channels = out_full.shape[0]
    units = down_grad.shape[0]
    shard = width // seqs
    gots = 3 if seqs == 4 else seqs
    hbm = pl.BlockSpec(memory_space=pltpu.HBM)
    vmem = pl.BlockSpec(memory_space=pltpu.VMEM)
    shape = jax.ShapeDtypeStruct
    return pl.pallas_call(
        functools.partial(mixer_backward_kernel, seqs, models),
        out_shape=[
            shape((slots, share, width), F32),
            shape((slots, share, width), F32),
            shape((8, channels), F32),
            shape((gots, 3, shard, channels), BF),
            shape((gots, channels, shard), BF),
            shape((gots, 2, shard, units), BF),
            shape((gots, units, shard), BF),
        ],
        in_specs=[hbm, hbm, vmem] + [hbm] * 8,
        out_specs=[hbm, hbm, vmem] + [hbm] * 4,
        scratch_shapes=[
            pltpu.VMEM((3, width, channels), BF),
            pltpu.VMEM((channels, width), BF),
            pltpu.VMEM((slots, block, width), BF),
            pltpu.VMEM((2, slots, block, 256), BF),
            pltpu.VMEM((slots, 3, block, channels), F32),
            pltpu.VMEM((slots, block + 8, channels), F32),
            pltpu.VMEM((slots, block, channels), BF),
            pltpu.VMEM((slots, block + 8, channels), F32),
            pltpu.VMEM((slots, block, 3 * channels), BF),
            pltpu.VMEM((slots, block, width), BF),
            pltpu.VMEM((slots, chips, share, width), BF),
            pltpu.VMEM((slots, chips + 1, share, width), BF),
            pltpu.VMEM((slots, share, width), F32),
            pltpu.VMEM((slots, share, width), F32),
            pltpu.VMEM((2, 2, 2, units // 4, shard), BF),
            pltpu.VMEM((4, 2, 2, shard // 4, units), BF),
            pltpu.VMEM((2, 2, 3, shard // 2, channels), BF),
            pltpu.VMEM((2, 2, channels // 2, shard), BF),
            pltpu.SemaphoreType.DMA((2 * slots + 5,)),
            pltpu.SemaphoreType.DMA((2,)),
            pltpu.SemaphoreType.DMA((8, max(6, seqs - 1))),
            pltpu.SemaphoreType.DMA((8, max(6, seqs - 1))),
            pltpu.SemaphoreType.DMA((8, 3)),
            pltpu.SemaphoreType.DMA((slots,)),
            pltpu.SemaphoreType.DMA((slots,)),
            pltpu.SemaphoreType.REGULAR((slots,)),
            *gather_sems(slots, chips),
            *scatter_sems(2 * slots, chips),
        ],
        compiler_params=pltpu.CompilerParams(collective_id=3, has_side_effects=True, vmem_limit_bytes=VMEM_LIMIT),
    )(low, mlp_part, taps, in_full, out_full, normed_rows, gates, product, mixed, pair_grad, down_grad)


def small_sum_kernel(seqs, models, value_ref, out_ref, by_model, by_seq, send, recv, seq_send, seq_recv):
    s, m = lax.axis_index("seq"), lax.axis_index("mp")
    cols = by_seq.shape[-1]
    along = [lax.rem(m + step, models) for step in range(1, models)]
    across = [lax.rem(s + step, seqs) for step in range(1, seqs)]

    def span(owner):
        return pl.ds(pl.multiple_of(owner * cols, cols), cols)

    barrier = pltpu.get_barrier_semaphore()
    for where in [{"mp": peer} for peer in along] + [{"seq": peer} for peer in across]:
        pl.semaphore_signal(barrier, inc=1, device_id=where, device_id_type=MESH)
    pl.semaphore_wait(barrier, models + seqs - 2)
    by_model[m] = value_ref[:, span(m)]
    copies = [
        remote(value_ref.at[:, span(peer)], by_model.at[m], send.at[0, i], recv.at[0, i], {"mp": peer})
        for i, peer in enumerate(along)
    ]
    for thing in copies:
        thing.start()
    for thing in copies:
        thing.wait()
    by_seq[s] = functools.reduce(lambda a, b: a + b, [by_model[i] for i in range(models)])
    copies = [
        remote(by_seq.at[s], by_seq.at[s], seq_send.at[i], seq_recv.at[i], {"seq": peer})
        for i, peer in enumerate(across)
    ]
    for thing in copies:
        thing.start()
    for thing in copies:
        thing.wait()
    out_ref[:, span(m)] = functools.reduce(lambda a, b: a + b, [by_seq[i] for i in range(seqs)])
    copies = [
        remote(out_ref.at[:, span(m)], out_ref.at[:, span(m)], send.at[1, i], recv.at[1, i], {"mp": peer})
        for i, peer in enumerate(along)
    ]
    for thing in copies:
        thing.start()
    for thing in copies:
        thing.wait()


def small_sum(seqs, models, value):
    vmem = pl.BlockSpec(memory_space=pltpu.VMEM)
    height, width = value.shape
    cols = width // models
    return pl.pallas_call(
        functools.partial(small_sum_kernel, seqs, models),
        out_shape=jax.ShapeDtypeStruct(value.shape, F32),
        in_specs=[vmem],
        out_specs=vmem,
        scratch_shapes=[
            pltpu.VMEM((models, height, cols), F32),
            pltpu.VMEM((seqs, height, cols), F32),
            pltpu.SemaphoreType.DMA((2, models - 1)),
            pltpu.SemaphoreType.DMA((2, models - 1)),
            pltpu.SemaphoreType.DMA((seqs - 1,)),
            pltpu.SemaphoreType.DMA((seqs - 1,)),
        ],
        compiler_params=pltpu.CompilerParams(collective_id=4, has_side_effects=True),
    )(value)


def normalize(values, gain):
    scale = lax.rsqrt(jnp.mean(values * values, axis=-1, keepdims=True) + EPS)
    return (values * scale * gain, scale)


def norm_back(grad, values, scale, gain):
    unit = values * scale
    scaled = grad * gain
    gain_grad = jnp.sum(grad * unit, axis=(0, 1))
    input_grad = scale * (scaled - unit * jnp.mean(scaled * unit, axis=-1, keepdims=True))
    return (input_grad, gain_grad)


def local(
    hidden,
    cotangent,
    lengths,
    gain_mix,
    gain_mlp,
    conv_weight,
    mixer_in,
    mixer_out,
    gate_up,
    mlp_down,
):
    seqs, models = lax.axis_size("seq"), lax.axis_size("mp")
    seq_pos = lax.axis_index("seq")
    model_pos = lax.axis_index("mp")
    slots, share, width = hidden.shape
    channels = mixer_in.shape[2]
    taps = conv_weight.shape[0]
    local_taps = lax.dynamic_slice_in_dim(conv_weight, model_pos * channels, channels, 1)
    share_start = (seq_pos * models + model_pos) * share
    share_pos = share_start + jnp.arange(share, dtype=jnp.int32)
    mask = (share_pos[None, :] < lengths[:, None]).astype(F32)[:, :, None]
    source = hidden.astype(F32)
    top_grad = cotangent.astype(F32) * mask
    normed, scale_mix = normalize(source, gain_mix)
    (
        normed_rows,
        _,
        in_full,
        out_full,
        gates,
        product,
        mixed,
        middle,
        middle_grad,
        mlp_part,
        _,
        pair_total,
        down_total,
    ) = forward(
        seqs,
        models,
        normed.astype(BF),
        hidden,
        gain_mlp[None],
        top_grad.astype(BF),
        local_taps,
        mixer_in,
        mixer_out,
        gate_up,
        mlp_down,
    )
    scale_mlp = lax.rsqrt(jnp.mean(middle * middle, axis=-1, keepdims=True) + EPS)
    middle_grad, gain_mlp_grad = norm_back(middle_grad, middle, scale_mlp, gain_mlp)
    middle_grad = middle_grad + top_grad
    mlp_share, source_grad, taps_part, in_got, out_got, pair_got, down_got = mixer_backward(
        seqs,
        models,
        middle_grad.astype(BF),
        mlp_part,
        local_taps,
        in_full,
        out_full,
        normed_rows,
        gates,
        product,
        mixed,
        pair_total,
        down_total,
    )
    output = (mask * (middle + mlp_share)).astype(BF)
    source_grad, gain_mix_grad = norm_back(source_grad, source, scale_mix, gain_mix)
    small = jnp.zeros((8, width), F32)
    small = lax.dynamic_update_slice(small, taps_part[:taps], (2, model_pos * channels))
    small = small.at[0].set(gain_mix_grad).at[1].set(gain_mlp_grad)
    small = small_sum(seqs, models, small)

    def total(got):
        return jnp.sum(got.astype(F32), axis=0)

    return (
        output,
        source_grad + middle_grad,
        small[0],
        small[1],
        small[2 : 2 + taps],
        total(in_got),
        total(out_got),
        total(pair_got),
        total(down_got),
    )


def solution(mesh):
    placed = (
        P(None, ("seq", "mp"), None),
        P(None, ("seq", "mp"), None),
        P(),
        P(),
        P(),
        P(),
        P(None, "seq", "mp"),
        P("mp", "seq"),
        P(None, "seq", "mp"),
        P("mp", "seq"),
    )
    return jax.shard_map(
        local,
        mesh=mesh,
        in_specs=placed,
        out_specs=(
            P(None, ("seq", "mp"), None),
            P(None, ("seq", "mp"), None),
            P(),
            P(),
            P(),
            P(None, "seq", "mp"),
            P("mp", "seq"),
            P(None, "seq", "mp"),
            P("mp", "seq"),
        ),
        check_vma=False,
    )
```

```python
import functools

import jax
import jax.numpy as jnp
from jax import lax
from jax.experimental import pallas as pl
from jax.experimental.pallas import tpu as pltpu
from jax.sharding import PartitionSpec as P

EPS = 1e-05
MESH = pl.DeviceIdType.MESH
BF = jnp.bfloat16
F32 = jnp.float32
HALVES = 2
VMEM_LIMIT = 63 * 2**20


def nn(a, b):
    return lax.dot_general(a, b, (((1,), (0,)), ((), ())), preferred_element_type=F32)


def nt(a, b):
    return lax.dot_general(a, b, (((1,), (1,)), ((), ())), preferred_element_type=F32)


def tn(a, b):
    return lax.dot_general(a, b, (((0,), (0,)), ((), ())), preferred_element_type=F32)


class Place:
    def __init__(self, seqs, models):
        self.seqs, self.chips = seqs, models // 2
        self.s = lax.axis_index("seq")
        self.m = lax.axis_index("mp")
        self.z = self.m // 2
        self.c = self.m % 2
        self.sibling = {"mp": self.m + 1 - 2 * self.c}
        self.above = {"mp": self.m + 2}
        self.below = {"mp": self.m - 2}
        self.has_above = self.z < self.chips - 1
        self.has_below = self.z > 0

    def peer(self, step):
        return {"seq": lax.rem(self.s + step, self.seqs)}

    def enter(self):
        barrier = pltpu.get_barrier_semaphore()
        models = 2 * self.chips
        peers = [{"mp": lax.rem(self.m + step, models)} for step in range(1, models)]
        for where in peers + [self.peer(step) for step in range(1, self.seqs)]:
            pl.semaphore_signal(barrier, inc=1, device_id=where, device_id_type=MESH)
        pl.semaphore_wait(barrier, models + self.seqs - 2)


def remote(src, dst, send, recv, where):
    return pltpu.make_async_remote_copy(
        src_ref=src, dst_ref=dst, send_sem=send, recv_sem=recv, device_id=where, device_id_type=MESH
    )


class Gather:
    def __init__(self, place, rows, own, sems):
        self.p, self.rows, self.own = place, rows, own
        self.share = rows.shape[0] // (2 * place.chips)
        self.piece = self.share // HALVES
        self.send, self.recv = sems

    def at(self, chip, core, half):
        return self.rows.at[pl.ds((chip * 2 + core) * self.share + half * self.piece, self.piece)]

    def copy(self, kind, chip, half, own=False):
        p = self.p
        where = (p.above, p.below, p.sibling)[kind]
        dst = self.at(chip, p.c, half)
        src = self.own.at[pl.ds(half * self.piece, self.piece)] if own and self.own is not None else dst
        return remote(src, dst, self.send.at[kind, chip, half], self.recv.at[kind // 2, chip, half], where)

    def start(self):
        p = self.p
        for half in range(HALVES):
            pl.when(p.has_above)(lambda h=half: self.copy(0, p.z, h, True).start())
            pl.when(p.has_below)(lambda h=half: self.copy(1, p.z, h, True).start())
        for half in range(HALVES):
            self.copy(2, p.z, half, True).start()

    def round(self, k):
        p = self.p
        for half in range(HALVES):

            @pl.when(p.z >= k)
            def _(half=half):
                chip = p.z - k
                self.copy(0, chip, half).wait_recv()
                pl.when(p.has_above)(lambda: self.copy(0, chip, half).start())
                self.copy(2, chip, half).start()

            @pl.when(p.z + k <= p.chips - 1)
            def _(half=half):
                chip = p.z + k
                self.copy(1, chip, half).wait_recv()
                pl.when(p.has_below)(lambda: self.copy(1, chip, half).start())
                self.copy(2, chip, half).start()

    def rounds(self):
        return [functools.partial(self.round, k) for k in range(1, self.p.chips)]

    def other_core(self, chip):
        p = self.p
        for half in range(HALVES):
            dst = self.at(chip, 1 - p.c, half)
            remote(dst, dst, self.send.at[2, chip, half], self.recv.at[1, chip, half], p.sibling).wait_recv()

    def arrived(self):
        for chip in range(self.p.chips):
            self.other_core(chip)

    def drain(self):
        p = self.p
        for chip in range(p.chips):
            for half in range(HALVES):
                pl.when(p.has_above & (chip <= p.z))(lambda ch=chip, h=half: self.copy(0, ch, h).wait_send())
                pl.when(p.has_below & (chip >= p.z))(lambda ch=chip, h=half: self.copy(1, ch, h).wait_send())
                self.copy(2, chip, half).wait_send()


class Scatter:
    def __init__(self, place, part, from_core, from_line, sems):
        self.p, self.part, self.from_core, self.from_line = place, part, from_core, from_line
        self.share = from_core.shape[1]
        self.piece = self.share // HALVES
        self.core_send, self.core_recv, self.line_send, self.line_recv = sems

    def rows(self, chip, core):
        return self.part.at[pl.ds((chip * 2 + core) * self.share, self.share)]

    def core_copy(self, chip):
        p = self.p
        return remote(
            self.rows(chip, 1 - p.c), self.from_core.at[chip], self.core_send.at[chip], self.core_recv.at[chip], p.sibling
        )

    def give(self, chip):
        self.core_copy(chip).start()

    def mine(self, chip, half):
        return self.part.at[pl.ds((chip * 2 + self.p.c) * self.share + half * self.piece, self.piece)]

    def line_copy(self, down, chip, slot, half):
        p = self.p
        dst = self.from_line.at[slot, pl.ds(half * self.piece, self.piece)]
        return remote(
            self.mine(chip, half),
            dst,
            self.line_send.at[down, chip, half],
            self.line_recv.at[slot, half],
            p.below if down else p.above,
        )

    def total(self, chip, half, slots):
        span = pl.ds(half * self.piece, self.piece)
        value = self.mine(chip, half)[...].astype(F32) + self.from_core[chip, span].astype(F32)
        for slot in slots:
            value = value + self.from_line[slot, span].astype(F32)
        return value

    def hop(self, down, chip, slot, has_source):
        self.core_copy(chip).wait_recv()
        for half in range(HALVES):

            @pl.when(has_source)
            def _(half=half):
                self.line_copy(down, chip, chip, half).wait_recv()
                self.mine(chip, half)[...] = self.total(chip, half, [chip]).astype(BF)

            @pl.when(jnp.logical_not(has_source))
            def _(half=half):
                self.mine(chip, half)[...] = self.total(chip, half, []).astype(BF)

            self.line_copy(down, chip, slot, half).start()

    def round(self, r):
        p = self.p
        last = p.chips - 1

        @pl.when((p.z <= r) & p.has_above)
        def _():
            chip = last - r + p.z
            self.hop(0, chip, chip, p.has_below)

        @pl.when((last - p.z <= r) & p.has_below)
        def _():
            chip = r - last + p.z
            self.hop(1, chip, p.chips if r == last - 1 else chip, p.has_above)

    def rounds(self):
        return [functools.partial(self.round, r) for r in range(self.p.chips - 1)]

    def finish(self, store):
        p = self.p
        self.core_copy(p.z).wait_recv()
        for half in range(HALVES):
            pl.when(p.has_below)(lambda h=half: self.line_copy(0, p.z, p.z, h).wait_recv())
            pl.when(p.has_above)(lambda h=half: self.line_copy(1, p.z, p.chips, h).wait_recv())
            for up in (False, True):
                for low in (False, True):

                    @pl.when((p.has_above == up) & (p.has_below == low))
                    def _(half=half, up=up, low=low):
                        slots = ([p.z] if low else []) + ([p.chips] if up else [])
                        store(half * self.piece, self.piece, self.total(p.z, half, slots))

    def drain(self):
        p = self.p
        for chip in range(p.chips):
            self.core_copy(chip).wait_send()
            for half in range(HALVES):
                pl.when(p.has_above & (chip > p.z))(lambda ch=chip, h=half: self.line_copy(0, ch, ch, h).wait_send())
                pl.when(p.has_below & (chip < p.z))(lambda ch=chip, h=half: self.line_copy(1, ch, ch, h).wait_send())


class StraightScatter(Scatter):
    def straight(self, chip, half):
        p = self.p
        return remote(
            self.mine(chip, half),
            self.from_line.at[p.z, pl.ds(half * self.piece, self.piece)],
            self.line_send.at[0, chip, half],
            self.line_recv.at[p.z, half],
            {"mp": chip * 2 + p.c},
        )

    def came(self, chip, half):
        view = self.from_line.at[chip, pl.ds(half * self.piece, self.piece)]
        return remote(view, view, self.line_send.at[0, chip, half], self.line_recv.at[chip, half], self.p.sibling)

    def go(self, chip):
        self.core_copy(chip).wait_recv()
        for half in range(HALVES):
            self.mine(chip, half)[...] = self.total(chip, half, []).astype(BF)
            self.straight(chip, half).start()

    def others(self):
        return [lax.rem(self.p.z + step, self.p.chips) for step in range(1, self.p.chips)]

    def finish(self, store):
        self.core_copy(self.p.z).wait_recv()
        for half in range(HALVES):
            for chip in self.others():
                self.came(chip, half).wait_recv()
            store(half * self.piece, self.piece, self.total(self.p.z, half, self.others()))

    def drain(self):
        for chip in range(self.p.chips):
            self.core_copy(chip).wait_send()
        for chip in self.others():
            for half in range(HALVES):
                self.straight(chip, half).wait_send()


def gather_sems(count, chips):
    return [pltpu.SemaphoreType.DMA((count, 3, chips, HALVES)), pltpu.SemaphoreType.DMA((count, 2, chips, HALVES))]


def scatter_sems(count, chips):
    return [
        pltpu.SemaphoreType.DMA((count, chips)),
        pltpu.SemaphoreType.DMA((count, chips)),
        pltpu.SemaphoreType.DMA((count, 2, chips, HALVES)),
        pltpu.SemaphoreType.DMA((count, chips + 1, HALVES)),
    ]


def picks(sems, index):
    return [sem.at[index] for sem in sems]


def far_first(place):
    low, high = 0, place.chips - 1
    order = []
    for _ in range(place.chips):
        left = place.z - low >= high - place.z
        order.append(jnp.where(left, low, high))
        low, high = jnp.where(left, low + 1, low), jnp.where(left, high, high - 1)
    return order


def weave(*lists):
    for step in range(max(len(steps) for steps in lists)):
        for steps in lists:
            if step < len(steps):
                steps[step]()


class Relay:
    def __init__(self, place, shard, full, first, size, sems):
        self.p, self.shard, self.full, self.first, self.size = place, shard, full, first, size
        self.send, self.recv, self.local = sems
        s = place.s
        self.square = place.seqs == 4
        if self.square:
            self.near = (s + 1 - 2 * lax.rem(s, 2), lax.rem(s + 2, 4))

    def half(self, index):
        return self.first + index * (self.size // 2), self.size // 2

    def direct(self, index, where):
        return remote(
            self.shard(self.first, self.size),
            self.full(self.p.s, self.first, self.size),
            self.send.at[index],
            self.recv.at[index],
            where,
        )

    def handed(self, index):
        view = self.full(self.near[index], *self.half(index))
        return remote(view, view, self.send.at[2 + index], self.recv.at[2 + index], {"seq": self.near[1 - index]})

    def local_copy(self):
        return pltpu.make_async_copy(
            self.shard(self.first, self.size), self.full(self.p.s, self.first, self.size), self.local
        )

    def copies(self):
        if self.square:
            return [self.direct(index, {"seq": self.near[index]}) for index in range(2)]
        return [self.direct(step - 1, self.p.peer(step)) for step in range(1, self.p.seqs)]

    def start(self):
        for thing in self.copies():
            thing.start()
        self.local_copy().start()

    def forward(self):
        if self.square:
            for thing in self.copies():
                thing.wait_recv()
            for index in range(2):
                self.handed(index).start()

    def arrived(self):
        self.local_copy().wait()
        for thing in [self.handed(index) for index in range(2)] if self.square else self.copies():
            thing.wait_recv()

    def drain(self):
        for thing in self.copies() + ([self.handed(index) for index in range(2)] if self.square else []):
            thing.wait_send()


def forward_kernel(
    seqs,
    models,
    source_ref,
    gain_mix_ref,
    gain_ref,
    top_ref,
    taps_ref,
    in_ref,
    out_ref,
    pair_ref,
    down_ref,
    normed_rows,
    top_rows,
    in_rows,
    out_rows,
    gates_out,
    product_out,
    mixed_out,
    middle_out,
    grad_out,
    low_out,
    gain_out,
    mlp_part,
    act_rows,
    pair_grad,
    down_grad,
    in_full,
    out_full,
    rows,
    gates,
    ends,
    product,
    mixed,
    pair,
    down,
    top_tile,
    acts,
    act_stage,
    stage,
    part,
    from_core,
    from_line,
    total,
    w_send,
    w_recv,
    w_local,
    halo_send,
    halo_recv,
    keep,
    tile_sem,
    out_sem,
    cols_sem,
    pair_sem,
    ends_sem,
    *sems,
):
    p = Place(seqs, models)
    chips = p.chips
    g_sems, s_sems = sems[:2], sems[2:]
    slots, block, width = rows.shape
    units = down.shape[0]
    tile = block // chips
    share = tile // 2
    channels = in_full.shape[2]
    shard = width // seqs
    unit_block = min(512, units)
    wide_block = 512
    gain_out[...] = jnp.zeros_like(gain_out)

    def first_norm(slot):
        for first in range(0, share, share // HALVES):
            value = source_ref[slot, pl.ds(first, share // HALVES)].astype(F32)
            scale = lax.rsqrt(jnp.mean(value * value, axis=-1, keepdims=True) + EPS)
            rows[slot, pl.ds(p.m * share + first, share // HALVES)] = (value * scale * gain_mix_ref[...]).astype(BF)

    for slot in range(slots):
        first_norm(slot)
    p.enter()

    firsts = [Gather(p, rows.at[slot], None, picks(g_sems, slot)) for slot in range(slots)]
    tops = [Gather(p, top_rows.at[slot], top_ref.at[slot], picks(g_sems, slots + slot)) for slot in range(slots)]
    seconds = [Gather(p, rows.at[slot], None, picks(g_sems, 2 * slots + slot)) for slot in range(slots)]

    def scatter(slot, index, kind=Scatter):
        return kind(p, part.at[slot], from_core.at[slot], from_line.at[slot], picks(s_sems, index))

    mix_sums = [scatter(slot, slot) for slot in range(slots)]
    grad_sums = [scatter(0, slots), scatter(1, slots + 1, StraightScatter)]

    def columns_of(owner):
        return pl.ds(pl.multiple_of(owner * shard, shard), shard)

    def pair_views(k):
        return (
            lambda first, size: pair_ref.at[k, pl.ds(first, size)],
            lambda owner, first, size: pair.at[k, pl.ds(owner * shard + first, size)],
        )

    views = [
        (
            lambda first, size: in_ref.at[:, pl.ds(first, size)],
            lambda owner, first, size: in_full.at[:, pl.ds(owner * shard + first, size)],
            0,
            shard,
        ),
        (
            lambda first, size: out_ref.at[pl.ds(first, size)],
            lambda owner, first, size: out_full.at[pl.ds(first, size), columns_of(owner)],
            0,
            channels,
        ),
    ]
    for i in range(2):
        views.append(
            (
                lambda first, size: down_ref.at[pl.ds(first, size)],
                lambda owner, first, size: down.at[pl.ds(first, size), columns_of(owner)],
                i * (units // 2),
                units // 2,
            )
        )
    for i in range(4):
        views.append((*pair_views(i // 2), (i % 2) * (shard // 2), shard // 2))
    pieces = [Relay(p, *view, (w_send.at[i], w_recv.at[i], w_local.at[i])) for i, view in enumerate(views)]
    early, late = pieces[:2], pieces[2:]
    moves = [[("start", 0), ("start", 1)], [("forward", 0), ("start", 2)], [("forward", 1), ("start", 3)]]
    moves += [[("forward", 2)], [("forward", 3)], [("start", 4), ("start", 5)], [("forward", 4)], [("forward", 5)]]

    def push():
        for name, index in moves.pop(0):
            getattr(late[index], name)()

    def own(slot):
        span = pl.ds(p.m * share, share)
        return pltpu.make_async_copy(top_ref.at[slot], top_rows.at[slot, span], keep.at[slot])

    for slot in range(slots):
        own(slot).start()

    def saved(index, src, dst):
        return pltpu.make_async_copy(src, dst, keep.at[2 * slots + index])

    rows_saved = [saved(slot, rows.at[slot], normed_rows.at[slot]) for slot in range(slots)]
    gates_saved = [saved(slots + slot, gates, gates_out.at[slot, 1]) for slot in range(slots)]
    middle_saved = [saved(2 * slots + slot, total.at[slot], middle_out.at[slot]) for slot in range(slots)]
    grad_saved = [saved(3 * slots + slot, total.at[slot], grad_out.at[slot]) for slot in range(slots)]
    low_saved = [
        saved(4 * slots + 6 + slot, stage.at[pl.ds(slot * share, share)], low_out.at[slot]) for slot in range(slots)
    ]
    own_tops = [
        saved(5 * slots + 6 + slot, top_ref.at[slot], top_tile.at[pl.ds(slot * share, share)]) for slot in range(slots)
    ]
    in_saved = saved(4 * slots, in_full, in_rows)
    out_saved = saved(4 * slots + 1, out_full, out_rows)
    product_saved = saved(4 * slots + 2, product, product_out)
    mixed_saved = [saved(6 * slots + 6 + slot, mixed, mixed_out.at[slot]) for slot in range(slots)]
    down_saved = saved(4 * slots + 4, down, down_grad)
    act_load = saved(4 * slots + 5, act_rows, acts.at[0])

    def halo(slot):
        return remote(
            product.at[slot, pl.ds(block, 8)],
            product.at[slot, pl.ds(0, 8)],
            halo_send.at[slot],
            halo_recv.at[slot],
            p.peer(1),
        )

    has_later, has_earlier = p.s < seqs - 1, p.s > 0
    for slot in range(slots):

        @pl.when(jnp.logical_not(has_earlier))
        def _(slot=slot):
            product[slot, pl.ds(0, 8)] = jnp.zeros((8, channels), F32)

    def ends_saved(slot, i):
        span = pl.ds(i * tile, tile)
        return [
            pltpu.make_async_copy(ends.at[j], gates_out.at[slot, 2 * j, span], ends_sem.at[j]) for j in range(2)
        ]

    def project(slot):
        @pl.loop(0, chips)
        def _(i):
            span = pl.ds(i * tile, tile)
            source = rows[slot, span]
            b_gate = nn(source, in_full[0])
            x_value = nn(source, in_full[2])
            gates[span] = nn(source, in_full[1])

            @pl.when(i > 0)
            def _():
                for thing in ends_saved(slot, i - 1):
                    thing.wait()

            ends[0] = b_gate
            ends[1] = x_value
            for thing in ends_saved(slot, i):
                thing.start()
            product[slot, pl.ds(8 + i * tile, tile)] = b_gate * x_value

        for thing in ends_saved(slot, chips - 1):
            thing.wait()
        pl.when(has_later)(lambda: halo(slot).start())

    def convolve(slot):
        pl.when(has_earlier)(lambda: halo(slot).wait_recv())
        for i in range(chips):
            conv = 0.0
            for offset in range(taps_ref.shape[0]):
                conv = conv + taps_ref[offset : offset + 1] * product[slot, pl.ds(8 + i * tile - offset, tile)]
            mixed[pl.ds(i * tile, tile)] = (gates[pl.ds(i * tile, tile)] * conv).astype(BF)

    def project_out(slot):
        for chip in far_first(p):
            span = pl.ds(chip * tile, tile)
            part[slot, span] = nn(mixed[span], out_full[...]).astype(BF)
            mix_sums[slot].give(chip)
        mixed_saved[slot].start()

    def middle(slot):
        def store(first, size, value):
            span = pl.ds(first, size)
            value = value + source_ref[slot, span].astype(F32)
            total[slot, span] = value
            scale = lax.rsqrt(jnp.mean(value * value, axis=-1, keepdims=True) + EPS)
            rows[slot, pl.ds(p.m * share + first, size)] = (value * scale * gain_ref[...]).astype(BF)

        mix_sums[slot].finish(store)
        middle_saved[slot].start()
        mix_sums[slot].drain()

    def finish_grad(slot):
        middle_saved[slot].wait()

        def store(first, size, value):
            span = pl.ds(first, size)
            at = pl.ds(slot * share + first, size)
            middle = total[slot, span]
            scale = lax.rsqrt(jnp.mean(middle * middle, axis=-1, keepdims=True) + EPS)
            unit = middle * scale
            gain_out[0:1] += jnp.sum(value * unit, axis=0, keepdims=True)
            scaled = value * gain_ref[...]
            grad = scale * (scaled - unit * jnp.mean(scaled * unit, axis=-1, keepdims=True))
            grad = grad + top_tile[at].astype(F32)
            total[slot, span] = grad
            stage[at] = grad.astype(BF)

        grad_sums[slot].finish(store)
        grad_saved[slot].start()
        low_saved[slot].start()

    order = far_first(p)
    tiles = [(0, chip) for chip in order] + [(slot, chip) for slot in range(1, slots) for chip in order[::-1]]

    def fetch(index):
        slot, chip = tiles[index]
        return pltpu.make_async_copy(top_rows.at[slot, pl.ds(chip * tile, tile)], top_tile, tile_sem)

    def puts(index):
        slot, chip = tiles[index]
        span = pl.ds(chip * tile, tile)
        return [
            pltpu.make_async_copy(stage, mlp_part.at[slot, span], out_sem.at[0]),
            pltpu.make_async_copy(act_stage, act_rows.at[slot, span], out_sem.at[1]),
        ]

    def work(index):
        slot, chip = tiles[index]
        span = pl.ds(chip * tile, tile)
        if index == 0 or slot > 0:
            fetch(index).start()
        fetch(index).wait()
        if index:
            for thing in puts(index - 1):
                thing.wait()

        @pl.loop(0, units // unit_block)
        def _(i):
            cut = pl.ds(pl.multiple_of(i * unit_block, unit_block), unit_block)
            source = rows[slot, span]
            gate = nn(source, pair[0, :, cut])
            up = nn(source, pair[1, :, cut])
            act_grad = nt(top_tile[...], down[cut])
            sigma = jax.nn.sigmoid(gate)
            silu = gate * sigma
            act_stage[:, cut] = (silu * up).astype(BF)
            acts[0, slot, span, cut] = (act_grad * up * sigma * (1.0 + gate * (1.0 - sigma))).astype(BF)
            acts[1, slot, span, cut] = (act_grad * silu).astype(BF)

        if index + 1 < len(tiles) and tiles[index + 1][0] == 0:
            fetch(index + 1).start()

        @pl.loop(0, width // wide_block)
        def _(i):
            cut = pl.ds(pl.multiple_of(i * wide_block, wide_block), wide_block)
            value = nt(acts[0, slot, span], pair[0, cut]) + nt(acts[1, slot, span], pair[1, cut])
            part[slot, span, cut] = value.astype(BF)
            stage[:, cut] = nn(act_stage[...], down[:, cut]).astype(BF)

        grad_sums[slot].give(chip)
        for thing in puts(index):
            thing.start()

    pair_block = 512
    pair_steps = 2 * (width // pair_block)

    def pair_saved(index):
        k, first = divmod(index, width // pair_block)
        cut = pl.ds(first * pair_block, pair_block)
        return pltpu.make_async_copy(pair.at[k, cut], pair_grad.at[k, cut], pair_sem.at[index])

    def pair_step(index):
        k, first = divmod(index, width // pair_block)
        cut = pl.ds(first * pair_block, pair_block)
        value = 0.0
        for slot in range(slots):
            value = value + tn(rows[slot, :, cut], acts[k, slot])
        pair[k, cut] = value.astype(BF)
        pair_saved(index).start()
        if first == width // pair_block - 1 and k == 0:
            act_load.start()

    def fetch_columns(index):
        cut = pl.ds(index * channels, channels)
        return [
            pltpu.make_async_copy(
                top_rows.at[slot, :, cut], in_full.at[index % 2, pl.ds(slot * block, block)], cols_sem.at[index % 2, slot]
            )
            for slot in range(slots)
        ]

    def down_step(index):
        if index == 0:
            act_load.wait()
        for thing in fetch_columns(index):
            thing.wait()
        for first in range(0, units, unit_block):
            cut = pl.ds(first, unit_block)
            value = 0.0
            for slot in range(slots):
                value = value + tn(acts[0, slot, :, cut], in_full[index % 2, pl.ds(slot * block, block)])
            down[cut, pl.ds(index * channels, channels)] = value.astype(BF)
        if index + 2 < width // channels:
            for thing in fetch_columns(index + 2):
                thing.start()

    firsts[0].start()
    for piece in early:
        piece.start()
    steps = firsts[0].rounds()
    for step in steps[:-1]:
        step()
    for piece in early:
        piece.forward()
    firsts[1].start()
    steps[-1]()
    firsts[0].arrived()
    rows_saved[0].start()
    for piece in early:
        piece.arrived()
    in_saved.start()
    out_saved.start()
    project(0)
    gates_saved[0].start()
    push()
    steps = firsts[1].rounds()
    steps[0]()
    push()
    rows_saved[0].wait()
    firsts[0].drain()
    convolve(0)
    project_out(0)
    weave(mix_sums[0].rounds(), steps[1:-1] + [tops[0].start, steps[-1]], [push] * 3)
    firsts[1].arrived()
    rows_saved[1].start()
    gates_saved[0].wait()
    project(1)
    gates_saved[1].start()
    push()
    middle(0)
    seconds[0].start()
    rows_saved[1].wait()
    firsts[1].drain()
    mixed_saved[0].wait()
    convolve(1)
    project_out(1)
    hops, steps, more = mix_sums[1].rounds(), tops[0].rounds(), seconds[0].rounds()
    weave(steps, hops, [push] * 2)
    weave(more[:-1])
    tops[1].start()
    more[-1]()
    middle(1)
    seconds[1].start()
    product_saved.start()
    own(0).wait()
    tops[0].arrived()
    seconds[0].arrived()
    for piece in late:
        piece.arrived()
    own(1).wait()
    hops, steps, more = grad_sums[0].rounds(), tops[1].rounds(), seconds[1].rounds()
    for index in range(chips):
        work(index)
        if index < len(steps):
            steps[index]()
        if 0 < index:
            hops[index - 1]()
    for index in range(chips):
        if index:
            more[index - 1]()
        else:
            tops[1].arrived()
        seconds[1].other_core(tiles[chips + index][1])
        work(chips + index)
        if index > 1:
            grad_sums[1].go(tiles[chips + index - 1][1])
    for thing in puts(len(tiles) - 1):
        thing.wait()
    for thing in own_tops:
        thing.start()
    grad_sums[1].go(tiles[-1][1])
    in_saved.wait()
    for piece in pieces:
        piece.drain()
    for index in range(2):
        for thing in fetch_columns(index):
            thing.start()
    for thing in own_tops:
        thing.wait()
    finish_grad(0)
    work_steps = [functools.partial(pair_step, index) for index in range(pair_steps)]
    work_steps += [functools.partial(down_step, index) for index in range(width // channels)]
    for step in work_steps:
        step()
    down_saved.start()
    finish_grad(1)
    for index in range(pair_steps):
        pair_saved(index).wait()
    for thing in [gates_saved[1], out_saved, product_saved, mixed_saved[1], down_saved, *grad_saved, *low_saved]:
        thing.wait()
    for thing in tops + seconds + grad_sums:
        thing.drain()
    for slot in range(slots):
        pl.when(has_later)(lambda slot=slot: halo(slot).wait_send())


def forward(seqs, models, source, gain_mix, gain, top, taps, mixer_in, mixer_out, gate_up, mlp_down):
    slots, share, width = source.shape
    chips = models // 2
    block = share * models
    channels = mixer_in.shape[2]
    units = gate_up.shape[2]
    tile = block // chips
    hbm = pl.BlockSpec(memory_space=pltpu.HBM)
    vmem = pl.BlockSpec(memory_space=pltpu.VMEM)
    shape = jax.ShapeDtypeStruct
    return pl.pallas_call(
        functools.partial(forward_kernel, seqs, models),
        out_shape=[
            shape((slots, block, width), BF),
            shape((slots, block, width), BF),
            shape((3, width, channels), BF),
            shape((channels, width), BF),
            shape((slots, 3, block, channels), F32),
            shape((slots, block + 8, channels), F32),
            shape((slots, block, channels), BF),
            shape((slots, share, width), F32),
            shape((slots, share, width), F32),
            shape((slots, share, width), BF),
            shape((8, width), F32),
            shape((slots, block, width), BF),
            shape((slots, block, units), BF),
            shape((2, width, units), BF),
            shape((units, width), BF),
        ],
        in_specs=[vmem, vmem, vmem, hbm, vmem] + [hbm] * 4,
        out_specs=[hbm] * 10 + [vmem] + [hbm] * 4,
        scratch_shapes=[
            pltpu.VMEM((3, width, channels), BF),
            pltpu.VMEM((channels, width), BF),
            pltpu.VMEM((slots, block, width), BF),
            pltpu.VMEM((block, channels), F32),
            pltpu.VMEM((2, tile, channels), F32),
            pltpu.VMEM((slots, block + 8, channels), F32),
            pltpu.VMEM((block, channels), BF),
            pltpu.VMEM((2, width, units), BF),
            pltpu.VMEM((units, width), BF),
            pltpu.VMEM((tile, width), BF),
            pltpu.VMEM((2, slots, block, units), BF),
            pltpu.VMEM((tile, units), BF),
            pltpu.VMEM((tile, width), BF),
            pltpu.VMEM((slots, block, width), BF),
            pltpu.VMEM((slots, chips, share, width), BF),
            pltpu.VMEM((slots, chips + 1, share, width), BF),
            pltpu.VMEM((slots, share, width), F32),
            pltpu.SemaphoreType.DMA((8, max(4, seqs - 1))),
            pltpu.SemaphoreType.DMA((8, max(4, seqs - 1))),
            pltpu.SemaphoreType.DMA((8,)),
            pltpu.SemaphoreType.DMA((slots,)),
            pltpu.SemaphoreType.DMA((slots,)),
            pltpu.SemaphoreType.DMA((10 * slots + 6,)),
            pltpu.SemaphoreType.DMA,
            pltpu.SemaphoreType.DMA((2,)),
            pltpu.SemaphoreType.DMA((2, slots)),
            pltpu.SemaphoreType.DMA((2 * (width // 512),)),
            pltpu.SemaphoreType.DMA((2,)),
            *gather_sems(3 * slots, chips),
            *scatter_sems(2 * slots, chips),
        ],
        compiler_params=pltpu.CompilerParams(collective_id=1, has_side_effects=True, vmem_limit_bytes=VMEM_LIMIT),
    )(source, gain_mix, gain, top, taps, mixer_in, mixer_out, gate_up, mlp_down)


class Exchange:
    def __init__(self, place, partial, got, first, size, sems, held, came):
        self.p, self.partial, self.got, self.first, self.size = place, partial, got, first, size
        self.send, self.recv, self.local = sems
        self.held, self.came = held, came
        s = place.s
        self.square = place.seqs == 4
        if self.square:
            self.near = (s + 1 - 2 * lax.rem(s, 2), lax.rem(s + 2, 4))
            self.across = 3 - s

    def half(self, index):
        return self.first + index * (self.size // 2), self.size // 2

    def to(self, index):
        return {"seq": self.near[index]}

    def relayed(self, index):
        return remote(
            self.partial(self.across, *self.half(index)),
            self.came.at[index],
            self.send.at[index],
            self.recv.at[index],
            self.to(index),
        )

    def plain(self, index):
        span = self.half(index)
        return remote(
            self.partial(self.near[index], *span),
            self.got(1 + index, *span),
            self.send.at[2 + index],
            self.recv.at[2 + index],
            self.to(index),
        )

    def added(self, index):
        return remote(
            self.held.at[1 - index],
            self.got(1 + index, *self.half(1 - index)),
            self.send.at[4 + index],
            self.recv.at[4 + index],
            self.to(index),
        )

    def load(self, index):
        return pltpu.make_async_copy(
            self.partial(self.near[index], *self.half(1 - index)), self.held.at[1 - index], self.local.at[1 + index]
        )

    def straight(self, step):
        p = self.p
        return remote(
            self.partial(lax.rem(p.s + step, p.seqs), self.first, self.size),
            self.got(step, self.first, self.size),
            self.send.at[step - 1],
            self.recv.at[step - 1],
            p.peer(step),
        )

    def own(self):
        return pltpu.make_async_copy(
            self.partial(self.p.s, self.first, self.size), self.got(0, self.first, self.size), self.local.at[0]
        )

    def copies(self):
        if self.square:
            return [self.relayed(0), self.relayed(1), self.plain(0), self.plain(1)]
        return [self.straight(step) for step in range(1, self.p.seqs)]

    def start(self):
        for thing in self.copies():
            thing.start()
        if self.square:
            for index in range(2):
                self.load(index).start()
        self.own().start()

    def forward(self):
        if self.square:
            for index in range(2):
                self.load(index).wait()
                self.relayed(1 - index).wait_recv()
                total = self.held[1 - index].astype(F32) + self.came[1 - index].astype(F32)
                self.held[1 - index] = total.astype(BF)
                self.added(index).start()

    def finish(self):
        self.own().wait()
        if self.square:
            for thing in self.copies():
                thing.wait_send()
            for index in range(2):
                self.plain(index).wait_recv()
                self.added(index).wait()
        else:
            for thing in self.copies():
                thing.wait()


def mixer_backward_kernel(
    seqs,
    models,
    low_ref,
    mlp_part,
    source_ref,
    gain_ref,
    gain_mlp_ref,
    taps_ref,
    in_ref,
    out_ref,
    normed_rows,
    gates_ref,
    product_ref,
    mixed_ref,
    pair_grad,
    down_grad,
    mlp_out,
    grad_out,
    small_out,
    in_got,
    out_got,
    pair_got,
    down_got,
    in_full,
    out_full,
    rows,
    columns,
    gates,
    product,
    mixed,
    conv_grad,
    stacked,
    part,
    from_core,
    from_line,
    mlp_total,
    grad_total,
    down_room,
    pair_room,
    in_room,
    out_room,
    taps_out,
    small,
    by_model,
    by_seq,
    load,
    cols_sem,
    w_send,
    w_recv,
    w_local,
    halo_send,
    halo_recv,
    free,
    mp_send,
    mp_recv,
    seq_send,
    seq_recv,
    *sems,
):
    p = Place(seqs, models)
    chips = p.chips
    g_sems, s_sems = sems[:2], sems[2:]
    slots, block, width = rows.shape
    channels = out_full.shape[0]
    taps = taps_ref.shape[0]
    tile = block // chips
    share = tile // 2
    wide_block = 512
    cols = columns.shape[-1]
    loads = [
        pltpu.make_async_copy(src, dst, load.at[i])
        for i, (src, dst) in enumerate(
            [(mlp_part.at[slot], part.at[slot]) for slot in range(slots)]
            + [
                (low_ref.at[slot], rows.at[slot, pl.ds(p.m * share, share)])
                for slot in range(slots)
            ]
            + [
                (in_ref, in_full),
                (out_ref, out_full),
                (gates_ref, gates),
                (product_ref, product),
                (mixed_ref, mixed),
            ]
        )
    ]
    for thing in loads:
        thing.start()
    p.enter()
    gathers = [Gather(p, rows.at[slot], low_ref.at[slot], picks(g_sems, slot)) for slot in range(slots)]

    def scatter(slot, index):
        return Scatter(p, part.at[slot], from_core.at[slot], from_line.at[slot], picks(s_sems, index))

    mlp_sums = [scatter(slot, slot) for slot in range(slots)]
    sums = [scatter(slot, slots + slot) for slot in range(slots)]
    shard = width // seqs
    units = down_grad.shape[0]

    def columns_of(owner):
        return pl.ds(pl.multiple_of(owner * shard, shard), shard)

    views = []
    for i in range(2):
        views.append(
            (
                lambda owner, first, size: down_grad.at[pl.ds(first, size), columns_of(owner)],
                lambda index, first, size: down_got.at[index, pl.ds(first, size)],
                i * (units // 2),
                units // 2,
                down_room.at[i],
            )
        )
    for i in range(4):
        views.append(
            (
                lambda owner, first, size, k=i // 2: pair_grad.at[k, pl.ds(owner * shard + first, size)],
                lambda index, first, size, k=i // 2: pair_got.at[index, k, pl.ds(first, size)],
                (i % 2) * (shard // 2),
                shard // 2,
                pair_room.at[i],
            )
        )
    views.append(
        (
            lambda owner, first, size: in_full.at[:, pl.ds(owner * shard + first, size)],
            lambda index, first, size: in_got.at[index, :, pl.ds(first, size)],
            0,
            shard,
            in_room,
        )
    )
    views.append(
        (
            lambda owner, first, size: out_full.at[pl.ds(first, size), columns_of(owner)],
            lambda index, first, size: out_got.at[index, pl.ds(first, size)],
            0,
            channels,
            out_room,
        )
    )
    pieces = [
        Exchange(p, *view[:4], (w_send.at[i], w_recv.at[i], w_local.at[i]), view[4].at[0], view[4].at[1])
        for i, view in enumerate(views)
    ]
    moves = [[("start", 0), ("start", 1)], [("forward", 0), ("start", 2)], [("forward", 1), ("start", 3)]]
    moves += [[("forward", 2)], [("forward", 3)], [("start", 4), ("start", 5)], [("forward", 4)], [("forward", 5)]]

    def push():
        for name, index in moves.pop(0):
            getattr(pieces[index], name)()

    has_later, has_earlier = p.s < seqs - 1, p.s > 0
    order = far_first(p)

    def halo(slot):
        return remote(
            conv_grad.at[slot, pl.ds(0, 8)],
            conv_grad.at[slot, pl.ds(block, 8)],
            halo_send.at[slot],
            halo_recv.at[slot],
            p.peer(seqs - 1),
        )

    for slot in range(slots):

        @pl.when(jnp.logical_not(has_later))
        def _(slot=slot):
            conv_grad[slot, pl.ds(block, 8)] = jnp.zeros((8, channels), F32)

    taps_out[...] = jnp.zeros_like(taps_out)
    small[...] = jnp.zeros_like(small)
    small[1:2] = gain_mlp_ref[0:1]

    def first_pass(slot):
        for i in range(chips):
            span = pl.ds(i * tile, tile)
            mixed_grad = nt(rows[slot, span], out_full[...])
            grad = mixed_grad * gates[slot, 1, span]
            conv_grad[slot, span] = grad
            conv = 0.0
            for offset in range(taps):
                earlier = product[slot, pl.ds(8 + i * tile - offset, tile)]
                conv = conv + taps_ref[offset : offset + 1] * earlier
                taps_out[offset : offset + 1] += jnp.sum(grad * earlier, axis=0, keepdims=True)
            stacked[slot, span, pl.ds(channels, channels)] = (mixed_grad * conv).astype(BF)
            if i == 0:
                pl.when(has_earlier)(lambda: halo(slot).start())

    def second_pass(slot):
        pl.when(has_later)(lambda: halo(slot).wait_recv())
        for i in range(chips):
            span = pl.ds(i * tile, tile)
            grad = 0.0
            for offset in range(taps):
                grad = grad + taps_ref[offset : offset + 1] * conv_grad[slot, pl.ds(i * tile + offset, tile)]
            stacked[slot, span, pl.ds(0, channels)] = (grad * gates[slot, 2, span]).astype(BF)
            stacked[slot, span, pl.ds(2 * channels, channels)] = (grad * gates[slot, 0, span]).astype(BF)

    def third_pass(slot):
        for chip in order:
            span = pl.ds(chip * tile, tile)

            @pl.loop(0, width // wide_block)
            def _(i):
                cut = pl.ds(pl.multiple_of(i * wide_block, wide_block), wide_block)
                value = 0.0
                for k in range(3):
                    value = value + nt(stacked[slot, span, pl.ds(k * channels, channels)], in_full[k, cut])
                part[slot, span, cut] = value.astype(BF)

            sums[slot].give(chip)

    def finish_mlp(slot):
        def store(first, size, value):
            mlp_total[slot, pl.ds(first, size)] = value

        mlp_sums[slot].finish(store)

    def finish_grad(slot):
        def store(first, size, value):
            span = pl.ds(first, size)
            source = source_ref[slot, span].astype(F32)
            scale = lax.rsqrt(jnp.mean(source * source, axis=-1, keepdims=True) + EPS)
            unit = source * scale
            small[0:1] += jnp.sum(value * unit, axis=0, keepdims=True)
            scaled = value * gain_ref[...]
            grad_total[slot, span] = scale * (scaled - unit * jnp.mean(scaled * unit, axis=-1, keepdims=True))

        sums[slot].finish(store)

    def mine(owner):
        return pl.ds(pl.multiple_of(owner * channels, channels), channels)

    def small_sums():
        small[2 : 2 + taps, mine(p.m)] = taps_out[0:taps]
        along = [lax.rem(p.m + step, models) for step in range(1, models)]
        by_model[p.m] = small[:, mine(p.m)]
        copies = [
            remote(small.at[:, mine(peer)], by_model.at[p.m], mp_send.at[0, i], mp_recv.at[0, i], {"mp": peer})
            for i, peer in enumerate(along)
        ]
        for thing in copies:
            thing.start()
        for thing in copies:
            thing.wait()
        by_seq[p.s] = functools.reduce(lambda a, b: a + b, [by_model[i] for i in range(models)])
        copies = [
            remote(by_seq.at[p.s], by_seq.at[p.s], seq_send.at[step - 1], seq_recv.at[step - 1], p.peer(step))
            for step in range(1, seqs)
        ]
        for thing in copies:
            thing.start()
        for thing in copies:
            thing.wait()
        small_out[:, mine(p.m)] = functools.reduce(lambda a, b: a + b, [by_seq[i] for i in range(seqs)])
        copies = [
            remote(small_out.at[:, mine(p.m)], small_out.at[:, mine(p.m)], mp_send.at[1, i], mp_recv.at[1, i], {"mp": peer})
            for i, peer in enumerate(along)
        ]
        for thing in copies:
            thing.start()
        for thing in copies:
            thing.wait()

    def neighbours(act):
        act(p.sibling)
        pl.when(p.has_above)(lambda: act(p.above))
        pl.when(p.has_below)(lambda: act(p.below))

    def give_free(slot):
        mlp_sums[slot].drain()
        neighbours(
            lambda where: pl.semaphore_signal(free.at[slot], inc=1, device_id=where, device_id_type=MESH)
        )

    def take_free(slot):
        lines = (p.z + chips - 1) // chips + (2 * chips - 2 - p.z) // chips
        pl.semaphore_wait(free.at[slot], 1 + lines)

    def fetch_columns(index):
        return pltpu.make_async_copy(
            normed_rows.at[:, :, pl.ds(index * cols, cols)], columns.at[index % 2], cols_sem.at[index % 2]
        )

    steps_in = width // cols

    def in_step(index):
        fetch_columns(index).wait()
        value = 0.0
        for slot in range(slots):
            value = value + tn(columns[index % 2, slot], stacked[slot])
        for k in range(3):
            in_full[k, pl.ds(index * cols, cols)] = value[:, k * channels : (k + 1) * channels].astype(BF)
        if index + 2 < steps_in:
            fetch_columns(index + 2).start()

    def out_step():
        for first in range(0, width, wide_block):
            cut = pl.ds(first, wide_block)
            value = 0.0
            for slot in range(slots):
                value = value + tn(mixed[slot], rows[slot, :, cut])
            out_full[:, cut] = value.astype(BF)

    gathers[0].start()
    push()
    loads[0].wait()
    for chip in order:
        mlp_sums[0].give(chip)
    hops, next_rows = mlp_sums[0].rounds(), gathers[0].rounds()
    weave(hops[:-1], next_rows[:-1], [push] * 2)
    gathers[1].start()
    weave(hops[-1:], next_rows[-1:], [push])
    loads[1].wait()
    for chip in order:
        mlp_sums[1].give(chip)
    loads[2].wait()
    for thing in loads[2 + slots :]:
        thing.wait()
    gathers[0].arrived()
    push()
    fetch_columns(0).start()
    fetch_columns(1).start()
    mlp_hops, next_rows, hops = mlp_sums[1].rounds(), gathers[1].rounds(), sums[0].rounds()
    first_pass(0)
    push()
    finish_mlp(0)
    give_free(0)
    weave(mlp_hops[:1], next_rows[:1])
    second_pass(0)
    take_free(0)
    third_pass(0)
    weave(mlp_hops[1:], next_rows[1:], hops[:1], [push] * 2)
    loads[3].wait()
    gathers[1].arrived()
    first_pass(1)
    finish_mlp(1)
    give_free(1)
    hops[1]()
    second_pass(1)
    take_free(1)
    weave(hops[2:])
    third_pass(1)
    hops = sums[1].rounds()
    hops[0]()
    out_step()
    pieces[7].start()
    for index in range(steps_in):
        in_step(index)
    pieces[6].start()
    hops[1]()
    pieces[7].forward()
    pieces[6].forward()
    weave(hops[2:])
    finish_grad(0)
    finish_grad(1)
    last = [
        pltpu.make_async_copy(mlp_total, mlp_out, load.at[0]),
        pltpu.make_async_copy(grad_total, grad_out, load.at[1]),
    ]
    for thing in last:
        thing.start()
    small_sums()
    for thing in pieces:
        thing.finish()
    for thing in last:
        thing.wait()
    for thing in gathers + sums:
        thing.drain()
    for slot in range(slots):
        pl.when(has_earlier)(lambda slot=slot: halo(slot).wait_send())


def mixer_backward(
    seqs, models, low, mlp_part, source, gain, gain_mlp_part, taps, in_full, out_full, normed_rows, gates, product, mixed, pair_grad, down_grad
):
    slots, share, width = low.shape
    chips = models // 2
    block = share * models
    channels = out_full.shape[0]
    units = down_grad.shape[0]
    shard = width // seqs
    gots = 3 if seqs == 4 else seqs
    hbm = pl.BlockSpec(memory_space=pltpu.HBM)
    vmem = pl.BlockSpec(memory_space=pltpu.VMEM)
    shape = jax.ShapeDtypeStruct
    return pl.pallas_call(
        functools.partial(mixer_backward_kernel, seqs, models),
        out_shape=[
            shape((slots, share, width), F32),
            shape((slots, share, width), F32),
            shape((8, width), F32),
            shape((gots, 3, shard, channels), BF),
            shape((gots, channels, shard), BF),
            shape((gots, 2, shard, units), BF),
            shape((gots, units, shard), BF),
        ],
        in_specs=[hbm, hbm, vmem, vmem, vmem, vmem] + [hbm] * 8,
        out_specs=[hbm, hbm, vmem] + [hbm] * 4,
        scratch_shapes=[
            pltpu.VMEM((3, width, channels), BF),
            pltpu.VMEM((channels, width), BF),
            pltpu.VMEM((slots, block, width), BF),
            pltpu.VMEM((2, slots, block, 256), BF),
            pltpu.VMEM((slots, 3, block, channels), F32),
            pltpu.VMEM((slots, block + 8, channels), F32),
            pltpu.VMEM((slots, block, channels), BF),
            pltpu.VMEM((slots, block + 8, channels), F32),
            pltpu.VMEM((slots, block, 3 * channels), BF),
            pltpu.VMEM((slots, block, width), BF),
            pltpu.VMEM((slots, chips, share, width), BF),
            pltpu.VMEM((slots, chips + 1, share, width), BF),
            pltpu.VMEM((slots, share, width), F32),
            pltpu.VMEM((slots, share, width), F32),
            pltpu.VMEM((2, 2, 2, units // 4, shard), BF),
            pltpu.VMEM((4, 2, 2, shard // 4, units), BF),
            pltpu.VMEM((2, 2, 3, shard // 2, channels), BF),
            pltpu.VMEM((2, 2, channels // 2, shard), BF),
            pltpu.VMEM((8, channels), F32),
            pltpu.VMEM((8, width), F32),
            pltpu.VMEM((models, 8, channels), F32),
            pltpu.VMEM((seqs, 8, channels), F32),
            pltpu.SemaphoreType.DMA((2 * slots + 5,)),
            pltpu.SemaphoreType.DMA((2,)),
            pltpu.SemaphoreType.DMA((8, max(6, seqs - 1))),
            pltpu.SemaphoreType.DMA((8, max(6, seqs - 1))),
            pltpu.SemaphoreType.DMA((8, 3)),
            pltpu.SemaphoreType.DMA((slots,)),
            pltpu.SemaphoreType.DMA((slots,)),
            pltpu.SemaphoreType.REGULAR((slots,)),
            pltpu.SemaphoreType.DMA((2, models - 1)),
            pltpu.SemaphoreType.DMA((2, models - 1)),
            pltpu.SemaphoreType.DMA((seqs - 1,)),
            pltpu.SemaphoreType.DMA((seqs - 1,)),
            *gather_sems(slots, chips),
            *scatter_sems(2 * slots, chips),
        ],
        compiler_params=pltpu.CompilerParams(collective_id=3, has_side_effects=True, vmem_limit_bytes=VMEM_LIMIT),
    )(low, mlp_part, source, gain, gain_mlp_part, taps, in_full, out_full, normed_rows, gates, product, mixed, pair_grad, down_grad)


def local(
    hidden,
    cotangent,
    lengths,
    gain_mix,
    gain_mlp,
    conv_weight,
    mixer_in,
    mixer_out,
    gate_up,
    mlp_down,
):
    seqs, models = lax.axis_size("seq"), lax.axis_size("mp")
    seq_pos = lax.axis_index("seq")
    model_pos = lax.axis_index("mp")
    share = hidden.shape[1]
    channels = mixer_in.shape[2]
    taps = conv_weight.shape[0]
    local_taps = lax.dynamic_slice_in_dim(conv_weight, model_pos * channels, channels, 1)
    share_start = (seq_pos * models + model_pos) * share
    share_pos = share_start + jnp.arange(share, dtype=jnp.int32)
    mask = (share_pos[None, :] < lengths[:, None]).astype(F32)[:, :, None]
    top_low = (cotangent.astype(F32) * mask).astype(BF)
    (
        normed_rows,
        _,
        in_full,
        out_full,
        gates,
        product,
        mixed,
        middle,
        middle_grad,
        low,
        gain_mlp_part,
        mlp_part,
        _,
        pair_total,
        down_total,
    ) = forward(
        seqs,
        models,
        hidden,
        gain_mix[None],
        gain_mlp[None],
        top_low,
        local_taps,
        mixer_in,
        mixer_out,
        gate_up,
        mlp_down,
    )
    mlp_share, source_grad, small, in_got, out_got, pair_got, down_got = mixer_backward(
        seqs,
        models,
        low,
        mlp_part,
        hidden,
        gain_mix[None],
        gain_mlp_part,
        local_taps,
        in_full,
        out_full,
        normed_rows,
        gates,
        product,
        mixed,
        pair_total,
        down_total,
    )

    def total(got):
        return jnp.sum(got.astype(F32), axis=0)

    return (
        (mask * (middle + mlp_share)).astype(BF),
        source_grad + middle_grad,
        small[0],
        small[1],
        small[2 : 2 + taps],
        total(in_got),
        total(out_got),
        total(pair_got),
        total(down_got),
    )


def solution(mesh):
    placed = (
        P(None, ("seq", "mp"), None),
        P(None, ("seq", "mp"), None),
        P(),
        P(),
        P(),
        P(),
        P(None, "seq", "mp"),
        P("mp", "seq"),
        P(None, "seq", "mp"),
        P("mp", "seq"),
    )
    return jax.shard_map(
        local,
        mesh=mesh,
        in_specs=placed,
        out_specs=(
            P(None, ("seq", "mp"), None),
            P(None, ("seq", "mp"), None),
            P(),
            P(),
            P(),
            P(None, "seq", "mp"),
            P("mp", "seq"),
            P(None, "seq", "mp"),
            P("mp", "seq"),
        ),
        check_vma=False,
    )
```

```python
import functools

import jax
import jax.numpy as jnp
from jax import lax
from jax.experimental import pallas as pl
from jax.experimental.pallas import tpu as pltpu
from jax.sharding import PartitionSpec as P

EPS = 1e-05
MESH = pl.DeviceIdType.MESH
BF = jnp.bfloat16
F32 = jnp.float32
HALVES = 2
VMEM_LIMIT = 63 * 2**20


def nn(a, b):
    return lax.dot_general(a, b, (((1,), (0,)), ((), ())), preferred_element_type=F32)


def nt(a, b):
    return lax.dot_general(a, b, (((1,), (1,)), ((), ())), preferred_element_type=F32)


def tn(a, b):
    return lax.dot_general(a, b, (((0,), (0,)), ((), ())), preferred_element_type=F32)


class Place:
    def __init__(self, seqs, models):
        self.seqs, self.chips = seqs, models // 2
        self.s = lax.axis_index("seq")
        self.m = lax.axis_index("mp")
        self.z = self.m // 2
        self.c = self.m % 2
        self.sibling = {"mp": self.m + 1 - 2 * self.c}
        self.above = {"mp": self.m + 2}
        self.below = {"mp": self.m - 2}
        self.has_above = self.z < self.chips - 1
        self.has_below = self.z > 0

    def peer(self, step):
        return {"seq": lax.rem(self.s + step, self.seqs)}

    def enter(self):
        barrier = pltpu.get_barrier_semaphore()
        models = 2 * self.chips
        peers = [{"mp": lax.rem(self.m + step, models)} for step in range(1, models)]
        for where in peers + [self.peer(step) for step in range(1, self.seqs)]:
            pl.semaphore_signal(barrier, inc=1, device_id=where, device_id_type=MESH)
        pl.semaphore_wait(barrier, models + self.seqs - 2)


def remote(src, dst, send, recv, where):
    return pltpu.make_async_remote_copy(
        src_ref=src, dst_ref=dst, send_sem=send, recv_sem=recv, device_id=where, device_id_type=MESH
    )


class Gather:
    def __init__(self, place, rows, own, sems):
        self.p, self.rows, self.own = place, rows, own
        self.share = rows.shape[0] // (2 * place.chips)
        self.piece = self.share // HALVES
        self.send, self.recv = sems

    def at(self, chip, core, half):
        return self.rows.at[pl.ds((chip * 2 + core) * self.share + half * self.piece, self.piece)]

    def copy(self, kind, chip, half, own=False):
        p = self.p
        where = (p.above, p.below, p.sibling)[kind]
        dst = self.at(chip, p.c, half)
        src = self.own.at[pl.ds(half * self.piece, self.piece)] if own and self.own is not None else dst
        return remote(src, dst, self.send.at[kind, chip, half], self.recv.at[kind // 2, chip, half], where)

    def start(self):
        p = self.p
        for half in range(HALVES):
            pl.when(p.has_above)(lambda h=half: self.copy(0, p.z, h, True).start())
            pl.when(p.has_below)(lambda h=half: self.copy(1, p.z, h, True).start())
        for half in range(HALVES):
            self.copy(2, p.z, half, True).start()

    def round(self, k):
        p = self.p
        for half in range(HALVES):

            @pl.when(p.z >= k)
            def _(half=half):
                chip = p.z - k
                self.copy(0, chip, half).wait_recv()
                pl.when(p.has_above)(lambda: self.copy(0, chip, half).start())
                self.copy(2, chip, half).start()

            @pl.when(p.z + k <= p.chips - 1)
            def _(half=half):
                chip = p.z + k
                self.copy(1, chip, half).wait_recv()
                pl.when(p.has_below)(lambda: self.copy(1, chip, half).start())
                self.copy(2, chip, half).start()

    def rounds(self):
        return [functools.partial(self.round, k) for k in range(1, self.p.chips)]

    def other_core(self, chip):
        p = self.p
        for half in range(HALVES):
            dst = self.at(chip, 1 - p.c, half)
            remote(dst, dst, self.send.at[2, chip, half], self.recv.at[1, chip, half], p.sibling).wait_recv()

    def arrived(self):
        for chip in range(self.p.chips):
            self.other_core(chip)

    def drain(self):
        p = self.p
        for chip in range(p.chips):
            for half in range(HALVES):
                pl.when(p.has_above & (chip <= p.z))(lambda ch=chip, h=half: self.copy(0, ch, h).wait_send())
                pl.when(p.has_below & (chip >= p.z))(lambda ch=chip, h=half: self.copy(1, ch, h).wait_send())
                self.copy(2, chip, half).wait_send()


class Scatter:
    def __init__(self, place, part, from_core, from_line, sems):
        self.p, self.part, self.from_core, self.from_line = place, part, from_core, from_line
        self.share = from_core.shape[1]
        self.piece = self.share // HALVES
        self.core_send, self.core_recv, self.line_send, self.line_recv = sems

    def rows(self, chip, core):
        return self.part.at[pl.ds((chip * 2 + core) * self.share, self.share)]

    def core_copy(self, chip):
        p = self.p
        return remote(
            self.rows(chip, 1 - p.c), self.from_core.at[chip], self.core_send.at[chip], self.core_recv.at[chip], p.sibling
        )

    def give(self, chip):
        self.core_copy(chip).start()

    def mine(self, chip, half):
        return self.part.at[pl.ds((chip * 2 + self.p.c) * self.share + half * self.piece, self.piece)]

    def line_copy(self, down, chip, slot, half):
        p = self.p
        dst = self.from_line.at[slot, pl.ds(half * self.piece, self.piece)]
        return remote(
            self.mine(chip, half),
            dst,
            self.line_send.at[down, chip, half],
            self.line_recv.at[slot, half],
            p.below if down else p.above,
        )

    def total(self, chip, half, slots):
        span = pl.ds(half * self.piece, self.piece)
        value = self.mine(chip, half)[...].astype(F32) + self.from_core[chip, span].astype(F32)
        for slot in slots:
            value = value + self.from_line[slot, span].astype(F32)
        return value

    def hop(self, down, chip, slot, has_source):
        self.core_copy(chip).wait_recv()
        for half in range(HALVES):

            @pl.when(has_source)
            def _(half=half):
                self.line_copy(down, chip, chip, half).wait_recv()
                self.mine(chip, half)[...] = self.total(chip, half, [chip]).astype(BF)

            @pl.when(jnp.logical_not(has_source))
            def _(half=half):
                self.mine(chip, half)[...] = self.total(chip, half, []).astype(BF)

            self.line_copy(down, chip, slot, half).start()

    def round(self, r):
        p = self.p
        last = p.chips - 1

        @pl.when((p.z <= r) & p.has_above)
        def _():
            chip = last - r + p.z
            self.hop(0, chip, chip, p.has_below)

        @pl.when((last - p.z <= r) & p.has_below)
        def _():
            chip = r - last + p.z
            self.hop(1, chip, p.chips if r == last - 1 else chip, p.has_above)

    def rounds(self):
        return [functools.partial(self.round, r) for r in range(self.p.chips - 1)]

    def finish(self, store):
        p = self.p
        self.core_copy(p.z).wait_recv()
        for half in range(HALVES):
            pl.when(p.has_below)(lambda h=half: self.line_copy(0, p.z, p.z, h).wait_recv())
            pl.when(p.has_above)(lambda h=half: self.line_copy(1, p.z, p.chips, h).wait_recv())
            for up in (False, True):
                for low in (False, True):

                    @pl.when((p.has_above == up) & (p.has_below == low))
                    def _(half=half, up=up, low=low):
                        slots = ([p.z] if low else []) + ([p.chips] if up else [])
                        store(half * self.piece, self.piece, self.total(p.z, half, slots))

    def drain(self):
        p = self.p
        for chip in range(p.chips):
            self.core_copy(chip).wait_send()
            for half in range(HALVES):
                pl.when(p.has_above & (chip > p.z))(lambda ch=chip, h=half: self.line_copy(0, ch, ch, h).wait_send())
                pl.when(p.has_below & (chip < p.z))(lambda ch=chip, h=half: self.line_copy(1, ch, ch, h).wait_send())


class StraightScatter(Scatter):
    def straight(self, chip, half):
        p = self.p
        return remote(
            self.mine(chip, half),
            self.from_line.at[p.z, pl.ds(half * self.piece, self.piece)],
            self.line_send.at[0, chip, half],
            self.line_recv.at[p.z, half],
            {"mp": chip * 2 + p.c},
        )

    def came(self, chip, half):
        view = self.from_line.at[chip, pl.ds(half * self.piece, self.piece)]
        return remote(view, view, self.line_send.at[0, chip, half], self.line_recv.at[chip, half], self.p.sibling)

    def go(self, chip):
        self.core_copy(chip).wait_recv()
        for half in range(HALVES):
            self.mine(chip, half)[...] = self.total(chip, half, []).astype(BF)
            self.straight(chip, half).start()

    def others(self):
        return [lax.rem(self.p.z + step, self.p.chips) for step in range(1, self.p.chips)]

    def finish(self, store):
        self.core_copy(self.p.z).wait_recv()
        for half in range(HALVES):
            for chip in self.others():
                self.came(chip, half).wait_recv()
            store(half * self.piece, self.piece, self.total(self.p.z, half, self.others()))

    def drain(self):
        for chip in range(self.p.chips):
            self.core_copy(chip).wait_send()
        for chip in self.others():
            for half in range(HALVES):
                self.straight(chip, half).wait_send()


def gather_sems(count, chips):
    return [pltpu.SemaphoreType.DMA((count, 3, chips, HALVES)), pltpu.SemaphoreType.DMA((count, 2, chips, HALVES))]


def scatter_sems(count, chips):
    return [
        pltpu.SemaphoreType.DMA((count, chips)),
        pltpu.SemaphoreType.DMA((count, chips)),
        pltpu.SemaphoreType.DMA((count, 2, chips, HALVES)),
        pltpu.SemaphoreType.DMA((count, chips + 1, HALVES)),
    ]


def picks(sems, index):
    return [sem.at[index] for sem in sems]


def far_first(place):
    low, high = 0, place.chips - 1
    order = []
    for _ in range(place.chips):
        left = place.z - low >= high - place.z
        order.append(jnp.where(left, low, high))
        low, high = jnp.where(left, low + 1, low), jnp.where(left, high, high - 1)
    return order


def weave(*lists):
    for step in range(max(len(steps) for steps in lists)):
        for steps in lists:
            if step < len(steps):
                steps[step]()


class Relay:
    def __init__(self, place, shard, full, first, size, sems):
        self.p, self.shard, self.full, self.first, self.size = place, shard, full, first, size
        self.send, self.recv, self.local = sems
        s = place.s
        self.square = place.seqs == 4
        if self.square:
            self.near = (s + 1 - 2 * lax.rem(s, 2), lax.rem(s + 2, 4))

    def half(self, index):
        return self.first + index * (self.size // 2), self.size // 2

    def direct(self, index, where):
        return remote(
            self.shard(self.first, self.size),
            self.full(self.p.s, self.first, self.size),
            self.send.at[index],
            self.recv.at[index],
            where,
        )

    def handed(self, index):
        view = self.full(self.near[index], *self.half(index))
        return remote(view, view, self.send.at[2 + index], self.recv.at[2 + index], {"seq": self.near[1 - index]})

    def local_copy(self):
        return pltpu.make_async_copy(
            self.shard(self.first, self.size), self.full(self.p.s, self.first, self.size), self.local
        )

    def copies(self):
        if self.square:
            return [self.direct(index, {"seq": self.near[index]}) for index in range(2)]
        return [self.direct(step - 1, self.p.peer(step)) for step in range(1, self.p.seqs)]

    def start(self):
        for thing in self.copies():
            thing.start()
        self.local_copy().start()

    def forward(self):
        if self.square:
            for thing in self.copies():
                thing.wait_recv()
            for index in range(2):
                self.handed(index).start()

    def arrived(self):
        self.local_copy().wait()
        for thing in [self.handed(index) for index in range(2)] if self.square else self.copies():
            thing.wait_recv()

    def drain(self):
        for thing in self.copies() + ([self.handed(index) for index in range(2)] if self.square else []):
            thing.wait_send()


def forward_kernel(
    seqs,
    models,
    source_ref,
    gain_mix_ref,
    gain_ref,
    top_ref,
    taps_ref,
    in_ref,
    out_ref,
    pair_ref,
    down_ref,
    normed_rows,
    top_rows,
    in_rows,
    out_rows,
    gates_out,
    product_out,
    mixed_out,
    middle_out,
    grad_out,
    low_out,
    gain_out,
    mlp_part,
    act_rows,
    pair_grad,
    down_grad,
    in_full,
    out_full,
    rows,
    gates,
    ends,
    product,
    mixed,
    pair,
    down,
    top_tile,
    acts,
    act_stage,
    stage,
    part,
    from_core,
    from_line,
    total,
    w_send,
    w_recv,
    w_local,
    halo_send,
    halo_recv,
    keep,
    tile_sem,
    out_sem,
    cols_sem,
    pair_sem,
    ends_sem,
    *sems,
):
    p = Place(seqs, models)
    chips = p.chips
    g_sems, s_sems = sems[:2], sems[2:]
    slots, block, width = rows.shape
    units = down.shape[0]
    tile = block // chips
    share = tile // 2
    channels = in_full.shape[2]
    shard = width // seqs
    unit_block = min(512, units)
    wide_block = 512
    gain_out[...] = jnp.zeros_like(gain_out)

    def first_norm(slot):
        for first in range(0, share, share // HALVES):
            value = source_ref[slot, pl.ds(first, share // HALVES)].astype(F32)
            scale = lax.rsqrt(jnp.mean(value * value, axis=-1, keepdims=True) + EPS)
            rows[slot, pl.ds(p.m * share + first, share // HALVES)] = (value * scale * gain_mix_ref[...]).astype(BF)

    for slot in range(slots):
        first_norm(slot)
    p.enter()

    firsts = [Gather(p, rows.at[slot], None, picks(g_sems, slot)) for slot in range(slots)]
    tops = [Gather(p, top_rows.at[slot], top_ref.at[slot], picks(g_sems, slots + slot)) for slot in range(slots)]
    seconds = [Gather(p, rows.at[slot], None, picks(g_sems, 2 * slots + slot)) for slot in range(slots)]

    def scatter(slot, index, kind=Scatter):
        return kind(p, part.at[slot], from_core.at[slot], from_line.at[slot], picks(s_sems, index))

    mix_sums = [scatter(slot, slot) for slot in range(slots)]
    grad_sums = [scatter(0, slots), scatter(1, slots + 1, StraightScatter)]

    def columns_of(owner):
        return pl.ds(pl.multiple_of(owner * shard, shard), shard)

    def pair_views(k):
        return (
            lambda first, size: pair_ref.at[k, pl.ds(first, size)],
            lambda owner, first, size: pair.at[k, pl.ds(owner * shard + first, size)],
        )

    views = [
        (
            lambda first, size: in_ref.at[:, pl.ds(first, size)],
            lambda owner, first, size: in_full.at[:, pl.ds(owner * shard + first, size)],
            0,
            shard,
        ),
        (
            lambda first, size: out_ref.at[pl.ds(first, size)],
            lambda owner, first, size: out_full.at[pl.ds(first, size), columns_of(owner)],
            0,
            channels,
        ),
    ]
    for i in range(2):
        views.append(
            (
                lambda first, size: down_ref.at[pl.ds(first, size)],
                lambda owner, first, size: down.at[pl.ds(first, size), columns_of(owner)],
                i * (units // 2),
                units // 2,
            )
        )
    for i in range(4):
        views.append((*pair_views(i // 2), (i % 2) * (shard // 2), shard // 2))
    pieces = [Relay(p, *view, (w_send.at[i], w_recv.at[i], w_local.at[i])) for i, view in enumerate(views)]
    early, late = pieces[:2], pieces[2:]
    moves = [[("start", 0), ("start", 1)], [("forward", 0), ("start", 2)], [("forward", 1), ("start", 3)]]
    moves += [[("forward", 2)], [("forward", 3)], [("start", 4), ("start", 5)], [("forward", 4)], [("forward", 5)]]

    def push():
        for name, index in moves.pop(0):
            getattr(late[index], name)()

    def own(slot):
        span = pl.ds(p.m * share, share)
        return pltpu.make_async_copy(top_ref.at[slot], top_rows.at[slot, span], keep.at[slot])

    for slot in range(slots):
        own(slot).start()

    def saved(index, src, dst):
        return pltpu.make_async_copy(src, dst, keep.at[2 * slots + index])

    rows_saved = [saved(slot, rows.at[slot], normed_rows.at[slot]) for slot in range(slots)]
    gates_saved = [saved(slots + slot, gates, gates_out.at[slot, 1]) for slot in range(slots)]
    middle_saved = [saved(2 * slots + slot, total.at[slot], middle_out.at[slot]) for slot in range(slots)]
    grad_saved = [saved(3 * slots + slot, total.at[slot], grad_out.at[slot]) for slot in range(slots)]
    low_saved = [
        saved(4 * slots + 6 + slot, stage.at[pl.ds(slot * share, share)], low_out.at[slot]) for slot in range(slots)
    ]
    own_tops = [
        saved(5 * slots + 6 + slot, top_ref.at[slot], top_tile.at[pl.ds(slot * share, share)]) for slot in range(slots)
    ]
    in_saved = saved(4 * slots, in_full, in_rows)
    out_saved = saved(4 * slots + 1, out_full, out_rows)
    product_saved = saved(4 * slots + 2, product, product_out)
    mixed_saved = [saved(6 * slots + 6 + slot, mixed, mixed_out.at[slot]) for slot in range(slots)]
    down_saved = saved(4 * slots + 4, down, down_grad)
    act_load = saved(4 * slots + 5, act_rows, acts.at[0])

    def halo(slot):
        return remote(
            product.at[slot, pl.ds(block, 8)],
            product.at[slot, pl.ds(0, 8)],
            halo_send.at[slot],
            halo_recv.at[slot],
            p.peer(1),
        )

    has_later, has_earlier = p.s < seqs - 1, p.s > 0
    for slot in range(slots):

        @pl.when(jnp.logical_not(has_earlier))
        def _(slot=slot):
            product[slot, pl.ds(0, 8)] = jnp.zeros((8, channels), F32)

    def ends_saved(slot, i):
        span = pl.ds(i * tile, tile)
        return [
            pltpu.make_async_copy(ends.at[j], gates_out.at[slot, 2 * j, span], ends_sem.at[j]) for j in range(2)
        ]

    def project(slot):
        @pl.loop(0, chips)
        def _(i):
            span = pl.ds(i * tile, tile)
            source = rows[slot, span]
            b_gate = nn(source, in_full[0])
            x_value = nn(source, in_full[2])
            gates[span] = nn(source, in_full[1])

            @pl.when(i > 0)
            def _():
                for thing in ends_saved(slot, i - 1):
                    thing.wait()

            ends[0] = b_gate
            ends[1] = x_value
            for thing in ends_saved(slot, i):
                thing.start()
            product[slot, pl.ds(8 + i * tile, tile)] = b_gate * x_value

        for thing in ends_saved(slot, chips - 1):
            thing.wait()
        pl.when(has_later)(lambda: halo(slot).start())

    def convolve(slot):
        pl.when(has_earlier)(lambda: halo(slot).wait_recv())
        for i in range(chips):
            conv = 0.0
            for offset in range(taps_ref.shape[0]):
                conv = conv + taps_ref[offset : offset + 1] * product[slot, pl.ds(8 + i * tile - offset, tile)]
            mixed[pl.ds(i * tile, tile)] = (gates[pl.ds(i * tile, tile)] * conv).astype(BF)

    def project_out(slot):
        for chip in far_first(p):
            span = pl.ds(chip * tile, tile)
            part[slot, span] = nn(mixed[span], out_full[...]).astype(BF)
            mix_sums[slot].give(chip)
        mixed_saved[slot].start()

    def middle(slot):
        def store(first, size, value):
            span = pl.ds(first, size)
            value = value + source_ref[slot, span].astype(F32)
            total[slot, span] = value
            scale = lax.rsqrt(jnp.mean(value * value, axis=-1, keepdims=True) + EPS)
            rows[slot, pl.ds(p.m * share + first, size)] = (value * scale * gain_ref[...]).astype(BF)

        mix_sums[slot].finish(store)
        middle_saved[slot].start()
        mix_sums[slot].drain()

    def finish_grad(slot):
        middle_saved[slot].wait()

        def store(first, size, value):
            span = pl.ds(first, size)
            at = pl.ds(slot * share + first, size)
            middle = total[slot, span]
            scale = lax.rsqrt(jnp.mean(middle * middle, axis=-1, keepdims=True) + EPS)
            unit = middle * scale
            gain_out[0:1] += jnp.sum(value * unit, axis=0, keepdims=True)
            scaled = value * gain_ref[...]
            grad = scale * (scaled - unit * jnp.mean(scaled * unit, axis=-1, keepdims=True))
            grad = grad + top_tile[at].astype(F32)
            total[slot, span] = grad
            stage[at] = grad.astype(BF)

        grad_sums[slot].finish(store)
        grad_saved[slot].start()
        low_saved[slot].start()

    order = far_first(p)
    tiles = [(0, chip) for chip in order] + [(slot, chip) for slot in range(1, slots) for chip in order[::-1]]

    def fetch(index):
        slot, chip = tiles[index]
        return pltpu.make_async_copy(top_rows.at[slot, pl.ds(chip * tile, tile)], top_tile, tile_sem)

    def puts(index):
        slot, chip = tiles[index]
        span = pl.ds(chip * tile, tile)
        return [
            pltpu.make_async_copy(stage, mlp_part.at[slot, span], out_sem.at[0]),
            pltpu.make_async_copy(act_stage, act_rows.at[slot, span], out_sem.at[1]),
        ]

    def work(index):
        slot, chip = tiles[index]
        span = pl.ds(chip * tile, tile)
        if index % chips == 0:
            fetch(index).start()
        fetch(index).wait()
        if index:
            for thing in puts(index - 1):
                thing.wait()

        @pl.loop(0, units // unit_block)
        def _(i):
            cut = pl.ds(pl.multiple_of(i * unit_block, unit_block), unit_block)
            source = rows[slot, span]
            gate = nn(source, pair[0, :, cut])
            up = nn(source, pair[1, :, cut])
            act_grad = nt(top_tile[...], down[cut])
            sigma = jax.nn.sigmoid(gate)
            silu = gate * sigma
            act_stage[:, cut] = (silu * up).astype(BF)
            acts[0, slot, span, cut] = (act_grad * up * sigma * (1.0 + gate * (1.0 - sigma))).astype(BF)
            acts[1, slot, span, cut] = (act_grad * silu).astype(BF)

        if (index + 1) % chips:
            fetch(index + 1).start()

        @pl.loop(0, width // wide_block)
        def _(i):
            cut = pl.ds(pl.multiple_of(i * wide_block, wide_block), wide_block)
            value = nt(acts[0, slot, span], pair[0, cut]) + nt(acts[1, slot, span], pair[1, cut])
            part[slot, span, cut] = value.astype(BF)
            stage[:, cut] = nn(act_stage[...], down[:, cut]).astype(BF)

        grad_sums[slot].give(chip)
        for thing in puts(index):
            thing.start()

    pair_block = 512
    pair_steps = 2 * (width // pair_block)

    def pair_saved(index):
        k, first = divmod(index, width // pair_block)
        cut = pl.ds(first * pair_block, pair_block)
        return pltpu.make_async_copy(pair.at[k, cut], pair_grad.at[k, cut], pair_sem.at[index])

    def pair_step(index):
        k, first = divmod(index, width // pair_block)
        cut = pl.ds(first * pair_block, pair_block)
        value = 0.0
        for slot in range(slots):
            value = value + tn(rows[slot, :, cut], acts[k, slot])
        pair[k, cut] = value.astype(BF)
        pair_saved(index).start()
        if first == width // pair_block - 1 and k == 0:
            act_load.start()

    def fetch_columns(index):
        cut = pl.ds(index * channels, channels)
        return [
            pltpu.make_async_copy(
                top_rows.at[slot, :, cut], in_full.at[index % 2, pl.ds(slot * block, block)], cols_sem.at[index % 2, slot]
            )
            for slot in range(slots)
        ]

    def down_step(index):
        if index == 0:
            act_load.wait()
        for thing in fetch_columns(index):
            thing.wait()
        for first in range(0, units, unit_block):
            cut = pl.ds(first, unit_block)
            value = 0.0
            for slot in range(slots):
                value = value + tn(acts[0, slot, :, cut], in_full[index % 2, pl.ds(slot * block, block)])
            down[cut, pl.ds(index * channels, channels)] = value.astype(BF)
        if index + 2 < width // channels:
            for thing in fetch_columns(index + 2):
                thing.start()

    firsts[0].start()
    for piece in early:
        piece.start()
    steps = firsts[0].rounds()
    for step in steps[:-1]:
        step()
    for piece in early:
        piece.forward()
    firsts[1].start()
    steps[-1]()
    firsts[0].arrived()
    rows_saved[0].start()
    for piece in early:
        piece.arrived()
    in_saved.start()
    out_saved.start()
    project(0)
    gates_saved[0].start()
    push()
    steps = firsts[1].rounds()
    steps[0]()
    push()
    rows_saved[0].wait()
    firsts[0].drain()
    convolve(0)
    project_out(0)
    weave(mix_sums[0].rounds(), steps[1:-1] + [tops[0].start, steps[-1]], [push] * 3)
    firsts[1].arrived()
    rows_saved[1].start()
    gates_saved[0].wait()
    project(1)
    gates_saved[1].start()
    push()
    middle(0)
    seconds[0].start()
    rows_saved[1].wait()
    firsts[1].drain()
    mixed_saved[0].wait()
    convolve(1)
    project_out(1)
    hops, steps, more = mix_sums[1].rounds(), tops[0].rounds(), seconds[0].rounds()
    weave(steps, hops, [push] * 2)
    weave(more[:-1])
    tops[1].start()
    more[-1]()
    middle(1)
    seconds[1].start()
    product_saved.start()
    own(0).wait()
    tops[0].arrived()
    seconds[0].arrived()
    for piece in late:
        piece.arrived()
    own(1).wait()
    hops, steps, more = grad_sums[0].rounds(), tops[1].rounds(), seconds[1].rounds()
    for index in range(chips):
        work(index)
        if index < len(steps):
            steps[index]()
        if 0 < index:
            hops[index - 1]()
    more[0]()
    tops[1].arrived()
    for index in range(chips):
        seconds[1].other_core(tiles[chips + index][1])
        work(chips + index)
        if index + 1 < len(more):
            more[index + 1]()
        if index > 1:
            grad_sums[1].go(tiles[chips + index - 1][1])
    for thing in puts(len(tiles) - 1):
        thing.wait()
    for thing in own_tops:
        thing.start()
    grad_sums[1].go(tiles[-1][1])
    in_saved.wait()
    for piece in pieces:
        piece.drain()
    for index in range(2):
        for thing in fetch_columns(index):
            thing.start()
    for thing in own_tops:
        thing.wait()
    finish_grad(0)
    work_steps = [functools.partial(pair_step, index) for index in range(pair_steps)]
    work_steps += [functools.partial(down_step, index) for index in range(width // channels)]
    for step in work_steps:
        step()
    down_saved.start()
    finish_grad(1)
    for index in range(pair_steps):
        pair_saved(index).wait()
    for thing in [gates_saved[1], out_saved, product_saved, mixed_saved[1], down_saved, *grad_saved, *low_saved]:
        thing.wait()
    for thing in tops + seconds + grad_sums:
        thing.drain()
    for slot in range(slots):
        pl.when(has_later)(lambda slot=slot: halo(slot).wait_send())


def forward(seqs, models, source, gain_mix, gain, top, taps, mixer_in, mixer_out, gate_up, mlp_down):
    slots, share, width = source.shape
    chips = models // 2
    block = share * models
    channels = mixer_in.shape[2]
    units = gate_up.shape[2]
    tile = block // chips
    hbm = pl.BlockSpec(memory_space=pltpu.HBM)
    vmem = pl.BlockSpec(memory_space=pltpu.VMEM)
    shape = jax.ShapeDtypeStruct
    return pl.pallas_call(
        functools.partial(forward_kernel, seqs, models),
        out_shape=[
            shape((slots, block, width), BF),
            shape((slots, block, width), BF),
            shape((3, width, channels), BF),
            shape((channels, width), BF),
            shape((slots, 3, block, channels), F32),
            shape((slots, block + 8, channels), F32),
            shape((slots, block, channels), BF),
            shape((slots, share, width), F32),
            shape((slots, share, width), F32),
            shape((slots, share, width), BF),
            shape((8, width), F32),
            shape((slots, block, width), BF),
            shape((slots, block, units), BF),
            shape((2, width, units), BF),
            shape((units, width), BF),
        ],
        in_specs=[vmem, vmem, vmem, hbm, vmem] + [hbm] * 4,
        out_specs=[hbm] * 10 + [vmem] + [hbm] * 4,
        scratch_shapes=[
            pltpu.VMEM((3, width, channels), BF),
            pltpu.VMEM((channels, width), BF),
            pltpu.VMEM((slots, block, width), BF),
            pltpu.VMEM((block, channels), F32),
            pltpu.VMEM((2, tile, channels), F32),
            pltpu.VMEM((slots, block + 8, channels), F32),
            pltpu.VMEM((block, channels), BF),
            pltpu.VMEM((2, width, units), BF),
            pltpu.VMEM((units, width), BF),
            pltpu.VMEM((tile, width), BF),
            pltpu.VMEM((2, slots, block, units), BF),
            pltpu.VMEM((tile, units), BF),
            pltpu.VMEM((tile, width), BF),
            pltpu.VMEM((slots, block, width), BF),
            pltpu.VMEM((slots, chips, share, width), BF),
            pltpu.VMEM((slots, chips + 1, share, width), BF),
            pltpu.VMEM((slots, share, width), F32),
            pltpu.SemaphoreType.DMA((8, max(4, seqs - 1))),
            pltpu.SemaphoreType.DMA((8, max(4, seqs - 1))),
            pltpu.SemaphoreType.DMA((8,)),
            pltpu.SemaphoreType.DMA((slots,)),
            pltpu.SemaphoreType.DMA((slots,)),
            pltpu.SemaphoreType.DMA((10 * slots + 6,)),
            pltpu.SemaphoreType.DMA,
            pltpu.SemaphoreType.DMA((2,)),
            pltpu.SemaphoreType.DMA((2, slots)),
            pltpu.SemaphoreType.DMA((2 * (width // 512),)),
            pltpu.SemaphoreType.DMA((2,)),
            *gather_sems(3 * slots, chips),
            *scatter_sems(2 * slots, chips),
        ],
        compiler_params=pltpu.CompilerParams(collective_id=1, has_side_effects=True, vmem_limit_bytes=VMEM_LIMIT),
    )(source, gain_mix, gain, top, taps, mixer_in, mixer_out, gate_up, mlp_down)


class Exchange:
    def __init__(self, place, partial, got, first, size, sems, held, came):
        self.p, self.partial, self.got, self.first, self.size = place, partial, got, first, size
        self.send, self.recv, self.local = sems
        self.held, self.came = held, came
        s = place.s
        self.square = place.seqs == 4
        if self.square:
            self.near = (s + 1 - 2 * lax.rem(s, 2), lax.rem(s + 2, 4))
            self.across = 3 - s

    def half(self, index):
        return self.first + index * (self.size // 2), self.size // 2

    def to(self, index):
        return {"seq": self.near[index]}

    def relayed(self, index):
        return remote(
            self.partial(self.across, *self.half(index)),
            self.came.at[index],
            self.send.at[index],
            self.recv.at[index],
            self.to(index),
        )

    def plain(self, index):
        span = self.half(index)
        return remote(
            self.partial(self.near[index], *span),
            self.got(1 + index, *span),
            self.send.at[2 + index],
            self.recv.at[2 + index],
            self.to(index),
        )

    def added(self, index):
        return remote(
            self.held.at[1 - index],
            self.got(1 + index, *self.half(1 - index)),
            self.send.at[4 + index],
            self.recv.at[4 + index],
            self.to(index),
        )

    def load(self, index):
        return pltpu.make_async_copy(
            self.partial(self.near[index], *self.half(1 - index)), self.held.at[1 - index], self.local.at[1 + index]
        )

    def straight(self, step):
        p = self.p
        return remote(
            self.partial(lax.rem(p.s + step, p.seqs), self.first, self.size),
            self.got(step, self.first, self.size),
            self.send.at[step - 1],
            self.recv.at[step - 1],
            p.peer(step),
        )

    def own(self):
        return pltpu.make_async_copy(
            self.partial(self.p.s, self.first, self.size), self.got(0, self.first, self.size), self.local.at[0]
        )

    def copies(self):
        if self.square:
            return [self.relayed(0), self.relayed(1), self.plain(0), self.plain(1)]
        return [self.straight(step) for step in range(1, self.p.seqs)]

    def start(self):
        for thing in self.copies():
            thing.start()
        if self.square:
            for index in range(2):
                self.load(index).start()
        self.own().start()

    def forward(self):
        if self.square:
            for index in range(2):
                self.load(index).wait()
                self.relayed(1 - index).wait_recv()
                total = self.held[1 - index].astype(F32) + self.came[1 - index].astype(F32)
                self.held[1 - index] = total.astype(BF)
                self.added(index).start()

    def finish(self):
        self.own().wait()
        if self.square:
            for thing in self.copies():
                thing.wait_send()
            for index in range(2):
                self.plain(index).wait_recv()
                self.added(index).wait()
        else:
            for thing in self.copies():
                thing.wait()


def mixer_backward_kernel(
    seqs,
    models,
    low_ref,
    mlp_part,
    source_ref,
    gain_ref,
    gain_mlp_ref,
    taps_ref,
    in_ref,
    out_ref,
    normed_rows,
    gates_ref,
    product_ref,
    mixed_ref,
    pair_grad,
    down_grad,
    mlp_out,
    grad_out,
    small_out,
    in_got,
    out_got,
    pair_got,
    down_got,
    in_full,
    out_full,
    rows,
    columns,
    gates,
    product,
    mixed,
    conv_grad,
    stacked,
    part,
    from_core,
    from_line,
    mlp_total,
    grad_total,
    down_room,
    pair_room,
    in_room,
    out_room,
    taps_out,
    small,
    by_model,
    by_seq,
    load,
    cols_sem,
    w_send,
    w_recv,
    w_local,
    halo_send,
    halo_recv,
    free,
    mp_send,
    mp_recv,
    seq_send,
    seq_recv,
    *sems,
):
    p = Place(seqs, models)
    chips = p.chips
    g_sems, s_sems = sems[:2], sems[2:]
    slots, block, width = rows.shape
    channels = out_full.shape[0]
    taps = taps_ref.shape[0]
    tile = block // chips
    share = tile // 2
    wide_block = 512
    cols = columns.shape[-1]
    loads = [
        pltpu.make_async_copy(src, dst, load.at[i])
        for i, (src, dst) in enumerate(
            [(mlp_part.at[slot], part.at[slot]) for slot in range(slots)]
            + [
                (low_ref.at[slot], rows.at[slot, pl.ds(p.m * share, share)])
                for slot in range(slots)
            ]
            + [
                (in_ref, in_full),
                (out_ref, out_full),
                (gates_ref, gates),
                (product_ref, product),
                (mixed_ref, mixed),
            ]
        )
    ]
    for index, thing in enumerate(loads):
        if index != 1:
            thing.start()
    p.enter()
    gathers = [Gather(p, rows.at[slot], low_ref.at[slot], picks(g_sems, slot)) for slot in range(slots)]

    def scatter(slot, index):
        return Scatter(p, part.at[slot], from_core.at[slot], from_line.at[slot], picks(s_sems, index))

    mlp_sums = [scatter(slot, slot) for slot in range(slots)]
    sums = [scatter(1 - slot, slots + slot) for slot in range(slots)]
    shard = width // seqs
    units = down_grad.shape[0]

    def columns_of(owner):
        return pl.ds(pl.multiple_of(owner * shard, shard), shard)

    views = []
    for i in range(2):
        views.append(
            (
                lambda owner, first, size: down_grad.at[pl.ds(first, size), columns_of(owner)],
                lambda index, first, size: down_got.at[index, pl.ds(first, size)],
                i * (units // 2),
                units // 2,
                down_room.at[i],
            )
        )
    for i in range(4):
        views.append(
            (
                lambda owner, first, size, k=i // 2: pair_grad.at[k, pl.ds(owner * shard + first, size)],
                lambda index, first, size, k=i // 2: pair_got.at[index, k, pl.ds(first, size)],
                (i % 2) * (shard // 2),
                shard // 2,
                pair_room.at[i],
            )
        )
    views.append(
        (
            lambda owner, first, size: in_full.at[:, pl.ds(owner * shard + first, size)],
            lambda index, first, size: in_got.at[index, :, pl.ds(first, size)],
            0,
            shard,
            in_room,
        )
    )
    views.append(
        (
            lambda owner, first, size: out_full.at[pl.ds(first, size), columns_of(owner)],
            lambda index, first, size: out_got.at[index, pl.ds(first, size)],
            0,
            channels,
            out_room,
        )
    )
    pieces = [
        Exchange(p, *view[:4], (w_send.at[i], w_recv.at[i], w_local.at[i]), view[4].at[0], view[4].at[1])
        for i, view in enumerate(views)
    ]
    moves = [[("start", 0), ("start", 1)], [("forward", 0), ("start", 2)], [("forward", 1), ("start", 3)]]
    moves += [[("forward", 2)], [("forward", 3)], [("start", 4), ("start", 5)], [("forward", 4)], [("forward", 5)]]

    def push():
        for name, index in moves.pop(0):
            getattr(pieces[index], name)()

    has_later, has_earlier = p.s < seqs - 1, p.s > 0
    order = far_first(p)

    def halo(slot):
        return remote(
            conv_grad.at[slot, pl.ds(0, 8)],
            conv_grad.at[slot, pl.ds(block, 8)],
            halo_send.at[slot],
            halo_recv.at[slot],
            p.peer(seqs - 1),
        )

    for slot in range(slots):

        @pl.when(jnp.logical_not(has_later))
        def _(slot=slot):
            conv_grad[slot, pl.ds(block, 8)] = jnp.zeros((8, channels), F32)

    taps_out[...] = jnp.zeros_like(taps_out)
    small[...] = jnp.zeros_like(small)
    small[1:2] = gain_mlp_ref[0:1]

    def first_pass(slot):
        for i in range(chips):
            span = pl.ds(i * tile, tile)
            mixed_grad = nt(rows[slot, span], out_full[...])
            grad = mixed_grad * gates[slot, 1, span]
            conv_grad[slot, span] = grad
            conv = 0.0
            for offset in range(taps):
                earlier = product[slot, pl.ds(8 + i * tile - offset, tile)]
                conv = conv + taps_ref[offset : offset + 1] * earlier
                taps_out[offset : offset + 1] += jnp.sum(grad * earlier, axis=0, keepdims=True)
            stacked[slot, span, pl.ds(channels, channels)] = (mixed_grad * conv).astype(BF)
            if i == 0:
                pl.when(has_earlier)(lambda: halo(slot).start())

    def second_pass(slot):
        pl.when(has_later)(lambda: halo(slot).wait_recv())
        for i in range(chips):
            span = pl.ds(i * tile, tile)
            grad = 0.0
            for offset in range(taps):
                grad = grad + taps_ref[offset : offset + 1] * conv_grad[slot, pl.ds(i * tile + offset, tile)]
            stacked[slot, span, pl.ds(0, channels)] = (grad * gates[slot, 2, span]).astype(BF)
            stacked[slot, span, pl.ds(2 * channels, channels)] = (grad * gates[slot, 0, span]).astype(BF)

    def third_pass(slot):
        for chip in order:
            span = pl.ds(chip * tile, tile)

            @pl.loop(0, width // wide_block)
            def _(i):
                cut = pl.ds(pl.multiple_of(i * wide_block, wide_block), wide_block)
                value = 0.0
                for k in range(3):
                    value = value + nt(stacked[slot, span, pl.ds(k * channels, channels)], in_full[k, cut])
                part[1 - slot, span, cut] = value.astype(BF)

            sums[slot].give(chip)

    def finish_mlp(slot):
        def store(first, size, value):
            mlp_total[slot, pl.ds(first, size)] = value

        mlp_sums[slot].finish(store)

    def finish_grad(slot):
        def store(first, size, value):
            span = pl.ds(first, size)
            source = source_ref[slot, span].astype(F32)
            scale = lax.rsqrt(jnp.mean(source * source, axis=-1, keepdims=True) + EPS)
            unit = source * scale
            small[0:1] += jnp.sum(value * unit, axis=0, keepdims=True)
            scaled = value * gain_ref[...]
            grad_total[slot, span] = scale * (scaled - unit * jnp.mean(scaled * unit, axis=-1, keepdims=True))

        sums[slot].finish(store)

    def mine(owner):
        return pl.ds(pl.multiple_of(owner * channels, channels), channels)

    along = [lax.rem(p.m + step, models) for step in range(1, models)]
    small_copies = [
        [
            remote(small.at[:, mine(peer)], by_model.at[p.m], mp_send.at[0, i], mp_recv.at[0, i], {"mp": peer})
            for i, peer in enumerate(along)
        ],
        [
            remote(by_seq.at[p.s], by_seq.at[p.s], seq_send.at[step - 1], seq_recv.at[step - 1], p.peer(step))
            for step in range(1, seqs)
        ],
        [
            remote(small_out.at[:, mine(p.m)], small_out.at[:, mine(p.m)], mp_send.at[1, i], mp_recv.at[1, i], {"mp": peer})
            for i, peer in enumerate(along)
        ],
    ]

    def small_stage(index):
        if index:
            for thing in small_copies[index - 1]:
                thing.wait()
        if index == 0:
            small[2 : 2 + taps, mine(p.m)] = taps_out[0:taps]
            by_model[p.m] = small[:, mine(p.m)]
        elif index == 1:
            by_seq[p.s] = functools.reduce(lambda a, b: a + b, [by_model[i] for i in range(models)])
        elif index == 2:
            small_out[:, mine(p.m)] = functools.reduce(lambda a, b: a + b, [by_seq[i] for i in range(seqs)])
        if index < 3:
            for thing in small_copies[index]:
                thing.start()

    def neighbours(act):
        act(p.sibling)
        pl.when(p.has_above)(lambda: act(p.above))
        pl.when(p.has_below)(lambda: act(p.below))

    def give_free(slot, user):
        user.drain()
        neighbours(
            lambda where: pl.semaphore_signal(free.at[slot], inc=1, device_id=where, device_id_type=MESH)
        )

    def take_free(slot):
        lines = (p.z + chips - 1) // chips + (2 * chips - 2 - p.z) // chips
        pl.semaphore_wait(free.at[slot], 1 + lines)

    def fetch_columns(index):
        return pltpu.make_async_copy(
            normed_rows.at[:, :, pl.ds(index * cols, cols)], columns.at[index % 2], cols_sem.at[index % 2]
        )

    steps_in = width // cols

    def in_step(index):
        fetch_columns(index).wait()
        value = 0.0
        for slot in range(slots):
            value = value + tn(columns[index % 2, slot], stacked[slot])
        for k in range(3):
            in_full[k, pl.ds(index * cols, cols)] = value[:, k * channels : (k + 1) * channels].astype(BF)
        if index + 2 < steps_in:
            fetch_columns(index + 2).start()

    def out_step():
        for first in range(0, width, wide_block):
            cut = pl.ds(first, wide_block)
            value = 0.0
            for slot in range(slots):
                value = value + tn(mixed[slot], rows[slot, :, cut])
            out_full[:, cut] = value.astype(BF)

    gathers[0].start()
    push()
    loads[0].wait()
    for chip in order:
        mlp_sums[0].give(chip)
    hops, next_rows = mlp_sums[0].rounds(), gathers[0].rounds()
    weave(hops[:-1], next_rows[:-1], [push] * 2)
    gathers[1].start()
    weave(hops[-1:], next_rows[-1:], [push])
    loads[2].wait()
    for thing in loads[2 + slots :]:
        thing.wait()
    gathers[0].arrived()
    push()
    fetch_columns(0).start()
    fetch_columns(1).start()
    first_pass(0)
    push()
    second_pass(0)
    third_pass(0)
    next_rows, hops = gathers[1].rounds(), sums[0].rounds()
    weave(hops[:1], next_rows[:1])
    finish_mlp(0)
    give_free(0, mlp_sums[0])
    weave(hops[1:], next_rows[1:], [push] * 2)
    loads[3].wait()
    gathers[1].arrived()
    first_pass(1)
    second_pass(1)
    take_free(0)
    third_pass(1)
    hops = sums[1].rounds()
    hops[0]()
    finish_grad(0)
    give_free(1, sums[0])
    loads[1].start()
    out_step()
    pieces[7].start()
    hops[1]()
    loads[1].wait()
    take_free(1)
    for chip in order:
        mlp_sums[1].give(chip)
    for index in range(steps_in):
        in_step(index)
    pieces[6].start()
    weave(hops[2:])
    hops = mlp_sums[1].rounds()
    hops[0]()
    pieces[7].forward()
    finish_grad(1)
    small_stage(0)
    pieces[6].forward()
    hops[1]()
    small_stage(1)
    weave(hops[2:])
    small_stage(2)
    finish_mlp(1)
    last = [
        pltpu.make_async_copy(mlp_total, mlp_out, load.at[0]),
        pltpu.make_async_copy(grad_total, grad_out, load.at[2]),
    ]
    for thing in last:
        thing.start()
    small_stage(3)
    for thing in pieces:
        thing.finish()
    for thing in last:
        thing.wait()
    for thing in gathers + [sums[1], mlp_sums[1]]:
        thing.drain()
    for slot in range(slots):
        pl.when(has_earlier)(lambda slot=slot: halo(slot).wait_send())


def mixer_backward(
    seqs, models, low, mlp_part, source, gain, gain_mlp_part, taps, in_full, out_full, normed_rows, gates, product, mixed, pair_grad, down_grad
):
    slots, share, width = low.shape
    chips = models // 2
    block = share * models
    channels = out_full.shape[0]
    units = down_grad.shape[0]
    shard = width // seqs
    gots = 3 if seqs == 4 else seqs
    hbm = pl.BlockSpec(memory_space=pltpu.HBM)
    vmem = pl.BlockSpec(memory_space=pltpu.VMEM)
    shape = jax.ShapeDtypeStruct
    return pl.pallas_call(
        functools.partial(mixer_backward_kernel, seqs, models),
        out_shape=[
            shape((slots, share, width), F32),
            shape((slots, share, width), F32),
            shape((8, width), F32),
            shape((gots, 3, shard, channels), BF),
            shape((gots, channels, shard), BF),
            shape((gots, 2, shard, units), BF),
            shape((gots, units, shard), BF),
        ],
        in_specs=[hbm, hbm, vmem, vmem, vmem, vmem] + [hbm] * 8,
        out_specs=[hbm, hbm, vmem] + [hbm] * 4,
        scratch_shapes=[
            pltpu.VMEM((3, width, channels), BF),
            pltpu.VMEM((channels, width), BF),
            pltpu.VMEM((slots, block, width), BF),
            pltpu.VMEM((2, slots, block, 256), BF),
            pltpu.VMEM((slots, 3, block, channels), F32),
            pltpu.VMEM((slots, block + 8, channels), F32),
            pltpu.VMEM((slots, block, channels), BF),
            pltpu.VMEM((slots, block + 8, channels), F32),
            pltpu.VMEM((slots, block, 3 * channels), BF),
            pltpu.VMEM((slots, block, width), BF),
            pltpu.VMEM((slots, chips, share, width), BF),
            pltpu.VMEM((slots, chips + 1, share, width), BF),
            pltpu.VMEM((slots, share, width), F32),
            pltpu.VMEM((slots, share, width), F32),
            pltpu.VMEM((2, 2, 2, units // 4, shard), BF),
            pltpu.VMEM((4, 2, 2, shard // 4, units), BF),
            pltpu.VMEM((2, 2, 3, shard // 2, channels), BF),
            pltpu.VMEM((2, 2, channels // 2, shard), BF),
            pltpu.VMEM((8, channels), F32),
            pltpu.VMEM((8, width), F32),
            pltpu.VMEM((models, 8, channels), F32),
            pltpu.VMEM((seqs, 8, channels), F32),
            pltpu.SemaphoreType.DMA((2 * slots + 5,)),
            pltpu.SemaphoreType.DMA((2,)),
            pltpu.SemaphoreType.DMA((8, max(6, seqs - 1))),
            pltpu.SemaphoreType.DMA((8, max(6, seqs - 1))),
            pltpu.SemaphoreType.DMA((8, 3)),
            pltpu.SemaphoreType.DMA((slots,)),
            pltpu.SemaphoreType.DMA((slots,)),
            pltpu.SemaphoreType.REGULAR((slots,)),
            pltpu.SemaphoreType.DMA((2, models - 1)),
            pltpu.SemaphoreType.DMA((2, models - 1)),
            pltpu.SemaphoreType.DMA((seqs - 1,)),
            pltpu.SemaphoreType.DMA((seqs - 1,)),
            *gather_sems(slots, chips),
            *scatter_sems(2 * slots, chips),
        ],
        compiler_params=pltpu.CompilerParams(collective_id=3, has_side_effects=True, vmem_limit_bytes=VMEM_LIMIT),
    )(low, mlp_part, source, gain, gain_mlp_part, taps, in_full, out_full, normed_rows, gates, product, mixed, pair_grad, down_grad)


def local(
    hidden,
    cotangent,
    lengths,
    gain_mix,
    gain_mlp,
    conv_weight,
    mixer_in,
    mixer_out,
    gate_up,
    mlp_down,
):
    seqs, models = lax.axis_size("seq"), lax.axis_size("mp")
    seq_pos = lax.axis_index("seq")
    model_pos = lax.axis_index("mp")
    share = hidden.shape[1]
    channels = mixer_in.shape[2]
    taps = conv_weight.shape[0]
    local_taps = lax.dynamic_slice_in_dim(conv_weight, model_pos * channels, channels, 1)
    share_start = (seq_pos * models + model_pos) * share
    share_pos = share_start + jnp.arange(share, dtype=jnp.int32)
    mask = (share_pos[None, :] < lengths[:, None]).astype(F32)[:, :, None]
    top_low = (cotangent.astype(F32) * mask).astype(BF)
    (
        normed_rows,
        _,
        in_full,
        out_full,
        gates,
        product,
        mixed,
        middle,
        middle_grad,
        low,
        gain_mlp_part,
        mlp_part,
        _,
        pair_total,
        down_total,
    ) = forward(
        seqs,
        models,
        hidden,
        gain_mix[None],
        gain_mlp[None],
        top_low,
        local_taps,
        mixer_in,
        mixer_out,
        gate_up,
        mlp_down,
    )
    mlp_share, source_grad, small, in_got, out_got, pair_got, down_got = mixer_backward(
        seqs,
        models,
        low,
        mlp_part,
        hidden,
        gain_mix[None],
        gain_mlp_part,
        local_taps,
        in_full,
        out_full,
        normed_rows,
        gates,
        product,
        mixed,
        pair_total,
        down_total,
    )

    def total(got):
        return jnp.sum(got.astype(F32), axis=0)

    return (
        (mask * (middle + mlp_share)).astype(BF),
        source_grad + middle_grad,
        small[0],
        small[1],
        small[2 : 2 + taps],
        total(in_got),
        total(out_got),
        total(pair_got),
        total(down_got),
    )


def solution(mesh):
    placed = (
        P(None, ("seq", "mp"), None),
        P(None, ("seq", "mp"), None),
        P(),
        P(),
        P(),
        P(),
        P(None, "seq", "mp"),
        P("mp", "seq"),
        P(None, "seq", "mp"),
        P("mp", "seq"),
    )
    return jax.shard_map(
        local,
        mesh=mesh,
        in_specs=placed,
        out_specs=(
            P(None, ("seq", "mp"), None),
            P(None, ("seq", "mp"), None),
            P(),
            P(),
            P(),
            P(None, "seq", "mp"),
            P("mp", "seq"),
            P(None, "seq", "mp"),
            P("mp", "seq"),
        ),
        check_vma=False,
    )
```

```python
import functools

import jax
import jax.numpy as jnp
from jax import lax
from jax.experimental import pallas as pl
from jax.experimental.pallas import tpu as pltpu
from jax.sharding import PartitionSpec as P

EPS = 1e-05
MESH = pl.DeviceIdType.MESH
BF = jnp.bfloat16
F32 = jnp.float32
HALVES = 2
VMEM_LIMIT = 63 * 2**20


def nn(a, b):
    return lax.dot_general(a, b, (((1,), (0,)), ((), ())), preferred_element_type=F32)


def nt(a, b):
    return lax.dot_general(a, b, (((1,), (1,)), ((), ())), preferred_element_type=F32)


def tn(a, b):
    return lax.dot_general(a, b, (((0,), (0,)), ((), ())), preferred_element_type=F32)


class Place:
    def __init__(self, seqs, models):
        self.seqs, self.chips = seqs, models // 2
        self.s = lax.axis_index("seq")
        self.m = lax.axis_index("mp")
        self.z = self.m // 2
        self.c = self.m % 2
        self.sibling = {"mp": self.m + 1 - 2 * self.c}
        self.above = {"mp": self.m + 2}
        self.below = {"mp": self.m - 2}
        self.has_above = self.z < self.chips - 1
        self.has_below = self.z > 0

    def peer(self, step):
        return {"seq": lax.rem(self.s + step, self.seqs)}

    def enter(self):
        barrier = pltpu.get_barrier_semaphore()
        models = 2 * self.chips
        peers = [{"mp": lax.rem(self.m + step, models)} for step in range(1, models)]
        for where in peers + [self.peer(step) for step in range(1, self.seqs)]:
            pl.semaphore_signal(barrier, inc=1, device_id=where, device_id_type=MESH)
        pl.semaphore_wait(barrier, models + self.seqs - 2)


def remote(src, dst, send, recv, where):
    return pltpu.make_async_remote_copy(
        src_ref=src, dst_ref=dst, send_sem=send, recv_sem=recv, device_id=where, device_id_type=MESH
    )


class Gather:
    def __init__(self, place, rows, own, sems):
        self.p, self.rows, self.own = place, rows, own
        self.share = rows.shape[0] // (2 * place.chips)
        self.piece = self.share // HALVES
        self.send, self.recv = sems

    def at(self, chip, core, half):
        return self.rows.at[pl.ds((chip * 2 + core) * self.share + half * self.piece, self.piece)]

    def copy(self, kind, chip, half, own=False):
        p = self.p
        where = (p.above, p.below, p.sibling)[kind]
        dst = self.at(chip, p.c, half)
        src = self.own.at[pl.ds(half * self.piece, self.piece)] if own and self.own is not None else dst
        return remote(src, dst, self.send.at[kind, chip, half], self.recv.at[kind // 2, chip, half], where)

    def start(self):
        p = self.p
        for half in range(HALVES):
            pl.when(p.has_above)(lambda h=half: self.copy(0, p.z, h, True).start())
            pl.when(p.has_below)(lambda h=half: self.copy(1, p.z, h, True).start())
        for half in range(HALVES):
            self.copy(2, p.z, half, True).start()

    def round(self, k):
        p = self.p
        for half in range(HALVES):

            @pl.when(p.z >= k)
            def _(half=half):
                chip = p.z - k
                self.copy(0, chip, half).wait_recv()
                pl.when(p.has_above)(lambda: self.copy(0, chip, half).start())
                self.copy(2, chip, half).start()

            @pl.when(p.z + k <= p.chips - 1)
            def _(half=half):
                chip = p.z + k
                self.copy(1, chip, half).wait_recv()
                pl.when(p.has_below)(lambda: self.copy(1, chip, half).start())
                self.copy(2, chip, half).start()

    def rounds(self):
        return [functools.partial(self.round, k) for k in range(1, self.p.chips)]

    def other_core(self, chip):
        p = self.p
        for half in range(HALVES):
            dst = self.at(chip, 1 - p.c, half)
            remote(dst, dst, self.send.at[2, chip, half], self.recv.at[1, chip, half], p.sibling).wait_recv()

    def arrived(self):
        for chip in range(self.p.chips):
            self.other_core(chip)

    def drain(self):
        p = self.p
        for chip in range(p.chips):
            for half in range(HALVES):
                pl.when(p.has_above & (chip <= p.z))(lambda ch=chip, h=half: self.copy(0, ch, h).wait_send())
                pl.when(p.has_below & (chip >= p.z))(lambda ch=chip, h=half: self.copy(1, ch, h).wait_send())
                self.copy(2, chip, half).wait_send()


class Scatter:
    def __init__(self, place, part, from_core, from_line, sems):
        self.p, self.part, self.from_core, self.from_line = place, part, from_core, from_line
        self.share = from_core.shape[1]
        self.piece = self.share // HALVES
        self.core_send, self.core_recv, self.line_send, self.line_recv = sems

    def rows(self, chip, core):
        return self.part.at[pl.ds((chip * 2 + core) * self.share, self.share)]

    def core_copy(self, chip):
        p = self.p
        return remote(
            self.rows(chip, 1 - p.c), self.from_core.at[chip], self.core_send.at[chip], self.core_recv.at[chip], p.sibling
        )

    def give(self, chip):
        self.core_copy(chip).start()

    def mine(self, chip, half):
        return self.part.at[pl.ds((chip * 2 + self.p.c) * self.share + half * self.piece, self.piece)]

    def line_copy(self, down, chip, slot, half):
        p = self.p
        dst = self.from_line.at[slot, pl.ds(half * self.piece, self.piece)]
        return remote(
            self.mine(chip, half),
            dst,
            self.line_send.at[down, chip, half],
            self.line_recv.at[slot, half],
            p.below if down else p.above,
        )

    def total(self, chip, half, slots):
        span = pl.ds(half * self.piece, self.piece)
        value = self.mine(chip, half)[...].astype(F32) + self.from_core[chip, span].astype(F32)
        for slot in slots:
            value = value + self.from_line[slot, span].astype(F32)
        return value

    def hop(self, down, chip, slot, has_source):
        self.core_copy(chip).wait_recv()
        for half in range(HALVES):

            @pl.when(has_source)
            def _(half=half):
                self.line_copy(down, chip, chip, half).wait_recv()
                self.mine(chip, half)[...] = self.total(chip, half, [chip]).astype(BF)

            @pl.when(jnp.logical_not(has_source))
            def _(half=half):
                self.mine(chip, half)[...] = self.total(chip, half, []).astype(BF)

            self.line_copy(down, chip, slot, half).start()

    def round(self, r):
        p = self.p
        last = p.chips - 1

        @pl.when((p.z <= r) & p.has_above)
        def _():
            chip = last - r + p.z
            self.hop(0, chip, chip, p.has_below)

        @pl.when((last - p.z <= r) & p.has_below)
        def _():
            chip = r - last + p.z
            self.hop(1, chip, p.chips if r == last - 1 else chip, p.has_above)

    def rounds(self):
        return [functools.partial(self.round, r) for r in range(self.p.chips - 1)]

    def finish(self, store):
        p = self.p
        self.core_copy(p.z).wait_recv()
        for half in range(HALVES):
            pl.when(p.has_below)(lambda h=half: self.line_copy(0, p.z, p.z, h).wait_recv())
            pl.when(p.has_above)(lambda h=half: self.line_copy(1, p.z, p.chips, h).wait_recv())
            for up in (False, True):
                for low in (False, True):

                    @pl.when((p.has_above == up) & (p.has_below == low))
                    def _(half=half, up=up, low=low):
                        slots = ([p.z] if low else []) + ([p.chips] if up else [])
                        store(half * self.piece, self.piece, self.total(p.z, half, slots))

    def drain(self):
        p = self.p
        for chip in range(p.chips):
            self.core_copy(chip).wait_send()
            for half in range(HALVES):
                pl.when(p.has_above & (chip > p.z))(lambda ch=chip, h=half: self.line_copy(0, ch, ch, h).wait_send())
                pl.when(p.has_below & (chip < p.z))(lambda ch=chip, h=half: self.line_copy(1, ch, ch, h).wait_send())


class StraightScatter(Scatter):
    def straight(self, chip, half):
        p = self.p
        return remote(
            self.mine(chip, half),
            self.from_line.at[p.z, pl.ds(half * self.piece, self.piece)],
            self.line_send.at[0, chip, half],
            self.line_recv.at[p.z, half],
            {"mp": chip * 2 + p.c},
        )

    def came(self, chip, half):
        view = self.from_line.at[chip, pl.ds(half * self.piece, self.piece)]
        return remote(view, view, self.line_send.at[0, chip, half], self.line_recv.at[chip, half], self.p.sibling)

    def go(self, chip):
        self.core_copy(chip).wait_recv()
        for half in range(HALVES):
            self.mine(chip, half)[...] = self.total(chip, half, []).astype(BF)
            self.straight(chip, half).start()

    def others(self):
        return [lax.rem(self.p.z + step, self.p.chips) for step in range(1, self.p.chips)]

    def finish(self, store):
        self.core_copy(self.p.z).wait_recv()
        for half in range(HALVES):
            for chip in self.others():
                self.came(chip, half).wait_recv()
            store(half * self.piece, self.piece, self.total(self.p.z, half, self.others()))

    def drain(self):
        for chip in range(self.p.chips):
            self.core_copy(chip).wait_send()
        for chip in self.others():
            for half in range(HALVES):
                self.straight(chip, half).wait_send()


def gather_sems(count, chips):
    return [pltpu.SemaphoreType.DMA((count, 3, chips, HALVES)), pltpu.SemaphoreType.DMA((count, 2, chips, HALVES))]


def scatter_sems(count, chips):
    return [
        pltpu.SemaphoreType.DMA((count, chips)),
        pltpu.SemaphoreType.DMA((count, chips)),
        pltpu.SemaphoreType.DMA((count, 2, chips, HALVES)),
        pltpu.SemaphoreType.DMA((count, chips + 1, HALVES)),
    ]


def picks(sems, index):
    return [sem.at[index] for sem in sems]


def far_first(place):
    low, high = 0, place.chips - 1
    inner = 1 - place.z // (place.chips // 2)
    order = []
    for _ in range(place.chips):
        left = 2 * place.z - low - high + inner > 0
        order.append(jnp.where(left, low, high))
        low, high = jnp.where(left, low + 1, low), jnp.where(left, high, high - 1)
    return order


def weave(*lists):
    for step in range(max(len(steps) for steps in lists)):
        for steps in lists:
            if step < len(steps):
                steps[step]()


class Relay:
    def __init__(self, place, shard, full, first, size, sems):
        self.p, self.shard, self.full, self.first, self.size = place, shard, full, first, size
        self.send, self.recv, self.local = sems
        s = place.s
        self.square = place.seqs == 4
        if self.square:
            self.near = (s + 1 - 2 * lax.rem(s, 2), lax.rem(s + 2, 4))

    def half(self, index):
        return self.first + index * (self.size // 2), self.size // 2

    def direct(self, index, where):
        return remote(
            self.shard(self.first, self.size),
            self.full(self.p.s, self.first, self.size),
            self.send.at[index],
            self.recv.at[index],
            where,
        )

    def handed(self, index):
        view = self.full(self.near[index], *self.half(index))
        return remote(view, view, self.send.at[2 + index], self.recv.at[2 + index], {"seq": self.near[1 - index]})

    def local_copy(self):
        return pltpu.make_async_copy(
            self.shard(self.first, self.size), self.full(self.p.s, self.first, self.size), self.local
        )

    def copies(self):
        if self.square:
            return [self.direct(index, {"seq": self.near[index]}) for index in range(2)]
        return [self.direct(step - 1, self.p.peer(step)) for step in range(1, self.p.seqs)]

    def start(self):
        for thing in self.copies():
            thing.start()
        self.local_copy().start()

    def forward(self):
        if self.square:
            for thing in self.copies():
                thing.wait_recv()
            for index in range(2):
                self.handed(index).start()

    def arrived(self):
        self.local_copy().wait()
        for thing in [self.handed(index) for index in range(2)] if self.square else self.copies():
            thing.wait_recv()

    def drain(self):
        for thing in self.copies() + ([self.handed(index) for index in range(2)] if self.square else []):
            thing.wait_send()


def forward_kernel(
    seqs,
    models,
    source_ref,
    gain_mix_ref,
    gain_ref,
    top_ref,
    taps_ref,
    in_ref,
    out_ref,
    pair_ref,
    down_ref,
    normed_rows,
    top_rows,
    in_rows,
    out_rows,
    gates_out,
    product_out,
    mixed_out,
    middle_out,
    grad_out,
    low_out,
    gain_out,
    mlp_part,
    act_rows,
    pair_grad,
    down_grad,
    in_full,
    out_full,
    rows,
    gates,
    ends,
    product,
    mixed,
    pair,
    down,
    top_tile,
    acts,
    act_stage,
    stage,
    part,
    from_core,
    from_line,
    total,
    w_send,
    w_recv,
    w_local,
    halo_send,
    halo_recv,
    keep,
    tile_sem,
    out_sem,
    cols_sem,
    pair_sem,
    ends_sem,
    *sems,
):
    p = Place(seqs, models)
    chips = p.chips
    g_sems, s_sems = sems[:2], sems[2:]
    slots, block, width = rows.shape
    units = down.shape[0]
    tile = block // chips
    share = tile // 2
    channels = in_full.shape[2]
    shard = width // seqs
    unit_block = min(512, units)
    wide_block = 512
    gain_out[...] = jnp.zeros_like(gain_out)

    def first_norm(slot):
        for first in range(0, share, share // HALVES):
            value = source_ref[slot, pl.ds(first, share // HALVES)].astype(F32)
            scale = lax.rsqrt(jnp.mean(value * value, axis=-1, keepdims=True) + EPS)
            rows[slot, pl.ds(p.m * share + first, share // HALVES)] = (value * scale * gain_mix_ref[...]).astype(BF)

    first_norm(0)
    p.enter()

    firsts = [Gather(p, rows.at[slot], None, picks(g_sems, slot)) for slot in range(slots)]
    tops = [Gather(p, top_rows.at[slot], top_ref.at[slot], picks(g_sems, slots + slot)) for slot in range(slots)]
    seconds = [Gather(p, rows.at[slot], None, picks(g_sems, 2 * slots + slot)) for slot in range(slots)]

    def scatter(slot, index, kind=Scatter):
        return kind(p, part.at[slot], from_core.at[slot], from_line.at[slot], picks(s_sems, index))

    mix_sums = [scatter(slot, slot) for slot in range(slots)]
    grad_sums = [scatter(0, slots), scatter(1, slots + 1, StraightScatter)]

    def columns_of(owner):
        return pl.ds(pl.multiple_of(owner * shard, shard), shard)

    def pair_views(k):
        return (
            lambda first, size: pair_ref.at[k, pl.ds(first, size)],
            lambda owner, first, size: pair.at[k, pl.ds(owner * shard + first, size)],
        )

    views = [
        (
            lambda first, size: in_ref.at[:, pl.ds(first, size)],
            lambda owner, first, size: in_full.at[:, pl.ds(owner * shard + first, size)],
            0,
            shard,
        ),
        (
            lambda first, size: out_ref.at[pl.ds(first, size)],
            lambda owner, first, size: out_full.at[pl.ds(first, size), columns_of(owner)],
            0,
            channels,
        ),
    ]
    for i in range(2):
        views.append(
            (
                lambda first, size: down_ref.at[pl.ds(first, size)],
                lambda owner, first, size: down.at[pl.ds(first, size), columns_of(owner)],
                i * (units // 2),
                units // 2,
            )
        )
    for i in range(4):
        views.append((*pair_views(i // 2), (i % 2) * (shard // 2), shard // 2))
    pieces = [Relay(p, *view, (w_send.at[i], w_recv.at[i], w_local.at[i])) for i, view in enumerate(views)]
    early, late = pieces[:2], pieces[2:]
    moves = [[("start", 0), ("start", 1)], [("forward", 0), ("start", 2)], [("forward", 1), ("start", 3)]]
    moves += [[("forward", 2)], [("forward", 3)], [("start", 4), ("start", 5)], [("forward", 4)], [("forward", 5)]]

    def push():
        for name, index in moves.pop(0):
            getattr(late[index], name)()

    def own(slot):
        span = pl.ds(p.m * share, share)
        return pltpu.make_async_copy(top_ref.at[slot], top_rows.at[slot, span], keep.at[slot])

    for slot in range(slots):
        own(slot).start()

    def saved(index, src, dst):
        return pltpu.make_async_copy(src, dst, keep.at[2 * slots + index])

    rows_saved = [saved(slot, rows.at[slot], normed_rows.at[slot]) for slot in range(slots)]
    gates_saved = [saved(slots + slot, gates, gates_out.at[slot, 1]) for slot in range(slots)]
    middle_saved = [saved(2 * slots + slot, total.at[slot], middle_out.at[slot]) for slot in range(slots)]
    grad_saved = [saved(3 * slots + slot, total.at[slot], grad_out.at[slot]) for slot in range(slots)]
    low_saved = [
        saved(4 * slots + 6 + slot, stage.at[pl.ds(slot * share, share)], low_out.at[slot]) for slot in range(slots)
    ]
    own_tops = [
        saved(5 * slots + 6 + slot, top_ref.at[slot], top_tile.at[pl.ds(slot * share, share)]) for slot in range(slots)
    ]
    in_saved = saved(4 * slots, in_full, in_rows)
    out_saved = saved(4 * slots + 1, out_full, out_rows)
    product_saved = saved(4 * slots + 2, product, product_out)
    mixed_saved = [saved(6 * slots + 6 + slot, mixed, mixed_out.at[slot]) for slot in range(slots)]
    down_saved = saved(4 * slots + 4, down, down_grad)
    act_load = saved(4 * slots + 5, act_rows, acts.at[0])

    def halo(slot):
        return remote(
            product.at[slot, pl.ds(block, 8)],
            product.at[slot, pl.ds(0, 8)],
            halo_send.at[slot],
            halo_recv.at[slot],
            p.peer(1),
        )

    has_later, has_earlier = p.s < seqs - 1, p.s > 0
    for slot in range(slots):

        @pl.when(jnp.logical_not(has_earlier))
        def _(slot=slot):
            product[slot, pl.ds(0, 8)] = jnp.zeros((8, channels), F32)

    def ends_saved(slot, i):
        span = pl.ds(i * tile, tile)
        return [
            pltpu.make_async_copy(ends.at[j], gates_out.at[slot, 2 * j, span], ends_sem.at[j]) for j in range(2)
        ]

    def project(slot):
        @pl.loop(0, chips)
        def _(i):
            span = pl.ds(i * tile, tile)
            source = rows[slot, span]
            b_gate = nn(source, in_full[0])
            x_value = nn(source, in_full[2])
            gates[span] = nn(source, in_full[1])

            @pl.when(i > 0)
            def _():
                for thing in ends_saved(slot, i - 1):
                    thing.wait()

            ends[0] = b_gate
            ends[1] = x_value
            for thing in ends_saved(slot, i):
                thing.start()
            product[slot, pl.ds(8 + i * tile, tile)] = b_gate * x_value

        for thing in ends_saved(slot, chips - 1):
            thing.wait()
        pl.when(has_later)(lambda: halo(slot).start())

    def convolve(slot):
        pl.when(has_earlier)(lambda: halo(slot).wait_recv())
        for i in range(chips):
            conv = 0.0
            for offset in range(taps_ref.shape[0]):
                conv = conv + taps_ref[offset : offset + 1] * product[slot, pl.ds(8 + i * tile - offset, tile)]
            mixed[pl.ds(i * tile, tile)] = (gates[pl.ds(i * tile, tile)] * conv).astype(BF)

    def project_out(slot):
        for chip in far_first(p):
            span = pl.ds(chip * tile, tile)
            part[slot, span] = nn(mixed[span], out_full[...]).astype(BF)
            mix_sums[slot].give(chip)
        mixed_saved[slot].start()

    def middle(slot):
        def store(first, size, value):
            span = pl.ds(first, size)
            value = value + source_ref[slot, span].astype(F32)
            total[slot, span] = value
            scale = lax.rsqrt(jnp.mean(value * value, axis=-1, keepdims=True) + EPS)
            rows[slot, pl.ds(p.m * share + first, size)] = (value * scale * gain_ref[...]).astype(BF)

        mix_sums[slot].finish(store)
        middle_saved[slot].start()
        mix_sums[slot].drain()

    def finish_grad(slot):
        middle_saved[slot].wait()

        def store(first, size, value):
            span = pl.ds(first, size)
            at = pl.ds(slot * share + first, size)
            middle = total[slot, span]
            scale = lax.rsqrt(jnp.mean(middle * middle, axis=-1, keepdims=True) + EPS)
            unit = middle * scale
            gain_out[0:1] += jnp.sum(value * unit, axis=0, keepdims=True)
            scaled = value * gain_ref[...]
            grad = scale * (scaled - unit * jnp.mean(scaled * unit, axis=-1, keepdims=True))
            grad = grad + top_tile[at].astype(F32)
            total[slot, span] = grad
            stage[at] = grad.astype(BF)

        grad_sums[slot].finish(store)
        grad_saved[slot].start()
        low_saved[slot].start()

    order = far_first(p)
    tiles = [(0, chip) for chip in order] + [(slot, chip) for slot in range(1, slots) for chip in order[::-1]]

    def fetch(index):
        slot, chip = tiles[index]
        return pltpu.make_async_copy(top_rows.at[slot, pl.ds(chip * tile, tile)], top_tile, tile_sem)

    def puts(index):
        slot, chip = tiles[index]
        span = pl.ds(chip * tile, tile)
        return [
            pltpu.make_async_copy(stage, mlp_part.at[slot, span], out_sem.at[0]),
            pltpu.make_async_copy(act_stage, act_rows.at[slot, span], out_sem.at[1]),
        ]

    def work(index):
        slot, chip = tiles[index]
        span = pl.ds(chip * tile, tile)
        if index % chips == 0:
            fetch(index).start()
        fetch(index).wait()
        if index:
            for thing in puts(index - 1):
                thing.wait()

        @pl.loop(0, units // unit_block)
        def _(i):
            cut = pl.ds(pl.multiple_of(i * unit_block, unit_block), unit_block)
            source = rows[slot, span]
            gate = nn(source, pair[0, :, cut])
            up = nn(source, pair[1, :, cut])
            act_grad = nt(top_tile[...], down[cut])
            sigma = jax.nn.sigmoid(gate)
            silu = gate * sigma
            act_stage[:, cut] = (silu * up).astype(BF)
            acts[0, slot, span, cut] = (act_grad * up * sigma * (1.0 + gate * (1.0 - sigma))).astype(BF)
            acts[1, slot, span, cut] = (act_grad * silu).astype(BF)

        if (index + 1) % chips:
            fetch(index + 1).start()

        @pl.loop(0, width // wide_block)
        def _(i):
            cut = pl.ds(pl.multiple_of(i * wide_block, wide_block), wide_block)
            value = nt(acts[0, slot, span], pair[0, cut]) + nt(acts[1, slot, span], pair[1, cut])
            part[slot, span, cut] = value.astype(BF)
            stage[:, cut] = nn(act_stage[...], down[:, cut]).astype(BF)

        grad_sums[slot].give(chip)
        for thing in puts(index):
            thing.start()

    pair_block = 512
    pair_steps = 2 * (width // pair_block)

    def pair_saved(index):
        k, first = divmod(index, width // pair_block)
        cut = pl.ds(first * pair_block, pair_block)
        return pltpu.make_async_copy(pair.at[k, cut], pair_grad.at[k, cut], pair_sem.at[index])

    def pair_step(index):
        k, first = divmod(index, width // pair_block)
        cut = pl.ds(first * pair_block, pair_block)
        value = 0.0
        for slot in range(slots):
            value = value + tn(rows[slot, :, cut], acts[k, slot])
        pair[k, cut] = value.astype(BF)
        pair_saved(index).start()
        if first == width // pair_block - 1 and k == 0:
            act_load.start()

    def fetch_columns(index):
        cut = pl.ds(index * channels, channels)
        return [
            pltpu.make_async_copy(
                top_rows.at[slot, :, cut], in_full.at[index % 2, pl.ds(slot * block, block)], cols_sem.at[index % 2, slot]
            )
            for slot in range(slots)
        ]

    def down_step(index):
        if index == 0:
            act_load.wait()
        for thing in fetch_columns(index):
            thing.wait()
        for first in range(0, units, unit_block):
            cut = pl.ds(first, unit_block)
            value = 0.0
            for slot in range(slots):
                value = value + tn(acts[0, slot, :, cut], in_full[index % 2, pl.ds(slot * block, block)])
            down[cut, pl.ds(index * channels, channels)] = value.astype(BF)
        if index + 2 < width // channels:
            for thing in fetch_columns(index + 2):
                thing.start()

    firsts[0].start()
    for piece in early:
        piece.start()
    first_norm(1)
    steps = firsts[0].rounds()
    for step in steps[:-1]:
        step()
    for piece in early:
        piece.forward()
    firsts[1].start()
    steps[-1]()
    firsts[0].arrived()
    rows_saved[0].start()
    for piece in early:
        piece.arrived()
    in_saved.start()
    out_saved.start()
    project(0)
    gates_saved[0].start()
    push()
    steps = firsts[1].rounds()
    steps[0]()
    push()
    rows_saved[0].wait()
    firsts[0].drain()
    convolve(0)
    project_out(0)
    weave(mix_sums[0].rounds(), steps[1:-1] + [tops[0].start, steps[-1]], [push] * 3)
    firsts[1].arrived()
    rows_saved[1].start()
    gates_saved[0].wait()
    project(1)
    gates_saved[1].start()
    push()
    middle(0)
    seconds[0].start()
    rows_saved[1].wait()
    firsts[1].drain()
    mixed_saved[0].wait()
    convolve(1)
    project_out(1)
    hops, steps, more = mix_sums[1].rounds(), tops[0].rounds(), seconds[0].rounds()
    weave(steps, hops, [push] * 2)
    weave(more[:-1])
    tops[1].start()
    more[-1]()
    middle(1)
    seconds[1].start()
    product_saved.start()
    own(0).wait()
    tops[0].arrived()
    seconds[0].arrived()
    for piece in late:
        piece.arrived()
    own(1).wait()
    hops, steps, more = grad_sums[0].rounds(), tops[1].rounds(), seconds[1].rounds()
    for index in range(chips):
        work(index)
        if index < len(steps):
            steps[index]()
        if 0 < index:
            hops[index - 1]()
    more[0]()
    tops[1].arrived()
    for index in range(chips):
        seconds[1].other_core(tiles[chips + index][1])
        work(chips + index)
        if 0 < index < chips - 1:
            grad_sums[1].go(tiles[chips + index][1])
        if index + 1 < len(more):
            more[index + 1]()
    for thing in puts(len(tiles) - 1):
        thing.wait()
    for thing in own_tops:
        thing.start()
    grad_sums[1].go(tiles[-1][1])
    in_saved.wait()
    for piece in pieces:
        piece.drain()
    for index in range(2):
        for thing in fetch_columns(index):
            thing.start()
    for thing in own_tops:
        thing.wait()
    finish_grad(0)
    work_steps = [functools.partial(pair_step, index) for index in range(pair_steps)]
    work_steps += [functools.partial(down_step, index) for index in range(width // channels)]
    for step in work_steps:
        step()
    down_saved.start()
    finish_grad(1)
    for index in range(pair_steps):
        pair_saved(index).wait()
    for thing in [gates_saved[1], out_saved, product_saved, mixed_saved[1], down_saved, *grad_saved, *low_saved]:
        thing.wait()
    for thing in tops + seconds + grad_sums:
        thing.drain()
    for slot in range(slots):
        pl.when(has_later)(lambda slot=slot: halo(slot).wait_send())


def forward(seqs, models, source, gain_mix, gain, top, taps, mixer_in, mixer_out, gate_up, mlp_down):
    slots, share, width = source.shape
    chips = models // 2
    block = share * models
    channels = mixer_in.shape[2]
    units = gate_up.shape[2]
    tile = block // chips
    hbm = pl.BlockSpec(memory_space=pltpu.HBM)
    vmem = pl.BlockSpec(memory_space=pltpu.VMEM)
    shape = jax.ShapeDtypeStruct
    return pl.pallas_call(
        functools.partial(forward_kernel, seqs, models),
        out_shape=[
            shape((slots, block, width), BF),
            shape((slots, block, width), BF),
            shape((3, width, channels), BF),
            shape((channels, width), BF),
            shape((slots, 3, block, channels), F32),
            shape((slots, block + 8, channels), F32),
            shape((slots, block, channels), BF),
            shape((slots, share, width), F32),
            shape((slots, share, width), F32),
            shape((slots, share, width), BF),
            shape((8, width), F32),
            shape((slots, block, width), BF),
            shape((slots, block, units), BF),
            shape((2, width, units), BF),
            shape((units, width), BF),
        ],
        in_specs=[vmem, vmem, vmem, hbm, vmem] + [hbm] * 4,
        out_specs=[hbm] * 10 + [vmem] + [hbm] * 4,
        scratch_shapes=[
            pltpu.VMEM((3, width, channels), BF),
            pltpu.VMEM((channels, width), BF),
            pltpu.VMEM((slots, block, width), BF),
            pltpu.VMEM((block, channels), F32),
            pltpu.VMEM((2, tile, channels), F32),
            pltpu.VMEM((slots, block + 8, channels), F32),
            pltpu.VMEM((block, channels), BF),
            pltpu.VMEM((2, width, units), BF),
            pltpu.VMEM((units, width), BF),
            pltpu.VMEM((tile, width), BF),
            pltpu.VMEM((2, slots, block, units), BF),
            pltpu.VMEM((tile, units), BF),
            pltpu.VMEM((tile, width), BF),
            pltpu.VMEM((slots, block, width), BF),
            pltpu.VMEM((slots, chips, share, width), BF),
            pltpu.VMEM((slots, chips + 1, share, width), BF),
            pltpu.VMEM((slots, share, width), F32),
            pltpu.SemaphoreType.DMA((8, max(4, seqs - 1))),
            pltpu.SemaphoreType.DMA((8, max(4, seqs - 1))),
            pltpu.SemaphoreType.DMA((8,)),
            pltpu.SemaphoreType.DMA((slots,)),
            pltpu.SemaphoreType.DMA((slots,)),
            pltpu.SemaphoreType.DMA((10 * slots + 6,)),
            pltpu.SemaphoreType.DMA,
            pltpu.SemaphoreType.DMA((2,)),
            pltpu.SemaphoreType.DMA((2, slots)),
            pltpu.SemaphoreType.DMA((2 * (width // 512),)),
            pltpu.SemaphoreType.DMA((2,)),
            *gather_sems(3 * slots, chips),
            *scatter_sems(2 * slots, chips),
        ],
        compiler_params=pltpu.CompilerParams(collective_id=1, has_side_effects=True, vmem_limit_bytes=VMEM_LIMIT),
    )(source, gain_mix, gain, top, taps, mixer_in, mixer_out, gate_up, mlp_down)


class Exchange:
    def __init__(self, place, partial, got, first, size, sems, held, came):
        self.p, self.partial, self.got, self.first, self.size = place, partial, got, first, size
        self.send, self.recv, self.local = sems
        self.held, self.came = held, came
        s = place.s
        self.square = place.seqs == 4
        if self.square:
            self.near = (s + 1 - 2 * lax.rem(s, 2), lax.rem(s + 2, 4))
            self.across = 3 - s

    def half(self, index):
        return self.first + index * (self.size // 2), self.size // 2

    def to(self, index):
        return {"seq": self.near[index]}

    def relayed(self, index):
        return remote(
            self.partial(self.across, *self.half(index)),
            self.came.at[index],
            self.send.at[index],
            self.recv.at[index],
            self.to(index),
        )

    def plain(self, index):
        span = self.half(index)
        return remote(
            self.partial(self.near[index], *span),
            self.got(1 + index, *span),
            self.send.at[2 + index],
            self.recv.at[2 + index],
            self.to(index),
        )

    def added(self, index):
        return remote(
            self.held.at[1 - index],
            self.got(1 + index, *self.half(1 - index)),
            self.send.at[4 + index],
            self.recv.at[4 + index],
            self.to(index),
        )

    def load(self, index):
        return pltpu.make_async_copy(
            self.partial(self.near[index], *self.half(1 - index)), self.held.at[1 - index], self.local.at[1 + index]
        )

    def straight(self, step):
        p = self.p
        return remote(
            self.partial(lax.rem(p.s + step, p.seqs), self.first, self.size),
            self.got(step, self.first, self.size),
            self.send.at[step - 1],
            self.recv.at[step - 1],
            p.peer(step),
        )

    def own(self):
        return pltpu.make_async_copy(
            self.partial(self.p.s, self.first, self.size), self.got(0, self.first, self.size), self.local.at[0]
        )

    def copies(self):
        if self.square:
            return [self.relayed(0), self.relayed(1), self.plain(0), self.plain(1)]
        return [self.straight(step) for step in range(1, self.p.seqs)]

    def start(self):
        for thing in self.copies():
            thing.start()
        if self.square:
            for index in range(2):
                self.load(index).start()
        self.own().start()

    def forward(self):
        if self.square:
            for index in range(2):
                self.load(index).wait()
                self.relayed(1 - index).wait_recv()
                total = self.held[1 - index].astype(F32) + self.came[1 - index].astype(F32)
                self.held[1 - index] = total.astype(BF)
                self.added(index).start()

    def finish(self):
        self.own().wait()
        if self.square:
            for thing in self.copies():
                thing.wait_send()
            for index in range(2):
                self.plain(index).wait_recv()
                self.added(index).wait()
        else:
            for thing in self.copies():
                thing.wait()


def mixer_backward_kernel(
    seqs,
    models,
    low_ref,
    mlp_part,
    source_ref,
    gain_ref,
    gain_mlp_ref,
    taps_ref,
    in_ref,
    out_ref,
    normed_rows,
    gates_ref,
    product_ref,
    mixed_ref,
    pair_grad,
    down_grad,
    mlp_out,
    grad_out,
    small_out,
    in_got,
    out_got,
    pair_got,
    down_got,
    in_full,
    out_full,
    rows,
    columns,
    gates,
    product,
    mixed,
    conv_grad,
    stacked,
    part,
    from_core,
    from_line,
    mlp_total,
    grad_total,
    down_room,
    pair_room,
    in_room,
    out_room,
    taps_out,
    small,
    by_model,
    by_seq,
    load,
    cols_sem,
    w_send,
    w_recv,
    w_local,
    halo_send,
    halo_recv,
    free,
    mp_send,
    mp_recv,
    seq_send,
    seq_recv,
    *sems,
):
    p = Place(seqs, models)
    chips = p.chips
    g_sems, s_sems = sems[:2], sems[2:]
    slots, block, width = rows.shape
    channels = out_full.shape[0]
    taps = taps_ref.shape[0]
    tile = block // chips
    share = tile // 2
    wide_block = 512
    cols = columns.shape[-1]
    loads = [
        pltpu.make_async_copy(src, dst, load.at[i])
        for i, (src, dst) in enumerate(
            [(mlp_part.at[slot], part.at[slot]) for slot in range(slots)]
            + [
                (low_ref.at[slot], rows.at[slot, pl.ds(p.m * share, share)])
                for slot in range(slots)
            ]
            + [
                (in_ref, in_full),
                (out_ref, out_full),
                (gates_ref, gates),
                (product_ref, product),
                (mixed_ref, mixed),
            ]
        )
    ]
    for thing in loads:
        thing.start()
    p.enter()
    gathers = [Gather(p, rows.at[slot], low_ref.at[slot], picks(g_sems, slot)) for slot in range(slots)]

    def scatter(slot, index):
        return Scatter(p, part.at[slot], from_core.at[slot], from_line.at[slot], picks(s_sems, index))

    mlp_sums = [scatter(slot, slot) for slot in range(slots)]
    sums = [scatter(slot, slots + slot) for slot in range(slots)]
    shard = width // seqs
    units = down_grad.shape[0]

    def columns_of(owner):
        return pl.ds(pl.multiple_of(owner * shard, shard), shard)

    views = []
    for i in range(2):
        views.append(
            (
                lambda owner, first, size: down_grad.at[pl.ds(first, size), columns_of(owner)],
                lambda index, first, size: down_got.at[index, pl.ds(first, size)],
                i * (units // 2),
                units // 2,
                down_room.at[i],
            )
        )
    for i in range(4):
        views.append(
            (
                lambda owner, first, size, k=i // 2: pair_grad.at[k, pl.ds(owner * shard + first, size)],
                lambda index, first, size, k=i // 2: pair_got.at[index, k, pl.ds(first, size)],
                (i % 2) * (shard // 2),
                shard // 2,
                pair_room.at[i],
            )
        )
    views.append(
        (
            lambda owner, first, size: in_full.at[:, pl.ds(owner * shard + first, size)],
            lambda index, first, size: in_got.at[index, :, pl.ds(first, size)],
            0,
            shard,
            in_room,
        )
    )
    views.append(
        (
            lambda owner, first, size: out_full.at[pl.ds(first, size), columns_of(owner)],
            lambda index, first, size: out_got.at[index, pl.ds(first, size)],
            0,
            channels,
            out_room,
        )
    )
    pieces = [
        Exchange(p, *view[:4], (w_send.at[i], w_recv.at[i], w_local.at[i]), view[4].at[0], view[4].at[1])
        for i, view in enumerate(views)
    ]
    moves = [[("start", 0), ("start", 1)], [("forward", 0), ("start", 2)], [("forward", 1), ("start", 3)]]
    moves += [[("forward", 2)], [("forward", 3)], [("start", 4), ("start", 5)], [("forward", 4)], [("forward", 5)]]

    def push():
        for name, index in moves.pop(0):
            getattr(pieces[index], name)()

    has_later, has_earlier = p.s < seqs - 1, p.s > 0
    order = far_first(p)

    def halo(slot):
        return remote(
            conv_grad.at[slot, pl.ds(0, 8)],
            conv_grad.at[slot, pl.ds(block, 8)],
            halo_send.at[slot],
            halo_recv.at[slot],
            p.peer(seqs - 1),
        )

    for slot in range(slots):

        @pl.when(jnp.logical_not(has_later))
        def _(slot=slot):
            conv_grad[slot, pl.ds(block, 8)] = jnp.zeros((8, channels), F32)

    taps_out[...] = jnp.zeros_like(taps_out)
    small[...] = jnp.zeros_like(small)
    small[1:2] = gain_mlp_ref[0:1]

    def first_pass(slot):
        for i in range(chips):
            span = pl.ds(i * tile, tile)
            mixed_grad = nt(rows[slot, span], out_full[...])
            grad = mixed_grad * gates[slot, 1, span]
            conv_grad[slot, span] = grad
            conv = 0.0
            for offset in range(taps):
                earlier = product[slot, pl.ds(8 + i * tile - offset, tile)]
                conv = conv + taps_ref[offset : offset + 1] * earlier
                taps_out[offset : offset + 1] += jnp.sum(grad * earlier, axis=0, keepdims=True)
            stacked[slot, span, pl.ds(channels, channels)] = (mixed_grad * conv).astype(BF)
            if i == 0:
                pl.when(has_earlier)(lambda: halo(slot).start())

    def second_pass(slot):
        pl.when(has_later)(lambda: halo(slot).wait_recv())
        for i in range(chips):
            span = pl.ds(i * tile, tile)
            grad = 0.0
            for offset in range(taps):
                grad = grad + taps_ref[offset : offset + 1] * conv_grad[slot, pl.ds(i * tile + offset, tile)]
            stacked[slot, span, pl.ds(0, channels)] = (grad * gates[slot, 2, span]).astype(BF)
            stacked[slot, span, pl.ds(2 * channels, channels)] = (grad * gates[slot, 0, span]).astype(BF)

    def third_pass(slot):
        for chip in order:
            span = pl.ds(chip * tile, tile)

            @pl.loop(0, width // wide_block)
            def _(i):
                cut = pl.ds(pl.multiple_of(i * wide_block, wide_block), wide_block)
                value = 0.0
                for k in range(3):
                    value = value + nt(stacked[slot, span, pl.ds(k * channels, channels)], in_full[k, cut])
                part[slot, span, cut] = value.astype(BF)

            sums[slot].give(chip)

    def finish_mlp(slot):
        def store(first, size, value):
            mlp_total[slot, pl.ds(first, size)] = value

        mlp_sums[slot].finish(store)

    def finish_grad(slot):
        def store(first, size, value):
            span = pl.ds(first, size)
            source = source_ref[slot, span].astype(F32)
            scale = lax.rsqrt(jnp.mean(source * source, axis=-1, keepdims=True) + EPS)
            unit = source * scale
            small[0:1] += jnp.sum(value * unit, axis=0, keepdims=True)
            scaled = value * gain_ref[...]
            grad_total[slot, span] = scale * (scaled - unit * jnp.mean(scaled * unit, axis=-1, keepdims=True))

        sums[slot].finish(store)

    def mine(owner):
        return pl.ds(pl.multiple_of(owner * channels, channels), channels)

    def small_sums():
        small[2 : 2 + taps, mine(p.m)] = taps_out[0:taps]
        along = [lax.rem(p.m + step, models) for step in range(1, models)]
        by_model[p.m] = small[:, mine(p.m)]
        copies = [
            remote(small.at[:, mine(peer)], by_model.at[p.m], mp_send.at[0, i], mp_recv.at[0, i], {"mp": peer})
            for i, peer in enumerate(along)
        ]
        for thing in copies:
            thing.start()
        for thing in copies:
            thing.wait()
        by_seq[p.s] = functools.reduce(lambda a, b: a + b, [by_model[i] for i in range(models)])
        copies = [
            remote(by_seq.at[p.s], by_seq.at[p.s], seq_send.at[step - 1], seq_recv.at[step - 1], p.peer(step))
            for step in range(1, seqs)
        ]
        for thing in copies:
            thing.start()
        for thing in copies:
            thing.wait()
        small_out[:, mine(p.m)] = functools.reduce(lambda a, b: a + b, [by_seq[i] for i in range(seqs)])
        copies = [
            remote(small_out.at[:, mine(p.m)], small_out.at[:, mine(p.m)], mp_send.at[1, i], mp_recv.at[1, i], {"mp": peer})
            for i, peer in enumerate(along)
        ]
        for thing in copies:
            thing.start()
        for thing in copies:
            thing.wait()

    def neighbours(act):
        act(p.sibling)
        pl.when(p.has_above)(lambda: act(p.above))
        pl.when(p.has_below)(lambda: act(p.below))

    def give_free(slot):
        mlp_sums[slot].drain()
        neighbours(
            lambda where: pl.semaphore_signal(free.at[slot], inc=1, device_id=where, device_id_type=MESH)
        )

    def take_free(slot):
        lines = (p.z + chips - 1) // chips + (2 * chips - 2 - p.z) // chips
        pl.semaphore_wait(free.at[slot], 1 + lines)

    def fetch_columns(index):
        return pltpu.make_async_copy(
            normed_rows.at[:, :, pl.ds(index * cols, cols)], columns.at[index % 2], cols_sem.at[index % 2]
        )

    steps_in = width // cols

    def in_step(index):
        fetch_columns(index).wait()
        value = 0.0
        for slot in range(slots):
            value = value + tn(columns[index % 2, slot], stacked[slot])
        for k in range(3):
            in_full[k, pl.ds(index * cols, cols)] = value[:, k * channels : (k + 1) * channels].astype(BF)
        if index + 2 < steps_in:
            fetch_columns(index + 2).start()

    def out_step():
        for first in range(0, width, wide_block):
            cut = pl.ds(first, wide_block)
            value = 0.0
            for slot in range(slots):
                value = value + tn(mixed[slot], rows[slot, :, cut])
            out_full[:, cut] = value.astype(BF)

    gathers[0].start()
    push()
    loads[0].wait()
    for chip in order:
        mlp_sums[0].give(chip)
    hops, next_rows = mlp_sums[0].rounds(), gathers[0].rounds()
    weave(hops[:-1], next_rows[:-1], [push] * 2)
    gathers[1].start()
    weave(hops[-1:], next_rows[-1:], [push])
    loads[1].wait()
    for chip in order:
        mlp_sums[1].give(chip)
    loads[2].wait()
    for thing in loads[2 + slots :]:
        thing.wait()
    gathers[0].arrived()
    push()
    fetch_columns(0).start()
    fetch_columns(1).start()
    mlp_hops, next_rows, hops = mlp_sums[1].rounds(), gathers[1].rounds(), sums[0].rounds()
    first_pass(0)
    push()
    finish_mlp(0)
    give_free(0)
    weave(mlp_hops[:1], next_rows[:1])
    second_pass(0)
    take_free(0)
    third_pass(0)
    weave(mlp_hops[1:], next_rows[1:], hops[:1], [push] * 2)
    loads[3].wait()
    gathers[1].arrived()
    first_pass(1)
    finish_mlp(1)
    give_free(1)
    hops[1]()
    second_pass(1)
    take_free(1)
    weave(hops[2:])
    third_pass(1)
    hops = sums[1].rounds()
    hops[0]()
    out_step()
    pieces[7].start()
    for index in range(steps_in):
        in_step(index)
    pieces[6].start()
    hops[1]()
    pieces[7].forward()
    pieces[6].forward()
    weave(hops[2:])
    finish_grad(0)
    finish_grad(1)
    last = [
        pltpu.make_async_copy(mlp_total, mlp_out, load.at[0]),
        pltpu.make_async_copy(grad_total, grad_out, load.at[1]),
    ]
    for thing in last:
        thing.start()
    small_sums()
    for thing in pieces:
        thing.finish()
    for thing in last:
        thing.wait()
    for thing in gathers + sums:
        thing.drain()
    for slot in range(slots):
        pl.when(has_earlier)(lambda slot=slot: halo(slot).wait_send())


def mixer_backward(
    seqs, models, low, mlp_part, source, gain, gain_mlp_part, taps, in_full, out_full, normed_rows, gates, product, mixed, pair_grad, down_grad
):
    slots, share, width = low.shape
    chips = models // 2
    block = share * models
    channels = out_full.shape[0]
    units = down_grad.shape[0]
    shard = width // seqs
    gots = 3 if seqs == 4 else seqs
    hbm = pl.BlockSpec(memory_space=pltpu.HBM)
    vmem = pl.BlockSpec(memory_space=pltpu.VMEM)
    shape = jax.ShapeDtypeStruct
    return pl.pallas_call(
        functools.partial(mixer_backward_kernel, seqs, models),
        out_shape=[
            shape((slots, share, width), F32),
            shape((slots, share, width), F32),
            shape((8, width), F32),
            shape((gots, 3, shard, channels), BF),
            shape((gots, channels, shard), BF),
            shape((gots, 2, shard, units), BF),
            shape((gots, units, shard), BF),
        ],
        in_specs=[hbm, hbm, vmem, vmem, vmem, vmem] + [hbm] * 8,
        out_specs=[hbm, hbm, vmem] + [hbm] * 4,
        scratch_shapes=[
            pltpu.VMEM((3, width, channels), BF),
            pltpu.VMEM((channels, width), BF),
            pltpu.VMEM((slots, block, width), BF),
            pltpu.VMEM((2, slots, block, 256), BF),
            pltpu.VMEM((slots, 3, block, channels), F32),
            pltpu.VMEM((slots, block + 8, channels), F32),
            pltpu.VMEM((slots, block, channels), BF),
            pltpu.VMEM((slots, block + 8, channels), F32),
            pltpu.VMEM((slots, block, 3 * channels), BF),
            pltpu.VMEM((slots, block, width), BF),
            pltpu.VMEM((slots, chips, share, width), BF),
            pltpu.VMEM((slots, chips + 1, share, width), BF),
            pltpu.VMEM((slots, share, width), F32),
            pltpu.VMEM((slots, share, width), F32),
            pltpu.VMEM((2, 2, 2, units // 4, shard), BF),
            pltpu.VMEM((4, 2, 2, shard // 4, units), BF),
            pltpu.VMEM((2, 2, 3, shard // 2, channels), BF),
            pltpu.VMEM((2, 2, channels // 2, shard), BF),
            pltpu.VMEM((8, channels), F32),
            pltpu.VMEM((8, width), F32),
            pltpu.VMEM((models, 8, channels), F32),
            pltpu.VMEM((seqs, 8, channels), F32),
            pltpu.SemaphoreType.DMA((2 * slots + 5,)),
            pltpu.SemaphoreType.DMA((2,)),
            pltpu.SemaphoreType.DMA((8, max(6, seqs - 1))),
            pltpu.SemaphoreType.DMA((8, max(6, seqs - 1))),
            pltpu.SemaphoreType.DMA((8, 3)),
            pltpu.SemaphoreType.DMA((slots,)),
            pltpu.SemaphoreType.DMA((slots,)),
            pltpu.SemaphoreType.REGULAR((slots,)),
            pltpu.SemaphoreType.DMA((2, models - 1)),
            pltpu.SemaphoreType.DMA((2, models - 1)),
            pltpu.SemaphoreType.DMA((seqs - 1,)),
            pltpu.SemaphoreType.DMA((seqs - 1,)),
            *gather_sems(slots, chips),
            *scatter_sems(2 * slots, chips),
        ],
        compiler_params=pltpu.CompilerParams(collective_id=3, has_side_effects=True, vmem_limit_bytes=VMEM_LIMIT),
    )(low, mlp_part, source, gain, gain_mlp_part, taps, in_full, out_full, normed_rows, gates, product, mixed, pair_grad, down_grad)


def local(
    hidden,
    cotangent,
    lengths,
    gain_mix,
    gain_mlp,
    conv_weight,
    mixer_in,
    mixer_out,
    gate_up,
    mlp_down,
):
    seqs, models = lax.axis_size("seq"), lax.axis_size("mp")
    seq_pos = lax.axis_index("seq")
    model_pos = lax.axis_index("mp")
    share = hidden.shape[1]
    channels = mixer_in.shape[2]
    taps = conv_weight.shape[0]
    local_taps = lax.dynamic_slice_in_dim(conv_weight, model_pos * channels, channels, 1)
    share_start = (seq_pos * models + model_pos) * share
    share_pos = share_start + jnp.arange(share, dtype=jnp.int32)
    mask = (share_pos[None, :] < lengths[:, None]).astype(F32)[:, :, None]
    top_low = (cotangent.astype(F32) * mask).astype(BF)
    (
        normed_rows,
        _,
        in_full,
        out_full,
        gates,
        product,
        mixed,
        middle,
        middle_grad,
        low,
        gain_mlp_part,
        mlp_part,
        _,
        pair_total,
        down_total,
    ) = forward(
        seqs,
        models,
        hidden,
        gain_mix[None],
        gain_mlp[None],
        top_low,
        local_taps,
        mixer_in,
        mixer_out,
        gate_up,
        mlp_down,
    )
    mlp_share, source_grad, small, in_got, out_got, pair_got, down_got = mixer_backward(
        seqs,
        models,
        low,
        mlp_part,
        hidden,
        gain_mix[None],
        gain_mlp_part,
        local_taps,
        in_full,
        out_full,
        normed_rows,
        gates,
        product,
        mixed,
        pair_total,
        down_total,
    )

    def total(got):
        return jnp.sum(got.astype(F32), axis=0)

    return (
        (mask * (middle + mlp_share)).astype(BF),
        source_grad + middle_grad,
        small[0],
        small[1],
        small[2 : 2 + taps],
        total(in_got),
        total(out_got),
        total(pair_got),
        total(down_got),
    )


def solution(mesh):
    placed = (
        P(None, ("seq", "mp"), None),
        P(None, ("seq", "mp"), None),
        P(),
        P(),
        P(),
        P(),
        P(None, "seq", "mp"),
        P("mp", "seq"),
        P(None, "seq", "mp"),
        P("mp", "seq"),
    )
    return jax.shard_map(
        local,
        mesh=mesh,
        in_specs=placed,
        out_specs=(
            P(None, ("seq", "mp"), None),
            P(None, ("seq", "mp"), None),
            P(),
            P(),
            P(),
            P(None, "seq", "mp"),
            P("mp", "seq"),
            P(None, "seq", "mp"),
            P("mp", "seq"),
        ),
        check_vma=False,
    )
```

```python
import functools

import jax
import jax.numpy as jnp
from jax import lax
from jax.experimental import pallas as pl
from jax.experimental.pallas import tpu as pltpu
from jax.sharding import PartitionSpec as P

EPS = 1e-05
MESH = pl.DeviceIdType.MESH
BF = jnp.bfloat16
F32 = jnp.float32
HALVES = 2
VMEM_LIMIT = 63 * 2**20


def nn(a, b):
    return lax.dot_general(a, b, (((1,), (0,)), ((), ())), preferred_element_type=F32)


def nt(a, b):
    return lax.dot_general(a, b, (((1,), (1,)), ((), ())), preferred_element_type=F32)


def tn(a, b):
    return lax.dot_general(a, b, (((0,), (0,)), ((), ())), preferred_element_type=F32)


class Place:
    def __init__(self, seqs, models):
        self.seqs, self.chips = seqs, models // 2
        self.s = lax.axis_index("seq")
        self.m = lax.axis_index("mp")
        self.z = self.m // 2
        self.c = self.m % 2
        self.sibling = {"mp": self.m + 1 - 2 * self.c}
        self.above = {"mp": self.m + 2}
        self.below = {"mp": self.m - 2}
        self.has_above = self.z < self.chips - 1
        self.has_below = self.z > 0

    def peer(self, step):
        return {"seq": lax.rem(self.s + step, self.seqs)}

    def enter(self):
        barrier = pltpu.get_barrier_semaphore()
        models = 2 * self.chips
        peers = [{"mp": lax.rem(self.m + step, models)} for step in range(1, models)]
        for where in peers + [self.peer(step) for step in range(1, self.seqs)]:
            pl.semaphore_signal(barrier, inc=1, device_id=where, device_id_type=MESH)
        pl.semaphore_wait(barrier, models + self.seqs - 2)


def remote(src, dst, send, recv, where):
    return pltpu.make_async_remote_copy(
        src_ref=src, dst_ref=dst, send_sem=send, recv_sem=recv, device_id=where, device_id_type=MESH
    )


class Gather:
    def __init__(self, place, rows, own, sems):
        self.p, self.rows, self.own = place, rows, own
        self.share = rows.shape[0] // (2 * place.chips)
        self.piece = self.share // HALVES
        self.send, self.recv = sems

    def at(self, chip, core, half):
        return self.rows.at[pl.ds((chip * 2 + core) * self.share + half * self.piece, self.piece)]

    def copy(self, kind, chip, half, own=False):
        p = self.p
        where = (p.above, p.below, p.sibling)[kind]
        dst = self.at(chip, p.c, half)
        src = self.own.at[pl.ds(half * self.piece, self.piece)] if own and self.own is not None else dst
        return remote(src, dst, self.send.at[kind, chip, half], self.recv.at[kind // 2, chip, half], where)

    def start(self):
        p = self.p
        for half in range(HALVES):
            pl.when(p.has_above)(lambda h=half: self.copy(0, p.z, h, True).start())
            pl.when(p.has_below)(lambda h=half: self.copy(1, p.z, h, True).start())
        for half in range(HALVES):
            self.copy(2, p.z, half, True).start()

    def round(self, k):
        p = self.p
        for half in range(HALVES):

            @pl.when(p.z >= k)
            def _(half=half):
                chip = p.z - k
                self.copy(0, chip, half).wait_recv()
                pl.when(p.has_above)(lambda: self.copy(0, chip, half).start())
                self.copy(2, chip, half).start()

            @pl.when(p.z + k <= p.chips - 1)
            def _(half=half):
                chip = p.z + k
                self.copy(1, chip, half).wait_recv()
                pl.when(p.has_below)(lambda: self.copy(1, chip, half).start())
                self.copy(2, chip, half).start()

    def rounds(self):
        return [functools.partial(self.round, k) for k in range(1, self.p.chips)]

    def other_core(self, chip):
        p = self.p
        for half in range(HALVES):
            dst = self.at(chip, 1 - p.c, half)
            remote(dst, dst, self.send.at[2, chip, half], self.recv.at[1, chip, half], p.sibling).wait_recv()

    def arrived(self):
        for chip in range(self.p.chips):
            self.other_core(chip)

    def drain(self):
        p = self.p
        for chip in range(p.chips):
            for half in range(HALVES):
                pl.when(p.has_above & (chip <= p.z))(lambda ch=chip, h=half: self.copy(0, ch, h).wait_send())
                pl.when(p.has_below & (chip >= p.z))(lambda ch=chip, h=half: self.copy(1, ch, h).wait_send())
                self.copy(2, chip, half).wait_send()


class Scatter:
    def __init__(self, place, part, from_core, from_line, sems):
        self.p, self.part, self.from_core, self.from_line = place, part, from_core, from_line
        self.share = from_core.shape[1]
        self.piece = self.share // HALVES
        self.core_send, self.core_recv, self.line_send, self.line_recv = sems

    def rows(self, chip, core):
        return self.part.at[pl.ds((chip * 2 + core) * self.share, self.share)]

    def core_copy(self, chip):
        p = self.p
        return remote(
            self.rows(chip, 1 - p.c), self.from_core.at[chip], self.core_send.at[chip], self.core_recv.at[chip], p.sibling
        )

    def give(self, chip):
        self.core_copy(chip).start()

    def mine(self, chip, half):
        return self.part.at[pl.ds((chip * 2 + self.p.c) * self.share + half * self.piece, self.piece)]

    def line_copy(self, down, chip, slot, half):
        p = self.p
        dst = self.from_line.at[slot, pl.ds(half * self.piece, self.piece)]
        return remote(
            self.mine(chip, half),
            dst,
            self.line_send.at[down, chip, half],
            self.line_recv.at[slot, half],
            p.below if down else p.above,
        )

    def total(self, chip, half, slots):
        span = pl.ds(half * self.piece, self.piece)
        value = self.mine(chip, half)[...].astype(F32) + self.from_core[chip, span].astype(F32)
        for slot in slots:
            value = value + self.from_line[slot, span].astype(F32)
        return value

    def hop(self, down, chip, slot, has_source):
        self.core_copy(chip).wait_recv()
        for half in range(HALVES):

            @pl.when(has_source)
            def _(half=half):
                self.line_copy(down, chip, chip, half).wait_recv()
                self.mine(chip, half)[...] = self.total(chip, half, [chip]).astype(BF)

            @pl.when(jnp.logical_not(has_source))
            def _(half=half):
                self.mine(chip, half)[...] = self.total(chip, half, []).astype(BF)

            self.line_copy(down, chip, slot, half).start()

    def round(self, r):
        p = self.p
        last = p.chips - 1

        @pl.when((p.z <= r) & p.has_above)
        def _():
            chip = last - r + p.z
            self.hop(0, chip, chip, p.has_below)

        @pl.when((last - p.z <= r) & p.has_below)
        def _():
            chip = r - last + p.z
            self.hop(1, chip, p.chips if r == last - 1 else chip, p.has_above)

    def rounds(self):
        return [functools.partial(self.round, r) for r in range(self.p.chips - 1)]

    def finish(self, store):
        p = self.p
        self.core_copy(p.z).wait_recv()
        for half in range(HALVES):
            pl.when(p.has_below)(lambda h=half: self.line_copy(0, p.z, p.z, h).wait_recv())
            pl.when(p.has_above)(lambda h=half: self.line_copy(1, p.z, p.chips, h).wait_recv())
            for up in (False, True):
                for low in (False, True):

                    @pl.when((p.has_above == up) & (p.has_below == low))
                    def _(half=half, up=up, low=low):
                        slots = ([p.z] if low else []) + ([p.chips] if up else [])
                        store(half * self.piece, self.piece, self.total(p.z, half, slots))

    def drain(self):
        p = self.p
        for chip in range(p.chips):
            self.core_copy(chip).wait_send()
            for half in range(HALVES):
                pl.when(p.has_above & (chip > p.z))(lambda ch=chip, h=half: self.line_copy(0, ch, ch, h).wait_send())
                pl.when(p.has_below & (chip < p.z))(lambda ch=chip, h=half: self.line_copy(1, ch, ch, h).wait_send())


class StraightScatter(Scatter):
    def straight(self, chip, half):
        p = self.p
        return remote(
            self.mine(chip, half),
            self.from_line.at[p.z, pl.ds(half * self.piece, self.piece)],
            self.line_send.at[0, chip, half],
            self.line_recv.at[p.z, half],
            {"mp": chip * 2 + p.c},
        )

    def came(self, chip, half):
        view = self.from_line.at[chip, pl.ds(half * self.piece, self.piece)]
        return remote(view, view, self.line_send.at[0, chip, half], self.line_recv.at[chip, half], self.p.sibling)

    def go(self, chip):
        self.core_copy(chip).wait_recv()
        for half in range(HALVES):
            self.mine(chip, half)[...] = self.total(chip, half, []).astype(BF)
            self.straight(chip, half).start()

    def others(self):
        return [lax.rem(self.p.z + step, self.p.chips) for step in range(1, self.p.chips)]

    def finish(self, store):
        self.core_copy(self.p.z).wait_recv()
        for half in range(HALVES):
            for chip in self.others():
                self.came(chip, half).wait_recv()
            store(half * self.piece, self.piece, self.total(self.p.z, half, self.others()))

    def drain(self):
        for chip in range(self.p.chips):
            self.core_copy(chip).wait_send()
        for chip in self.others():
            for half in range(HALVES):
                self.straight(chip, half).wait_send()


def gather_sems(count, chips):
    return [pltpu.SemaphoreType.DMA((count, 3, chips, HALVES)), pltpu.SemaphoreType.DMA((count, 2, chips, HALVES))]


def scatter_sems(count, chips):
    return [
        pltpu.SemaphoreType.DMA((count, chips)),
        pltpu.SemaphoreType.DMA((count, chips)),
        pltpu.SemaphoreType.DMA((count, 2, chips, HALVES)),
        pltpu.SemaphoreType.DMA((count, chips + 1, HALVES)),
    ]


def picks(sems, index):
    return [sem.at[index] for sem in sems]


def far_first(place):
    low, high = 0, place.chips - 1
    inner = 1 - place.z // (place.chips // 2)
    order = []
    for _ in range(place.chips):
        left = 2 * place.z - low - high + inner > 0
        order.append(jnp.where(left, low, high))
        low, high = jnp.where(left, low + 1, low), jnp.where(left, high, high - 1)
    return order


def weave(*lists):
    for step in range(max(len(steps) for steps in lists)):
        for steps in lists:
            if step < len(steps):
                steps[step]()


class Relay:
    def __init__(self, place, shard, full, first, size, sems):
        self.p, self.shard, self.full, self.first, self.size = place, shard, full, first, size
        self.send, self.recv, self.local = sems
        s = place.s
        self.square = place.seqs == 4
        if self.square:
            self.near = (s + 1 - 2 * lax.rem(s, 2), lax.rem(s + 2, 4))

    def half(self, index):
        return self.first + index * (self.size // 2), self.size // 2

    def direct(self, index, where):
        return remote(
            self.shard(self.first, self.size),
            self.full(self.p.s, self.first, self.size),
            self.send.at[index],
            self.recv.at[index],
            where,
        )

    def handed(self, index):
        view = self.full(self.near[index], *self.half(index))
        return remote(view, view, self.send.at[2 + index], self.recv.at[2 + index], {"seq": self.near[1 - index]})

    def local_copy(self):
        return pltpu.make_async_copy(
            self.shard(self.first, self.size), self.full(self.p.s, self.first, self.size), self.local
        )

    def copies(self):
        if self.square:
            return [self.direct(index, {"seq": self.near[index]}) for index in range(2)]
        return [self.direct(step - 1, self.p.peer(step)) for step in range(1, self.p.seqs)]

    def start(self):
        for thing in self.copies():
            thing.start()
        self.local_copy().start()

    def forward(self):
        if self.square:
            for thing in self.copies():
                thing.wait_recv()
            for index in range(2):
                self.handed(index).start()

    def arrived(self):
        self.local_copy().wait()
        for thing in [self.handed(index) for index in range(2)] if self.square else self.copies():
            thing.wait_recv()

    def drain(self):
        for thing in self.copies() + ([self.handed(index) for index in range(2)] if self.square else []):
            thing.wait_send()


def forward_kernel(
    seqs,
    models,
    source_ref,
    gain_mix_ref,
    gain_ref,
    top_ref,
    taps_ref,
    in_ref,
    out_ref,
    pair_ref,
    down_ref,
    normed_rows,
    top_rows,
    in_rows,
    out_rows,
    gates_out,
    product_out,
    mixed_out,
    middle_out,
    grad_out,
    low_out,
    gain_out,
    mlp_part,
    act_rows,
    pair_grad,
    down_grad,
    in_full,
    out_full,
    rows,
    gates,
    ends,
    product,
    mixed,
    pair,
    down,
    top_tile,
    acts,
    act_stage,
    stage,
    part,
    from_core,
    from_line,
    total,
    w_send,
    w_recv,
    w_local,
    halo_send,
    halo_recv,
    keep,
    tile_sem,
    out_sem,
    cols_sem,
    pair_sem,
    ends_sem,
    *sems,
):
    p = Place(seqs, models)
    chips = p.chips
    g_sems, s_sems = sems[:2], sems[2:]
    slots, block, width = rows.shape
    units = down.shape[0]
    tile = block // chips
    share = tile // 2
    channels = in_full.shape[2]
    shard = width // seqs
    unit_block = min(512, units)
    wide_block = 512
    gain_out[...] = jnp.zeros_like(gain_out)

    def first_norm(slot):
        for first in range(0, share, share // HALVES):
            value = source_ref[slot, pl.ds(first, share // HALVES)].astype(F32)
            scale = lax.rsqrt(jnp.mean(value * value, axis=-1, keepdims=True) + EPS)
            rows[slot, pl.ds(p.m * share + first, share // HALVES)] = (value * scale * gain_mix_ref[...]).astype(BF)

    first_norm(0)
    p.enter()

    firsts = [Gather(p, rows.at[slot], None, picks(g_sems, slot)) for slot in range(slots)]
    tops = [Gather(p, top_rows.at[slot], top_ref.at[slot], picks(g_sems, slots + slot)) for slot in range(slots)]
    seconds = [Gather(p, rows.at[slot], None, picks(g_sems, 2 * slots + slot)) for slot in range(slots)]

    def scatter(slot, index, kind=Scatter):
        return kind(p, part.at[slot], from_core.at[slot], from_line.at[slot], picks(s_sems, index))

    mix_sums = [scatter(slot, slot) for slot in range(slots)]
    grad_sums = [scatter(0, slots), scatter(1, slots + 1, StraightScatter)]

    def columns_of(owner):
        return pl.ds(pl.multiple_of(owner * shard, shard), shard)

    def pair_views(k):
        return (
            lambda first, size: pair_ref.at[k, pl.ds(first, size)],
            lambda owner, first, size: pair.at[k, pl.ds(owner * shard + first, size)],
        )

    views = [
        (
            lambda first, size: in_ref.at[:, pl.ds(first, size)],
            lambda owner, first, size: in_full.at[:, pl.ds(owner * shard + first, size)],
            0,
            shard,
        ),
        (
            lambda first, size: out_ref.at[pl.ds(first, size)],
            lambda owner, first, size: out_full.at[pl.ds(first, size), columns_of(owner)],
            0,
            channels,
        ),
    ]
    for i in range(2):
        views.append(
            (
                lambda first, size: down_ref.at[pl.ds(first, size)],
                lambda owner, first, size: down.at[pl.ds(first, size), columns_of(owner)],
                i * (units // 2),
                units // 2,
            )
        )
    for i in range(4):
        views.append((*pair_views(i // 2), (i % 2) * (shard // 2), shard // 2))
    pieces = [Relay(p, *view, (w_send.at[i], w_recv.at[i], w_local.at[i])) for i, view in enumerate(views)]
    early, late = pieces[:2], pieces[2:]
    moves = [[("start", 0), ("start", 1)], [("forward", 0), ("start", 2)], [("forward", 1), ("start", 3)]]
    moves += [[("forward", 2)], [("forward", 3)], [("start", 4), ("start", 5)], [("forward", 4)], [("forward", 5)]]

    def push():
        for name, index in moves.pop(0):
            getattr(late[index], name)()

    def own(slot):
        span = pl.ds(p.m * share, share)
        return pltpu.make_async_copy(top_ref.at[slot], top_rows.at[slot, span], keep.at[slot])

    for slot in range(slots):
        own(slot).start()

    def saved(index, src, dst):
        return pltpu.make_async_copy(src, dst, keep.at[2 * slots + index])

    rows_saved = [saved(slot, rows.at[slot], normed_rows.at[slot]) for slot in range(slots)]
    gates_saved = [saved(slots + slot, gates, gates_out.at[slot, 1]) for slot in range(slots)]
    middle_saved = [saved(2 * slots + slot, total.at[slot], middle_out.at[slot]) for slot in range(slots)]
    grad_saved = [saved(3 * slots + slot, total.at[slot], grad_out.at[slot]) for slot in range(slots)]
    low_saved = [
        saved(4 * slots + 6 + slot, stage.at[pl.ds(slot * share, share)], low_out.at[slot]) for slot in range(slots)
    ]
    own_tops = [
        saved(5 * slots + 6 + slot, top_ref.at[slot], top_tile.at[pl.ds(slot * share, share)]) for slot in range(slots)
    ]
    in_saved = saved(4 * slots, in_full, in_rows)
    out_saved = saved(4 * slots + 1, out_full, out_rows)
    product_saved = saved(4 * slots + 2, product, product_out)
    mixed_saved = [saved(6 * slots + 6 + slot, mixed, mixed_out.at[slot]) for slot in range(slots)]
    down_saved = saved(4 * slots + 4, down, down_grad)
    act_load = saved(4 * slots + 5, act_rows, acts.at[0])

    def halo(slot):
        return remote(
            product.at[slot, pl.ds(block, 8)],
            product.at[slot, pl.ds(0, 8)],
            halo_send.at[slot],
            halo_recv.at[slot],
            p.peer(1),
        )

    has_later, has_earlier = p.s < seqs - 1, p.s > 0
    for slot in range(slots):

        @pl.when(jnp.logical_not(has_earlier))
        def _(slot=slot):
            product[slot, pl.ds(0, 8)] = jnp.zeros((8, channels), F32)

    def ends_saved(slot, i):
        span = pl.ds(i * tile, tile)
        return [
            pltpu.make_async_copy(ends.at[j], gates_out.at[slot, 2 * j, span], ends_sem.at[j]) for j in range(2)
        ]

    def project(slot):
        @pl.loop(0, chips)
        def _(i):
            span = pl.ds(i * tile, tile)
            source = rows[slot, span]
            b_gate = nn(source, in_full[0])
            x_value = nn(source, in_full[2])
            gates[span] = nn(source, in_full[1])

            @pl.when(i > 0)
            def _():
                for thing in ends_saved(slot, i - 1):
                    thing.wait()

            ends[0] = b_gate
            ends[1] = x_value
            for thing in ends_saved(slot, i):
                thing.start()
            product[slot, pl.ds(8 + i * tile, tile)] = b_gate * x_value

        for thing in ends_saved(slot, chips - 1):
            thing.wait()
        pl.when(has_later)(lambda: halo(slot).start())

    def convolve(slot):
        pl.when(has_earlier)(lambda: halo(slot).wait_recv())
        for i in range(chips):
            conv = 0.0
            for offset in range(taps_ref.shape[0]):
                conv = conv + taps_ref[offset : offset + 1] * product[slot, pl.ds(8 + i * tile - offset, tile)]
            mixed[pl.ds(i * tile, tile)] = (gates[pl.ds(i * tile, tile)] * conv).astype(BF)

    def project_out(slot):
        for chip in far_first(p):
            span = pl.ds(chip * tile, tile)
            part[slot, span] = nn(mixed[span], out_full[...]).astype(BF)
            mix_sums[slot].give(chip)
        mixed_saved[slot].start()

    def middle(slot):
        def store(first, size, value):
            span = pl.ds(first, size)
            value = value + source_ref[slot, span].astype(F32)
            total[slot, span] = value
            scale = lax.rsqrt(jnp.mean(value * value, axis=-1, keepdims=True) + EPS)
            rows[slot, pl.ds(p.m * share + first, size)] = (value * scale * gain_ref[...]).astype(BF)

        mix_sums[slot].finish(store)
        middle_saved[slot].start()
        mix_sums[slot].drain()

    def finish_grad(slot):
        middle_saved[slot].wait()

        def store(first, size, value):
            span = pl.ds(first, size)
            at = pl.ds(slot * share + first, size)
            middle = total[slot, span]
            scale = lax.rsqrt(jnp.mean(middle * middle, axis=-1, keepdims=True) + EPS)
            unit = middle * scale
            gain_out[0:1] += jnp.sum(value * unit, axis=0, keepdims=True)
            scaled = value * gain_ref[...]
            grad = scale * (scaled - unit * jnp.mean(scaled * unit, axis=-1, keepdims=True))
            grad = grad + top_tile[at].astype(F32)
            total[slot, span] = grad
            stage[at] = grad.astype(BF)

        grad_sums[slot].finish(store)
        grad_saved[slot].start()
        low_saved[slot].start()

    order = far_first(p)
    tiles = [(0, chip) for chip in order] + [(slot, chip) for slot in range(1, slots) for chip in order[::-1]]

    def fetch(index):
        slot, chip = tiles[index]
        return pltpu.make_async_copy(top_rows.at[slot, pl.ds(chip * tile, tile)], top_tile, tile_sem)

    def puts(index):
        slot, chip = tiles[index]
        span = pl.ds(chip * tile, tile)
        return [
            pltpu.make_async_copy(stage, mlp_part.at[slot, span], out_sem.at[0]),
            pltpu.make_async_copy(act_stage, act_rows.at[slot, span], out_sem.at[1]),
        ]

    def work(index, midway=None):
        slot, chip = tiles[index]
        span = pl.ds(chip * tile, tile)
        if index % chips == 0:
            fetch(index).start()
        fetch(index).wait()
        if index:
            for thing in puts(index - 1):
                thing.wait()

        @pl.loop(0, units // unit_block)
        def _(i):
            cut = pl.ds(pl.multiple_of(i * unit_block, unit_block), unit_block)
            source = rows[slot, span]
            gate = nn(source, pair[0, :, cut])
            up = nn(source, pair[1, :, cut])
            act_grad = nt(top_tile[...], down[cut])
            sigma = jax.nn.sigmoid(gate)
            silu = gate * sigma
            act_stage[:, cut] = (silu * up).astype(BF)
            acts[0, slot, span, cut] = (act_grad * up * sigma * (1.0 + gate * (1.0 - sigma))).astype(BF)
            acts[1, slot, span, cut] = (act_grad * silu).astype(BF)

        if (index + 1) % chips:
            fetch(index + 1).start()

        if midway:
            midway()

        @pl.loop(0, width // wide_block)
        def _(i):
            cut = pl.ds(pl.multiple_of(i * wide_block, wide_block), wide_block)
            value = nt(acts[0, slot, span], pair[0, cut]) + nt(acts[1, slot, span], pair[1, cut])
            part[slot, span, cut] = value.astype(BF)
            stage[:, cut] = nn(act_stage[...], down[:, cut]).astype(BF)

        grad_sums[slot].give(chip)
        for thing in puts(index):
            thing.start()

    pair_block = 512
    pair_steps = 2 * (width // pair_block)

    def pair_saved(index):
        k, first = divmod(index, width // pair_block)
        cut = pl.ds(first * pair_block, pair_block)
        return pltpu.make_async_copy(pair.at[k, cut], pair_grad.at[k, cut], pair_sem.at[index])

    def pair_step(index):
        k, first = divmod(index, width // pair_block)
        cut = pl.ds(first * pair_block, pair_block)
        value = 0.0
        for slot in range(slots):
            value = value + tn(rows[slot, :, cut], acts[k, slot])
        pair[k, cut] = value.astype(BF)
        pair_saved(index).start()
        if first == width // pair_block - 1 and k == 0:
            act_load.start()

    def fetch_columns(index):
        cut = pl.ds(index * channels, channels)
        return [
            pltpu.make_async_copy(
                top_rows.at[slot, :, cut], in_full.at[index % 2, pl.ds(slot * block, block)], cols_sem.at[index % 2, slot]
            )
            for slot in range(slots)
        ]

    def down_step(index):
        if index == 0:
            act_load.wait()
        for thing in fetch_columns(index):
            thing.wait()
        for first in range(0, units, unit_block):
            cut = pl.ds(first, unit_block)
            value = 0.0
            for slot in range(slots):
                value = value + tn(acts[0, slot, :, cut], in_full[index % 2, pl.ds(slot * block, block)])
            down[cut, pl.ds(index * channels, channels)] = value.astype(BF)
        if index + 2 < width // channels:
            for thing in fetch_columns(index + 2):
                thing.start()

    firsts[0].start()
    for piece in early:
        piece.start()
    first_norm(1)
    steps = firsts[0].rounds()
    for step in steps[:-1]:
        step()
    for piece in early:
        piece.forward()
    firsts[1].start()
    steps[-1]()
    firsts[0].arrived()
    rows_saved[0].start()
    for piece in early:
        piece.arrived()
    in_saved.start()
    out_saved.start()
    project(0)
    gates_saved[0].start()
    push()
    steps = firsts[1].rounds()
    steps[0]()
    push()
    rows_saved[0].wait()
    firsts[0].drain()
    convolve(0)
    project_out(0)
    weave(mix_sums[0].rounds(), steps[1:-1] + [tops[0].start, steps[-1]], [push] * 3)
    firsts[1].arrived()
    rows_saved[1].start()
    gates_saved[0].wait()
    project(1)
    gates_saved[1].start()
    push()
    middle(0)
    seconds[0].start()
    rows_saved[1].wait()
    firsts[1].drain()
    mixed_saved[0].wait()
    convolve(1)
    project_out(1)
    hops, steps, more = mix_sums[1].rounds(), tops[0].rounds(), seconds[0].rounds()
    weave(steps, hops, [push] * 2)
    weave(more[:-1])
    tops[1].start()
    more[-1]()
    middle(1)
    seconds[1].start()
    product_saved.start()
    own(0).wait()
    tops[0].arrived()
    seconds[0].arrived()
    for piece in late:
        piece.arrived()
    own(1).wait()
    hops, steps, more = grad_sums[0].rounds(), tops[1].rounds(), seconds[1].rounds()
    for index in range(chips):
        work(index, more[0] if index == chips - 1 else None)
        if index < len(steps):
            steps[index]()
        if 0 < index:
            hops[index - 1]()
    tops[1].arrived()
    for index in range(chips):
        seconds[1].other_core(tiles[chips + index][1])
        work(chips + index, more[index + 1] if index + 1 < len(more) else None)
        if 0 < index < chips - 1:
            grad_sums[1].go(tiles[chips + index][1])
    for thing in puts(len(tiles) - 1):
        thing.wait()
    for thing in own_tops:
        thing.start()
    grad_sums[1].go(tiles[-1][1])
    in_saved.wait()
    for piece in pieces:
        piece.drain()
    for index in range(2):
        for thing in fetch_columns(index):
            thing.start()
    for thing in own_tops:
        thing.wait()
    finish_grad(0)
    work_steps = [functools.partial(pair_step, index) for index in range(pair_steps)]
    work_steps += [functools.partial(down_step, index) for index in range(width // channels)]
    for step in work_steps:
        step()
    down_saved.start()
    finish_grad(1)
    for index in range(pair_steps):
        pair_saved(index).wait()
    for thing in [gates_saved[1], out_saved, product_saved, mixed_saved[1], down_saved, *grad_saved, *low_saved]:
        thing.wait()
    for thing in tops + seconds + grad_sums:
        thing.drain()
    for slot in range(slots):
        pl.when(has_later)(lambda slot=slot: halo(slot).wait_send())


def forward(seqs, models, source, gain_mix, gain, top, taps, mixer_in, mixer_out, gate_up, mlp_down):
    slots, share, width = source.shape
    chips = models // 2
    block = share * models
    channels = mixer_in.shape[2]
    units = gate_up.shape[2]
    tile = block // chips
    hbm = pl.BlockSpec(memory_space=pltpu.HBM)
    vmem = pl.BlockSpec(memory_space=pltpu.VMEM)
    shape = jax.ShapeDtypeStruct
    return pl.pallas_call(
        functools.partial(forward_kernel, seqs, models),
        out_shape=[
            shape((slots, block, width), BF),
            shape((slots, block, width), BF),
            shape((3, width, channels), BF),
            shape((channels, width), BF),
            shape((slots, 3, block, channels), F32),
            shape((slots, block + 8, channels), F32),
            shape((slots, block, channels), BF),
            shape((slots, share, width), F32),
            shape((slots, share, width), F32),
            shape((slots, share, width), BF),
            shape((8, width), F32),
            shape((slots, block, width), BF),
            shape((slots, block, units), BF),
            shape((2, width, units), BF),
            shape((units, width), BF),
        ],
        in_specs=[vmem, vmem, vmem, hbm, vmem] + [hbm] * 4,
        out_specs=[hbm] * 10 + [vmem] + [hbm] * 4,
        scratch_shapes=[
            pltpu.VMEM((3, width, channels), BF),
            pltpu.VMEM((channels, width), BF),
            pltpu.VMEM((slots, block, width), BF),
            pltpu.VMEM((block, channels), F32),
            pltpu.VMEM((2, tile, channels), F32),
            pltpu.VMEM((slots, block + 8, channels), F32),
            pltpu.VMEM((block, channels), BF),
            pltpu.VMEM((2, width, units), BF),
            pltpu.VMEM((units, width), BF),
            pltpu.VMEM((tile, width), BF),
            pltpu.VMEM((2, slots, block, units), BF),
            pltpu.VMEM((tile, units), BF),
            pltpu.VMEM((tile, width), BF),
            pltpu.VMEM((slots, block, width), BF),
            pltpu.VMEM((slots, chips, share, width), BF),
            pltpu.VMEM((slots, chips + 1, share, width), BF),
            pltpu.VMEM((slots, share, width), F32),
            pltpu.SemaphoreType.DMA((8, max(4, seqs - 1))),
            pltpu.SemaphoreType.DMA((8, max(4, seqs - 1))),
            pltpu.SemaphoreType.DMA((8,)),
            pltpu.SemaphoreType.DMA((slots,)),
            pltpu.SemaphoreType.DMA((slots,)),
            pltpu.SemaphoreType.DMA((10 * slots + 6,)),
            pltpu.SemaphoreType.DMA,
            pltpu.SemaphoreType.DMA((2,)),
            pltpu.SemaphoreType.DMA((2, slots)),
            pltpu.SemaphoreType.DMA((2 * (width // 512),)),
            pltpu.SemaphoreType.DMA((2,)),
            *gather_sems(3 * slots, chips),
            *scatter_sems(2 * slots, chips),
        ],
        compiler_params=pltpu.CompilerParams(collective_id=1, has_side_effects=True, vmem_limit_bytes=VMEM_LIMIT),
    )(source, gain_mix, gain, top, taps, mixer_in, mixer_out, gate_up, mlp_down)


class Exchange:
    def __init__(self, place, partial, got, first, size, sems, held, came):
        self.p, self.partial, self.got, self.first, self.size = place, partial, got, first, size
        self.send, self.recv, self.local = sems
        self.held, self.came = held, came
        s = place.s
        self.square = place.seqs == 4
        if self.square:
            self.near = (s + 1 - 2 * lax.rem(s, 2), lax.rem(s + 2, 4))
            self.across = 3 - s

    def half(self, index):
        return self.first + index * (self.size // 2), self.size // 2

    def to(self, index):
        return {"seq": self.near[index]}

    def relayed(self, index):
        return remote(
            self.partial(self.across, *self.half(index)),
            self.came.at[index],
            self.send.at[index],
            self.recv.at[index],
            self.to(index),
        )

    def plain(self, index):
        span = self.half(index)
        return remote(
            self.partial(self.near[index], *span),
            self.got(1 + index, *span),
            self.send.at[2 + index],
            self.recv.at[2 + index],
            self.to(index),
        )

    def added(self, index):
        return remote(
            self.held.at[1 - index],
            self.got(1 + index, *self.half(1 - index)),
            self.send.at[4 + index],
            self.recv.at[4 + index],
            self.to(index),
        )

    def load(self, index):
        return pltpu.make_async_copy(
            self.partial(self.near[index], *self.half(1 - index)), self.held.at[1 - index], self.local.at[1 + index]
        )

    def straight(self, step):
        p = self.p
        return remote(
            self.partial(lax.rem(p.s + step, p.seqs), self.first, self.size),
            self.got(step, self.first, self.size),
            self.send.at[step - 1],
            self.recv.at[step - 1],
            p.peer(step),
        )

    def own(self):
        return pltpu.make_async_copy(
            self.partial(self.p.s, self.first, self.size), self.got(0, self.first, self.size), self.local.at[0]
        )

    def copies(self):
        if self.square:
            return [self.relayed(0), self.relayed(1), self.plain(0), self.plain(1)]
        return [self.straight(step) for step in range(1, self.p.seqs)]

    def start(self):
        for thing in self.copies():
            thing.start()
        if self.square:
            for index in range(2):
                self.load(index).start()
        self.own().start()

    def forward(self):
        if self.square:
            for index in range(2):
                self.load(index).wait()
                self.relayed(1 - index).wait_recv()
                total = self.held[1 - index].astype(F32) + self.came[1 - index].astype(F32)
                self.held[1 - index] = total.astype(BF)
                self.added(index).start()

    def finish(self):
        self.own().wait()
        if self.square:
            for thing in self.copies():
                thing.wait_send()
            for index in range(2):
                self.plain(index).wait_recv()
                self.added(index).wait()
        else:
            for thing in self.copies():
                thing.wait()


def mixer_backward_kernel(
    seqs,
    models,
    low_ref,
    mlp_part,
    source_ref,
    gain_ref,
    gain_mlp_ref,
    taps_ref,
    in_ref,
    out_ref,
    normed_rows,
    gates_ref,
    product_ref,
    mixed_ref,
    pair_grad,
    down_grad,
    mlp_out,
    grad_out,
    small_out,
    in_got,
    out_got,
    pair_got,
    down_got,
    in_full,
    out_full,
    rows,
    columns,
    gates,
    product,
    mixed,
    conv_grad,
    stacked,
    part,
    from_core,
    from_line,
    mlp_total,
    grad_total,
    down_room,
    pair_room,
    in_room,
    out_room,
    taps_out,
    small,
    by_model,
    by_seq,
    load,
    cols_sem,
    w_send,
    w_recv,
    w_local,
    halo_send,
    halo_recv,
    free,
    mp_send,
    mp_recv,
    seq_send,
    seq_recv,
    *sems,
):
    p = Place(seqs, models)
    chips = p.chips
    g_sems, s_sems = sems[:2], sems[2:]
    slots, block, width = rows.shape
    channels = out_full.shape[0]
    taps = taps_ref.shape[0]
    tile = block // chips
    share = tile // 2
    wide_block = 512
    cols = columns.shape[-1]
    loads = [
        pltpu.make_async_copy(src, dst, load.at[i])
        for i, (src, dst) in enumerate(
            [(mlp_part.at[slot], part.at[slot]) for slot in range(slots)]
            + [
                (low_ref.at[slot], rows.at[slot, pl.ds(p.m * share, share)])
                for slot in range(slots)
            ]
            + [
                (in_ref, in_full),
                (out_ref, out_full),
                (gates_ref, gates),
                (product_ref, product),
                (mixed_ref, mixed),
            ]
        )
    ]
    for thing in loads:
        thing.start()
    p.enter()
    gathers = [Gather(p, rows.at[slot], low_ref.at[slot], picks(g_sems, slot)) for slot in range(slots)]

    def scatter(slot, index):
        return Scatter(p, part.at[slot], from_core.at[slot], from_line.at[slot], picks(s_sems, index))

    mlp_sums = [scatter(slot, slot) for slot in range(slots)]
    sums = [scatter(slot, slots + slot) for slot in range(slots)]
    shard = width // seqs
    units = down_grad.shape[0]

    def columns_of(owner):
        return pl.ds(pl.multiple_of(owner * shard, shard), shard)

    views = []
    for i in range(2):
        views.append(
            (
                lambda owner, first, size: down_grad.at[pl.ds(first, size), columns_of(owner)],
                lambda index, first, size: down_got.at[index, pl.ds(first, size)],
                i * (units // 2),
                units // 2,
                down_room.at[i],
            )
        )
    for i in range(4):
        views.append(
            (
                lambda owner, first, size, k=i // 2: pair_grad.at[k, pl.ds(owner * shard + first, size)],
                lambda index, first, size, k=i // 2: pair_got.at[index, k, pl.ds(first, size)],
                (i % 2) * (shard // 2),
                shard // 2,
                pair_room.at[i],
            )
        )
    views.append(
        (
            lambda owner, first, size: in_full.at[:, pl.ds(owner * shard + first, size)],
            lambda index, first, size: in_got.at[index, :, pl.ds(first, size)],
            0,
            shard,
            in_room,
        )
    )
    views.append(
        (
            lambda owner, first, size: out_full.at[pl.ds(first, size), columns_of(owner)],
            lambda index, first, size: out_got.at[index, pl.ds(first, size)],
            0,
            channels,
            out_room,
        )
    )
    pieces = [
        Exchange(p, *view[:4], (w_send.at[i], w_recv.at[i], w_local.at[i]), view[4].at[0], view[4].at[1])
        for i, view in enumerate(views)
    ]
    moves = [[("start", 0), ("start", 1)], [("forward", 0), ("start", 2)], [("forward", 1), ("start", 3)]]
    moves += [[("forward", 2)], [("forward", 3)], [("start", 4), ("start", 5)], [("forward", 4)], [("forward", 5)]]

    def push():
        for name, index in moves.pop(0):
            getattr(pieces[index], name)()

    has_later, has_earlier = p.s < seqs - 1, p.s > 0
    order = far_first(p)

    def halo(slot):
        return remote(
            conv_grad.at[slot, pl.ds(0, 8)],
            conv_grad.at[slot, pl.ds(block, 8)],
            halo_send.at[slot],
            halo_recv.at[slot],
            p.peer(seqs - 1),
        )

    for slot in range(slots):

        @pl.when(jnp.logical_not(has_later))
        def _(slot=slot):
            conv_grad[slot, pl.ds(block, 8)] = jnp.zeros((8, channels), F32)

    taps_out[...] = jnp.zeros_like(taps_out)
    small[...] = jnp.zeros_like(small)
    small[1:2] = gain_mlp_ref[0:1]

    def first_pass(slot):
        for i in range(chips):
            span = pl.ds(i * tile, tile)
            mixed_grad = nt(rows[slot, span], out_full[...])
            grad = mixed_grad * gates[slot, 1, span]
            conv_grad[slot, span] = grad
            conv = 0.0
            for offset in range(taps):
                earlier = product[slot, pl.ds(8 + i * tile - offset, tile)]
                conv = conv + taps_ref[offset : offset + 1] * earlier
                taps_out[offset : offset + 1] += jnp.sum(grad * earlier, axis=0, keepdims=True)
            stacked[slot, span, pl.ds(channels, channels)] = (mixed_grad * conv).astype(BF)
            if i == 0:
                pl.when(has_earlier)(lambda: halo(slot).start())

    def second_pass(slot):
        pl.when(has_later)(lambda: halo(slot).wait_recv())
        for i in range(chips):
            span = pl.ds(i * tile, tile)
            grad = 0.0
            for offset in range(taps):
                grad = grad + taps_ref[offset : offset + 1] * conv_grad[slot, pl.ds(i * tile + offset, tile)]
            stacked[slot, span, pl.ds(0, channels)] = (grad * gates[slot, 2, span]).astype(BF)
            stacked[slot, span, pl.ds(2 * channels, channels)] = (grad * gates[slot, 0, span]).astype(BF)

    def third_pass(slot):
        for chip in order:
            span = pl.ds(chip * tile, tile)

            @pl.loop(0, width // wide_block)
            def _(i):
                cut = pl.ds(pl.multiple_of(i * wide_block, wide_block), wide_block)
                value = 0.0
                for k in range(3):
                    value = value + nt(stacked[slot, span, pl.ds(k * channels, channels)], in_full[k, cut])
                part[slot, span, cut] = value.astype(BF)

            sums[slot].give(chip)

    def finish_mlp(slot):
        def store(first, size, value):
            mlp_total[slot, pl.ds(first, size)] = value

        mlp_sums[slot].finish(store)

    def finish_grad(slot):
        def store(first, size, value):
            span = pl.ds(first, size)
            source = source_ref[slot, span].astype(F32)
            scale = lax.rsqrt(jnp.mean(source * source, axis=-1, keepdims=True) + EPS)
            unit = source * scale
            small[0:1] += jnp.sum(value * unit, axis=0, keepdims=True)
            scaled = value * gain_ref[...]
            grad_total[slot, span] = scale * (scaled - unit * jnp.mean(scaled * unit, axis=-1, keepdims=True))

        sums[slot].finish(store)

    def mine(owner):
        return pl.ds(pl.multiple_of(owner * channels, channels), channels)

    def small_sums():
        small[2 : 2 + taps, mine(p.m)] = taps_out[0:taps]
        along = [lax.rem(p.m + step, models) for step in range(1, models)]
        by_model[p.m] = small[:, mine(p.m)]
        copies = [
            remote(small.at[:, mine(peer)], by_model.at[p.m], mp_send.at[0, i], mp_recv.at[0, i], {"mp": peer})
            for i, peer in enumerate(along)
        ]
        for thing in copies:
            thing.start()
        for thing in copies:
            thing.wait()
        by_seq[p.s] = functools.reduce(lambda a, b: a + b, [by_model[i] for i in range(models)])
        copies = [
            remote(by_seq.at[p.s], by_seq.at[p.s], seq_send.at[step - 1], seq_recv.at[step - 1], p.peer(step))
            for step in range(1, seqs)
        ]
        for thing in copies:
            thing.start()
        for thing in copies:
            thing.wait()
        small_out[:, mine(p.m)] = functools.reduce(lambda a, b: a + b, [by_seq[i] for i in range(seqs)])
        copies = [
            remote(small_out.at[:, mine(p.m)], small_out.at[:, mine(p.m)], mp_send.at[1, i], mp_recv.at[1, i], {"mp": peer})
            for i, peer in enumerate(along)
        ]
        for thing in copies:
            thing.start()
        for thing in copies:
            thing.wait()

    def neighbours(act):
        act(p.sibling)
        pl.when(p.has_above)(lambda: act(p.above))
        pl.when(p.has_below)(lambda: act(p.below))

    def give_free(slot):
        mlp_sums[slot].drain()
        neighbours(
            lambda where: pl.semaphore_signal(free.at[slot], inc=1, device_id=where, device_id_type=MESH)
        )

    def take_free(slot):
        lines = (p.z + chips - 1) // chips + (2 * chips - 2 - p.z) // chips
        pl.semaphore_wait(free.at[slot], 1 + lines)

    def fetch_columns(index):
        return pltpu.make_async_copy(
            normed_rows.at[:, :, pl.ds(index * cols, cols)], columns.at[index % 2], cols_sem.at[index % 2]
        )

    steps_in = width // cols

    def in_step(index):
        fetch_columns(index).wait()
        value = 0.0
        for slot in range(slots):
            value = value + tn(columns[index % 2, slot], stacked[slot])
        for k in range(3):
            in_full[k, pl.ds(index * cols, cols)] = value[:, k * channels : (k + 1) * channels].astype(BF)
        if index + 2 < steps_in:
            fetch_columns(index + 2).start()

    def out_step():
        for first in range(0, width, wide_block):
            cut = pl.ds(first, wide_block)
            value = 0.0
            for slot in range(slots):
                value = value + tn(mixed[slot], rows[slot, :, cut])
            out_full[:, cut] = value.astype(BF)

    gathers[0].start()
    push()
    loads[0].wait()
    for chip in order:
        mlp_sums[0].give(chip)
    hops, next_rows = mlp_sums[0].rounds(), gathers[0].rounds()
    weave(hops[:-1], next_rows[:-1], [push] * 2)
    gathers[1].start()
    weave(hops[-1:], next_rows[-1:], [push])
    loads[1].wait()
    for chip in order:
        mlp_sums[1].give(chip)
    loads[2].wait()
    for thing in loads[2 + slots :]:
        thing.wait()
    gathers[0].arrived()
    push()
    fetch_columns(0).start()
    fetch_columns(1).start()
    mlp_hops, next_rows, hops = mlp_sums[1].rounds(), gathers[1].rounds(), sums[0].rounds()
    first_pass(0)
    push()
    finish_mlp(0)
    give_free(0)
    weave(mlp_hops[:1], next_rows[:1])
    second_pass(0)
    take_free(0)
    third_pass(0)
    weave(mlp_hops[1:], next_rows[1:], hops[:1], [push] * 2)
    loads[3].wait()
    gathers[1].arrived()
    first_pass(1)
    finish_mlp(1)
    give_free(1)
    hops[1]()
    second_pass(1)
    take_free(1)
    weave(hops[2:])
    third_pass(1)
    hops = sums[1].rounds()
    hops[0]()
    out_step()
    pieces[7].start()
    for index in range(steps_in):
        in_step(index)
    pieces[6].start()
    hops[1]()
    pieces[7].forward()
    pieces[6].forward()
    weave(hops[2:])
    finish_grad(0)
    finish_grad(1)
    last = [
        pltpu.make_async_copy(mlp_total, mlp_out, load.at[0]),
        pltpu.make_async_copy(grad_total, grad_out, load.at[1]),
    ]
    for thing in last:
        thing.start()
    small_sums()
    for thing in pieces:
        thing.finish()
    for thing in last:
        thing.wait()
    for thing in gathers + sums:
        thing.drain()
    for slot in range(slots):
        pl.when(has_earlier)(lambda slot=slot: halo(slot).wait_send())


def mixer_backward(
    seqs, models, low, mlp_part, source, gain, gain_mlp_part, taps, in_full, out_full, normed_rows, gates, product, mixed, pair_grad, down_grad
):
    slots, share, width = low.shape
    chips = models // 2
    block = share * models
    channels = out_full.shape[0]
    units = down_grad.shape[0]
    shard = width // seqs
    gots = 3 if seqs == 4 else seqs
    hbm = pl.BlockSpec(memory_space=pltpu.HBM)
    vmem = pl.BlockSpec(memory_space=pltpu.VMEM)
    shape = jax.ShapeDtypeStruct
    return pl.pallas_call(
        functools.partial(mixer_backward_kernel, seqs, models),
        out_shape=[
            shape((slots, share, width), F32),
            shape((slots, share, width), F32),
            shape((8, width), F32),
            shape((gots, 3, shard, channels), BF),
            shape((gots, channels, shard), BF),
            shape((gots, 2, shard, units), BF),
            shape((gots, units, shard), BF),
        ],
        in_specs=[hbm, hbm, vmem, vmem, vmem, vmem] + [hbm] * 8,
        out_specs=[hbm, hbm, vmem] + [hbm] * 4,
        scratch_shapes=[
            pltpu.VMEM((3, width, channels), BF),
            pltpu.VMEM((channels, width), BF),
            pltpu.VMEM((slots, block, width), BF),
            pltpu.VMEM((2, slots, block, 256), BF),
            pltpu.VMEM((slots, 3, block, channels), F32),
            pltpu.VMEM((slots, block + 8, channels), F32),
            pltpu.VMEM((slots, block, channels), BF),
            pltpu.VMEM((slots, block + 8, channels), F32),
            pltpu.VMEM((slots, block, 3 * channels), BF),
            pltpu.VMEM((slots, block, width), BF),
            pltpu.VMEM((slots, chips, share, width), BF),
            pltpu.VMEM((slots, chips + 1, share, width), BF),
            pltpu.VMEM((slots, share, width), F32),
            pltpu.VMEM((slots, share, width), F32),
            pltpu.VMEM((2, 2, 2, units // 4, shard), BF),
            pltpu.VMEM((4, 2, 2, shard // 4, units), BF),
            pltpu.VMEM((2, 2, 3, shard // 2, channels), BF),
            pltpu.VMEM((2, 2, channels // 2, shard), BF),
            pltpu.VMEM((8, channels), F32),
            pltpu.VMEM((8, width), F32),
            pltpu.VMEM((models, 8, channels), F32),
            pltpu.VMEM((seqs, 8, channels), F32),
            pltpu.SemaphoreType.DMA((2 * slots + 5,)),
            pltpu.SemaphoreType.DMA((2,)),
            pltpu.SemaphoreType.DMA((8, max(6, seqs - 1))),
            pltpu.SemaphoreType.DMA((8, max(6, seqs - 1))),
            pltpu.SemaphoreType.DMA((8, 3)),
            pltpu.SemaphoreType.DMA((slots,)),
            pltpu.SemaphoreType.DMA((slots,)),
            pltpu.SemaphoreType.REGULAR((slots,)),
            pltpu.SemaphoreType.DMA((2, models - 1)),
            pltpu.SemaphoreType.DMA((2, models - 1)),
            pltpu.SemaphoreType.DMA((seqs - 1,)),
            pltpu.SemaphoreType.DMA((seqs - 1,)),
            *gather_sems(slots, chips),
            *scatter_sems(2 * slots, chips),
        ],
        compiler_params=pltpu.CompilerParams(collective_id=3, has_side_effects=True, vmem_limit_bytes=VMEM_LIMIT),
    )(low, mlp_part, source, gain, gain_mlp_part, taps, in_full, out_full, normed_rows, gates, product, mixed, pair_grad, down_grad)


def local(
    hidden,
    cotangent,
    lengths,
    gain_mix,
    gain_mlp,
    conv_weight,
    mixer_in,
    mixer_out,
    gate_up,
    mlp_down,
):
    seqs, models = lax.axis_size("seq"), lax.axis_size("mp")
    seq_pos = lax.axis_index("seq")
    model_pos = lax.axis_index("mp")
    share = hidden.shape[1]
    channels = mixer_in.shape[2]
    taps = conv_weight.shape[0]
    local_taps = lax.dynamic_slice_in_dim(conv_weight, model_pos * channels, channels, 1)
    share_start = (seq_pos * models + model_pos) * share
    share_pos = share_start + jnp.arange(share, dtype=jnp.int32)
    mask = (share_pos[None, :] < lengths[:, None]).astype(F32)[:, :, None]
    top_low = (cotangent.astype(F32) * mask).astype(BF)
    (
        normed_rows,
        _,
        in_full,
        out_full,
        gates,
        product,
        mixed,
        middle,
        middle_grad,
        low,
        gain_mlp_part,
        mlp_part,
        _,
        pair_total,
        down_total,
    ) = forward(
        seqs,
        models,
        hidden,
        gain_mix[None],
        gain_mlp[None],
        top_low,
        local_taps,
        mixer_in,
        mixer_out,
        gate_up,
        mlp_down,
    )
    mlp_share, source_grad, small, in_got, out_got, pair_got, down_got = mixer_backward(
        seqs,
        models,
        low,
        mlp_part,
        hidden,
        gain_mix[None],
        gain_mlp_part,
        local_taps,
        in_full,
        out_full,
        normed_rows,
        gates,
        product,
        mixed,
        pair_total,
        down_total,
    )

    def total(got):
        return jnp.sum(got.astype(F32), axis=0)

    return (
        (mask * (middle + mlp_share)).astype(BF),
        source_grad + middle_grad,
        small[0],
        small[1],
        small[2 : 2 + taps],
        total(in_got),
        total(out_got),
        total(pair_got),
        total(down_got),
    )


def solution(mesh):
    placed = (
        P(None, ("seq", "mp"), None),
        P(None, ("seq", "mp"), None),
        P(),
        P(),
        P(),
        P(),
        P(None, "seq", "mp"),
        P("mp", "seq"),
        P(None, "seq", "mp"),
        P("mp", "seq"),
    )
    return jax.shard_map(
        local,
        mesh=mesh,
        in_specs=placed,
        out_specs=(
            P(None, ("seq", "mp"), None),
            P(None, ("seq", "mp"), None),
            P(),
            P(),
            P(),
            P(None, "seq", "mp"),
            P("mp", "seq"),
            P(None, "seq", "mp"),
            P("mp", "seq"),
        ),
        check_vma=False,
    )
```
